32 devices in a mesh: seq: 8 (over z, x), head: 4 (over y, core).
Axes of the slice: x: 2, y: 2, z: 4, core: 2. Of those that a mesh axis runs over, the one named last changes fastest.
Arguments:
- hidden_in: bfloat16 [4096, 1536], P('seq'), may hold values from -6 to 6
- seg_ids: int32 [4096], P('seq'), may hold values from 0 to 1, as said below
- out_cotangent: bfloat16 [4096, 1536], P('seq'), may hold values from -6 to 6
- norm_gain: float32 [2, 1536], replicated, may hold values from 0.1 to 1.9
- w_zx: bfloat16 [2, 1536, 2, 3072], P(None, None, None, 'head'), may hold values from -0.15625 to 0.15625
- w_bc: bfloat16 [2, 1536, 256], replicated, may hold values from -0.15625 to 0.15625
- w_dt: bfloat16 [2, 1536, 48], P(None, None, 'head'), may hold values from -0.15625 to 0.15625
- conv_x: float32 [2, 5, 3072], P(None, None, 'head'), may hold values from -3 to 3
- conv_bc: float32 [2, 5, 256], replicated, may hold values from -3 to 3
- dt_bias: float32 [2, 48], P(None, 'head'), may hold values from -8 to 0
- a_log: float32 [2, 48], P(None, 'head'), may hold values from -9 to 0
- skip_d: float32 [2, 48], P(None, 'head'), may hold values from 0.5 to 2
- gate_gain: float32 [2, 3072], P(None, 'head'), may hold values from 0.1 to 1.9
- w_out: bfloat16 [2, 3072, 1536], P(None, 'head'), may hold values from -0.109375 to 0.109375
Outputs:
- hidden_out: bfloat16 [4096, 1536], P('seq')
- grad_in: float32 [4096, 1536], P('seq')
- g_norm_gain: float32 [2, 1536], P(None, 'seq')
- g_w_zx: float32 [2, 1536, 2, 3072], P(None, 'seq', None, 'head')
- g_w_bc: float32 [2, 1536, 256], P(None, 'seq', 'head')
- g_w_dt: float32 [2, 1536, 48], P(None, 'seq', 'head')
- g_conv_x: float32 [2, 5, 3072], P(None, None, 'head')
- g_conv_bc: float32 [2, 5, 256], replicated
- g_dt_bias: float32 [2, 48], P(None, 'head')
- g_a_log: float32 [2, 48], P(None, 'head')
- g_skip_d: float32 [2, 48], P(None, 'head')
- g_gate_gain: float32 [2, 3072], P(None, 'head')
- g_w_out: float32 [2, 3072, 1536], P(None, 'head', 'seq')
The draws below stay inside these ranges and needn't reach their ends.
Inputs may be any that keep to these rules, and one draw needn't show every extreme that they name: `seg_ids`: 0 for the tokens of the first sequence and 1 for those of the second; never falling; the first token of the second sequence lies within the first or the last 512 tokens, at a place whose remainder modulo 512 is 3 to 509.
All inputs are finite; a program needn't handle non-finite values.
Results may differ from the reference program's by a relative error of at most 0.03.
The reference program's roundings to bfloat16 on the way (of `normed` and `scaled`) count: a program that leaves them out, or rounds other values in their place, can miss the bound.
Values may be sent and summed in bfloat16 or wider, within the bound.
A program may use at most 256 MiB of HBM per device.

```python
import jax
import jax.numpy as jnp
from jax import lax

D = 1536
NS = 128
HEADDIM = 64
DI = 3072
NH = 48
CONV = 4
BLOCK = 256
LAYERS = 2
TOK_DEV = 512
TOKENS = 4096


def head_speeds(key, slow_share):
    pick = jax.random.uniform(jax.random.fold_in(key, 11), (LAYERS, NH))
    slow_rate = jax.random.uniform(jax.random.fold_in(key, 12), (LAYERS, NH), minval=0.2, maxval=1.2) / TOKENS
    fast_rate = jax.random.uniform(jax.random.fold_in(key, 13), (LAYERS, NH), minval=1.0 / 60.0, maxval=1.0 / 25.0)
    decay_rate = jnp.where(pick < slow_share, slow_rate, fast_rate)
    step_size = 1.5 * jnp.sqrt(decay_rate)
    return (decay_rate, step_size)


def draw_dt_bias(key, part):
    slow_share = 0.5
    decay_rate, step_size = head_speeds(key, slow_share)
    key = jax.random.fold_in(key, 1)
    jitter = jax.random.uniform(key, (LAYERS, NH), minval=-0.1, maxval=0.1)
    return jnp.log(jnp.expm1(step_size)) + jitter


def draw_a_log(key, part):
    slow_share = 0.5
    decay_rate, step_size = head_speeds(key, slow_share)
    key = jax.random.fold_in(key, 2)
    jitter = jax.random.uniform(key, (LAYERS, NH), minval=-0.1, maxval=0.1)
    return jnp.log(decay_rate / step_size) + jitter


def draw_seg_ids(key, part):
    key = jax.random.fold_in(key, 3)
    side_key, place_key = jax.random.split(key)
    upper_side = jax.random.randint(side_key, (), 0, 2)
    offset = jax.random.randint(place_key, (), TOK_DEV // 4, TOK_DEV - CONV + 2)
    boundary = jnp.where(upper_side == 1, TOKENS - offset, offset)
    return (jnp.arange(TOKENS) >= boundary).astype(jnp.int32)


def block_levels(key, dims, shards, smallest, high):
    def one(dim, parts):
        heights = jax.random.uniform(jax.random.fold_in(jax.random.fold_in(key, 6), dim), (parts,), jnp.float32, smallest / len(shards), high / len(shards))
        return jnp.repeat(jnp.exp(heights), dims[dim] // parts).reshape((-1,) + (1,) * (len(dims) - dim - 1))

    level = one(*shards[0])
    for cut in shards[1:]:
        level = level * one(*cut)
    return level


def scatter_about(stream_key, dims, scale, reach, cuts=(), held_as=jnp.bfloat16):
    array = jax.random.normal(stream_key, dims, jnp.float32) * scale
    if len(cuts) > 0:
        array = block_levels(stream_key, dims, cuts, -0.22, 0.18) * array
    return jnp.clip(array, min=-reach, max=reach).astype(held_as)


def setup_inputs(seed: int = 0) -> dict:
    keys = jax.random.split(jax.random.key(seed), 15)
    return {
        "hidden_in": scatter_about(keys[0], (TOKENS, D), 1.0, 6.0, ((0, 8),)),
        "seg_ids": draw_seg_ids(jax.random.fold_in(keys[14], 71), 0),
        "out_cotangent": scatter_about(keys[2], (TOKENS, D), 1.0, 6.0, ((0, 8),)),
        "norm_gain": jnp.clip(1.0 + 0.18 * jax.random.normal(keys[3], (LAYERS, D), jnp.float32), 0.1, 1.9),
        "w_zx": scatter_about(keys[4], (LAYERS, D, 2, DI), D ** -0.5, 0.15625, ((3, 4),)),
        "w_bc": scatter_about(keys[5], (LAYERS, D, 2 * NS), D ** -0.5, 0.15625),
        "w_dt": scatter_about(keys[6], (LAYERS, D, NH), D ** -0.5, 0.15625, ((2, 4),)),
        "conv_x": scatter_about(keys[7], (LAYERS, CONV + 1, DI), 0.5, 3.0, ((2, 4),), jnp.float32),
        "conv_bc": scatter_about(keys[8], (LAYERS, CONV + 1, 2 * NS), 0.5, 3.0, (), jnp.float32),
        "dt_bias": draw_dt_bias(jax.random.fold_in(keys[14], 71), 0),
        "a_log": draw_a_log(jax.random.fold_in(keys[14], 71), 0),
        "skip_d": jnp.clip(0.5 + 1.5 * jax.random.uniform(keys[11], (LAYERS, NH), jnp.float32) ** block_levels(keys[11], (LAYERS, NH), ((1, 4),), -0.2, 0.2), 0.5, 2.0),
        "gate_gain": jnp.clip(1.0 + 0.18 * jax.random.normal(keys[12], (LAYERS, DI), jnp.float32), 0.1, 1.9),
        "w_out": scatter_about(keys[13], (LAYERS, DI, D), DI ** -0.5, 0.109375, ((1, 4),)),
    }


EPS = 1e-05
HIGH = lax.Precision.HIGHEST

@jax.custom_vjp
def low(v):
    return lax.optimization_barrier(v.astype(jnp.bfloat16)).astype(jnp.float32)

@jax.custom_vjp
def low_back(v):
    return v

def low_keep(v):
    return (low(v), None)

def low_pass(kept, grad):
    return (grad,)

def back_keep(v):
    return (v, None)

def back_low(kept, grad):
    return (low(grad),)
low.defvjp(low_keep, low_pass)
low_back.defvjp(back_keep, back_low)

def matmul(left, right):
    return jnp.dot(left, right, precision=HIGH, preferred_element_type=jnp.float32)

def block_step(carried, block_inputs):
    carry_state, seg_before = carried
    values, keys_b, reads_c, step_sizes, log_decay, segments = block_inputs
    cumulative = jnp.cumsum(log_decay, axis=0)
    gram_block = matmul(reads_c, keys_b.T)
    places = jnp.arange(BLOCK)
    keep_mask = (places[:, None] >= places[None, :]) & (segments[:, None] == segments[None, :])
    spread = cumulative.T[:, :, None] - cumulative.T[:, None, :]
    kernel = jnp.where(keep_mask[None], jnp.exp(jnp.minimum(spread, 0.0)), 0.0)
    mixing = kernel * gram_block[None] * step_sizes.T[:, None, :]
    inside_y = jnp.einsum('hqs,shp->qhp', mixing, values, precision=HIGH)
    entry_weight = jnp.where((segments == seg_before)[:, None], jnp.exp(cumulative), 0.0)
    carried_y = jnp.einsum('hpn,qn->qhp', carry_state, reads_c, precision=HIGH) * entry_weight[:, :, None]
    tail_weight = jnp.where((segments == segments[-1])[:, None], jnp.exp(cumulative[-1][None, :] - cumulative), 0.0) * step_sizes
    fresh_state = jnp.einsum('qh,qhp,qn->hpn', tail_weight, values, keys_b, precision=HIGH)
    block_decay = jnp.where(segments[-1] == seg_before, jnp.exp(cumulative[-1]), 0.0)
    next_state = block_decay[:, None, None] * carry_state + fresh_state
    return ((next_state, segments[-1]), inside_y + carried_y)

def conv_mix(joined, segments, taps):
    token_total = joined.shape[0]
    padded = jnp.concatenate([jnp.zeros((CONV - 1, joined.shape[1]), joined.dtype), joined], axis=0)
    seg_pad = jnp.concatenate([jnp.full((CONV - 1,), -1, jnp.int32), segments], axis=0)
    mixed = jnp.broadcast_to(taps[CONV][None, :], joined.shape)
    for shift_back in range(CONV):
        begin_at = CONV - 1 - shift_back
        matching = (seg_pad[begin_at:begin_at + token_total] == segments)[:, None]
        mixed = mixed + jnp.where(matching, padded[begin_at:begin_at + token_total] * taps[shift_back][None, :], 0.0)
    return mixed

def layer_ref(residual, segments, params):
    norm_scale, zx_weight, bc_weight, dt_weight, taps_x, taps_bc, dt_shift, log_rate, skip_gain, out_gain, out_weight = params
    inv_rms = lax.rsqrt(lax.optimization_barrier(jnp.mean(residual * residual, axis=1, keepdims=True)) + EPS)
    normed = low(residual * inv_rms * norm_scale[None, :])
    gate_z = low_back(low(matmul(normed, zx_weight[:, 0, :])))
    proj_x = low_back(low(matmul(normed, zx_weight[:, 1, :])))
    proj_bc = low_back(low(matmul(normed, bc_weight)))
    proj_dt = low_back(low(matmul(normed, dt_weight)))
    mixed = conv_mix(jnp.concatenate([proj_x, proj_bc], axis=1), segments, jnp.concatenate([taps_x, taps_bc], axis=1))
    conv_out = jax.nn.silu(mixed)
    values = conv_out[:, :DI].reshape(TOKENS, NH, HEADDIM)
    keys_b = conv_out[:, DI:DI + NS]
    reads_c = conv_out[:, DI + NS:]
    step_sizes = jax.nn.softplus(proj_dt + dt_shift[None, :])
    decay_rates = -jnp.exp(log_rate)
    log_decay = step_sizes * decay_rates[None, :]
    blocks = TOKENS // BLOCK
    start_state = jnp.zeros((NH, HEADDIM, NS), jnp.float32)
    inputs_all = (values.reshape(blocks, BLOCK, NH, HEADDIM), keys_b.reshape(blocks, BLOCK, NS), reads_c.reshape(blocks, BLOCK, NS), step_sizes.reshape(blocks, BLOCK, NH), log_decay.reshape(blocks, BLOCK, NH), segments.reshape(blocks, BLOCK))
    ignored, block_y = lax.scan(jax.checkpoint(block_step), (start_state, segments[0]), inputs_all)
    ssd_y = block_y.reshape(TOKENS, NH, HEADDIM) + skip_gain[None, :, None] * values
    gated = ssd_y.reshape(TOKENS, DI) * jax.nn.silu(gate_z)
    scaled = low(gated * lax.rsqrt(lax.optimization_barrier(jnp.mean(gated * gated, axis=1, keepdims=True)) + EPS) * out_gain[None, :])
    branch = low_back(matmul(scaled, out_weight))
    return residual + branch

def reference(hidden_in, seg_ids, out_cotangent, norm_gain, w_zx, w_bc, w_dt, conv_x, conv_bc, dt_bias, a_log, skip_d, gate_gain, w_out):
    weights_all = tuple((weight.astype(jnp.float32) for weight in (norm_gain, w_zx, w_bc, w_dt, conv_x, conv_bc, dt_bias, a_log, skip_d, gate_gain, w_out)))
    segments = seg_ids.astype(jnp.int32)

    def forward(hidden_state, weights):
        for layer_index in range(LAYERS):
            layer_params = tuple((weight[layer_index] for weight in weights))
            hidden_state = jax.checkpoint(layer_ref)(hidden_state, segments, layer_params)
        return hidden_state
    result, pull_back = jax.vjp(forward, hidden_in.astype(jnp.float32), weights_all)
    grad_in, grads = pull_back(out_cotangent.astype(jnp.float32))
    return (result.astype(jnp.bfloat16), grad_in, grads[0], grads[1], grads[2], grads[3], grads[4], grads[5], grads[6], grads[7], grads[8], grads[9], grads[10])
```

```python
from functools import partial

import jax
import jax.numpy as jnp
from jax import lax
from jax.experimental import pallas as pl
from jax.experimental.pallas import tpu as pltpu
from jax.sharding import PartitionSpec as P

CONV = 4
LAYERS = 2
EPS = 1e-05
F32 = jnp.float32
BF16 = jnp.bfloat16


def dot(a, b, dims):
    return lax.dot_general(a.astype(BF16), b.astype(BF16), (dims, ((), ())), preferred_element_type=F32)


def mm(a, b):
    return dot(a, b, ((1,), (0,)))


def mm_nt(a, b):
    return dot(a, b, ((1,), (1,)))


def mm_tn(a, b):
    return dot(a, b, ((0,), (0,)))


def swap(x, axis, bit):
    n = lax.axis_size(axis)
    return lax.ppermute(x, axis, [(i, i ^ bit) for i in range(n)])


def shift(x, axis, by):
    n = lax.axis_size(axis)
    return lax.ppermute(x, axis, [(i, i + by) for i in range(n) if 0 <= i + by < n])


def bits_of(axis):
    n = lax.axis_size(axis)
    bits = []
    b = 1
    while b < n:
        bits.append(b)
        b *= 2
    return bits


def my_bit(axis, bit):
    return (lax.axis_index(axis) // bit) % 2


def take(x, dim, index):
    return lax.dynamic_index_in_dim(x, index, dim, keepdims=False)


def head_scatter(x):
    for bit in bits_of("head"):
        me = my_bit("head", bit)
        halves = x.reshape((2, x.shape[0] // 2) + x.shape[1:])
        got = swap(take(halves, 0, 1 - me).astype(BF16), "head", bit)
        x = take(halves, 0, me).astype(F32) + got.astype(F32)
    return x


def head_scatter_exact(x):
    for bit in bits_of("head"):
        me = my_bit("head", bit)
        halves = x.reshape((2, x.shape[0] // 2) + x.shape[1:])
        x = take(halves, 0, me) + swap(take(halves, 0, 1 - me), "head", bit)
    return x


def head_gather(x):
    for bit in reversed(bits_of("head")):
        me = my_bit("head", bit)
        got = swap(x, "head", bit)
        x = jnp.where(me == 0, jnp.concatenate([x, got], 0), jnp.concatenate([got, x], 0))
    return x


def own_rows(x):
    for bit in bits_of("head"):
        x = take(x.reshape((2, x.shape[0] // 2) + x.shape[1:]), 0, my_bit("head", bit))
    return x


def carry_scan(state, decay, reverse):
    total, total_d = state, decay
    entering = jnp.zeros_like(state)
    enter_d = jnp.ones_like(decay)
    for bit in bits_of("seq"):
        me = my_bit("seq", bit)
        other = swap(total.astype(BF16), "seq", bit).astype(F32)
        other_d = swap(total_d, "seq", bit)
        second = (me == 0) if reverse else (me == 1)
        entering = jnp.where(second, entering + enter_d[:, None, None] * other, entering)
        enter_d = jnp.where(second, enter_d * other_d, enter_d)
        total = jnp.where(
            second, total_d[:, None, None] * other + total, other_d[:, None, None] * total + other
        )
        total_d = total_d * other_d
    return entering


def silu_slope(v):
    s = jax.nn.sigmoid(v)
    return s * (1.0 + v * (1.0 - s))


def scatter_rows(x):
    bits = bits_of("seq")
    k = len(bits)
    n = lax.axis_size("seq")
    x = x.reshape((2,) * k + (x.shape[0] // n, x.shape[1]))
    for b in range(k):
        axis = k - 1 - b
        me = my_bit("seq", bits[b])
        got = swap(take(x, axis, 1 - me).astype(BF16), "seq", bits[b])
        x = take(x, axis, me).astype(F32) + got.astype(F32)
    return x


HALO = 16
LANE = 128
NT = ((1,), (1,))
NN = ((1,), (0,))
TN = ((0,), (0,))


def bdot(a, b, dims):
    return lax.dot_general(a.astype(BF16), b.astype(BF16), (dims, ((), ())), preferred_element_type=F32)


def hdot(a, b, dims):
    return lax.dot_general(a, b, (dims, ((), ())), precision=lax.Precision.HIGHEST, preferred_element_type=F32)


def sig(v):
    return 0.5 * jnp.tanh(0.5 * v) + 0.5


def softplus(v):
    e = jnp.exp(-jnp.abs(v))
    s = e / (2.0 + e)
    q = s * s
    series = 1.0 / 13.0
    for k in (11, 9, 7, 5, 3, 1):
        series = series * q + 1.0 / k
    return jnp.maximum(v, 0.0) + 2.0 * s * series


def mix_taps(us, taps, aux, width):
    tokens = aux.shape[1]
    wide = lambda m: m if width == LANE else jnp.concatenate([m] * (width // LANE), axis=1)
    acc = us[pl.ds(HALO, tokens), :] * taps[0:1, :] + taps[CONV : CONV + 1, :]
    for j in range(1, CONV):
        acc = acc + us[pl.ds(HALO - j, tokens), :] * wide(aux[j - 1]) * taps[j : j + 1, :]
    return acc


def pick_lane(values, h, lanes):
    return jnp.sum(jnp.where(lanes == h, values, 0.0), axis=1, keepdims=True)


def fwd_mix_body(heads, size, nx, wzx, wbc, wdt, tapx, tapbc, dtb, lograte, skip, aux, segrow,
                 gate, ux, ubc, krs, pdt, steps_o, cum_o, cT, gram, mixed_o, ypart, entry_o, state, dec, decl,
                 us, usbc, cb):
    p = pl.program_id(0)
    tokens = aux.shape[1]
    states = wbc.shape[1] // 2
    lanes = lax.broadcasted_iota(jnp.int32, (tokens, LANE), 1)
    half = lanes < size

    @pl.when(p == 0)
    def _():
        bc = bdot(nx[...], wbc[...], NN).astype(BF16)
        ubc[...] = bc
        usbc[...] = bc.astype(F32)
        m = mix_taps(usbc, tapbc, aux, 2 * states)
        act = (m * sig(m)).astype(BF16)
        krs[...] = act
        g = bdot(act[:, states:], act[:, :states], NT)
        ii = lax.broadcasted_iota(jnp.int32, (tokens, tokens), 0)
        jj = lax.broadcasted_iota(jnp.int32, (tokens, tokens), 1)
        segc = jnp.concatenate([aux[5]] * (tokens // LANE), axis=1)
        keep = (ii >= jj) & (segc == segrow[...])
        gram[...] = jnp.where(keep, g, 0.0)
        pd = bdot(nx[pl.ds(HALO, tokens), :], wdt[...], NN).astype(BF16)
        pdt[...] = pd
        st = softplus(pd.astype(F32) + dtb[...])
        steps_o[...] = st
        log = st * -jnp.exp(lograte[...])
        cum = hdot(jnp.where(ii >= jj, 1.0, 0.0), log, NN)
        cum_o[...] = cum
        cT[...] = cum.T
        keeps = aux[3, tokens - 1 : tokens, :]
        decl[...] = jnp.broadcast_to(jnp.exp(cum[tokens - 1 : tokens, :]) * keeps, (8, LANE))
        dec[...] = jnp.exp(jnp.broadcast_to(cT[0:16, tokens - 1 : tokens], (16, LANE))) * keeps

    gate[...] = bdot(nx[pl.ds(HALO, tokens), :], wzx[0], NN).astype(BF16)
    u = bdot(nx[...], wzx[1], NN).astype(BF16)
    ux[...] = u
    us[...] = u.astype(F32)
    m = mix_taps(us, tapx, aux, LANE)
    mixed_o[...] = m
    v = m * sig(m)
    cum = cum_o[...]
    st = steps_o[...]
    h0 = p * (LANE // size)
    dd = jnp.where(half, pick_lane(st, h0, lanes), pick_lane(st, h0 + 1, lanes))
    vd = v * dd
    vdb = vd.astype(BF16)
    ys = []
    for k in range(LANE // size):
        h = h0 + k
        cb[k] = jnp.broadcast_to(pick_lane(cum, h, lanes), (tokens, LANE))
        row = cT[pl.ds(h, 1), :]
        parts = []
        for ib in range(tokens // LANE):
            tiles = []
            ci = cb[k, pl.ds(ib * LANE, LANE), :]
            for jb in range(ib + 1):
                spread = ci - row[:, jb * LANE : (jb + 1) * LANE]
                if jb == ib:
                    spread = jnp.minimum(spread, 0.0)
                tiles.append((jnp.exp(spread) * gram[pl.ds(ib * LANE, LANE), pl.ds(jb * LANE, LANE)]).astype(BF16))
            w = tiles[0] if ib == 0 else jnp.concatenate(tiles, axis=1)
            parts.append(bdot(w, vdb[: (ib + 1) * LANE], NN))
        ys.append(jnp.concatenate(parts, axis=0))
    y = jnp.where(half, ys[0], ys[1])
    ypart[...] = y + skip[...] * v
    ct = jnp.where(half, cb[0], cb[1])
    entry_o[...] = jnp.exp(ct) * aux[3]
    tail = jnp.exp(ct[tokens - 1 : tokens, :] - ct) * aux[4]
    state[...] = bdot(vd * tail, krs[:, :states], TN)


def full(shape):
    n = len(shape)
    return pl.BlockSpec(shape, lambda p: (0,) * n)


def cols(rows):
    return pl.BlockSpec((rows, LANE), lambda p: (0, p))


def rowsb(width):
    return pl.BlockSpec((LANE, width), lambda p: (p, 0))


VMEM_LIMIT = 56 * 1024 * 1024


def fwd_mix(heads, size, nx, wzx, wbc, wdt, tapx, tapbc, dtb, lograte, skip, aux, segrow):
    tokens = aux.shape[1]
    ext, d = nx.shape
    inner = wzx.shape[2]
    two = wbc.shape[1]
    S = jax.ShapeDtypeStruct
    return pl.pallas_call(
        partial(fwd_mix_body, heads, size),
        name="fwd_mix",
        grid=(inner // LANE,),
        in_specs=[full(nx.shape), pl.BlockSpec((2, d, LANE), lambda p: (0, 0, p)), full(wbc.shape), full(wdt.shape),
                  cols(tapx.shape[0]), full(tapbc.shape), full(dtb.shape), full(lograte.shape), cols(1),
                  full(aux.shape), full(segrow.shape)],
        out_specs=[cols(tokens), cols(ext), full((ext, two)), full((tokens, two)), full((tokens, LANE)), full((tokens, LANE)),
                   full((tokens, LANE)), full((LANE, tokens)), full((tokens, tokens)), cols(tokens), cols(tokens),
                   cols(tokens), rowsb(two // 2), full((16, LANE)), full((8, LANE))],
        out_shape=[S((tokens, inner), BF16), S((ext, inner), BF16), S((ext, two), BF16), S((tokens, two), BF16),
                   S((tokens, LANE), BF16), S((tokens, LANE), F32), S((tokens, LANE), F32), S((LANE, tokens), F32),
                   S((tokens, tokens), F32), S((tokens, inner), F32), S((tokens, inner), F32), S((tokens, inner), F32),
                   S((inner, two // 2), F32), S((16, LANE), F32), S((8, LANE), F32)],
        scratch_shapes=[pltpu.VMEM((ext, LANE), F32), pltpu.VMEM((ext, two), F32), pltpu.VMEM((2, tokens, LANE), F32)],
        compiler_params=pltpu.CompilerParams(vmem_limit_bytes=VMEM_LIMIT),
        cost_estimate=pl.CostEstimate(flops=2 * ext * d * (2 * inner + two) + 6 * tokens * tokens * inner,
                                      bytes_accessed=4 * d * inner + 16 * tokens * inner, transcendentals=tokens * tokens * heads),
    )(nx, wzx, wbc, wdt, tapx, tapbc, dtb, lograte, skip, aux, segrow)


def fwd_gate_body(ypart, entry, gate, krs, enter, y, carr, gated, sq, sqacc):
    p = pl.program_id(0)
    states = krs.shape[1] // 2
    c = bdot(krs[:, states:], enter[...], NT) * entry[...]
    carr[...] = c
    yy = ypart[...] + c
    y[...] = yy
    z = gate[...].astype(F32)
    g = yy * (z * sig(z))
    gated[...] = g

    @pl.when(p == 0)
    def _():
        sqacc[...] = g * g

    @pl.when(p > 0)
    def _():
        sqacc[...] += g * g

    @pl.when(p == pl.num_programs(0) - 1)
    def _():
        sq[...] = jnp.broadcast_to(jnp.sum(jnp.transpose(sqacc[...]), axis=0, keepdims=True), sq.shape)


def fwd_gate(ypart, entry, gate, krs, enter):
    tokens, inner = ypart.shape
    S = jax.ShapeDtypeStruct
    return pl.pallas_call(
        fwd_gate_body,
        name="fwd_gate",
        grid=(inner // LANE,),
        in_specs=[cols(tokens), cols(tokens), cols(tokens), full(krs.shape), rowsb(enter.shape[1])],
        out_specs=[cols(tokens), cols(tokens), cols(tokens), full((8, tokens))],
        scratch_shapes=[pltpu.VMEM((tokens, LANE), F32)],
        out_shape=[S((tokens, inner), F32)] * 3 + [S((8, tokens), F32)],
        compiler_params=pltpu.CompilerParams(vmem_limit_bytes=VMEM_LIMIT),
        cost_estimate=pl.CostEstimate(flops=2 * tokens * inner * LANE, bytes_accessed=26 * tokens * inner, transcendentals=tokens * inner),
    )(ypart, entry, gate, krs, enter)


def bwd_gate_body(gb, wout, gate, y, mixed, entry, krs, r2b, krb, gain, gy_o, gz_o, scaled_o, qloc, ggate, gskip):
    states = krs.shape[1] // 2
    gs = bdot(gb[...], wout[...], NT)
    z = gate[...].astype(F32)
    s = sig(z)
    sil = z * s
    yy = y[...]
    gated = yy * sil
    r2 = r2b[...]
    gr = gated * r2
    ggate[...] = jnp.sum(gs * gr, axis=0, keepdims=True)
    scaled_o[...] = (gr * gain[...]).astype(BF16)
    gg = r2 * gain[...] * gs - gated * krb[...]
    gy = gg * sil
    gy_o[...] = gy
    gz_o[...] = (gg * yy * (s * (1.0 + z * (1.0 - s)))).astype(BF16)
    m = mixed[...]
    gskip[...] = jnp.sum(gy * (m * sig(m)), axis=0, keepdims=True)
    qloc[...] = bdot(gy * entry[...], krs[:, states:], TN)


def bwd_gate(gb, wout, gate, y, mixed, entry, krs, r2b, krb, gain):
    tokens, inner = y.shape
    d = gb.shape[1]
    states = krs.shape[1] // 2
    S = jax.ShapeDtypeStruct
    return pl.pallas_call(
        bwd_gate_body,
        name="bwd_gate",
        grid=(inner // LANE,),
        in_specs=[full(gb.shape), rowsb(d), cols(tokens), cols(tokens), cols(tokens), cols(tokens), full(krs.shape),
                  full(r2b.shape), full(krb.shape), cols(1)],
        out_specs=[cols(tokens), cols(tokens), cols(tokens), rowsb(states), cols(1), cols(1)],
        out_shape=[S((tokens, inner), F32), S((tokens, inner), BF16), S((tokens, inner), BF16), S((inner, states), F32),
                   S((1, inner), F32), S((1, inner), F32)],
        compiler_params=pltpu.CompilerParams(vmem_limit_bytes=VMEM_LIMIT),
        cost_estimate=pl.CostEstimate(flops=2 * tokens * inner * d, bytes_accessed=26 * tokens * inner + 2 * d * inner, transcendentals=2 * tokens * inner),
    )(gb, wout, gate, y, mixed, entry, krs, r2b, krb, gain)


def bwd_local_body(size, gy_r, mixed, krs, cum, steps, cT, gram, entry, enter, segc, segrow,
                   dvd, dd_o, rowT, dkr, cb, db, gramT, dgT, vb, gk):
    p = pl.program_id(0)
    tokens = gy_r.shape[0]
    states = krs.shape[1] // 2
    lanes = lax.broadcasted_iota(jnp.int32, (tokens, LANE), 1)
    half = lanes < size

    @pl.when(p == 0)
    def _():
        gramT[...] = gram[...].T
        dgT[...] = jnp.zeros_like(dgT)
        dd_o[...] = jnp.zeros_like(dd_o)
        rowT[...] = jnp.zeros_like(rowT)
        dkr[...] = jnp.zeros_like(dkr)

    m = mixed[...]
    vb[...] = (m * sig(m)).astype(BF16)
    gy = gy_r[...]
    gyb = gy.astype(BF16)
    h0 = p * (LANE // size)
    outs = []
    for k in range(LANE // size):
        h = h0 + k
        gk[...] = jnp.where(half if k == 0 else jnp.logical_not(half), gy, 0.0).astype(BF16)
        cb[...] = jnp.broadcast_to(pick_lane(cum[...], h, lanes), (tokens, LANE))
        db[...] = jnp.broadcast_to(pick_lane(steps[...], h, lanes), (tokens, LANE))
        row = cT[pl.ds(h, 1), :]
        parts = []
        dds = []
        rows_acc = [jnp.zeros((8, LANE), F32) for _ in range(tokens // LANE)]
        for jb in range(tokens // LANE):
            js = pl.ds(jb * LANE, LANE)
            cj = cb[js, :]
            dj = db[js, :]
            pt = bdot(vb[js, :], gk[pl.ds(jb * LANE, tokens - jb * LANE), :], NT)
            ws = []
            dsum = None
            for ib in range(jb, tokens // LANE):
                sl = pl.ds(ib * LANE, LANE)
                spread = row[:, ib * LANE : (ib + 1) * LANE] - cj
                if jb == ib:
                    spread = jnp.minimum(spread, 0.0)
                e = jnp.exp(spread)
                w = e * gramT[js, sl]
                ws.append(w.astype(BF16))
                pp = pt[:, (ib - jb) * LANE : (ib - jb + 1) * LANE]
                wp = w * pp
                dgT[js, sl] += e * (pp * dj)
                x = wp * dj
                rows_acc[ib] = rows_acc[ib] + jnp.sum(x.reshape(LANE // 8, 8, LANE), axis=0)
                dsum = wp if dsum is None else dsum + wp
            dds.append(jnp.sum(dsum, axis=1, keepdims=True))
            w = ws[0] if len(ws) == 1 else jnp.concatenate(ws, axis=1)
            parts.append(bdot(w, gyb[jb * LANE :], NN))
        outs.append(jnp.concatenate(parts, axis=0))
        dd_o[...] += jnp.where(lanes == h, jnp.concatenate(dds, axis=0), 0.0)
        rowT[pl.ds(h, 1), :] = jnp.concatenate([jnp.sum(r, axis=0, keepdims=True) for r in rows_acc], axis=1)
    dvd[...] = jnp.where(half, outs[0], outs[1])
    dkr[:, states:] += bdot(gy * entry[...], enter[...], NN)

    @pl.when(p == pl.num_programs(0) - 1)
    def _():
        jj = lax.broadcasted_iota(jnp.int32, (tokens, tokens), 0)
        ii = lax.broadcasted_iota(jnp.int32, (tokens, tokens), 1)
        segs = jnp.concatenate([segc[...]] * (tokens // LANE), axis=1)
        g = jnp.where((ii >= jj) & (segs == segrow[...]), dgT[...], 0.0)
        dkr[:, :states] += bdot(g, krs[:, states:], NN)
        dkr[:, states:] += bdot(g, krs[:, :states], TN)


def bwd_local(size, gy, mixed, krs, cum, steps, cT, gram, entry, enter, segc, segrow):
    tokens, inner = gy.shape
    two = krs.shape[1]
    S = jax.ShapeDtypeStruct
    return pl.pallas_call(
        partial(bwd_local_body, size),
        name="bwd_local",
        grid=(inner // LANE,),
        in_specs=[cols(tokens), cols(tokens), full(krs.shape), full(cum.shape), full(steps.shape), full(cT.shape), full(gram.shape),
                  cols(tokens), rowsb(two // 2), full(segc.shape), full(segrow.shape)],
        out_specs=[cols(tokens), full((tokens, LANE)), full((LANE, tokens)), full((tokens, two))],
        out_shape=[S((tokens, inner), F32), S((tokens, LANE), F32), S((LANE, tokens), F32), S((tokens, two), F32)],
        scratch_shapes=[pltpu.VMEM((tokens, LANE), F32), pltpu.VMEM((tokens, LANE), F32), pltpu.VMEM((tokens, tokens), F32),
                        pltpu.VMEM((tokens, tokens), F32), pltpu.VMEM((tokens, LANE), BF16), pltpu.VMEM((tokens, LANE), BF16)],
        compiler_params=pltpu.CompilerParams(vmem_limit_bytes=VMEM_LIMIT),
        cost_estimate=pl.CostEstimate(flops=12 * tokens * tokens * inner, bytes_accessed=20 * tokens * inner, transcendentals=tokens * tokens * inner // size),
    )(gy, mixed, krs, cum, steps, cT, gram, entry, enter, segc, segrow)


def bwd_carry_body(size, gy_r, dvd_r, mixed, carr, entry, krs, cum, steps, pdt, dtb, lograte, skip, ux, tapx, aux, later, enter,
                   dd_r, rowT, dkr_r, decay,
                   gm_o, gu_o, gtail_o, gtaps, gdt_o, gvec, dkr, us, ms, ddacc, dcum, last):
    p = pl.program_id(0)
    tokens = gy_r.shape[0]
    states = krs.shape[1] // 2
    lanes = lax.broadcasted_iota(jnp.int32, (tokens, LANE), 1)
    lane1 = lax.broadcasted_iota(jnp.int32, (1, LANE), 1)
    half = lanes < size

    @pl.when(p == 0)
    def _():
        ddacc[...] = dd_r[...]
        dcum[...] = jnp.transpose(rowT[...]) - dd_r[...] * steps[...]
        last[...] = jnp.zeros_like(last)
        dkr[...] = dkr_r[...]

    h0 = p * (LANE // size)
    st = steps[...]
    cu = cum[...]
    cc = [pick_lane(cu, h0 + k, lanes) for k in range(2)]
    dcol = [pick_lane(st, h0 + k, lanes) for k in range(2)]
    ct = jnp.where(half, cc[0], cc[1])
    dpair = jnp.where(half, dcol[0], dcol[1])
    tail = jnp.exp(ct[tokens - 1 : tokens, :] - ct) * aux[4]
    m = mixed[...]
    s = sig(m)
    v = m * s
    gy = gy_r[...]
    qk = bdot(krs[:, :states], later[...], NT) * tail
    dvd = dvd_r[...] + qk
    dkr[:, :states] += bdot(v * dpair * tail, later[...], NN)
    tq = v * qk
    eq = gy * carr[...]
    qs = later[...] * enter[...]
    for k in range(2):
        h = h0 + k
        mine = half if k == 0 else jnp.logical_not(half)
        td = jnp.sum(jnp.where(mine, tq, 0.0), axis=1, keepdims=True)
        ec = jnp.sum(jnp.where(mine, eq, 0.0), axis=1, keepdims=True)
        tdd = td * dcol[k]
        ddacc[...] += jnp.where(lanes == h, td, 0.0)
        dcum[...] += jnp.where(lanes == h, ec - tdd, 0.0)
        dot_qs = jnp.sum(jnp.sum(qs[k * size : (k + 1) * size, :], axis=0, keepdims=True), axis=1, keepdims=True)
        last[...] += jnp.where(lane1 == h, jnp.sum(tdd, axis=0, keepdims=True) + dot_qs * decay[...], 0.0)
    dv = dvd * dpair + skip[...] * gy
    gm = dv * (s * (1.0 + m * (1.0 - s)))
    gm_o[...] = gm[:8]
    us[...] = ux[...].astype(F32)
    acc = gm * tapx[0:1, :]
    gtaps[0:1, :] = jnp.sum(gm * us[pl.ds(HALO, tokens), :], axis=0, keepdims=True)
    gtaps[CONV : CONV + 1, :] = jnp.sum(gm, axis=0, keepdims=True)
    ms[pl.ds(tokens, 8), :] = jnp.zeros((8, LANE), F32)
    for j in range(1, CONV):
        gmj = gm * aux[j - 1]
        gtaps[j : j + 1, :] = jnp.sum(gmj * us[pl.ds(HALO - j, tokens), :], axis=0, keepdims=True)
        ms[pl.ds(0, tokens), :] = gmj
        acc = acc + ms[pl.ds(j, tokens), :] * tapx[j : j + 1, :]
    gu_o[...] = acc.astype(BF16)
    gtail_o[...] = acc[tokens - 16 :]

    @pl.when(p == pl.num_programs(0) - 1)
    def _():
        ii = lax.broadcasted_iota(jnp.int32, (tokens, tokens), 0)
        jj = lax.broadcasted_iota(jnp.int32, (tokens, tokens), 1)
        dlog = hdot(jnp.where(jj >= ii, 1.0, 0.0), dcum[...], NN) + last[...]
        rates = -jnp.exp(lograte[...])
        dsteps = ddacc[...] + rates * dlog
        gdt = dsteps * sig(pdt[...].astype(F32) + dtb[...])
        gdt_o[...] = gdt.astype(BF16)
        gvec[0:1, :] = jnp.sum(gdt, axis=0, keepdims=True)
        gvec[1:2, :] = jnp.sum(st * dlog, axis=0, keepdims=True) * rates


def bwd_carry(size, gy, dvd, mixed, carr, entry, krs, cum, steps, pdt, dtb, lograte, skip, ux, tapx, aux, later, enter, dd, rowT, dkr, decay):
    tokens, inner = gy.shape
    ext = ux.shape[0]
    two = krs.shape[1]
    S = jax.ShapeDtypeStruct
    return pl.pallas_call(
        partial(bwd_carry_body, size),
        name="bwd_carry",
        grid=(inner // LANE,),
        in_specs=[cols(tokens), cols(tokens), cols(tokens), cols(tokens), cols(tokens), full(krs.shape), full(cum.shape), full(steps.shape),
                  full(pdt.shape), full(dtb.shape), full(lograte.shape), cols(1), cols(ext), cols(tapx.shape[0]), full(aux.shape),
                  rowsb(two // 2), rowsb(two // 2), full(dd.shape), full(rowT.shape), full(dkr.shape), full(decay.shape)],
        out_specs=[cols(8), cols(tokens), cols(16), cols(8), full((tokens, LANE)), full((8, LANE)), full((tokens, two))],
        out_shape=[S((8, inner), F32), S((tokens, inner), BF16), S((16, inner), F32), S((8, inner), F32), S((tokens, LANE), BF16),
                   S((8, LANE), F32), S((tokens, two), F32)],
        scratch_shapes=[pltpu.VMEM((ext, LANE), F32), pltpu.VMEM((tokens + 8, LANE), F32), pltpu.VMEM((tokens, LANE), F32),
                        pltpu.VMEM((tokens, LANE), F32), pltpu.VMEM((1, LANE), F32)],
        compiler_params=pltpu.CompilerParams(vmem_limit_bytes=VMEM_LIMIT),
        cost_estimate=pl.CostEstimate(flops=4 * tokens * inner * LANE, bytes_accessed=24 * tokens * inner, transcendentals=2 * tokens * inner),
    )(gy, dvd, mixed, carr, entry, krs, cum, steps, pdt, dtb, lograte, skip, ux, tapx, aux, later, enter, dd, rowT, dkr, decay)


MESH = pl.DeviceIdType.MESH
SUBS = 2


def greet(partners):
    barrier = pltpu.get_barrier_semaphore()
    for where in partners:
        pl.semaphore_signal(barrier, inc=1, device_id=where, device_id_type=MESH)
    pl.semaphore_wait(barrier, len(partners))


def send(src, dst, sems, where):
    copy = pltpu.make_async_remote_copy(
        src_ref=src, dst_ref=dst, send_sem=sems[0], recv_sem=sems[1], device_id=where, device_id_type=MESH)
    copy.start()
    return copy


def flip(me, bit):
    return me + bit * (1 - 2 * ((me // bit) % 2))


def carry_body(bits, reverse, heads, size, st, dec, out, tx, rx, dtx, drx, tot, ssem, rsem):
    me = lax.axis_index("seq")
    wheres = [{"seq": flip(me, b)} for b in bits]
    greet(wheres)
    enter_d = jnp.ones_like(dec[...])
    total_d = dec[...]
    for i, b in enumerate(bits):
        src = st if i == 0 else tot
        tx[...] = src[...].astype(BF16)
        dtx[...] = total_d
        one = send(tx, rx.at[i], (ssem.at[2 * i], rsem.at[2 * i]), wheres[i])
        two = send(dtx, drx.at[i], (ssem.at[2 * i + 1], rsem.at[2 * i + 1]), wheres[i])
        bit = (me // b) % 2
        second = (1 - bit) if reverse else bit
        two.wait()
        other_d = drx[i]
        one.wait()
        keep = second.astype(F32)
        for h in range(heads):
            rows = pl.ds(h * size, size)
            other = rx[i, rows, :].astype(F32)
            add = other * (enter_d[h : h + 1] * keep)
            if i == 0:
                out[rows, :] = add
            else:
                out[rows, :] += add
            if i + 1 < len(bits):
                mine = src[rows, :]
                a = jnp.where(second == 1, total_d[h : h + 1], 1.0)
                c = jnp.where(second == 1, 1.0, other_d[h : h + 1])
                tot[rows, :] = a * other + c * mine
        enter_d = jnp.where(second == 1, enter_d * other_d, enter_d)
        total_d = total_d * other_d


def carry_kernel(state, dec, heads, size, reverse, cid):
    bits = bits_of("seq")
    rows, states = state.shape
    n = len(bits)
    return pl.pallas_call(
        partial(carry_body, bits, reverse, heads, size),
        name="carry_back" if reverse else "carry_on",
        in_specs=[pl.BlockSpec(memory_space=pltpu.VMEM)] * 2,
        out_specs=pl.BlockSpec(memory_space=pltpu.VMEM),
        out_shape=jax.ShapeDtypeStruct((rows, states), F32),
        scratch_shapes=[pltpu.VMEM((rows, states), BF16), pltpu.VMEM((n, rows, states), BF16), pltpu.VMEM(dec.shape, F32),
                        pltpu.VMEM((n,) + dec.shape, F32), pltpu.VMEM((rows, states), F32),
                        pltpu.SemaphoreType.DMA((2 * n,)), pltpu.SemaphoreType.DMA((2 * n,))],
        compiler_params=pltpu.CompilerParams(collective_id=cid, has_side_effects=True, vmem_limit_bytes=VMEM_LIMIT),
    )(state, dec)


def head_core(tokens, part, middle, nx, off, side, tx0, rx0, tx1, rx1, acc, ssem, rsem, me, core_at, y_at):
    quarter = tokens // 4
    sub = quarter // SUBS
    c = me % 2
    y = me // 2
    half = 2 * quarter
    other_y = pl.multiple_of((1 - y) * quarter, quarter)
    own_y = pl.multiple_of(y * quarter, quarter)
    n = 0
    sends = []

    def go(src, dst, where):
        nonlocal n
        copy = send(src, dst, (ssem.at[n], rsem.at[n]), where)
        sends.append(copy)
        n += 1
        return copy

    acc[...] = part(pl.multiple_of((1 - c) * half, half), half)
    first = []
    for i, base in enumerate((other_y, own_y)):
        for s in range(SUBS):
            tx0[i, s] = acc[pl.ds(pl.multiple_of(base + s * sub, sub), sub), :].astype(BF16)
            first.append(go(tx0.at[i, s], rx0.at[i, s], core_at))
    acc[...] = part(pl.multiple_of(c * half, half), half)
    second = []
    for s in range(SUBS):
        first[s].wait_recv()
        tx1[s] = (acc[pl.ds(pl.multiple_of(other_y + s * sub, sub), sub), :] + rx0[0, s].astype(F32)).astype(BF16)
        second.append(go(tx1.at[s], rx1.at[s], y_at))
    own = (c * 2 + y) * quarter
    theirs = (c * 2 + 1 - y) * quarter
    to_y, to_core, onward = [], [], []
    for s in range(SUBS):
        first[SUBS + s].wait_recv()
        second[s].wait_recv()
        total = acc[pl.ds(pl.multiple_of(own_y + s * sub, sub), sub), :] + rx0[1, s].astype(F32) + rx1[s].astype(F32)
        rows = pl.ds(pl.multiple_of(off + own + s * sub, 16), sub)
        nx[rows, :] = middle(s, sub, total)
        to_y.append(go(nx.at[rows, :], nx.at[rows, :], y_at))
        to_core.append(go(nx.at[rows, :], nx.at[rows, :], core_at))
    if side is not None:
        srows = pl.ds(pl.multiple_of((c * 2 + y) * 8, 8), 8)
        to_y.append(go(side.at[srows, :], side.at[srows, :], y_at))
        to_core.append(go(side.at[srows, :], side.at[srows, :], core_at))
    for s in range(SUBS):
        to_y[s].wait_recv()
        rows = pl.ds(pl.multiple_of(off + theirs + s * sub, 16), sub)
        onward.append(go(nx.at[rows, :], nx.at[rows, :], core_at))
    if side is not None:
        to_y[SUBS].wait_recv()
        srows = pl.ds(pl.multiple_of((c * 2 + 1 - y) * 8, 8), 8)
        onward.append(go(side.at[srows, :], side.at[srows, :], core_at))
    for copy in to_core + onward:
        copy.wait_recv()
    for copy in sends:
        copy.wait_send()


HEAD_COPIES = 3 * SUBS + 3 * SUBS + 3


def head_fwd_body(tokens, last, width, gated, sq, ggain, wout, h_own, extra,
                  nx, h_new, branch, r2b, side, sqrx, tx0, rx0, tx1, rx1, acc, krc, ssem, rsem, qs, qr, hs, hr):
    me = lax.axis_index("head")
    at = lax.axis_index("seq")
    count = lax.axis_size("seq")
    peers = [lax.rem(me + k, 4) for k in (1, 2, 3)]
    barrier = pltpu.get_barrier_semaphore()
    for pr in peers:
        pl.semaphore_signal(barrier, inc=1, device_id={"head": pr}, device_id_type=MESH)
    if not last:
        @pl.when(at > 0)
        def _():
            pl.semaphore_signal(barrier, inc=1, device_id={"seq": at - 1}, device_id_type=MESH)
    if last:
        pl.semaphore_wait(barrier, 3)
    else:
        pl.semaphore_wait(barrier, 3 + (at < count - 1).astype(jnp.int32))
    copies = [send(sq, sqrx.at[2 - k], (qs.at[k], qr.at[2 - k]), {"head": pr}) for k, pr in enumerate(peers)]
    for copy in copies:
        copy.wait_send()
    for k in range(3):
        pltpu.make_async_remote_copy(src_ref=sq, dst_ref=sqrx.at[k], send_sem=qs.at[k], recv_sem=qr.at[k],
                                     device_id={"head": peers[2 - k]}, device_id_type=MESH).wait_recv()
    total_sq = ((sq[...] + sqrx[0]) + (sqrx[1] + sqrx[2]))[0:1, :]
    r2row = lax.rsqrt(total_sq / width + EPS)
    r2b[...] = jnp.transpose(jnp.broadcast_to(r2row, (LANE, tokens)))
    inner = gated.shape[1]

    def part(start, rows):
        where = pl.ds(start, rows)
        r2 = jnp.concatenate([r2b[where, :]] * (inner // LANE), axis=1)
        return bdot(gated[where, :] * r2 * ggain[...], wout[...], NN)

    d = wout.shape[1]

    def middle(s, sub, total):
        rows = pl.ds(s * sub, sub)
        branch[rows, :] = total
        h = h_own[rows, :] + total
        h_new[rows, :] = h
        if last:
            krc[rows, :] = jnp.broadcast_to(jnp.sum(extra[rows, :].astype(F32) * total, axis=1, keepdims=True), (sub, LANE))
            if s == SUBS - 1:
                mine = pl.ds(pl.multiple_of(((me % 2) * 2 + me // 2) * 8, 8), 8)
                side[mine, :] = jnp.transpose(krc[...])[0:8, :]
            return h.astype(BF16)
        r1 = lax.rsqrt(jnp.sum(h * h, axis=1, keepdims=True) / d + EPS)
        return (h * r1 * extra[...]).astype(BF16)

    off = 0 if last else HALO
    if not last:
        side[...] = jnp.zeros_like(side)
    head_core(tokens, part, middle, nx, off, side if last else None, tx0, rx0, tx1, rx1, acc, ssem, rsem, me,
              {"head": flip(me, 1)}, {"head": flip(me, 2)})
    if not last:
        src = nx.at[pl.ds(tokens, HALO), :]
        dst = nx.at[pl.ds(0, HALO), :]
        copy = pltpu.make_async_remote_copy(src_ref=src, dst_ref=dst, send_sem=hs.at[0], recv_sem=hr.at[0],
                                            device_id={"seq": lax.rem(at + 1, count)}, device_id_type=MESH)

        @pl.when(at < count - 1)
        def _():
            copy.start()
            copy.wait_send()

        @pl.when(at > 0)
        def _():
            copy.wait_recv()

        @pl.when(at == 0)
        def _():
            nx[pl.ds(0, HALO), :] = jnp.zeros((HALO, d), BF16)


def head_scratch(tokens, d):
    sub = tokens // 4 // SUBS
    return [pltpu.VMEM((2, SUBS, sub, d), BF16), pltpu.VMEM((2, SUBS, sub, d), BF16), pltpu.VMEM((SUBS, sub, d), BF16),
            pltpu.VMEM((SUBS, sub, d), BF16), pltpu.VMEM((tokens // 2, d), F32), pltpu.VMEM((tokens // 4, LANE), F32),
            pltpu.SemaphoreType.DMA((HEAD_COPIES,)), pltpu.SemaphoreType.DMA((HEAD_COPIES,))]


def head_fwd(gated, sq, ggain, wout, h_own, extra, last, width, cid):
    tokens, inner = gated.shape
    d = wout.shape[1]
    S = jax.ShapeDtypeStruct
    vm = pl.BlockSpec(memory_space=pltpu.VMEM)
    return pl.pallas_call(
        partial(head_fwd_body, tokens, last, width),
        name="head_fwd_last" if last else "head_fwd",
        in_specs=[vm] * 6,
        out_specs=[vm] * 5,
        out_shape=[S((tokens if last else tokens + HALO, d), BF16), S((tokens // 4, d), F32), S((tokens // 4, d), F32),
                   S((tokens, LANE), F32), S((32, LANE), F32)],
        scratch_shapes=[pltpu.VMEM((3, 8, tokens), F32)] + head_scratch(tokens, d)
        + [pltpu.SemaphoreType.DMA((3,)), pltpu.SemaphoreType.DMA((3,)), pltpu.SemaphoreType.DMA((1,)), pltpu.SemaphoreType.DMA((1,))],
        compiler_params=pltpu.CompilerParams(collective_id=cid, has_side_effects=True, vmem_limit_bytes=VMEM_LIMIT),
    )(gated, sq, ggain, wout, h_own, extra)


def head_bwd_body(tokens, gz, gu, small, wzx, wsmall, h_own, gain, g_own, branch,
                  gb, g_new, ggain, side, tx0, rx0, tx1, rx1, acc, krc, ssem, rsem):
    me = lax.axis_index("head")
    core_at, y_at = {"head": flip(me, 1)}, {"head": flip(me, 2)}
    greet([core_at, y_at])
    d = gain.shape[1]

    def part(start, rows):
        where = pl.ds(start, rows)
        return bdot(gz[where, :], wzx[0], NT) + bdot(gu[where, :], wzx[1], NT) + bdot(small[where, :], wsmall[...], NT)

    def middle(s, sub, total):
        rows = pl.ds(s * sub, sub)
        h = h_own[rows, :]
        r1 = lax.rsqrt(jnp.sum(h * h, axis=1, keepdims=True) / d + EPS)
        th = total * h
        gg = jnp.sum(th * r1, axis=0, keepdims=True)
        if s == 0:
            ggain[...] = gg
        else:
            ggain[...] += gg
        k1 = jnp.sum(th * gain[...], axis=1, keepdims=True)
        g = g_own[rows, :] + r1 * (gain[...] * total) - h * (r1 * r1 * r1 * (k1 / d))
        g_new[rows, :] = g
        low = g.astype(BF16)
        krc[rows, :] = jnp.broadcast_to(jnp.sum(low.astype(F32) * branch[rows, :], axis=1, keepdims=True), (sub, LANE))
        if s == SUBS - 1:
            mine = pl.ds(pl.multiple_of(((me % 2) * 2 + me // 2) * 8, 8), 8)
            side[mine, :] = jnp.transpose(krc[...])[0:8, :]
        return low

    head_core(tokens, part, middle, gb, 0, side, tx0, rx0, tx1, rx1, acc, ssem, rsem, me, core_at, y_at)


def head_bwd(gz, gu, small, wzx, wsmall, h_own, gain, g_own, branch, cid):
    tokens = gz.shape[0]
    d = gain.shape[1]
    S = jax.ShapeDtypeStruct
    vm = pl.BlockSpec(memory_space=pltpu.VMEM)
    return pl.pallas_call(
        partial(head_bwd_body, tokens),
        name="head_bwd",
        in_specs=[vm] * 9,
        out_specs=[vm] * 4,
        out_shape=[S((tokens, d), BF16), S((tokens // 4, d), F32), S((1, d), F32), S((32, LANE), F32)],
        scratch_shapes=head_scratch(tokens, d),
        compiler_params=pltpu.CompilerParams(collective_id=cid, has_side_effects=True, vmem_limit_bytes=VMEM_LIMIT),
    )(gz, gu, small, wzx, wsmall, h_own, gain, g_own, branch)


def maps_bwd_body(tokens, dkr, ubc, taps, aux, gdt, gtail, gm8, tapx,
                  small, gtaps, gtail_o, ytx, yrx, yacc, ctx, crx, us, ms, nextx, nextb, gmb, sems, semr):
    me = lax.axis_index("head")
    at = lax.axis_index("seq")
    count = lax.axis_size("seq")
    c = me % 2
    y = me // 2
    core_at, y_at = {"head": flip(me, 1)}, {"head": flip(me, 2)}
    barrier = pltpu.get_barrier_semaphore()
    for where in (core_at, y_at):
        pl.semaphore_signal(barrier, inc=1, device_id=where, device_id_type=MESH)

    @pl.when(at < count - 1)
    def _():
        pl.semaphore_signal(barrier, inc=1, device_id={"seq": at + 1}, device_id_type=MESH)
    pl.semaphore_wait(barrier, 2 + (at > 0).astype(jnp.int32))
    lanes = lax.broadcasted_iota(jnp.int32, (tokens, LANE), 1)
    before = {"seq": lax.rem(at + count - 1, count)}
    ahead_x = pltpu.make_async_remote_copy(src_ref=gm8, dst_ref=nextx, send_sem=sems.at[2], recv_sem=semr.at[2],
                                           device_id=before, device_id_type=MESH)

    @pl.when(at > 0)
    def _():
        ahead_x.start()
    low, high = dkr[:, :LANE], dkr[:, LANE:]
    ytx[...] = jnp.where(y == 0, high, low)
    one = send(ytx, yrx, (sems.at[0], semr.at[0]), y_at)
    tile = pl.ds(pl.multiple_of(y * LANE, LANE), LANE)
    us[...] = ubc[:, tile].astype(F32)
    tp = taps[:, tile]
    m = mix_taps(us, tp, aux, LANE)
    s = sig(m)
    slope = s * (1.0 + m * (1.0 - s))
    one.wait()
    ctx[...] = jnp.where(y == 0, low, high) + yrx[...]
    two = send(ctx, crx, (sems.at[1], semr.at[1]), core_at)
    two.wait()
    gm = (ctx[...] + crx[...]) * slope
    gmb[...] = gm[0:8]
    ahead_b = pltpu.make_async_remote_copy(src_ref=gmb, dst_ref=nextb, send_sem=sems.at[3], recv_sem=semr.at[3],
                                           device_id=before, device_id_type=MESH)

    @pl.when(at > 0)
    def _():
        ahead_b.start()

    @pl.when(at == count - 1)
    def _():
        nextx[...] = jnp.zeros_like(nextx)
        nextb[...] = jnp.zeros_like(nextb)
    gtaps[...] = jnp.zeros_like(gtaps)
    gtaps[0:1, :] = jnp.sum(gm * us[pl.ds(HALO, tokens), :], axis=0, keepdims=True)
    gtaps[CONV : CONV + 1, :] = jnp.sum(gm, axis=0, keepdims=True)
    for j in range(1, CONV):
        gtaps[j : j + 1, :] = jnp.sum(gm * aux[j - 1] * us[pl.ds(HALO - j, tokens), :], axis=0, keepdims=True)

    @pl.when(at < count - 1)
    def _():
        ahead_x.wait_recv()
        ahead_b.wait_recv()
    acc = gm * tp[0:1, :]
    for j in range(1, CONV):
        ms[pl.ds(0, tokens), :] = gm * aux[j - 1]
        ms[pl.ds(tokens, 8), :] = nextb[...]
        acc = acc + ms[pl.ds(j, tokens), :] * tp[j : j + 1, :]
    own = jnp.where(c == 0, lanes, LANE - 1 - lanes) < 64
    g = gdt[...].astype(F32)
    moved = jnp.concatenate([g[:, 64:], g[:, :64]], axis=1)
    small[...] = jnp.where(own, acc, jnp.where(c == 0, moved, g)).astype(BF16)
    gtail_o[...] = gtail[...].astype(BF16)
    nx = nextx[...]
    tail = gtail[...]
    rows = lax.broadcasted_iota(jnp.int32, tail.shape, 0)
    for j in range(1, CONV):
        for k in range(j):
            tail = tail + jnp.where(rows == 16 - j + k, nx[k : k + 1, :] * tapx[j : j + 1, :], 0.0)
    gtail_o[...] = tail.astype(BF16)

    @pl.when(at > 0)
    def _():
        ahead_x.wait_send()
        ahead_b.wait_send()


def maps_bwd(dkr, ubc, taps, aux, gdt, gtail, gm8, tapx, cid):
    tokens = dkr.shape[0]
    inner = tapx.shape[1]
    S = jax.ShapeDtypeStruct
    vm = pl.BlockSpec(memory_space=pltpu.VMEM)
    tile = pltpu.VMEM((tokens, LANE), F32)
    return pl.pallas_call(
        partial(maps_bwd_body, tokens),
        name="maps_bwd",
        in_specs=[vm] * 8,
        out_specs=[vm] * 3,
        out_shape=[S((tokens, LANE), BF16), S((8, LANE), F32), S((16, inner), BF16)],
        scratch_shapes=[tile, tile, tile, tile, tile, pltpu.VMEM((tokens + HALO, LANE), F32), pltpu.VMEM((tokens + 8, LANE), F32),
                        pltpu.VMEM((8, inner), F32), pltpu.VMEM((8, LANE), F32), pltpu.VMEM((8, LANE), F32),
                        pltpu.SemaphoreType.DMA((4,)), pltpu.SemaphoreType.DMA((4,))],
        compiler_params=pltpu.CompilerParams(collective_id=cid, has_side_effects=True, vmem_limit_bytes=VMEM_LIMIT),
    )(dkr, ubc, taps, aux, gdt, gtail, gm8, tapx)


def sums_body(parts, *refs):
    ins = refs[: 6 * parts]
    conv_x, conv_bc, ggate, gskip, gvec, ggain = refs[6 * parts : 6 * parts + 6]
    stage, rx, ssem, rsem = refs[6 * parts + 6 :]
    inner = stage.shape[2]
    me = lax.axis_index("head")
    tile = pl.multiple_of((me // 2) * LANE, LANE)
    steps = [("seq", b) for b in bits_of("seq")] + [("head", b) for b in bits_of("head")]
    wheres = [{axis: flip(lax.axis_index(axis), b)} for axis, b in steps]
    greet(wheres)
    stage[...] = jnp.zeros_like(stage)
    for l in range(parts):
        taps, gate, skip, vec, maps, gain = ins[6 * l : 6 * l + 6]
        stage[l, 0 : CONV + 1, :] = taps[0 : CONV + 1, :]
        stage[l, 5:6, :] = gate[...]
        stage[l, 6:7, :] = skip[...]
        stage[l, 7:8, 0:LANE] = vec[0:1, :]
        stage[l, 7:8, LANE : 2 * LANE] = vec[1:2, :]
        stage[l, 8:9, :] = gain[:, :inner]
        stage[l, 9:10, :] = gain[:, inner:]
        for r in range(CONV + 1):
            row = maps[r : r + 1, :] * 0.5
            here = [jnp.where(me // 2 == k, row, 0.0) for k in range(2)]
            stage[l, 10 + r // 3 : 11 + r // 3, (r % 3) * 2 * LANE : ((r % 3) * 2 + 2) * LANE] = jnp.concatenate(here, axis=1)
    for i, (axis, b) in enumerate(steps):
        if axis == "seq":
            copy = send(stage, rx.at[i], (ssem.at[i], rsem.at[i]), wheres[i])
            copy.wait()
            stage[...] += rx[i]
        else:
            where = pl.ds(8, 8)
            copy = send(stage.at[:, where, :], rx.at[i, :, where, :], (ssem.at[i], rsem.at[i]), wheres[i])
            copy.wait()
            stage[:, 8:16, :] += rx[i, :, 8:16, :]
    for l in range(parts):
        conv_x[l] = stage[l, 0 : CONV + 1, :]
        ggate[l : l + 1, :] = stage[l, 5:6, :]
        gskip[l : l + 1, :] = stage[l, 6:7, :]
        gvec[l : l + 1, :] = stage[l, 7:8, 0 : 2 * LANE]
        ggain[l : l + 1, :inner] = stage[l, 8:9, :]
        ggain[l : l + 1, inner:] = stage[l, 9:10, :]
        for r in range(CONV + 1):
            conv_bc[l, r : r + 1, :] = stage[l, 10 + r // 3 : 11 + r // 3, (r % 3) * 2 * LANE : ((r % 3) * 2 + 2) * LANE]


def sums_kernel(smalls, inner, d, cid):
    parts = len(smalls)
    n = len(bits_of("seq")) + len(bits_of("head"))
    vm = pl.BlockSpec(memory_space=pltpu.VMEM)
    S = jax.ShapeDtypeStruct
    return pl.pallas_call(
        partial(sums_body, parts),
        name="sums_small",
        in_specs=[vm] * (6 * parts),
        out_specs=[vm] * 6,
        out_shape=[S((parts, CONV + 1, inner), F32), S((parts, CONV + 1, 2 * LANE), F32), S((parts, inner), F32), S((parts, inner), F32),
                   S((parts, 2 * LANE), F32), S((parts, d), F32)],
        scratch_shapes=[pltpu.VMEM((parts, 16, inner), F32), pltpu.VMEM((n, parts, 16, inner), F32),
                        pltpu.SemaphoreType.DMA((n,)), pltpu.SemaphoreType.DMA((n,))],
        compiler_params=pltpu.CompilerParams(collective_id=cid, has_side_effects=True, vmem_limit_bytes=VMEM_LIMIT),
    )(*[x for part in smalls for x in part])


def pad_lanes(x, to=LANE):
    return jnp.pad(x, [(0, 0)] * (x.ndim - 1) + [(0, to - x.shape[-1])])


def forward_layer(nx, h_own, extra, q, aux, segrow, layer):
    heads, size, inner = q["heads"], q["size"], q["inner"]
    (gate, ux, ubc, krs, pdt, steps, cum, cT, gram, mixed, ypart, entry, state, dec, decl) = fwd_mix(
        heads, size, nx, q["w_zx"], q["w_bc"], q["w_dt"], q["taps_x"], q["taps_bc"], q["dt_bias"], q["a_log"], q["skip"], aux, segrow)
    enter = carry_kernel(state, dec, heads, size, False, layer)
    y, carr, gated, sq = fwd_gate(ypart, entry, gate, krs, enter)
    width = inner * lax.axis_size("head")
    nx_next, h_new, branch, r2b, side = head_fwd(gated, sq, q["gate_gain"], q["w_out"], h_own, extra, layer == LAYERS - 1, width, LAYERS + layer)
    stored = dict(nx=nx, gate=gate, ux=ux, ubc=ubc, krs=krs, pdt=pdt, steps=steps, cum=cum, cT=cT, gram=gram, mixed=mixed,
                  entry=entry, dec=dec, decl=decl, enter=enter, y=y, carr=carr, r2b=r2b, branch=branch, h_own=h_own)
    return nx_next, h_new, side, stored


def backward_layer(g_own, gb, side, s, q, aux, segrow, layer, branch_before):
    tokens = gb.shape[0]
    heads, size, inner = q["heads"], q["size"], q["inner"]
    width = inner * lax.axis_size("head")
    kr = side.reshape(4, 8, LANE)[:, 0, :].reshape(tokens)
    r2b = s["r2b"]
    krb = r2b * r2b * (kr[:, None] / width)
    gy, gz, scaled, qloc, ggate, gskip = bwd_gate(gb, q["w_out"], s["gate"], s["y"], s["mixed"], s["entry"], s["krs"], r2b, krb, q["gate_gain"])
    g_w_out = scatter_rows(mm_tn(gb, scaled))
    later = carry_kernel(qloc, s["dec"], heads, size, True, 2 * LAYERS + layer)
    dvd, dd, rowT, dkr = bwd_local(size, gy, s["mixed"], s["krs"], s["cum"], s["steps"], s["cT"], s["gram"], s["entry"], s["enter"], aux[5], segrow)
    gm8, gu, gtail, gtaps_x, gdt, gvec, dkr = bwd_carry(
        size, gy, dvd, s["mixed"], s["carr"], s["entry"], s["krs"], s["cum"], s["steps"], s["pdt"], q["dt_bias"], q["a_log"], q["skip"],
        s["ux"], q["taps_x"], aux, later, s["enter"], dd, rowT, dkr, s["decl"][:1])
    small, gtaps_bc, gtail = maps_bwd(dkr, s["ubc"], q["taps_bc"], aux, gdt, gtail, gm8, q["taps_x"], 3 * LAYERS + layer)
    gu = lax.dynamic_update_slice(gu, gtail, (tokens - 16, 0))
    normed = s["nx"][HALO:]
    g_w_zx = scatter_rows(mm_tn(normed, jnp.concatenate([gz, gu], 1)))
    g_w_small = scatter_rows(mm_tn(normed, small))
    gb, g_own, g_gain, side = head_bwd(gz, gu, small, q["w_zx"], q["w_small"], s["h_own"], q["gain"][None], g_own, branch_before, 4 * LAYERS + layer)
    return gb, g_own, side, (g_w_zx, g_w_small, g_w_out), (gtaps_x, ggate, gskip, gvec, gtaps_bc, g_gain)


def local(hidden_in, seg, cot, norm_gain, w_zx, w_bc, w_dt, conv_x, conv_bc, dt_bias, a_log, skip_d, gate_gain, w_out):
    tokens = hidden_in.shape[0]
    inner = w_zx.shape[3]
    heads = w_dt.shape[2]
    size = inner // heads
    rank = lax.axis_index("head")
    segf = seg.astype(F32)
    ext = jnp.concatenate([jnp.full((HALO,), segf[0], F32), segf], 0)
    vecs = [(ext[HALO - j : HALO - j + tokens] == segf).astype(F32) for j in range(1, CONV)]
    vecs += [(segf == segf[0]).astype(F32), (segf == segf[-1]).astype(F32), segf]
    aux = jnp.broadcast_to(jnp.stack(vecs, 0)[:, :, None], (len(vecs), tokens, LANE))
    segrow = segf[None]
    wt = jnp.transpose(w_zx, (0, 2, 1, 3))
    lanes = jnp.arange(LANE)
    own = jnp.where(rank % 2 == 0, lanes, LANE - 1 - lanes) < LANE // 2
    qs = []
    for l in range(LAYERS):
        dt_pad = pad_lanes(w_dt[l])
        tile = lax.dynamic_slice_in_dim(w_bc[l], (rank // 2) * LANE, LANE, 1)
        w_small = jnp.where(own[None], tile, jnp.where(rank % 2 == 0, jnp.roll(dt_pad, LANE // 2, axis=1), dt_pad))
        qs.append(dict(heads=heads, size=size, inner=inner, gain=norm_gain[l], w_zx=wt[l], w_bc=w_bc[l], w_dt=dt_pad, w_small=w_small,
                       taps_x=jnp.pad(conv_x[l], ((0, 3), (0, 0))), taps_bc=jnp.pad(conv_bc[l], ((0, 3), (0, 0))),
                       dt_bias=pad_lanes(dt_bias[l][None]), a_log=pad_lanes(a_log[l][None]), skip=jnp.repeat(skip_d[l], size)[None],
                       gate_gain=gate_gain[l][None], w_out=w_out[l]))
    h = hidden_in.astype(F32)
    h_own = own_rows(h)
    cot_own = own_rows(cot)
    normed = (h * lax.rsqrt(jnp.mean(h * h, axis=1, keepdims=True) + EPS) * norm_gain[0][None]).astype(BF16)
    nx = jnp.concatenate([shift(normed[tokens - HALO :], "seq", 1), normed], 0)
    stored = []
    for l in range(LAYERS):
        extra = cot_own if l == LAYERS - 1 else norm_gain[l + 1][None]
        nx, h_own, side, s = forward_layer(nx, h_own, extra, qs[l], aux, segrow, l)
        stored.append(s)
    hidden_out = nx
    gb = cot
    g_own = cot_own.astype(F32)
    larges, smalls = [], []
    for l in reversed(range(LAYERS)):
        before = stored[max(l - 1, 0)]["branch"]
        gb, g_own, side, large, small = backward_layer(g_own, gb, side, stored[l], qs[l], aux, segrow, l, before)
        larges.insert(0, large)
        smalls.insert(0, small)
    grad_in = gb.astype(F32)
    stack = lambda which, i: jnp.stack([m[i] for m in which], 0)
    g_w_zx = stack(larges, 0)
    g_w_zx = g_w_zx.reshape(g_w_zx.shape[0], g_w_zx.shape[1], 2, inner)
    g_small = stack(larges, 1)
    even = rank % 2 == 0
    g_w_bc = jnp.where(even, g_small[:, :, : LANE // 2], g_small[:, :, LANE // 2 :])
    g_w_dt = jnp.where(even, g_small[:, :, LANE // 2 : LANE // 2 + heads], g_small[:, :, :heads])
    g_w_out = jnp.transpose(stack(larges, 2), (0, 2, 1))
    g_conv_x, g_conv_bc, g_gate, g_skip, g_vec, g_gain = sums_kernel(smalls, inner, norm_gain.shape[1], 5 * LAYERS)
    g_skip = jnp.sum(g_skip.reshape(LAYERS, heads, size), axis=2)
    part = g_gain.shape[1] // lax.axis_size("seq")
    g_gain = lax.dynamic_slice_in_dim(g_gain, lax.axis_index("seq") * part, part, 1)
    return (hidden_out, grad_in, g_gain, g_w_zx, g_w_bc, g_w_dt, g_conv_x, g_conv_bc,
            g_vec[:, :heads], g_vec[:, LANE : LANE + heads], g_skip, g_gate, g_w_out)


def solution(mesh):
    placed = (
        P("seq", None), P("seq"), P("seq", None), P(), P(None, None, None, "head"), P(), P(None, None, "head"),
        P(None, None, "head"), P(), P(None, "head"), P(None, "head"), P(None, "head"), P(None, "head"), P(None, "head", None),
    )
    return jax.shard_map(
        local,
        mesh=mesh,
        in_specs=placed,
        out_specs=(
            P("seq", None), P("seq", None), P(None, "seq"), P(None, "seq", None, "head"), P(None, "seq", "head"),
            P(None, "seq", "head"), P(None, None, "head"), P(), P(None, "head"), P(None, "head"), P(None, "head"),
            P(None, "head"), P(None, "head", "seq"),
        ),
        check_vma=False,
    )
```

```python
from functools import partial

import jax
import jax.numpy as jnp
from jax import lax
from jax.experimental import pallas as pl
from jax.experimental.pallas import tpu as pltpu
from jax.sharding import PartitionSpec as P

CONV = 4
LAYERS = 2
EPS = 1e-05
F32 = jnp.float32
BF16 = jnp.bfloat16


def dot(a, b, dims):
    return lax.dot_general(a.astype(BF16), b.astype(BF16), (dims, ((), ())), preferred_element_type=F32)


def mm(a, b):
    return dot(a, b, ((1,), (0,)))


def mm_nt(a, b):
    return dot(a, b, ((1,), (1,)))


def mm_tn(a, b):
    return dot(a, b, ((0,), (0,)))


def swap(x, axis, bit):
    n = lax.axis_size(axis)
    return lax.ppermute(x, axis, [(i, i ^ bit) for i in range(n)])


def shift(x, axis, by):
    n = lax.axis_size(axis)
    return lax.ppermute(x, axis, [(i, i + by) for i in range(n) if 0 <= i + by < n])


def bits_of(axis):
    n = lax.axis_size(axis)
    bits = []
    b = 1
    while b < n:
        bits.append(b)
        b *= 2
    return bits


def my_bit(axis, bit):
    return (lax.axis_index(axis) // bit) % 2


def take(x, dim, index):
    return lax.dynamic_index_in_dim(x, index, dim, keepdims=False)


def head_scatter(x):
    for bit in bits_of("head"):
        me = my_bit("head", bit)
        halves = x.reshape((2, x.shape[0] // 2) + x.shape[1:])
        got = swap(take(halves, 0, 1 - me).astype(BF16), "head", bit)
        x = take(halves, 0, me).astype(F32) + got.astype(F32)
    return x


def head_scatter_exact(x):
    for bit in bits_of("head"):
        me = my_bit("head", bit)
        halves = x.reshape((2, x.shape[0] // 2) + x.shape[1:])
        x = take(halves, 0, me) + swap(take(halves, 0, 1 - me), "head", bit)
    return x


def head_gather(x):
    for bit in reversed(bits_of("head")):
        me = my_bit("head", bit)
        got = swap(x, "head", bit)
        x = jnp.where(me == 0, jnp.concatenate([x, got], 0), jnp.concatenate([got, x], 0))
    return x


def own_rows(x):
    for bit in bits_of("head"):
        x = take(x.reshape((2, x.shape[0] // 2) + x.shape[1:]), 0, my_bit("head", bit))
    return x


def carry_scan(state, decay, reverse):
    total, total_d = state, decay
    entering = jnp.zeros_like(state)
    enter_d = jnp.ones_like(decay)
    for bit in bits_of("seq"):
        me = my_bit("seq", bit)
        other = swap(total.astype(BF16), "seq", bit).astype(F32)
        other_d = swap(total_d, "seq", bit)
        second = (me == 0) if reverse else (me == 1)
        entering = jnp.where(second, entering + enter_d[:, None, None] * other, entering)
        enter_d = jnp.where(second, enter_d * other_d, enter_d)
        total = jnp.where(
            second, total_d[:, None, None] * other + total, other_d[:, None, None] * total + other
        )
        total_d = total_d * other_d
    return entering


def silu_slope(v):
    s = jax.nn.sigmoid(v)
    return s * (1.0 + v * (1.0 - s))


def scatter_rows(x):
    bits = bits_of("seq")
    k = len(bits)
    n = lax.axis_size("seq")
    x = x.reshape((2,) * k + (x.shape[0] // n, x.shape[1]))
    for b in range(k):
        axis = k - 1 - b
        me = my_bit("seq", bits[b])
        got = swap(take(x, axis, 1 - me).astype(BF16), "seq", bits[b])
        x = take(x, axis, me).astype(F32) + got.astype(F32)
    return x


HALO = 16
LANE = 128
NT = ((1,), (1,))
NN = ((1,), (0,))
TN = ((0,), (0,))


def bdot(a, b, dims):
    return lax.dot_general(a.astype(BF16), b.astype(BF16), (dims, ((), ())), preferred_element_type=F32)


def halves(x):
    high = x.astype(BF16)
    return high, (x - high.astype(F32)).astype(BF16)


def dot3(a, b, dims):
    ah, al = halves(a)
    bh, bl = halves(b)
    return bdot(ah, bh, dims) + (bdot(ah, bl, dims) + bdot(al, bh, dims))


def hdot(a, b, dims):
    return lax.dot_general(a, b, (dims, ((), ())), precision=lax.Precision.HIGHEST, preferred_element_type=F32)


def sig(v):
    return 0.5 * jnp.tanh(0.5 * v) + 0.5


def softplus(v):
    e = jnp.exp(-jnp.abs(v))
    s = e / (2.0 + e)
    q = s * s
    series = 1.0 / 13.0
    for k in (11, 9, 7, 5, 3, 1):
        series = series * q + 1.0 / k
    return jnp.maximum(v, 0.0) + 2.0 * s * series


def mix_taps(us, taps, aux, width):
    tokens = aux.shape[1]
    wide = lambda m: m if width == LANE else jnp.concatenate([m] * (width // LANE), axis=1)
    acc = us[pl.ds(HALO, tokens), :] * taps[0:1, :] + taps[CONV : CONV + 1, :]
    for j in range(1, CONV):
        acc = acc + us[pl.ds(HALO - j, tokens), :] * wide(aux[j - 1]) * taps[j : j + 1, :]
    return acc


def pick_lane(values, h, lanes):
    return jnp.sum(jnp.where(lanes == h, values, 0.0), axis=1, keepdims=True)


def fwd_mix_body(heads, size, nx, wzx, wbc, wdt, tapx, tapbc, dtb, lograte, skip, aux, segrow,
                 gate, ux, ubc, krs, pdt, steps_o, cum_o, cT, gram, mixed_o, ypart, entry_o, state, dec, decl,
                 us, usbc, cb):
    p = pl.program_id(0)
    tokens = aux.shape[1]
    states = wbc.shape[1] // 2
    lanes = lax.broadcasted_iota(jnp.int32, (tokens, LANE), 1)
    half = lanes < size

    @pl.when(p == 0)
    def _():
        bc = bdot(nx[...], wbc[...], NN).astype(BF16)
        ubc[...] = bc
        usbc[...] = bc.astype(F32)
        m = mix_taps(usbc, tapbc, aux, 2 * states)
        act = m * sig(m)
        krs[...] = act
        g = dot3(act[:, states:], act[:, :states], NT)
        ii = lax.broadcasted_iota(jnp.int32, (tokens, tokens), 0)
        jj = lax.broadcasted_iota(jnp.int32, (tokens, tokens), 1)
        segc = jnp.concatenate([aux[5]] * (tokens // LANE), axis=1)
        keep = (ii >= jj) & (segc == segrow[...])
        gram[...] = jnp.where(keep, g, 0.0)
        pd = bdot(nx[pl.ds(HALO, tokens), :], wdt[...], NN).astype(BF16)
        pdt[...] = pd
        st = softplus(pd.astype(F32) + dtb[...])
        steps_o[...] = st
        log = st * -jnp.exp(lograte[...])
        cum = hdot(jnp.where(ii >= jj, 1.0, 0.0), log, NN)
        cum_o[...] = cum
        cT[...] = cum.T
        keeps = aux[3, tokens - 1 : tokens, :]
        decl[...] = jnp.broadcast_to(jnp.exp(cum[tokens - 1 : tokens, :]) * keeps, (8, LANE))
        dec[...] = jnp.exp(jnp.broadcast_to(cT[0:16, tokens - 1 : tokens], (16, LANE))) * keeps

    gate[...] = bdot(nx[pl.ds(HALO, tokens), :], wzx[0], NN).astype(BF16)
    u = bdot(nx[...], wzx[1], NN).astype(BF16)
    ux[...] = u
    us[...] = u.astype(F32)
    m = mix_taps(us, tapx, aux, LANE)
    mixed_o[...] = m
    v = m * sig(m)
    cum = cum_o[...]
    st = steps_o[...]
    h0 = p * (LANE // size)
    dd = jnp.where(half, pick_lane(st, h0, lanes), pick_lane(st, h0 + 1, lanes))
    vd = v * dd
    vh, vl = halves(vd)
    vhl = jnp.concatenate([vh, vl], axis=1)
    ys = []
    for k in range(LANE // size):
        h = h0 + k
        cb[k] = jnp.broadcast_to(pick_lane(cum, h, lanes), (tokens, LANE))
        row = cT[pl.ds(h, 1), :]
        parts = []
        for ib in range(tokens // LANE):
            tiles, lows = [], []
            ci = cb[k, pl.ds(ib * LANE, LANE), :]
            for jb in range(ib + 1):
                spread = ci - row[:, jb * LANE : (jb + 1) * LANE]
                if jb == ib:
                    spread = jnp.minimum(spread, 0.0)
                wh, wl = halves(jnp.exp(spread) * gram[pl.ds(ib * LANE, LANE), pl.ds(jb * LANE, LANE)])
                tiles.append(wh)
                lows.append(wl)
            joined = lambda t: t[0] if ib == 0 else jnp.concatenate(t, axis=1)
            both = bdot(joined(tiles), vhl[: (ib + 1) * LANE], NN)
            parts.append(both[:, :LANE] + (both[:, LANE:] + bdot(joined(lows), vh[: (ib + 1) * LANE], NN)))
        ys.append(jnp.concatenate(parts, axis=0))
    y = jnp.where(half, ys[0], ys[1])
    ypart[...] = y + skip[...] * v
    ct = jnp.where(half, cb[0], cb[1])
    entry_o[...] = jnp.exp(ct) * aux[3]
    tail = jnp.exp(ct[tokens - 1 : tokens, :] - ct) * aux[4]
    state[...] = dot3(vd * tail, krs[:, :states], TN)


def full(shape):
    n = len(shape)
    return pl.BlockSpec(shape, lambda p: (0,) * n)


def cols(rows):
    return pl.BlockSpec((rows, LANE), lambda p: (0, p))


def rowsb(width):
    return pl.BlockSpec((LANE, width), lambda p: (p, 0))


def fwd_gate_body(ypart, entry, gate, krs, enter, y, carr, gated, sq, sqacc):
    p = pl.program_id(0)
    states = krs.shape[1] // 2
    c = dot3(krs[:, states:], enter[...], NT) * entry[...]
    carr[...] = c
    yy = ypart[...] + c
    y[...] = yy
    z = gate[...].astype(F32)
    g = yy * (z * sig(z))
    gated[...] = g

    @pl.when(p == 0)
    def _():
        sqacc[...] = g * g

    @pl.when(p > 0)
    def _():
        sqacc[...] += g * g

    @pl.when(p == pl.num_programs(0) - 1)
    def _():
        sq[...] = jnp.broadcast_to(jnp.sum(jnp.transpose(sqacc[...]), axis=0, keepdims=True), sq.shape)


def bwd_gate_body(gb, wout, gate, y, mixed, entry, krs, r2b, krb, gain, gy_o, gz_o, scaled_o, qloc, ggate, gskip):
    states = krs.shape[1] // 2
    gs = bdot(gb[...], wout[...], NT)
    z = gate[...].astype(F32)
    s = sig(z)
    sil = z * s
    yy = y[...]
    gated = yy * sil
    r2 = r2b[...]
    gr = gated * r2
    ggate[...] = jnp.sum(gs * gr, axis=0, keepdims=True)
    scaled_o[...] = (gr * gain[...]).astype(BF16)
    gg = r2 * gain[...] * gs - gated * krb[...]
    gy = gg * sil
    gy_o[...] = gy
    gz_o[...] = (gg * yy * (s * (1.0 + z * (1.0 - s)))).astype(BF16)
    m = mixed[...]
    gskip[...] = jnp.sum(gy * (m * sig(m)), axis=0, keepdims=True)
    qloc[...] = bdot(gy * entry[...], krs[:, states:], TN)


def bwd_local_body(size, gy_r, mixed, krs, cum, steps, cT, gram, entry, enter, segc, segrow,
                   dvd, dd_o, rowT, dkr, cb, db, gramT, dgT, vb, gk):
    p = pl.program_id(0)
    tokens = gy_r.shape[0]
    states = krs.shape[1] // 2
    lanes = lax.broadcasted_iota(jnp.int32, (tokens, LANE), 1)
    half = lanes < size

    @pl.when(p == 0)
    def _():
        gramT[...] = gram[...].T
        dgT[...] = jnp.zeros_like(dgT)
        dd_o[...] = jnp.zeros_like(dd_o)
        rowT[...] = jnp.zeros_like(rowT)
        dkr[...] = jnp.zeros_like(dkr)

    m = mixed[...]
    vb[...] = (m * sig(m)).astype(BF16)
    gy = gy_r[...]
    gyb = gy.astype(BF16)
    h0 = p * (LANE // size)
    outs = []
    for k in range(LANE // size):
        h = h0 + k
        gk[...] = jnp.where(half if k == 0 else jnp.logical_not(half), gy, 0.0).astype(BF16)
        cb[...] = jnp.broadcast_to(pick_lane(cum[...], h, lanes), (tokens, LANE))
        db[...] = jnp.broadcast_to(pick_lane(steps[...], h, lanes), (tokens, LANE))
        row = cT[pl.ds(h, 1), :]
        parts = []
        dds = []
        rows_acc = [jnp.zeros((8, LANE), F32) for _ in range(tokens // LANE)]
        for jb in range(tokens // LANE):
            js = pl.ds(jb * LANE, LANE)
            cj = cb[js, :]
            dj = db[js, :]
            pt = bdot(vb[js, :], gk[pl.ds(jb * LANE, tokens - jb * LANE), :], NT)
            ws = []
            dsum = None
            for ib in range(jb, tokens // LANE):
                sl = pl.ds(ib * LANE, LANE)
                spread = row[:, ib * LANE : (ib + 1) * LANE] - cj
                if jb == ib:
                    spread = jnp.minimum(spread, 0.0)
                e = jnp.exp(spread)
                w = e * gramT[js, sl]
                ws.append(w.astype(BF16))
                pp = pt[:, (ib - jb) * LANE : (ib - jb + 1) * LANE]
                wp = w * pp
                dgT[js, sl] += e * (pp * dj)
                x = wp * dj
                rows_acc[ib] = rows_acc[ib] + jnp.sum(x.reshape(LANE // 8, 8, LANE), axis=0)
                dsum = wp if dsum is None else dsum + wp
            dds.append(jnp.sum(dsum, axis=1, keepdims=True))
            w = ws[0] if len(ws) == 1 else jnp.concatenate(ws, axis=1)
            parts.append(bdot(w, gyb[jb * LANE :], NN))
        outs.append(jnp.concatenate(parts, axis=0))
        dd_o[...] += jnp.where(lanes == h, jnp.concatenate(dds, axis=0), 0.0)
        rowT[pl.ds(h, 1), :] = jnp.concatenate([jnp.sum(r, axis=0, keepdims=True) for r in rows_acc], axis=1)
    dvd[...] = jnp.where(half, outs[0], outs[1])
    dkr[:, states:] += bdot(gy * entry[...], enter[...], NN)

    @pl.when(p == pl.num_programs(0) - 1)
    def _():
        jj = lax.broadcasted_iota(jnp.int32, (tokens, tokens), 0)
        ii = lax.broadcasted_iota(jnp.int32, (tokens, tokens), 1)
        segs = jnp.concatenate([segc[...]] * (tokens // LANE), axis=1)
        g = jnp.where((ii >= jj) & (segs == segrow[...]), dgT[...], 0.0)
        dkr[:, :states] += bdot(g, krs[:, states:], NN)
        dkr[:, states:] += bdot(g, krs[:, :states], TN)


def bwd_carry_body(size, gy_r, dvd_r, mixed, carr, entry, krs, cum, steps, pdt, dtb, lograte, skip, ux, tapx, aux, later, enter,
                   dd_r, rowT, dkr_r, decay,
                   gm_o, gu_o, gtail_o, gtaps, gdt_o, gvec, dkr, us, ms, ddacc, dcum, last):
    p = pl.program_id(0)
    tokens = gy_r.shape[0]
    states = krs.shape[1] // 2
    lanes = lax.broadcasted_iota(jnp.int32, (tokens, LANE), 1)
    lane1 = lax.broadcasted_iota(jnp.int32, (1, LANE), 1)
    half = lanes < size

    @pl.when(p == 0)
    def _():
        ddacc[...] = dd_r[...]
        dcum[...] = jnp.transpose(rowT[...]) - dd_r[...] * steps[...]
        last[...] = jnp.zeros_like(last)
        dkr[...] = dkr_r[...]

    h0 = p * (LANE // size)
    st = steps[...]
    cu = cum[...]
    cc = [pick_lane(cu, h0 + k, lanes) for k in range(2)]
    dcol = [pick_lane(st, h0 + k, lanes) for k in range(2)]
    ct = jnp.where(half, cc[0], cc[1])
    dpair = jnp.where(half, dcol[0], dcol[1])
    tail = jnp.exp(ct[tokens - 1 : tokens, :] - ct) * aux[4]
    m = mixed[...]
    s = sig(m)
    v = m * s
    gy = gy_r[...]
    qk = bdot(krs[:, :states], later[...], NT) * tail
    dvd = dvd_r[...] + qk
    dkr[:, :states] += bdot(v * dpair * tail, later[...], NN)
    tq = v * qk
    eq = gy * carr[...]
    qs = later[...] * enter[...]
    for k in range(2):
        h = h0 + k
        mine = half if k == 0 else jnp.logical_not(half)
        td = jnp.sum(jnp.where(mine, tq, 0.0), axis=1, keepdims=True)
        ec = jnp.sum(jnp.where(mine, eq, 0.0), axis=1, keepdims=True)
        tdd = td * dcol[k]
        ddacc[...] += jnp.where(lanes == h, td, 0.0)
        dcum[...] += jnp.where(lanes == h, ec - tdd, 0.0)
        dot_qs = jnp.sum(jnp.sum(qs[k * size : (k + 1) * size, :], axis=0, keepdims=True), axis=1, keepdims=True)
        last[...] += jnp.where(lane1 == h, jnp.sum(tdd, axis=0, keepdims=True) + dot_qs * decay[0:1, :], 0.0)
    dv = dvd * dpair + skip[...] * gy
    gm = dv * (s * (1.0 + m * (1.0 - s)))
    gm_o[...] = gm[:8]
    us[...] = ux[...].astype(F32)
    acc = gm * tapx[0:1, :]
    gtaps[0:1, :] = jnp.sum(gm * us[pl.ds(HALO, tokens), :], axis=0, keepdims=True)
    gtaps[CONV : CONV + 1, :] = jnp.sum(gm, axis=0, keepdims=True)
    ms[pl.ds(tokens, 8), :] = jnp.zeros((8, LANE), F32)
    for j in range(1, CONV):
        gmj = gm * aux[j - 1]
        gtaps[j : j + 1, :] = jnp.sum(gmj * us[pl.ds(HALO - j, tokens), :], axis=0, keepdims=True)
        ms[pl.ds(0, tokens), :] = gmj
        acc = acc + ms[pl.ds(j, tokens), :] * tapx[j : j + 1, :]
    gu_o[...] = acc.astype(BF16)
    gtail_o[...] = acc[tokens - 16 :]

    @pl.when(p == pl.num_programs(0) - 1)
    def _():
        ii = lax.broadcasted_iota(jnp.int32, (tokens, tokens), 0)
        jj = lax.broadcasted_iota(jnp.int32, (tokens, tokens), 1)
        dlog = hdot(jnp.where(jj >= ii, 1.0, 0.0), dcum[...], NN) + last[...]
        rates = -jnp.exp(lograte[...])
        dsteps = ddacc[...] + rates * dlog
        gdt = dsteps * sig(pdt[...].astype(F32) + dtb[...])
        gdt_o[...] = gdt.astype(BF16)
        gvec[0:1, :] = jnp.sum(gdt, axis=0, keepdims=True)
        gvec[1:2, :] = jnp.sum(st * dlog, axis=0, keepdims=True) * rates


MESH = pl.DeviceIdType.MESH
VMEM_LIMIT = 56 * 1024 * 1024
SUBS = 2


def greet(partners):
    barrier = pltpu.get_barrier_semaphore()
    for where in partners:
        pl.semaphore_signal(barrier, inc=1, device_id=where, device_id_type=MESH)
    pl.semaphore_wait(barrier, len(partners))


def send(src, dst, sems, where):
    copy = pltpu.make_async_remote_copy(
        src_ref=src, dst_ref=dst, send_sem=sems[0], recv_sem=sems[1], device_id=where, device_id_type=MESH)
    copy.start()
    return copy


def flip(me, bit):
    return me + bit * (1 - 2 * ((me // bit) % 2))


def carry_body(bits, reverse, heads, size, st, dec, out, tx, rx, dtx, drx, tot, ssem, rsem):
    me = lax.axis_index("seq")
    wheres = [{"seq": flip(me, b)} for b in bits]
    greet(wheres)
    enter_d = jnp.ones_like(dec[...])
    total_d = dec[...]
    for i, b in enumerate(bits):
        src = st if i == 0 else tot
        if reverse:
            tx[...] = src[...].astype(BF16)
        dtx[...] = total_d
        one = send(tx if reverse else src, rx.at[i], (ssem.at[2 * i], rsem.at[2 * i]), wheres[i])
        two = send(dtx, drx.at[i], (ssem.at[2 * i + 1], rsem.at[2 * i + 1]), wheres[i])
        bit = (me // b) % 2
        second = (1 - bit) if reverse else bit
        two.wait()
        other_d = drx[i]
        one.wait()
        keep = second.astype(F32)
        for h in range(heads):
            rows = pl.ds(h * size, size)
            other = rx[i, rows, :].astype(F32)
            add = other * (enter_d[h : h + 1] * keep)
            if i == 0:
                out[rows, :] = add
            else:
                out[rows, :] += add
            if i + 1 < len(bits):
                mine = src[rows, :]
                a = jnp.where(second == 1, total_d[h : h + 1], 1.0)
                c = jnp.where(second == 1, 1.0, other_d[h : h + 1])
                tot[rows, :] = a * other + c * mine
        enter_d = jnp.where(second == 1, enter_d * other_d, enter_d)
        total_d = total_d * other_d


def head_core(tokens, part, middle, nx, off, side, tx0, rx0, tx1, rx1, acc, ssem, rsem, me, core_at, y_at):
    quarter = tokens // 4
    sub = quarter // SUBS
    c = me % 2
    y = me // 2
    half = 2 * quarter
    other_y = pl.multiple_of((1 - y) * quarter, quarter)
    own_y = pl.multiple_of(y * quarter, quarter)
    n = 0
    sends = []

    def go(src, dst, where):
        nonlocal n
        copy = send(src, dst, (ssem.at[n], rsem.at[n]), where)
        sends.append(copy)
        n += 1
        return copy

    acc[...] = part(pl.multiple_of((1 - c) * half, half), half)
    first = []
    for i, base in enumerate((other_y, own_y)):
        for s in range(SUBS):
            tx0[i, s] = acc[pl.ds(pl.multiple_of(base + s * sub, sub), sub), :].astype(tx0.dtype)
            first.append(go(tx0.at[i, s], rx0.at[i, s], core_at))
    acc[...] = part(pl.multiple_of(c * half, half), half)
    second = []
    for s in range(SUBS):
        first[s].wait_recv()
        tx1[s] = (acc[pl.ds(pl.multiple_of(other_y + s * sub, sub), sub), :] + rx0[0, s].astype(F32)).astype(tx1.dtype)
        second.append(go(tx1.at[s], rx1.at[s], y_at))
    own = (c * 2 + y) * quarter
    theirs = (c * 2 + 1 - y) * quarter
    to_y, to_core, onward = [], [], []
    for s in range(SUBS):
        first[SUBS + s].wait_recv()
        second[s].wait_recv()
        total = acc[pl.ds(pl.multiple_of(own_y + s * sub, sub), sub), :] + rx0[1, s].astype(F32) + rx1[s].astype(F32)
        rows = pl.ds(pl.multiple_of(off + own + s * sub, 16), sub)
        nx[rows, :] = middle(s, sub, total)
        to_y.append(go(nx.at[rows, :], nx.at[rows, :], y_at))
        to_core.append(go(nx.at[rows, :], nx.at[rows, :], core_at))
    if side is not None:
        srows = pl.ds(pl.multiple_of((c * 2 + y) * 8, 8), 8)
        to_y.append(go(side.at[srows, :], side.at[srows, :], y_at))
        to_core.append(go(side.at[srows, :], side.at[srows, :], core_at))
    for s in range(SUBS):
        to_y[s].wait_recv()
        rows = pl.ds(pl.multiple_of(off + theirs + s * sub, 16), sub)
        onward.append(go(nx.at[rows, :], nx.at[rows, :], core_at))
    if side is not None:
        to_y[SUBS].wait_recv()
        srows = pl.ds(pl.multiple_of((c * 2 + 1 - y) * 8, 8), 8)
        onward.append(go(side.at[srows, :], side.at[srows, :], core_at))
    for copy in to_core + onward:
        copy.wait_recv()
    for copy in sends:
        copy.wait_send()


HEAD_COPIES = 3 * SUBS + 3 * SUBS + 3


def head_fwd_body(l, tokens, last, width, gated, sq, ggain_all, wout_all, h_own, extra,
                  nx, h_new, branch, r2b, side, sqrx, tx0, rx0, tx1, rx1, acc, krc, ssem, rsem, qs, qr, hs, hr, wout, wsem):
    load = pltpu.make_async_copy(wout_all.at[l], wout, wsem.at[0])
    load.start()
    ggain = ggain_all.at[l]
    extra = extra if last else extra.at[l + 1]
    me = lax.axis_index("head")
    at = lax.axis_index("seq")
    count = lax.axis_size("seq")
    peers = [lax.rem(me + k, 4) for k in (1, 2, 3)]
    barrier = pltpu.get_barrier_semaphore()
    for pr in peers:
        pl.semaphore_signal(barrier, inc=1, device_id={"head": pr}, device_id_type=MESH)
    if not last:
        @pl.when(at > 0)
        def _():
            pl.semaphore_signal(barrier, inc=1, device_id={"seq": at - 1}, device_id_type=MESH)
    if last:
        pl.semaphore_wait(barrier, 3)
    else:
        pl.semaphore_wait(barrier, 3 + (at < count - 1).astype(jnp.int32))
    copies = [send(sq, sqrx.at[2 - k], (qs.at[k], qr.at[2 - k]), {"head": pr}) for k, pr in enumerate(peers)]
    for copy in copies:
        copy.wait_send()
    for k in range(3):
        pltpu.make_async_remote_copy(src_ref=sq, dst_ref=sqrx.at[k], send_sem=qs.at[k], recv_sem=qr.at[k],
                                     device_id={"head": peers[2 - k]}, device_id_type=MESH).wait_recv()
    total_sq = ((sq[...] + sqrx[0]) + (sqrx[1] + sqrx[2]))[0:1, :]
    r2row = lax.rsqrt(total_sq / width + EPS)
    r2b[...] = jnp.transpose(jnp.broadcast_to(r2row, (LANE, tokens)))
    inner = gated.shape[1]

    def part(start, rows):
        where = pl.ds(start, rows)
        r2 = jnp.concatenate([r2b[where, :]] * (inner // LANE), axis=1)
        return bdot(gated[where, :] * r2 * ggain[...], wout[...], NN)

    d = wout.shape[1]

    def middle(s, sub, total):
        rows = pl.ds(s * sub, sub)
        branch[rows, :] = total
        h = h_own[rows, :] + total
        h_new[rows, :] = h
        if last:
            krc[rows, :] = jnp.broadcast_to(jnp.sum(extra[rows, :].astype(F32) * total, axis=1, keepdims=True), (sub, LANE))
            if s == SUBS - 1:
                mine = pl.ds(pl.multiple_of(((me % 2) * 2 + me // 2) * 8, 8), 8)
                side[mine, :] = jnp.transpose(krc[...])[0:8, :]
            return h.astype(BF16)
        r1 = lax.rsqrt(jnp.sum(h * h, axis=1, keepdims=True) / d + EPS)
        return (h * r1 * extra[...]).astype(BF16)

    off = 0 if last else HALO
    load.wait()
    if not last:
        side[...] = jnp.zeros_like(side)
    head_core(tokens, part, middle, nx, off, side if last else None, tx0, rx0, tx1, rx1, acc, ssem, rsem, me,
              {"head": flip(me, 1)}, {"head": flip(me, 2)})
    if not last:
        src = nx.at[pl.ds(tokens, HALO), :]
        dst = nx.at[pl.ds(0, HALO), :]
        copy = pltpu.make_async_remote_copy(src_ref=src, dst_ref=dst, send_sem=hs.at[0], recv_sem=hr.at[0],
                                            device_id={"seq": lax.rem(at + 1, count)}, device_id_type=MESH)

        @pl.when(at < count - 1)
        def _():
            copy.start()
            copy.wait_send()

        @pl.when(at > 0)
        def _():
            copy.wait_recv()

        @pl.when(at == 0)
        def _():
            nx[pl.ds(0, HALO), :] = jnp.zeros((HALO, d), BF16)


def head_scratch(tokens, d, kind=BF16):
    sub = tokens // 4 // SUBS
    return [pltpu.VMEM((2, SUBS, sub, d), kind), pltpu.VMEM((2, SUBS, sub, d), kind), pltpu.VMEM((SUBS, sub, d), kind),
            pltpu.VMEM((SUBS, sub, d), kind), pltpu.VMEM((tokens // 2, d), F32), pltpu.VMEM((tokens // 4, LANE), F32),
            pltpu.SemaphoreType.DMA((HEAD_COPIES,)), pltpu.SemaphoreType.DMA((HEAD_COPIES,))]


def head_bwd_body(l, tokens, gz, gu, small, wzx_all, wsmall_all, h_own, gain_all, g_own, branch,
                  gb, g_new, ggain, side, tx0, rx0, tx1, rx1, acc, krc, ssem, rsem, wzx, wsem):
    load = pltpu.make_async_copy(wzx_all.at[l], wzx, wsem.at[0])
    load.start()
    wsmall = wsmall_all.at[l]
    gain = gain_all.at[l]
    me = lax.axis_index("head")
    core_at, y_at = {"head": flip(me, 1)}, {"head": flip(me, 2)}
    greet([core_at, y_at])
    d = gain.shape[1]

    def part(start, rows):
        where = pl.ds(start, rows)
        return bdot(gz[where, :], wzx[0], NT) + bdot(gu[where, :], wzx[1], NT) + bdot(small[where, :], wsmall[...], NT)

    def middle(s, sub, total):
        rows = pl.ds(s * sub, sub)
        h = h_own[rows, :]
        r1 = lax.rsqrt(jnp.sum(h * h, axis=1, keepdims=True) / d + EPS)
        th = total * h
        gg = jnp.sum(th * r1, axis=0, keepdims=True)
        if s == 0:
            ggain[...] = gg
        else:
            ggain[...] += gg
        k1 = jnp.sum(th * gain[...], axis=1, keepdims=True)
        g = g_own[rows, :] + r1 * (gain[...] * total) - h * (r1 * r1 * r1 * (k1 / d))
        g_new[rows, :] = g
        low = g.astype(BF16)
        krc[rows, :] = jnp.broadcast_to(jnp.sum(low.astype(F32) * branch[rows, :], axis=1, keepdims=True), (sub, LANE))
        if s == SUBS - 1:
            mine = pl.ds(pl.multiple_of(((me % 2) * 2 + me // 2) * 8, 8), 8)
            side[mine, :] = jnp.transpose(krc[...])[0:8, :]
        return low

    load.wait()
    head_core(tokens, part, middle, gb, 0, side, tx0, rx0, tx1, rx1, acc, ssem, rsem, me, core_at, y_at)


def maps_bwd_body(l, tokens, dkr, ubc, taps_all, aux, gdt, gtail, gm8, tapx_all,
                  small, gtaps, gtail_o, ytx, yrx, yacc, ctx, crx, us, ms, nextx, nextb, gmb, sems, semr):
    taps, tapx = taps_all.at[l], tapx_all.at[l]
    me = lax.axis_index("head")
    at = lax.axis_index("seq")
    count = lax.axis_size("seq")
    c = me % 2
    y = me // 2
    core_at, y_at = {"head": flip(me, 1)}, {"head": flip(me, 2)}
    barrier = pltpu.get_barrier_semaphore()
    for where in (core_at, y_at):
        pl.semaphore_signal(barrier, inc=1, device_id=where, device_id_type=MESH)

    @pl.when(at < count - 1)
    def _():
        pl.semaphore_signal(barrier, inc=1, device_id={"seq": at + 1}, device_id_type=MESH)
    pl.semaphore_wait(barrier, 2 + (at > 0).astype(jnp.int32))
    lanes = lax.broadcasted_iota(jnp.int32, (tokens, LANE), 1)
    before = {"seq": lax.rem(at + count - 1, count)}
    ahead_x = pltpu.make_async_remote_copy(src_ref=gm8, dst_ref=nextx, send_sem=sems.at[2], recv_sem=semr.at[2],
                                           device_id=before, device_id_type=MESH)

    @pl.when(at > 0)
    def _():
        ahead_x.start()
    low, high = dkr[:, :LANE], dkr[:, LANE:]
    ytx[...] = jnp.where(y == 0, high, low)
    one = send(ytx, yrx, (sems.at[0], semr.at[0]), y_at)
    tile = pl.ds(pl.multiple_of(y * LANE, LANE), LANE)
    us[...] = ubc[:, tile].astype(F32)
    tp = taps[:, tile]
    m = mix_taps(us, tp, aux, LANE)
    s = sig(m)
    slope = s * (1.0 + m * (1.0 - s))
    one.wait()
    ctx[...] = jnp.where(y == 0, low, high) + yrx[...]
    two = send(ctx, crx, (sems.at[1], semr.at[1]), core_at)
    two.wait()
    gm = (ctx[...] + crx[...]) * slope
    gmb[...] = gm[0:8]
    ahead_b = pltpu.make_async_remote_copy(src_ref=gmb, dst_ref=nextb, send_sem=sems.at[3], recv_sem=semr.at[3],
                                           device_id=before, device_id_type=MESH)

    @pl.when(at > 0)
    def _():
        ahead_b.start()

    @pl.when(at == count - 1)
    def _():
        nextx[...] = jnp.zeros_like(nextx)
        nextb[...] = jnp.zeros_like(nextb)
    gtaps[...] = jnp.zeros_like(gtaps)
    gtaps[0:1, :] = jnp.sum(gm * us[pl.ds(HALO, tokens), :], axis=0, keepdims=True)
    gtaps[CONV : CONV + 1, :] = jnp.sum(gm, axis=0, keepdims=True)
    for j in range(1, CONV):
        gtaps[j : j + 1, :] = jnp.sum(gm * aux[j - 1] * us[pl.ds(HALO - j, tokens), :], axis=0, keepdims=True)

    @pl.when(at < count - 1)
    def _():
        ahead_x.wait_recv()
        ahead_b.wait_recv()
    acc = gm * tp[0:1, :]
    for j in range(1, CONV):
        ms[pl.ds(0, tokens), :] = gm * aux[j - 1]
        ms[pl.ds(tokens, 8), :] = nextb[...]
        acc = acc + ms[pl.ds(j, tokens), :] * tp[j : j + 1, :]
    own = jnp.where(c == 0, lanes, LANE - 1 - lanes) < 64
    g = gdt[...].astype(F32)
    moved = jnp.concatenate([g[:, 64:], g[:, :64]], axis=1)
    small[...] = jnp.where(own, acc, jnp.where(c == 0, moved, g)).astype(BF16)
    gtail_o[...] = gtail[...].astype(BF16)
    nx = nextx[...]
    tail = gtail[...]
    rows = lax.broadcasted_iota(jnp.int32, tail.shape, 0)
    for j in range(1, CONV):
        for k in range(j):
            tail = tail + jnp.where(rows == 16 - j + k, nx[k : k + 1, :] * tapx[j : j + 1, :], 0.0)
    gtail_o[...] = tail.astype(BF16)

    @pl.when(at > 0)
    def _():
        ahead_x.wait_send()
        ahead_b.wait_send()


def pack_body(parts, *refs):
    ins = refs[: 6 * parts]
    stage, rx, ssem, rsem = refs[6 * parts :]
    inner = stage.shape[2]
    me = lax.axis_index("head")
    bits = bits_of("head")
    wheres = [{"head": flip(me, b)} for b in bits]
    greet(wheres)
    stage[...] = jnp.zeros_like(stage)
    for l in range(parts):
        taps, gate, skip, vec, maps, gain = ins[6 * l : 6 * l + 6]
        stage[l, 0 : CONV + 1, :] = taps[0 : CONV + 1, :]
        stage[l, 5:6, :] = gate[...]
        stage[l, 6:7, :] = skip[...]
        stage[l, 7:8, 0:LANE] = vec[0:1, :]
        stage[l, 7:8, LANE : 2 * LANE] = vec[1:2, :]
        stage[l, 8:9, :] = gain[:, :inner]
        stage[l, 9:10, :] = gain[:, inner:]
        for r in range(CONV + 1):
            row = maps[r : r + 1, :] * 0.5
            here = [jnp.where(me // 2 == k, row, 0.0) for k in range(2)]
            stage[l, 10 + r // 3 : 11 + r // 3, (r % 3) * 2 * LANE : ((r % 3) * 2 + 2) * LANE] = jnp.concatenate(here, axis=1)
    where = pl.ds(8, 8)
    for i in range(len(bits)):
        copy = send(stage.at[:, where, :], rx.at[i], (ssem.at[i], rsem.at[i]), wheres[i])
        copy.wait()
        stage[:, 8:16, :] += rx[i]


def unpack_body(parts, stage, conv_x, conv_bc, ggate, gskip, gvec, ggain):
    inner = stage.shape[2]
    for l in range(parts):
        conv_x[l] = stage[l, 0 : CONV + 1, :]
        ggate[l : l + 1, :] = stage[l, 5:6, :]
        gskip[l : l + 1, :] = stage[l, 6:7, :]
        gvec[l : l + 1, :] = stage[l, 7:8, 0 : 2 * LANE]
        ggain[l : l + 1, :inner] = stage[l, 8:9, :]
        ggain[l : l + 1, inner:] = stage[l, 9:10, :]
        for r in range(CONV + 1):
            conv_bc[l, r : r + 1, :] = stage[l, 10 + r // 3 : 11 + r // 3, (r % 3) * 2 * LANE : ((r % 3) * 2 + 2) * LANE]


VM = pl.BlockSpec(memory_space=pltpu.VMEM)
S = jax.ShapeDtypeStruct


def of_layer(l, shape, steps=False):
    n = len(shape) - 1
    if steps:
        return pl.BlockSpec((None,) + shape[1:-1] + (LANE,), lambda p: (l,) + (0,) * (n - 1) + (p,))
    return pl.BlockSpec((None,) + shape[1:], lambda *p: (l,) + (0,) * n)


def rows_of_layer(l, shape):
    return pl.BlockSpec((None, LANE, shape[2]), lambda p: (l, p, 0))


def kcall(body, args, specs, us, after=(), cid=None, **kw):
    n, k = len(args), len(after)

    def wrapped(*refs):
        body(*refs[:n], *refs[n + k :])

    extra = {} if cid is None else dict(collective_id=cid, has_side_effects=True)
    return pl.pallas_call(
        wrapped,
        in_specs=list(specs) + [pl.BlockSpec(memory_space=pl.ANY)] * k,
        compiler_params=pltpu.CompilerParams(vmem_limit_bytes=VMEM_LIMIT, **extra),
        cost_estimate=pl.CostEstimate(flops=int(us * 1e9), bytes_accessed=int(us * 3e6), transcendentals=0),
        **kw,
    )(*args, *after)


def fwd_mix(l, heads, size, nx, q, aux, segrow):
    tokens = aux.shape[1]
    ext, d = nx.shape
    inner = q["conv_x"].shape[2]
    two = q["w_bc"].shape[2]
    args = [nx, q["w_zx"], q["w_bc"], q["w_dt"], q["conv_x"], q["conv_bc"], q["dt_bias"], q["a_log"], q["skip"], aux, segrow]
    specs = [full(nx.shape), of_layer(l, q["w_zx"].shape, True), of_layer(l, q["w_bc"].shape), of_layer(l, q["w_dt"].shape),
             of_layer(l, q["conv_x"].shape, True), of_layer(l, q["conv_bc"].shape), of_layer(l, q["dt_bias"].shape),
             of_layer(l, q["a_log"].shape), of_layer(l, q["skip"].shape, True), full(aux.shape), full(segrow.shape)]
    return kcall(
        partial(fwd_mix_body, heads, size), args, specs, 16,
        name="fwd_mix",
        grid=(inner // LANE,),
        out_specs=[cols(tokens), cols(ext), full((ext, two)), full((tokens, two)), full((tokens, LANE)), full((tokens, LANE)),
                   full((tokens, LANE)), full((LANE, tokens)), full((tokens, tokens)), cols(tokens), cols(tokens),
                   cols(tokens), rowsb(two // 2), full((16, LANE)), full((8, LANE))],
        out_shape=[S((tokens, inner), BF16), S((ext, inner), BF16), S((ext, two), BF16), S((tokens, two), F32),
                   S((tokens, LANE), BF16), S((tokens, LANE), F32), S((tokens, LANE), F32), S((LANE, tokens), F32),
                   S((tokens, tokens), F32), S((tokens, inner), F32), S((tokens, inner), F32), S((tokens, inner), F32),
                   S((inner, two // 2), F32), S((16, LANE), F32), S((8, LANE), F32)],
        scratch_shapes=[pltpu.VMEM((ext, LANE), F32), pltpu.VMEM((ext, two), F32), pltpu.VMEM((2, tokens, LANE), F32)],
    )


def fwd_gate(ypart, entry, gate, krs, enter):
    tokens, inner = ypart.shape
    return kcall(
        fwd_gate_body, [ypart, entry, gate, krs, enter],
        [cols(tokens), cols(tokens), cols(tokens), full(krs.shape), rowsb(enter.shape[1])], 7,
        name="fwd_gate",
        grid=(inner // LANE,),
        out_specs=[cols(tokens), cols(tokens), cols(tokens), full((8, tokens))],
        out_shape=[S((tokens, inner), F32)] * 3 + [S((8, tokens), F32)],
        scratch_shapes=[pltpu.VMEM((tokens, LANE), F32)],
    )


def bwd_gate(l, gb, q, gate, y, mixed, entry, krs, r2b, krb):
    tokens, inner = y.shape
    states = krs.shape[1] // 2
    return kcall(
        bwd_gate_body, [gb, q["w_out"], gate, y, mixed, entry, krs, r2b, krb, q["gate_gain"]],
        [full(gb.shape), rows_of_layer(l, q["w_out"].shape), cols(tokens), cols(tokens), cols(tokens), cols(tokens), full(krs.shape),
         full(r2b.shape), full(krb.shape), of_layer(l, q["gate_gain"].shape, True)], 9,
        name="bwd_gate",
        grid=(inner // LANE,),
        out_specs=[cols(tokens), cols(tokens), cols(tokens), rowsb(states), cols(1), cols(1)],
        out_shape=[S((tokens, inner), F32), S((tokens, inner), BF16), S((tokens, inner), BF16), S((inner, states), F32),
                   S((1, inner), F32), S((1, inner), F32)],
    )


def bwd_local(size, gy, mixed, krs, cum, steps, cT, gram, entry, enter, aux, segrow, after):
    tokens, inner = gy.shape
    two = krs.shape[1]
    return kcall(
        partial(bwd_local_body, size), [gy, mixed, krs, cum, steps, cT, gram, entry, enter, aux, segrow],
        [cols(tokens), cols(tokens), full(krs.shape), full(cum.shape), full(steps.shape), full(cT.shape), full(gram.shape),
         cols(tokens), rowsb(two // 2), pl.BlockSpec((None, tokens, LANE), lambda p: (5, 0, 0)), full(segrow.shape)], 10, after,
        name="bwd_local",
        grid=(inner // LANE,),
        out_specs=[cols(tokens), full((tokens, LANE)), full((LANE, tokens)), full((tokens, two))],
        out_shape=[S((tokens, inner), F32), S((tokens, LANE), F32), S((LANE, tokens), F32), S((tokens, two), F32)],
        scratch_shapes=[pltpu.VMEM((tokens, LANE), F32), pltpu.VMEM((tokens, LANE), F32), pltpu.VMEM((tokens, tokens), F32),
                        pltpu.VMEM((tokens, tokens), F32), pltpu.VMEM((tokens, LANE), BF16), pltpu.VMEM((tokens, LANE), BF16)],
    )


def bwd_carry(l, size, gy, dvd, mixed, carr, entry, krs, cum, steps, pdt, q, ux, aux, later, enter, dd, rowT, dkr, decl):
    tokens, inner = gy.shape
    ext = ux.shape[0]
    two = krs.shape[1]
    return kcall(
        partial(bwd_carry_body, size),
        [gy, dvd, mixed, carr, entry, krs, cum, steps, pdt, q["dt_bias"], q["a_log"], q["skip"], ux, q["conv_x"], aux, later, enter,
         dd, rowT, dkr, decl],
        [cols(tokens), cols(tokens), cols(tokens), cols(tokens), cols(tokens), full(krs.shape), full(cum.shape), full(steps.shape),
         full(pdt.shape), of_layer(l, q["dt_bias"].shape), of_layer(l, q["a_log"].shape), of_layer(l, q["skip"].shape, True), cols(ext),
         of_layer(l, q["conv_x"].shape, True), full(aux.shape), rowsb(two // 2), rowsb(two // 2), full(dd.shape), full(rowT.shape),
         full(dkr.shape), full(decl.shape)], 11,
        name="bwd_carry",
        grid=(inner // LANE,),
        out_specs=[cols(8), cols(tokens), cols(16), cols(8), full((tokens, LANE)), full((8, LANE)), full((tokens, two))],
        out_shape=[S((8, inner), F32), S((tokens, inner), BF16), S((16, inner), F32), S((8, inner), F32), S((tokens, LANE), BF16),
                   S((8, LANE), F32), S((tokens, two), F32)],
        scratch_shapes=[pltpu.VMEM((ext, LANE), F32), pltpu.VMEM((tokens + 8, LANE), F32), pltpu.VMEM((tokens, LANE), F32),
                        pltpu.VMEM((tokens, LANE), F32), pltpu.VMEM((1, LANE), F32)],
    )


def carry_kernel(state, dec, heads, size, reverse, cid, after=()):
    bits = bits_of("seq")
    rows, states = state.shape
    n = len(bits)
    return kcall(
        partial(carry_body, bits, reverse, heads, size), [state, dec], [VM] * 2, 25, after, cid,
        name="carry_back" if reverse else "carry_on",
        out_specs=VM,
        out_shape=S((rows, states), F32),
        scratch_shapes=[pltpu.VMEM((rows, states), BF16), pltpu.VMEM((n, rows, states), BF16 if reverse else F32), pltpu.VMEM(dec.shape, F32),
                        pltpu.VMEM((n,) + dec.shape, F32), pltpu.VMEM((rows, states), F32),
                        pltpu.SemaphoreType.DMA((2 * n,)), pltpu.SemaphoreType.DMA((2 * n,))],
    )


def head_fwd(l, gated, sq, q, h_own, extra, last, width, cid):
    tokens, inner = gated.shape
    d = q["w_out"].shape[2]
    return kcall(
        partial(head_fwd_body, l, tokens, last, width), [gated, sq, q["gate_gain"], q["w_out"], h_own, extra],
        [VM, VM, VM, pl.BlockSpec(memory_space=pl.ANY), VM, VM], 30, (), cid,
        name="head_fwd_last" if last else "head_fwd",
        out_specs=[VM] * 5,
        out_shape=[S((tokens if last else tokens + HALO, d), BF16), S((tokens // 4, d), F32), S((tokens // 4, d), F32),
                   S((tokens, LANE), F32), S((32, LANE), F32)],
        scratch_shapes=[pltpu.VMEM((3, 8, tokens), F32)] + head_scratch(tokens, d, BF16 if last else F32)
        + [pltpu.SemaphoreType.DMA((3,)), pltpu.SemaphoreType.DMA((3,)), pltpu.SemaphoreType.DMA((1,)), pltpu.SemaphoreType.DMA((1,)), pltpu.VMEM((inner, d), BF16), pltpu.SemaphoreType.DMA((1,))],
    )


def head_bwd(l, gz, gu, small, q, h_own, g_own, branch, cid, after=()):
    tokens = gz.shape[0]
    d = h_own.shape[1]
    return kcall(
        partial(head_bwd_body, l, tokens), [gz, gu, small, q["w_zx"], q["w_small"], h_own, q["gain"], g_own, branch],
        [VM, VM, VM, pl.BlockSpec(memory_space=pl.ANY), VM, VM, VM, VM, VM], 29, after, cid,
        name="head_bwd",
        out_specs=[VM] * 4,
        out_shape=[S((tokens, d), BF16), S((tokens // 4, d), F32), S((1, d), F32), S((32, LANE), F32)],
        scratch_shapes=head_scratch(tokens, d) + [pltpu.VMEM(q["w_zx"].shape[1:], BF16), pltpu.SemaphoreType.DMA((1,))],
    )


def maps_bwd(l, dkr, ubc, q, aux, gdt, gtail, gm8, cid, after=()):
    tokens = dkr.shape[0]
    inner = gtail.shape[1]
    tile = pltpu.VMEM((tokens, LANE), F32)
    return kcall(
        partial(maps_bwd_body, l, tokens), [dkr, ubc, q["conv_bc"], aux, gdt, gtail, gm8, q["conv_x"]],
        [VM] * 8, 14, after, cid,
        name="maps_bwd",
        out_specs=[VM] * 3,
        out_shape=[S((tokens, LANE), BF16), S((8, LANE), F32), S((16, inner), BF16)],
        scratch_shapes=[tile, tile, tile, tile, tile, pltpu.VMEM((tokens + HALO, LANE), F32), pltpu.VMEM((tokens + 8, LANE), F32),
                        pltpu.VMEM((8, inner), F32), pltpu.VMEM((8, LANE), F32), pltpu.VMEM((8, LANE), F32),
                        pltpu.SemaphoreType.DMA((4,)), pltpu.SemaphoreType.DMA((4,))],
    )


def pack_small(smalls, inner, cid):
    parts = len(smalls)
    n = len(bits_of("head"))
    return kcall(
        partial(pack_body, parts), [x for part in smalls for x in part], [VM] * (6 * parts), 8, (), cid,
        name="pack_small",
        out_specs=VM,
        out_shape=S((parts, 16, inner), F32),
        scratch_shapes=[pltpu.VMEM((n, parts, 8, inner), F32), pltpu.SemaphoreType.DMA((n,)), pltpu.SemaphoreType.DMA((n,))],
    )


def unpack_small(stage, d):
    parts, _, inner = stage.shape
    return kcall(
        partial(unpack_body, parts), [stage], [VM], 2,
        name="unpack_small",
        out_specs=[VM] * 6,
        out_shape=[S((parts, CONV + 1, inner), F32), S((parts, CONV + 1, 2 * LANE), F32), S((parts, inner), F32), S((parts, inner), F32),
                   S((parts, 2 * LANE), F32), S((parts, d), F32)],
    )


def wgrad_body(blocks, bit, off, n_rhs, lhs, *refs):
    rhs, (away, keep, lt) = refs[:n_rhs], refs[n_rhs:]
    tokens = rhs[0].shape[0]
    lt[...] = jnp.transpose(lhs[pl.ds(off, tokens), :])
    mine = (lax.axis_index("seq") // bit) % 2
    block = lt.shape[0] // blocks

    def one(k, carry):
        for dst, want in ((away, 1 - mine), (keep, mine)):
            at = (k // bit) * (2 * bit) + want * bit + lax.rem(k, bit)
            rows = lt[pl.ds(pl.multiple_of(at * block, 16), block), :]
            c = 0
            for r in rhs:
                w = r.shape[1]
                dst[k, :, c : c + w] = bdot(rows, r[...], NN).astype(BF16)
                c += w
        return carry

    lax.fori_loop(0, blocks // 2, one, 0)


def wgrad(lhs, rhs, bit, after=()):
    blocks = lax.axis_size("seq")
    tokens = rhs[0].shape[0]
    d = lhs.shape[1]
    width = sum(r.shape[1] for r in rhs)
    shape = (blocks // 2, d // blocks, width)
    return kcall(
        partial(wgrad_body, blocks, bit, lhs.shape[0] - tokens, len(rhs)), [lhs] + list(rhs), [VM] * (1 + len(rhs)), 3, after,
        name="wgrad",
        out_specs=[VM] * 2,
        out_shape=[S(shape, BF16)] * 2,
        scratch_shapes=[pltpu.VMEM((d, tokens), BF16)],
    )


class Halving:
    def __init__(self, lhs, rhs, order, after=()):
        bits = bits_of("seq")
        self.order = [bits[i % len(bits)] for i in order] + [b for i, b in enumerate(bits) if i not in order]
        self.left = [b for b in reversed(bits)]
        self.away, self.keep = wgrad(lhs, rhs, self.order[0], after)
        self.left.remove(self.order[0])
        self.step = 0
        self.got = None

    def go(self):
        self.got = swap(self.away, "seq", self.order[self.step])
        self.step += 1
        return self.got

    def fold(self):
        total = self.keep.astype(F32) + self.got.astype(F32)
        if self.step == len(self.order):
            self.total = total[0] if total.ndim == 3 else total
            return self.total
        bit = self.order[self.step]
        axis = self.left.index(bit)
        view = total.reshape((2,) * len(self.left) + total.shape[-2:])
        me = my_bit("seq", bit)
        pick = lambda i: take(view, axis, i).astype(BF16).reshape((-1,) + total.shape[-2:])
        self.away, self.keep = pick(1 - me), pick(me)
        self.left.remove(bit)

    def finish(self):
        while self.step < len(self.order):
            self.go()
            self.fold()
        return self.total


def pad_lanes(x, to=LANE):
    return jnp.pad(x, [(0, 0)] * (x.ndim - 1) + [(0, to - x.shape[-1])])


def forward_layer(nx, h_own, extra, q, aux, segrow, layer):
    heads, size, inner = q["heads"], q["size"], q["inner"]
    (gate, ux, ubc, krs, pdt, steps, cum, cT, gram, mixed, ypart, entry, state, dec, decl) = fwd_mix(layer, heads, size, nx, q, aux, segrow)
    enter = carry_kernel(state, dec, heads, size, False, layer)
    y, carr, gated, sq = fwd_gate(ypart, entry, gate, krs, enter)
    width = inner * lax.axis_size("head")
    nx_next, h_new, branch, r2b, side = head_fwd(layer, gated, sq, q, h_own, extra, layer == LAYERS - 1, width, LAYERS + layer)
    stored = dict(nx=nx, gate=gate, ux=ux, ubc=ubc, krs=krs, pdt=pdt, steps=steps, cum=cum, cT=cT, gram=gram, mixed=mixed,
                  entry=entry, dec=dec, decl=decl, enter=enter, y=y, carr=carr, r2b=r2b, branch=branch, h_own=h_own)
    return nx_next, h_new, side, stored


def backward_gate(gb, side, s, q, layer):
    tokens = gb.shape[0]
    width = q["inner"] * lax.axis_size("head")
    kr = side.reshape(4, 8, LANE)[:, 0, :].reshape(tokens)
    r2b = s["r2b"]
    krb = r2b * r2b * (kr[:, None] / width)
    return bwd_gate(layer, gb, q, s["gate"], s["y"], s["mixed"], s["entry"], s["krs"], r2b, krb)


def backward_mix(gy, later, s, q, aux, segrow, layer, after_local):
    size = q["size"]
    dvd, dd, rowT, dkr = bwd_local(size, gy, s["mixed"], s["krs"], s["cum"], s["steps"], s["cT"], s["gram"], s["entry"], s["enter"], aux, segrow, after_local)
    return bwd_carry(layer, size, gy, dvd, s["mixed"], s["carr"], s["entry"], s["krs"], s["cum"], s["steps"], s["pdt"], q,
                     s["ux"], aux, later, s["enter"], dd, rowT, dkr, s["decl"])


def local(hidden_in, seg, cot, norm_gain, w_zx, w_bc, w_dt, conv_x, conv_bc, dt_bias, a_log, skip_d, gate_gain, w_out):
    tokens = hidden_in.shape[0]
    inner = w_zx.shape[3]
    heads = w_dt.shape[2]
    size = inner // heads
    rank = lax.axis_index("head")
    segf = seg.astype(F32)
    ext = jnp.concatenate([jnp.full((HALO,), segf[0], F32), segf], 0)
    vecs = [(ext[HALO - j : HALO - j + tokens] == segf).astype(F32) for j in range(1, CONV)]
    vecs += [(segf == segf[0]).astype(F32), (segf == segf[-1]).astype(F32), segf]
    aux = jnp.broadcast_to(jnp.stack(vecs, 0)[:, :, None], (len(vecs), tokens, LANE))
    segrow = segf[None]
    lanes = jnp.arange(LANE)
    even = rank % 2 == 0
    own = jnp.where(even, lanes, LANE - 1 - lanes) < LANE // 2
    dt_pad = pad_lanes(w_dt)
    tile = lax.dynamic_slice_in_dim(w_bc, (rank // 2) * LANE, LANE, 2)
    w_small = jnp.where(own[None, None], tile, jnp.where(even, jnp.roll(dt_pad, LANE // 2, axis=2), dt_pad))
    q = dict(heads=heads, size=size, inner=inner, gain=norm_gain[:, None, :], w_zx=jnp.transpose(w_zx, (0, 2, 1, 3)), w_bc=w_bc, w_dt=dt_pad,
             w_small=w_small, conv_x=conv_x, conv_bc=conv_bc, dt_bias=pad_lanes(dt_bias[:, None, :]), a_log=pad_lanes(a_log[:, None, :]),
             skip=jnp.repeat(skip_d, size, axis=1)[:, None, :], gate_gain=gate_gain[:, None, :], w_out=w_out)
    h = hidden_in.astype(F32)
    h_own = own_rows(h)
    cot_own = own_rows(cot)
    normed = (h * lax.rsqrt(jnp.mean(h * h, axis=1, keepdims=True) + EPS) * norm_gain[0][None]).astype(BF16)
    nx = jnp.concatenate([shift(normed[tokens - HALO :], "seq", 1), normed], 0)
    stored = []
    for l in range(LAYERS):
        extra = cot_own if l == LAYERS - 1 else q["gain"]
        nx, h_own, side, s = forward_layer(nx, h_own, extra, q, aux, segrow, l)
        stored.append(s)
    hidden_out = nx
    gb = cot
    g_own = cot_own.astype(F32)
    smalls = [None] * LAYERS
    sums = [None] * LAYERS
    pending = []
    for l in reversed(range(LAYERS)):
        s = stored[l]
        gy, gz, scaled, qloc, ggate, gskip = backward_gate(gb, side, s, q, l)
        later = carry_kernel(qloc, s["dec"], heads, size, True, 2 * LAYERS + l, after=[p.got for p in pending])
        if pending:
            for p in pending:
                p.fold()
            out_up, z_up, x_up = pending
        out = Halving(gb, [scaled], (0, 1, 2), after=[later])
        z = Halving(s["nx"], [gz], (0, 1, 2), after=[later])
        first = [out.go()]
        gm8, gu, gtail, gtaps_x, gdt, gvec, dkr = backward_mix(gy, later, s, q, aux, segrow, l, ())
        small, gtaps_bc, gtail = maps_bwd(l, dkr, s["ubc"], q, aux, gdt, gtail, gm8, 3 * LAYERS + l, after=first)
        gu = lax.dynamic_update_slice(gu, gtail, (tokens - 16, 0))
        out.fold()
        z.go()
        out.go()
        x = Halving(s["nx"], [gu, small], (0, 1, 2))
        before = stored[max(l - 1, 0)]["branch"]
        gb, g_own, g_gain, side = head_bwd(l, gz, gu, small, q, s["h_own"], g_own, before, 4 * LAYERS + l, after=[x.away])
        x.go()
        smalls[l] = (gtaps_x, ggate, gskip, gvec, gtaps_bc, g_gain)
        pending = [out, z, x]
        sums[l] = pending
    grad_in = gb.astype(F32)
    for l in range(LAYERS):
        for p in sums[l]:
            if l == 0:
                p.fold()
            p.finish()
    g_w_zx = jnp.stack([jnp.stack([z.total, x.total[:, :inner]], 1) for _, z, x in sums], 0)
    g_small = jnp.stack([x.total[:, inner:] for _, _, x in sums], 0)
    g_w_bc = jnp.where(even, g_small[:, :, : LANE // 2], g_small[:, :, LANE // 2 :])
    g_w_dt = jnp.where(even, g_small[:, :, LANE // 2 : LANE // 2 + heads], g_small[:, :, :heads])
    g_w_out = jnp.stack([jnp.transpose(out.total) for out, _, _ in sums], 0)
    stage = pack_small(smalls, inner, 5 * LAYERS)
    for bit in bits_of("seq"):
        stage = stage + swap(stage, "seq", bit)
    g_conv_x, g_conv_bc, g_gate, g_skip, g_vec, g_gain = unpack_small(stage, norm_gain.shape[1])
    g_skip = jnp.sum(g_skip.reshape(LAYERS, heads, size), axis=2)
    part = g_gain.shape[1] // lax.axis_size("seq")
    g_gain = lax.dynamic_slice_in_dim(g_gain, lax.axis_index("seq") * part, part, 1)
    return (hidden_out, grad_in, g_gain, g_w_zx, g_w_bc, g_w_dt, g_conv_x, g_conv_bc,
            g_vec[:, :heads], g_vec[:, LANE : LANE + heads], g_skip, g_gate, g_w_out)


def solution(mesh):
    placed = (
        P("seq", None), P("seq"), P("seq", None), P(), P(None, None, None, "head"), P(), P(None, None, "head"),
        P(None, None, "head"), P(), P(None, "head"), P(None, "head"), P(None, "head"), P(None, "head"), P(None, "head", None),
    )
    return jax.shard_map(
        local,
        mesh=mesh,
        in_specs=placed,
        out_specs=(
            P("seq", None), P("seq", None), P(None, "seq"), P(None, "seq", None, "head"), P(None, "seq", "head"),
            P(None, "seq", "head"), P(None, None, "head"), P(), P(None, "head"), P(None, "head"), P(None, "head"),
            P(None, "head"), P(None, "head", "seq"),
        ),
        check_vma=False,
    )
```

```python
from functools import partial

import jax
import jax.numpy as jnp
from jax import lax
from jax.experimental import pallas as pl
from jax.experimental.pallas import tpu as pltpu
from jax.sharding import PartitionSpec as P

CONV = 4
LAYERS = 2
Z_ORDER = (1, 2, 0)
EPS = 1e-05
F32 = jnp.float32
BF16 = jnp.bfloat16


def dot(a, b, dims):
    return lax.dot_general(a.astype(BF16), b.astype(BF16), (dims, ((), ())), preferred_element_type=F32)


def mm(a, b):
    return dot(a, b, ((1,), (0,)))


def mm_nt(a, b):
    return dot(a, b, ((1,), (1,)))


def mm_tn(a, b):
    return dot(a, b, ((0,), (0,)))


def swap(x, axis, bit):
    n = lax.axis_size(axis)
    return lax.ppermute(x, axis, [(i, i ^ bit) for i in range(n)])


def shift(x, axis, by):
    n = lax.axis_size(axis)
    return lax.ppermute(x, axis, [(i, i + by) for i in range(n) if 0 <= i + by < n])


def bits_of(axis):
    n = lax.axis_size(axis)
    bits = []
    b = 1
    while b < n:
        bits.append(b)
        b *= 2
    return bits


def my_bit(axis, bit):
    return (lax.axis_index(axis) // bit) % 2


def take(x, dim, index):
    return lax.dynamic_index_in_dim(x, index, dim, keepdims=False)


def head_scatter(x):
    for bit in bits_of("head"):
        me = my_bit("head", bit)
        halves = x.reshape((2, x.shape[0] // 2) + x.shape[1:])
        got = swap(take(halves, 0, 1 - me).astype(BF16), "head", bit)
        x = take(halves, 0, me).astype(F32) + got.astype(F32)
    return x


def head_scatter_exact(x):
    for bit in bits_of("head"):
        me = my_bit("head", bit)
        halves = x.reshape((2, x.shape[0] // 2) + x.shape[1:])
        x = take(halves, 0, me) + swap(take(halves, 0, 1 - me), "head", bit)
    return x


def head_gather(x):
    for bit in reversed(bits_of("head")):
        me = my_bit("head", bit)
        got = swap(x, "head", bit)
        x = jnp.where(me == 0, jnp.concatenate([x, got], 0), jnp.concatenate([got, x], 0))
    return x


def own_rows(x):
    for bit in bits_of("head"):
        x = take(x.reshape((2, x.shape[0] // 2) + x.shape[1:]), 0, my_bit("head", bit))
    return x


def carry_scan(state, decay, reverse):
    total, total_d = state, decay
    entering = jnp.zeros_like(state)
    enter_d = jnp.ones_like(decay)
    for bit in bits_of("seq"):
        me = my_bit("seq", bit)
        other = swap(total.astype(BF16), "seq", bit).astype(F32)
        other_d = swap(total_d, "seq", bit)
        second = (me == 0) if reverse else (me == 1)
        entering = jnp.where(second, entering + enter_d[:, None, None] * other, entering)
        enter_d = jnp.where(second, enter_d * other_d, enter_d)
        total = jnp.where(
            second, total_d[:, None, None] * other + total, other_d[:, None, None] * total + other
        )
        total_d = total_d * other_d
    return entering


def silu_slope(v):
    s = jax.nn.sigmoid(v)
    return s * (1.0 + v * (1.0 - s))


def scatter_rows(x):
    bits = bits_of("seq")
    k = len(bits)
    n = lax.axis_size("seq")
    x = x.reshape((2,) * k + (x.shape[0] // n, x.shape[1]))
    for b in range(k):
        axis = k - 1 - b
        me = my_bit("seq", bits[b])
        got = swap(take(x, axis, 1 - me).astype(BF16), "seq", bits[b])
        x = take(x, axis, me).astype(F32) + got.astype(F32)
    return x


HALO = 16
LANE = 128
NT = ((1,), (1,))
NN = ((1,), (0,))
TN = ((0,), (0,))


def bdot(a, b, dims):
    return lax.dot_general(a.astype(BF16), b.astype(BF16), (dims, ((), ())), preferred_element_type=F32)


def halves(x):
    high = x.astype(BF16)
    return high, (x - high.astype(F32)).astype(BF16)


def dot3(a, b, dims):
    ah, al = halves(a)
    bh, bl = halves(b)
    return bdot(ah, bh, dims) + (bdot(ah, bl, dims) + bdot(al, bh, dims))


def hdot(a, b, dims):
    return lax.dot_general(a, b, (dims, ((), ())), precision=lax.Precision.HIGHEST, preferred_element_type=F32)


def sig(v):
    return 0.5 * jnp.tanh(0.5 * v) + 0.5


def softplus(v):
    e = jnp.exp(-jnp.abs(v))
    s = e / (2.0 + e)
    q = s * s
    series = 1.0 / 13.0
    for k in (11, 9, 7, 5, 3, 1):
        series = series * q + 1.0 / k
    return jnp.maximum(v, 0.0) + 2.0 * s * series


def mix_taps(us, taps, aux, width):
    tokens = aux.shape[1]
    wide = lambda m: m if width == LANE else jnp.concatenate([m] * (width // LANE), axis=1)
    acc = us[pl.ds(HALO, tokens), :] * taps[0:1, :] + taps[CONV : CONV + 1, :]
    for j in range(1, CONV):
        acc = acc + us[pl.ds(HALO - j, tokens), :] * wide(aux[j - 1]) * taps[j : j + 1, :]
    return acc


def pick_lane(values, h, lanes):
    return jnp.sum(jnp.where(lanes == h, values, 0.0), axis=1, keepdims=True)


def fwd_mix_body(size, nx, wzx, wbc, wdt, tapx, tapbc, dtb, lograte, aux, segrow,
                 gate, ux, ubc, krs, pdt, steps_o, cum_o, cT, gram, mixed_o, entry_o, state, dec, decl,
                 us, usbc):
    p = pl.program_id(0)
    tokens = aux.shape[1]
    states = wbc.shape[1] // 2
    lanes = lax.broadcasted_iota(jnp.int32, (tokens, LANE), 1)
    half = lanes < size

    @pl.when(p == 0)
    def _():
        bc = bdot(nx[...], wbc[...], NN).astype(BF16)
        ubc[...] = bc
        usbc[...] = bc.astype(F32)
        m = mix_taps(usbc, tapbc, aux, 2 * states)
        act = m * sig(m)
        krs[...] = act
        g = dot3(act[:, states:], act[:, :states], NT)
        ii = lax.broadcasted_iota(jnp.int32, (tokens, tokens), 0)
        jj = lax.broadcasted_iota(jnp.int32, (tokens, tokens), 1)
        segc = jnp.concatenate([aux[5]] * (tokens // LANE), axis=1)
        keep = (ii >= jj) & (segc == segrow[...])
        gram[...] = jnp.where(keep, g, 0.0)
        pd = bdot(nx[pl.ds(HALO, tokens), :], wdt[...], NN).astype(BF16)
        pdt[...] = pd
        st = softplus(pd.astype(F32) + dtb[...])
        steps_o[...] = st
        log = st * -jnp.exp(lograte[...])
        cum = hdot(jnp.where(ii >= jj, 1.0, 0.0), log, NN)
        cum_o[...] = cum
        cT[...] = cum.T
        keeps = aux[3, tokens - 1 : tokens, :]
        decl[...] = jnp.broadcast_to(jnp.exp(cum[tokens - 1 : tokens, :]) * keeps, (8, LANE))
        dec[...] = jnp.exp(jnp.broadcast_to(cT[0:16, tokens - 1 : tokens], (16, LANE))) * keeps

    gate[...] = bdot(nx[pl.ds(HALO, tokens), :], wzx[0], NN).astype(BF16)
    u = bdot(nx[...], wzx[1], NN).astype(BF16)
    ux[...] = u
    us[...] = u.astype(F32)
    m = mix_taps(us, tapx, aux, LANE)
    mixed_o[...] = m
    v = m * sig(m)
    cum = cum_o[...]
    st = steps_o[...]
    h0 = p * (LANE // size)
    dd = jnp.where(half, pick_lane(st, h0, lanes), pick_lane(st, h0 + 1, lanes))
    vd = v * dd
    ct = jnp.where(half, pick_lane(cum, h0, lanes), pick_lane(cum, h0 + 1, lanes))
    entry_o[...] = jnp.exp(ct) * aux[3]
    tail = jnp.exp(ct[tokens - 1 : tokens, :] - ct) * aux[4]
    state[...] = dot3(vd * tail, krs[:, :states], TN)


def fwd_inside_body(stages_of, size, mixed, steps, cum, cT, gram, skip, state, dec, ypart, enter, cb, *rest):
    p = pl.program_id(0)
    tokens = mixed.shape[0]
    stages = stages_of(state, dec, enter, *rest)
    for k, stage in enumerate(stages[:-1]):
        pl.when(p == k)(stage)
    lanes = lax.broadcasted_iota(jnp.int32, (tokens, LANE), 1)
    half = lanes < size
    h0 = p * (LANE // size)
    m = mixed[...]
    v = m * sig(m)
    st = steps[...]
    vh, vl = halves(v * jnp.where(half, pick_lane(st, h0, lanes), pick_lane(st, h0 + 1, lanes)))
    vhl = jnp.concatenate([vh, vl], axis=1)
    ys = []
    for k in range(LANE // size):
        h = h0 + k
        cb[k] = jnp.broadcast_to(pick_lane(cum[...], h, lanes), (tokens, LANE))
        row = cT[pl.ds(h, 1), :]
        parts = []
        for ib in range(tokens // LANE):
            tiles, lows = [], []
            ci = cb[k, pl.ds(ib * LANE, LANE), :]
            for jb in range(ib + 1):
                spread = ci - row[:, jb * LANE : (jb + 1) * LANE]
                if jb == ib:
                    spread = jnp.minimum(spread, 0.0)
                wh, wl = halves(jnp.exp(spread) * gram[pl.ds(ib * LANE, LANE), pl.ds(jb * LANE, LANE)])
                tiles.append(wh)
                lows.append(wl)
            joined = lambda t: t[0] if ib == 0 else jnp.concatenate(t, axis=1)
            both = bdot(joined(tiles), vhl[: (ib + 1) * LANE], NN)
            parts.append(both[:, :LANE] + (both[:, LANE:] + bdot(joined(lows), vh[: (ib + 1) * LANE], NN)))
        ys.append(jnp.concatenate(parts, axis=0))
    ypart[...] = jnp.where(half, ys[0], ys[1]) + skip[...] * v
    pl.when(p == pl.num_programs(0) - 1)(stages[-1])


def full(shape):
    n = len(shape)
    return pl.BlockSpec(shape, lambda p: (0,) * n)


def cols(rows):
    return pl.BlockSpec((rows, LANE), lambda p: (0, p))


def rowsb(width):
    return pl.BlockSpec((LANE, width), lambda p: (p, 0))


def fwd_gate_body(ypart, entry, gate, krs, enter, y, carr, gated, sq, sqacc):
    p = pl.program_id(0)
    states = krs.shape[1] // 2
    c = dot3(krs[:, states:], enter[...], NT) * entry[...]
    carr[...] = c
    yy = ypart[...] + c
    y[...] = yy
    z = gate[...].astype(F32)
    g = yy * (z * sig(z))
    gated[...] = g

    @pl.when(p == 0)
    def _():
        sqacc[...] = g * g

    @pl.when(p > 0)
    def _():
        sqacc[...] += g * g

    @pl.when(p == pl.num_programs(0) - 1)
    def _():
        sq[...] = jnp.broadcast_to(jnp.sum(jnp.transpose(sqacc[...]), axis=0, keepdims=True), sq.shape)


def bwd_gate_body(gb, wout, gate, y, mixed, entry, krs, r2b, krb, gain, gy_o, gz_o, scaled_o, qloc, ggate, gskip):
    states = krs.shape[1] // 2
    gs = bdot(gb[...], wout[...], NT)
    z = gate[...].astype(F32)
    s = sig(z)
    sil = z * s
    yy = y[...]
    gated = yy * sil
    r2 = r2b[...]
    gr = gated * r2
    ggate[...] = jnp.sum(gs * gr, axis=0, keepdims=True)
    scaled_o[...] = (gr * gain[...]).astype(BF16)
    gg = r2 * gain[...] * gs - gated * krb[...]
    gy = gg * sil
    gy_o[...] = gy
    gz_o[...] = (gg * yy * (s * (1.0 + z * (1.0 - s)))).astype(BF16)
    m = mixed[...]
    gskip[...] = jnp.sum(gy * (m * sig(m)), axis=0, keepdims=True)
    qloc[...] = bdot(gy * entry[...], krs[:, states:], TN)


def bwd_local_body(stages_of, size, gy_r, mixed, krs, cum, steps, cT, gram, entry, enter, segc, segrow, qloc, dec,
                   dvd, dd_o, rowT, dkr, later, cb, db, gramT, dgT, vb, gk, *rest):
    p = pl.program_id(0)
    stages = stages_of(qloc, dec, later, *rest)
    for k, stage in enumerate(stages[:-1]):
        pl.when(p == k)(stage)
    tokens = gy_r.shape[0]
    states = krs.shape[1] // 2
    lanes = lax.broadcasted_iota(jnp.int32, (tokens, LANE), 1)
    half = lanes < size

    @pl.when(p == 0)
    def _():
        gramT[...] = gram[...].T
        dgT[...] = jnp.zeros_like(dgT)
        dd_o[...] = jnp.zeros_like(dd_o)
        rowT[...] = jnp.zeros_like(rowT)
        dkr[...] = jnp.zeros_like(dkr)

    m = mixed[...]
    vb[...] = (m * sig(m)).astype(BF16)
    gy = gy_r[...]
    gyb = gy.astype(BF16)
    h0 = p * (LANE // size)
    outs = []
    for k in range(LANE // size):
        h = h0 + k
        gk[...] = jnp.where(half if k == 0 else jnp.logical_not(half), gy, 0.0).astype(BF16)
        cb[...] = jnp.broadcast_to(pick_lane(cum[...], h, lanes), (tokens, LANE))
        db[...] = jnp.broadcast_to(pick_lane(steps[...], h, lanes), (tokens, LANE))
        row = cT[pl.ds(h, 1), :]
        parts = []
        dds = []
        rows_acc = [jnp.zeros((8, LANE), F32) for _ in range(tokens // LANE)]
        for jb in range(tokens // LANE):
            js = pl.ds(jb * LANE, LANE)
            cj = cb[js, :]
            dj = db[js, :]
            pt = bdot(vb[js, :], gk[pl.ds(jb * LANE, tokens - jb * LANE), :], NT)
            ws = []
            dsum = None
            for ib in range(jb, tokens // LANE):
                sl = pl.ds(ib * LANE, LANE)
                spread = row[:, ib * LANE : (ib + 1) * LANE] - cj
                if jb == ib:
                    spread = jnp.minimum(spread, 0.0)
                e = jnp.exp(spread)
                w = e * gramT[js, sl]
                ws.append(w.astype(BF16))
                pp = pt[:, (ib - jb) * LANE : (ib - jb + 1) * LANE]
                wp = w * pp
                dgT[js, sl] += e * (pp * dj)
                x = wp * dj
                rows_acc[ib] = rows_acc[ib] + jnp.sum(x.reshape(LANE // 8, 8, LANE), axis=0)
                dsum = wp if dsum is None else dsum + wp
            dds.append(jnp.sum(dsum, axis=1, keepdims=True))
            w = ws[0] if len(ws) == 1 else jnp.concatenate(ws, axis=1)
            parts.append(bdot(w, gyb[jb * LANE :], NN))
        outs.append(jnp.concatenate(parts, axis=0))
        dd_o[...] += jnp.where(lanes == h, jnp.concatenate(dds, axis=0), 0.0)
        rowT[pl.ds(h, 1), :] = jnp.concatenate([jnp.sum(r, axis=0, keepdims=True) for r in rows_acc], axis=1)
    dvd[...] = jnp.where(half, outs[0], outs[1])
    dkr[:, states:] += bdot(gy * entry[...], enter[...], NN)

    @pl.when(p == pl.num_programs(0) - 1)
    def _():
        jj = lax.broadcasted_iota(jnp.int32, (tokens, tokens), 0)
        ii = lax.broadcasted_iota(jnp.int32, (tokens, tokens), 1)
        segs = jnp.concatenate([segc[...]] * (tokens // LANE), axis=1)
        g = jnp.where((ii >= jj) & (segs == segrow[...]), dgT[...], 0.0)
        dkr[:, :states] += bdot(g, krs[:, states:], NN)
        dkr[:, states:] += bdot(g, krs[:, :states], TN)
        stages[-1]()


def bwd_carry_body(size, gy_r, dvd_r, mixed, carr, entry, krs, cum, steps, pdt, dtb, lograte, skip, ux, tapx, aux, later, enter,
                   dd_r, rowT, dkr_r, decay,
                   gm_o, gu_o, gtail_o, gtaps, gdt_o, gvec, dkr, us, ms, ddacc, dcum, last):
    p = pl.program_id(0)
    tokens = gy_r.shape[0]
    states = krs.shape[1] // 2
    lanes = lax.broadcasted_iota(jnp.int32, (tokens, LANE), 1)
    lane1 = lax.broadcasted_iota(jnp.int32, (1, LANE), 1)
    half = lanes < size

    @pl.when(p == 0)
    def _():
        ddacc[...] = dd_r[...]
        dcum[...] = jnp.transpose(rowT[...]) - dd_r[...] * steps[...]
        last[...] = jnp.zeros_like(last)
        dkr[...] = dkr_r[...]

    h0 = p * (LANE // size)
    st = steps[...]
    cu = cum[...]
    cc = [pick_lane(cu, h0 + k, lanes) for k in range(2)]
    dcol = [pick_lane(st, h0 + k, lanes) for k in range(2)]
    ct = jnp.where(half, cc[0], cc[1])
    dpair = jnp.where(half, dcol[0], dcol[1])
    tail = jnp.exp(ct[tokens - 1 : tokens, :] - ct) * aux[4]
    m = mixed[...]
    s = sig(m)
    v = m * s
    gy = gy_r[...]
    qk = bdot(krs[:, :states], later[...], NT) * tail
    dvd = dvd_r[...] + qk
    dkr[:, :states] += bdot(v * dpair * tail, later[...], NN)
    tq = v * qk
    eq = gy * carr[...]
    qs = later[...] * enter[...]
    for k in range(2):
        h = h0 + k
        mine = half if k == 0 else jnp.logical_not(half)
        td = jnp.sum(jnp.where(mine, tq, 0.0), axis=1, keepdims=True)
        ec = jnp.sum(jnp.where(mine, eq, 0.0), axis=1, keepdims=True)
        tdd = td * dcol[k]
        ddacc[...] += jnp.where(lanes == h, td, 0.0)
        dcum[...] += jnp.where(lanes == h, ec - tdd, 0.0)
        dot_qs = jnp.sum(jnp.sum(qs[k * size : (k + 1) * size, :], axis=0, keepdims=True), axis=1, keepdims=True)
        last[...] += jnp.where(lane1 == h, jnp.sum(tdd, axis=0, keepdims=True) + dot_qs * decay[0:1, :], 0.0)
    dv = dvd * dpair + skip[...] * gy
    gm = dv * (s * (1.0 + m * (1.0 - s)))
    gm_o[...] = gm[:8]
    us[...] = ux[...].astype(F32)
    acc = gm * tapx[0:1, :]
    gtaps[0:1, :] = jnp.sum(gm * us[pl.ds(HALO, tokens), :], axis=0, keepdims=True)
    gtaps[CONV : CONV + 1, :] = jnp.sum(gm, axis=0, keepdims=True)
    ms[pl.ds(tokens, 8), :] = jnp.zeros((8, LANE), F32)
    for j in range(1, CONV):
        gmj = gm * aux[j - 1]
        gtaps[j : j + 1, :] = jnp.sum(gmj * us[pl.ds(HALO - j, tokens), :], axis=0, keepdims=True)
        ms[pl.ds(0, tokens), :] = gmj
        acc = acc + ms[pl.ds(j, tokens), :] * tapx[j : j + 1, :]
    gu_o[...] = acc.astype(BF16)
    gtail_o[...] = acc[tokens - 16 :]

    @pl.when(p == pl.num_programs(0) - 1)
    def _():
        ii = lax.broadcasted_iota(jnp.int32, (tokens, tokens), 0)
        jj = lax.broadcasted_iota(jnp.int32, (tokens, tokens), 1)
        dlog = hdot(jnp.where(jj >= ii, 1.0, 0.0), dcum[...], NN) + last[...]
        rates = -jnp.exp(lograte[...])
        dsteps = ddacc[...] + rates * dlog
        gdt = dsteps * sig(pdt[...].astype(F32) + dtb[...])
        gdt_o[...] = gdt.astype(BF16)
        gvec[0:1, :] = jnp.sum(gdt, axis=0, keepdims=True)
        gvec[1:2, :] = jnp.sum(st * dlog, axis=0, keepdims=True) * rates


MESH = pl.DeviceIdType.MESH
VMEM_LIMIT = 56 * 1024 * 1024
SUBS = 2


def greet(partners):
    barrier = pltpu.get_barrier_semaphore()
    for where in partners:
        pl.semaphore_signal(barrier, inc=1, device_id=where, device_id_type=MESH)
    pl.semaphore_wait(barrier, len(partners))


def send(src, dst, sems, where):
    copy = pltpu.make_async_remote_copy(
        src_ref=src, dst_ref=dst, send_sem=sems[0], recv_sem=sems[1], device_id=where, device_id_type=MESH)
    copy.start()
    return copy


def flip(me, bit):
    return me + bit * (1 - 2 * ((me // bit) % 2))


def carry_stages(bits, reverse, heads, size, st, dec, out, tx, rx, rxd, tot, zp, btx, brx, bdtx, bdrx, pd, ed, ptx, prx, ssem, rsem):
    me = lax.axis_index("seq")
    n = len(bits)
    hh = heads // 2
    rows = hh * size
    x = me % 2
    r = (1 - x) if reverse else x
    pair_at = {"seq": flip(me, bits[0])}
    wheres = [{"seq": flip(me, b)} for b in bits[1:]]
    kind = tx.dtype
    mine = pl.ds(pl.multiple_of(r * rows, rows), rows)
    theirs = pl.ds(pl.multiple_of((1 - r) * rows, rows), rows)

    def copy(k, src, dst, where):
        return pltpu.make_async_remote_copy(src_ref=src, dst_ref=dst, send_sem=ssem.at[k], recv_sem=rsem.at[k],
                                            device_id=where, device_id_type=MESH)

    one = [copy(0, tx, rx, pair_at), copy(1, dec, rxd, pair_at)]
    steps = [[copy(2 + 2 * i, btx, brx.at[i], w), copy(3 + 2 * i, bdtx, bdrx.at[i], w)] for i, w in enumerate(wheres)]
    last = [copy(2 * n, ptx, prx, pair_at)]

    def begin(copies):
        for c in copies:
            c.start()

    def end(copies):
        for c in copies:
            c.wait()

    def per_head(fn):
        for k in range(hh):
            fn(pl.ds(k * size, size), r * hh + k, pl.ds(pl.multiple_of(r * rows + k * size, size), size))

    def open_():
        greet([pair_at] + wheres)
        tx[...] = st[theirs, :].astype(kind)
        begin(one)

    def pair():
        end(one)
        pd[...] = dec[...] * rxd[...]
        ed[...] = jnp.ones_like(ed)
        zp[...] = jnp.zeros_like(zp)

        def add(rk, h, own):
            a, b = st[own, :], rx[rk, :].astype(F32)
            row = pl.ds(h, 1)
            tot[rk, :] = jnp.where(r == 0, rxd[row, :] * a + b, dec[row, :] * b + a)

        per_head(add)
        go(0)

    def go(i):
        btx[...] = tot[...].astype(kind)
        bdtx[...] = pd[...]
        begin(steps[i])

    def butterfly(i):
        end(steps[i])
        bit = (me // bits[1 + i]) % 2
        second = (1 - bit) if reverse else bit
        keep = second.astype(F32)

        def add(rk, h, own):
            other = brx[i, rk, :].astype(F32)
            row = pl.ds(h, 1)
            zp[rk, :] += other * (ed[row, :] * keep)
            if i + 1 < len(steps):
                a = jnp.where(second == 1, pd[row, :], 1.0)
                c = jnp.where(second == 1, 1.0, bdrx[i, row, :])
                tot[rk, :] = a * other + c * tot[rk, :]

        per_head(add)
        ed[...] = jnp.where(second == 1, ed[...] * bdrx[i], ed[...])
        pd[...] = pd[...] * bdrx[i]
        if i + 1 < len(steps):
            go(i + 1)
        else:
            hand()

    def hand():
        def add(rk, h, own):
            row = pl.ds(h, 1)
            z = zp[rk, :]
            after = jnp.where(r == 0, dec[row, :], rxd[row, :]) * z + jnp.where(r == 0, st[own, :], rx[rk, :].astype(F32))
            out[own, :] = jnp.where(r == 0, z, after)
            ptx[rk, :] = jnp.where(r == 0, after, z).astype(kind)

        per_head(add)
        begin(last)

    def close():
        end(last)
        out[theirs, :] = prx[...].astype(F32)

    return [open_, pair] + [partial(butterfly, i) for i in range(len(steps))] + [close]


def carry_scratch(n, rows, states, kind):
    part = pltpu.VMEM((rows // 2, states), kind)
    wide = pltpu.VMEM((rows // 2, states), F32)
    dec = pltpu.VMEM((16, states), F32)
    return [part, part, dec, wide, wide, part, pltpu.VMEM((n - 1, rows // 2, states), kind), dec, pltpu.VMEM((n - 1, 16, states), F32),
            dec, dec, part, part, pltpu.SemaphoreType.DMA((2 * n + 1,)), pltpu.SemaphoreType.DMA((2 * n + 1,))]


def head_core(tokens, part, middle, nx, off, side, tx0, rx0, tx1, rx1, acc, ssem, rsem, me, core_at, y_at):
    quarter = tokens // 4
    sub = quarter // SUBS
    c = me % 2
    y = me // 2
    half = 2 * quarter
    other_y = pl.multiple_of((1 - y) * quarter, quarter)
    own_y = pl.multiple_of(y * quarter, quarter)
    n = 0
    sends = []

    def go(src, dst, where):
        nonlocal n
        copy = send(src, dst, (ssem.at[n], rsem.at[n]), where)
        sends.append(copy)
        n += 1
        return copy

    acc[...] = part(pl.multiple_of((1 - c) * half, half), half)
    first = []
    for i, base in enumerate((other_y, own_y)):
        for s in range(SUBS):
            tx0[i, s] = acc[pl.ds(pl.multiple_of(base + s * sub, sub), sub), :].astype(tx0.dtype)
            first.append(go(tx0.at[i, s], rx0.at[i, s], core_at))
    acc[...] = part(pl.multiple_of(c * half, half), half)
    second = []
    for s in range(SUBS):
        first[s].wait_recv()
        tx1[s] = (acc[pl.ds(pl.multiple_of(other_y + s * sub, sub), sub), :] + rx0[0, s].astype(F32)).astype(tx1.dtype)
        second.append(go(tx1.at[s], rx1.at[s], y_at))
    own = (c * 2 + y) * quarter
    theirs = (c * 2 + 1 - y) * quarter
    to_y, to_core, onward = [], [], []
    for s in range(SUBS):
        first[SUBS + s].wait_recv()
        second[s].wait_recv()
        total = acc[pl.ds(pl.multiple_of(own_y + s * sub, sub), sub), :] + rx0[1, s].astype(F32) + rx1[s].astype(F32)
        rows = pl.ds(pl.multiple_of(off + own + s * sub, 16), sub)
        nx[rows, :] = middle(s, sub, total)
        to_y.append(go(nx.at[rows, :], nx.at[rows, :], y_at))
        to_core.append(go(nx.at[rows, :], nx.at[rows, :], core_at))
    if side is not None:
        srows = pl.ds(pl.multiple_of((c * 2 + y) * 8, 8), 8)
        to_y.append(go(side.at[srows, :], side.at[srows, :], y_at))
        to_core.append(go(side.at[srows, :], side.at[srows, :], core_at))
    for s in range(SUBS):
        to_y[s].wait_recv()
        rows = pl.ds(pl.multiple_of(off + theirs + s * sub, 16), sub)
        onward.append(go(nx.at[rows, :], nx.at[rows, :], core_at))
    if side is not None:
        to_y[SUBS].wait_recv()
        srows = pl.ds(pl.multiple_of((c * 2 + 1 - y) * 8, 8), 8)
        onward.append(go(side.at[srows, :], side.at[srows, :], core_at))
    for copy in to_core + onward:
        copy.wait_recv()
    for copy in sends:
        copy.wait_send()


HEAD_COPIES = 3 * SUBS + 3 * SUBS + 3


def head_fwd_body(l, tokens, last, width, gated, sq, ggain_all, wout_all, h_own, extra,
                  nx, h_new, branch, r2b, side, sqrx, tx0, rx0, tx1, rx1, acc, krc, ssem, rsem, qs, qr, hs, hr, wout, wsem):
    load = pltpu.make_async_copy(wout_all.at[l], wout, wsem.at[0])
    load.start()
    ggain = ggain_all.at[l]
    extra = extra if last else extra.at[l + 1]
    me = lax.axis_index("head")
    at = lax.axis_index("seq")
    count = lax.axis_size("seq")
    peers = [lax.rem(me + k, 4) for k in (1, 2, 3)]
    barrier = pltpu.get_barrier_semaphore()
    for pr in peers:
        pl.semaphore_signal(barrier, inc=1, device_id={"head": pr}, device_id_type=MESH)
    if not last:
        @pl.when(at > 0)
        def _():
            pl.semaphore_signal(barrier, inc=1, device_id={"seq": at - 1}, device_id_type=MESH)
    if last:
        pl.semaphore_wait(barrier, 3)
    else:
        pl.semaphore_wait(barrier, 3 + (at < count - 1).astype(jnp.int32))
    copies = [send(sq, sqrx.at[2 - k], (qs.at[k], qr.at[2 - k]), {"head": pr}) for k, pr in enumerate(peers)]
    for copy in copies:
        copy.wait_send()
    for k in range(3):
        pltpu.make_async_remote_copy(src_ref=sq, dst_ref=sqrx.at[k], send_sem=qs.at[k], recv_sem=qr.at[k],
                                     device_id={"head": peers[2 - k]}, device_id_type=MESH).wait_recv()
    total_sq = ((sq[...] + sqrx[0]) + (sqrx[1] + sqrx[2]))[0:1, :]
    r2row = lax.rsqrt(total_sq / width + EPS)
    r2b[...] = jnp.transpose(jnp.broadcast_to(r2row, (LANE, tokens)))
    inner = gated.shape[1]

    def part(start, rows):
        where = pl.ds(start, rows)
        r2 = jnp.concatenate([r2b[where, :]] * (inner // LANE), axis=1)
        return bdot(gated[where, :] * r2 * ggain[...], wout[...], NN)

    d = wout.shape[1]

    def middle(s, sub, total):
        rows = pl.ds(s * sub, sub)
        branch[rows, :] = total
        h = h_own[rows, :] + total
        h_new[rows, :] = h
        if last:
            krc[rows, :] = jnp.broadcast_to(jnp.sum(extra[rows, :].astype(F32) * total, axis=1, keepdims=True), (sub, LANE))
            if s == SUBS - 1:
                mine = pl.ds(pl.multiple_of(((me % 2) * 2 + me // 2) * 8, 8), 8)
                side[mine, :] = jnp.transpose(krc[...])[0:8, :]
            return h.astype(BF16)
        r1 = lax.rsqrt(jnp.sum(h * h, axis=1, keepdims=True) / d + EPS)
        return (h * r1 * extra[...]).astype(BF16)

    off = 0 if last else HALO
    load.wait()
    if not last:
        side[...] = jnp.zeros_like(side)
    head_core(tokens, part, middle, nx, off, side if last else None, tx0, rx0, tx1, rx1, acc, ssem, rsem, me,
              {"head": flip(me, 1)}, {"head": flip(me, 2)})
    if not last:
        src = nx.at[pl.ds(tokens, HALO), :]
        dst = nx.at[pl.ds(0, HALO), :]
        copy = pltpu.make_async_remote_copy(src_ref=src, dst_ref=dst, send_sem=hs.at[0], recv_sem=hr.at[0],
                                            device_id={"seq": lax.rem(at + 1, count)}, device_id_type=MESH)

        @pl.when(at < count - 1)
        def _():
            copy.start()
            copy.wait_send()

        @pl.when(at > 0)
        def _():
            copy.wait_recv()

        @pl.when(at == 0)
        def _():
            nx[pl.ds(0, HALO), :] = jnp.zeros((HALO, d), BF16)


def head_scratch(tokens, d, kind=BF16):
    sub = tokens // 4 // SUBS
    return [pltpu.VMEM((2, SUBS, sub, d), kind), pltpu.VMEM((2, SUBS, sub, d), kind), pltpu.VMEM((SUBS, sub, d), kind),
            pltpu.VMEM((SUBS, sub, d), kind), pltpu.VMEM((tokens // 2, d), F32), pltpu.VMEM((tokens // 4, LANE), F32),
            pltpu.SemaphoreType.DMA((HEAD_COPIES,)), pltpu.SemaphoreType.DMA((HEAD_COPIES,))]


def head_bwd_body(l, tokens, gz, gu, small, wzx_all, wsmall_all, h_own, gain_all, g_own, branch,
                  gb, g_new, ggain, side, tx0, rx0, tx1, rx1, acc, krc, ssem, rsem, wzx, wsem):
    load = pltpu.make_async_copy(wzx_all.at[l], wzx, wsem.at[0])
    load.start()
    wsmall = wsmall_all.at[l]
    gain = gain_all.at[l]
    me = lax.axis_index("head")
    core_at, y_at = {"head": flip(me, 1)}, {"head": flip(me, 2)}
    greet([core_at, y_at])
    d = gain.shape[1]

    def part(start, rows):
        where = pl.ds(start, rows)
        return bdot(gz[where, :], wzx[0], NT) + bdot(gu[where, :], wzx[1], NT) + bdot(small[where, :], wsmall[...], NT)

    def middle(s, sub, total):
        rows = pl.ds(s * sub, sub)
        h = h_own[rows, :]
        r1 = lax.rsqrt(jnp.sum(h * h, axis=1, keepdims=True) / d + EPS)
        th = total * h
        gg = jnp.sum(th * r1, axis=0, keepdims=True)
        if s == 0:
            ggain[...] = gg
        else:
            ggain[...] += gg
        k1 = jnp.sum(th * gain[...], axis=1, keepdims=True)
        g = g_own[rows, :] + r1 * (gain[...] * total) - h * (r1 * r1 * r1 * (k1 / d))
        g_new[rows, :] = g
        low = g.astype(BF16)
        krc[rows, :] = jnp.broadcast_to(jnp.sum(low.astype(F32) * branch[rows, :], axis=1, keepdims=True), (sub, LANE))
        if s == SUBS - 1:
            mine = pl.ds(pl.multiple_of(((me % 2) * 2 + me // 2) * 8, 8), 8)
            side[mine, :] = jnp.transpose(krc[...])[0:8, :]
        return low

    load.wait()
    head_core(tokens, part, middle, gb, 0, side, tx0, rx0, tx1, rx1, acc, ssem, rsem, me, core_at, y_at)


def maps_bwd_body(l, tokens, dkr, ubc, taps_all, aux, gdt, gtail, gm8, tapx_all,
                  small, gtaps, gtail_o, ytx, yrx, yacc, ctx, crx, us, ms, nextx, nextb, gmb, sems, semr):
    taps, tapx = taps_all.at[l], tapx_all.at[l]
    me = lax.axis_index("head")
    at = lax.axis_index("seq")
    count = lax.axis_size("seq")
    c = me % 2
    y = me // 2
    core_at, y_at = {"head": flip(me, 1)}, {"head": flip(me, 2)}
    barrier = pltpu.get_barrier_semaphore()
    for where in (core_at, y_at):
        pl.semaphore_signal(barrier, inc=1, device_id=where, device_id_type=MESH)

    @pl.when(at < count - 1)
    def _():
        pl.semaphore_signal(barrier, inc=1, device_id={"seq": at + 1}, device_id_type=MESH)
    pl.semaphore_wait(barrier, 2 + (at > 0).astype(jnp.int32))
    lanes = lax.broadcasted_iota(jnp.int32, (tokens, LANE), 1)
    before = {"seq": lax.rem(at + count - 1, count)}
    ahead_x = pltpu.make_async_remote_copy(src_ref=gm8, dst_ref=nextx, send_sem=sems.at[2], recv_sem=semr.at[2],
                                           device_id=before, device_id_type=MESH)

    @pl.when(at > 0)
    def _():
        ahead_x.start()
    low, high = dkr[:, :LANE], dkr[:, LANE:]
    ytx[...] = jnp.where(y == 0, high, low)
    one = send(ytx, yrx, (sems.at[0], semr.at[0]), y_at)
    tile = pl.ds(pl.multiple_of(y * LANE, LANE), LANE)
    us[...] = ubc[:, tile].astype(F32)
    tp = taps[:, tile]
    m = mix_taps(us, tp, aux, LANE)
    s = sig(m)
    slope = s * (1.0 + m * (1.0 - s))
    one.wait()
    ctx[...] = jnp.where(y == 0, low, high) + yrx[...]
    two = send(ctx, crx, (sems.at[1], semr.at[1]), core_at)
    two.wait()
    gm = (ctx[...] + crx[...]) * slope
    gmb[...] = gm[0:8]
    ahead_b = pltpu.make_async_remote_copy(src_ref=gmb, dst_ref=nextb, send_sem=sems.at[3], recv_sem=semr.at[3],
                                           device_id=before, device_id_type=MESH)

    @pl.when(at > 0)
    def _():
        ahead_b.start()

    @pl.when(at == count - 1)
    def _():
        nextx[...] = jnp.zeros_like(nextx)
        nextb[...] = jnp.zeros_like(nextb)
    gtaps[...] = jnp.zeros_like(gtaps)
    gtaps[0:1, :] = jnp.sum(gm * us[pl.ds(HALO, tokens), :], axis=0, keepdims=True)
    gtaps[CONV : CONV + 1, :] = jnp.sum(gm, axis=0, keepdims=True)
    for j in range(1, CONV):
        gtaps[j : j + 1, :] = jnp.sum(gm * aux[j - 1] * us[pl.ds(HALO - j, tokens), :], axis=0, keepdims=True)

    @pl.when(at < count - 1)
    def _():
        ahead_x.wait_recv()
        ahead_b.wait_recv()
    acc = gm * tp[0:1, :]
    for j in range(1, CONV):
        ms[pl.ds(0, tokens), :] = gm * aux[j - 1]
        ms[pl.ds(tokens, 8), :] = nextb[...]
        acc = acc + ms[pl.ds(j, tokens), :] * tp[j : j + 1, :]
    own = jnp.where(c == 0, lanes, LANE - 1 - lanes) < 64
    g = gdt[...].astype(F32)
    moved = jnp.concatenate([g[:, 64:], g[:, :64]], axis=1)
    small[...] = jnp.where(own, acc, jnp.where(c == 0, moved, g)).astype(BF16)
    gtail_o[...] = gtail[...].astype(BF16)
    nx = nextx[...]
    tail = gtail[...]
    rows = lax.broadcasted_iota(jnp.int32, tail.shape, 0)
    for j in range(1, CONV):
        for k in range(j):
            tail = tail + jnp.where(rows == 16 - j + k, nx[k : k + 1, :] * tapx[j : j + 1, :], 0.0)
    gtail_o[...] = tail.astype(BF16)

    @pl.when(at > 0)
    def _():
        ahead_x.wait_send()
        ahead_b.wait_send()


class Job:
    def __init__(self, got, keep, left, steps, out, bufs, sems):
        self.got, self.keep, self.left, self.steps, self.out = got, keep, list(left), list(steps), out
        self.bufs, (self.ssem, self.rsem) = bufs, sems
        self.copy = None

    def advance(self):
        got, keep = self.got, self.keep
        if self.copy is not None:
            self.copy.wait()
        if not self.steps:
            if self.out is not None:
                self.out[...] = keep[0].astype(F32) + got[0].astype(F32)
            return
        bit = self.steps.pop(0)
        away, kept, came = self.bufs.pop(0)
        stride = 1 << (len(self.left) - 1 - self.left.index(bit))
        self.left.remove(bit)
        me = (lax.axis_index("seq") // bit) % 2
        for dst, want in ((away, 1 - me), (kept, me)):
            for k in range(dst.shape[0]):
                at = (k // stride) * 2 * stride + want * stride + k % stride
                dst[k] = (keep[at].astype(F32) + got[at].astype(F32)).astype(dst.dtype)
        where = {"seq": flip(lax.axis_index("seq"), bit)}
        k = len(self.steps)
        self.copy = send(away, came, (self.ssem.at[k], self.rsem.at[k]), where)
        self.got, self.keep = came, kept


def tail_body(parts, plan, *refs):
    jobs_n = len(plan)
    pairs = refs[: 2 * jobs_n]
    ins = refs[2 * jobs_n : 2 * jobs_n + 6 * parts]
    rest = refs[2 * jobs_n + 6 * parts :]
    outs, rest = rest[:jobs_n], rest[jobs_n:]
    conv_x, conv_bc, ggate, gskip, gvec, ggain = rest[:6]
    stage, rx, hx, ssem, rsem = rest[6:11]
    rest = list(rest[11:])
    jobs = []
    for i, (left, steps) in enumerate(plan):
        bufs = []
        for _ in steps:
            bufs.append((rest.pop(0), rest.pop(0), rest.pop(0)))
        jobs.append(Job(pairs[2 * i], pairs[2 * i + 1], left, steps, outs[i], bufs, (rest.pop(0), rest.pop(0))))
    inner = stage.shape[2]
    me = lax.axis_index("head")
    steps = [("head", b) for b in bits_of("head")] + [("seq", b) for b in bits_of("seq")]
    wheres = [{axis: flip(lax.axis_index(axis), b)} for axis, b in steps]
    greet(wheres)
    for job in jobs:
        job.advance()
    stage[...] = jnp.zeros_like(stage)
    for l in range(parts):
        taps, gate, skip, vec, maps, gain = ins[6 * l : 6 * l + 6]
        stage[l, 0 : CONV + 1, :] = taps[0 : CONV + 1, :]
        stage[l, 5:6, :] = gate[...]
        stage[l, 6:7, :] = skip[...]
        stage[l, 7:8, 0:LANE] = vec[0:1, :]
        stage[l, 7:8, LANE : 2 * LANE] = vec[1:2, :]
        stage[l, 8:9, :] = gain[:, :inner]
        stage[l, 9:10, :] = gain[:, inner:]
        for r in range(CONV + 1):
            row = maps[r : r + 1, :] * 0.5
            here = [jnp.where(me // 2 == k, row, 0.0) for k in range(2)]
            stage[l, 10 + r // 3 : 11 + r // 3, (r % 3) * 2 * LANE : ((r % 3) * 2 + 2) * LANE] = jnp.concatenate(here, axis=1)
    where = pl.ds(8, 8)
    heads = len(bits_of("head"))
    longest = max(len(job.steps) for job in jobs)
    for i, (axis, b) in enumerate(steps):
        if axis == "head":
            copy = send(stage.at[:, where, :], hx.at[i], (ssem.at[i], rsem.at[i]), wheres[i])
            copy.wait()
            stage[:, 8:16, :] += hx[i]
        else:
            copy = send(stage, rx.at[i - heads], (ssem.at[i], rsem.at[i]), wheres[i])
            if i == heads:
                for job in jobs:
                    if len(job.steps) == longest:
                        job.advance()
            copy.wait()
            stage[...] += rx[i - heads]
    for _ in range(longest + 1):
        for job in jobs:
            if job.copy is not None and (job.steps or job.out is not None):
                done = not job.steps
                job.advance()
                if done:
                    job.out = None
    for l in range(parts):
        conv_x[l] = stage[l, 0 : CONV + 1, :]
        ggate[l : l + 1, :] = stage[l, 5:6, :]
        gskip[l : l + 1, :] = stage[l, 6:7, :]
        gvec[l : l + 1, :] = stage[l, 7:8, 0 : 2 * LANE]
        ggain[l : l + 1, :inner] = stage[l, 8:9, :]
        ggain[l : l + 1, inner:] = stage[l, 9:10, :]
        for r in range(CONV + 1):
            conv_bc[l, r : r + 1, :] = stage[l, 10 + r // 3 : 11 + r // 3, (r % 3) * 2 * LANE : ((r % 3) * 2 + 2) * LANE]


VM = pl.BlockSpec(memory_space=pltpu.VMEM)
S = jax.ShapeDtypeStruct


def of_layer(l, shape, steps=False):
    n = len(shape) - 1
    if steps:
        return pl.BlockSpec((None,) + shape[1:-1] + (LANE,), lambda p: (l,) + (0,) * (n - 1) + (p,))
    return pl.BlockSpec((None,) + shape[1:], lambda *p: (l,) + (0,) * n)


def rows_of_layer(l, shape):
    return pl.BlockSpec((None, LANE, shape[2]), lambda p: (l, p, 0))


def kcall(body, args, specs, us, after=(), cid=None, **kw):
    n, k = len(args), len(after)

    def wrapped(*refs):
        body(*refs[:n], *refs[n + k :])

    extra = {} if cid is None else dict(collective_id=cid, has_side_effects=True)
    return pl.pallas_call(
        wrapped,
        in_specs=list(specs) + [pl.BlockSpec(memory_space=pl.ANY)] * k,
        compiler_params=pltpu.CompilerParams(vmem_limit_bytes=VMEM_LIMIT, **extra),
        cost_estimate=pl.CostEstimate(flops=int(us * 1e9), bytes_accessed=int(us * 3e6), transcendentals=0),
        **kw,
    )(*args, *after)


def fwd_mix(l, size, nx, q, aux, segrow):
    tokens = aux.shape[1]
    ext, d = nx.shape
    inner = q["conv_x"].shape[2]
    two = q["w_bc"].shape[2]
    args = [nx, q["w_zx"], q["w_bc"], q["w_dt"], q["conv_x"], q["conv_bc"], q["dt_bias"], q["a_log"], aux, segrow]
    specs = [full(nx.shape), of_layer(l, q["w_zx"].shape, True), of_layer(l, q["w_bc"].shape), of_layer(l, q["w_dt"].shape),
             of_layer(l, q["conv_x"].shape, True), of_layer(l, q["conv_bc"].shape), of_layer(l, q["dt_bias"].shape),
             of_layer(l, q["a_log"].shape), full(aux.shape), full(segrow.shape)]
    return kcall(
        partial(fwd_mix_body, size), args, specs, 12,
        name="fwd_mix",
        grid=(inner // LANE,),
        out_specs=[cols(tokens), cols(ext), full((ext, two)), full((tokens, two)), full((tokens, LANE)), full((tokens, LANE)),
                   full((tokens, LANE)), full((LANE, tokens)), full((tokens, tokens)), cols(tokens),
                   cols(tokens), rowsb(two // 2), full((16, LANE)), full((8, LANE))],
        out_shape=[S((tokens, inner), BF16), S((ext, inner), BF16), S((ext, two), BF16), S((tokens, two), F32),
                   S((tokens, LANE), BF16), S((tokens, LANE), F32), S((tokens, LANE), F32), S((LANE, tokens), F32),
                   S((tokens, tokens), F32), S((tokens, inner), F32), S((tokens, inner), F32),
                   S((inner, two // 2), F32), S((16, LANE), F32), S((8, LANE), F32)],
        scratch_shapes=[pltpu.VMEM((ext, LANE), F32), pltpu.VMEM((ext, two), F32)],
    )


def fwd_inside(l, heads, size, mixed, steps, cum, cT, gram, q, state, dec, cid):
    tokens, inner = mixed.shape
    rows, states = state.shape
    bits = bits_of("seq")
    return kcall(
        partial(fwd_inside_body, partial(carry_stages, bits, False, heads, size), size),
        [mixed, steps, cum, cT, gram, q["skip"], state, dec],
        [cols(tokens), full(steps.shape), full(cum.shape), full(cT.shape), full(gram.shape), of_layer(l, q["skip"].shape, True),
         full(state.shape), full(dec.shape)], 28, (), cid,
        name="fwd_inside",
        grid=(inner // LANE,),
        out_specs=[cols(tokens), full((rows, states))],
        out_shape=[S((tokens, inner), F32), S((rows, states), F32)],
        scratch_shapes=[pltpu.VMEM((2, tokens, LANE), F32)] + carry_scratch(len(bits), rows, states, F32),
    )


def fwd_gate(ypart, entry, gate, krs, enter):
    tokens, inner = ypart.shape
    return kcall(
        fwd_gate_body, [ypart, entry, gate, krs, enter],
        [cols(tokens), cols(tokens), cols(tokens), full(krs.shape), rowsb(enter.shape[1])], 7,
        name="fwd_gate",
        grid=(inner // LANE,),
        out_specs=[cols(tokens), cols(tokens), cols(tokens), full((8, tokens))],
        out_shape=[S((tokens, inner), F32)] * 3 + [S((8, tokens), F32)],
        scratch_shapes=[pltpu.VMEM((tokens, LANE), F32)],
    )


def bwd_gate(l, gb, q, gate, y, mixed, entry, krs, r2b, krb):
    tokens, inner = y.shape
    states = krs.shape[1] // 2
    return kcall(
        bwd_gate_body, [gb, q["w_out"], gate, y, mixed, entry, krs, r2b, krb, q["gate_gain"]],
        [full(gb.shape), rows_of_layer(l, q["w_out"].shape), cols(tokens), cols(tokens), cols(tokens), cols(tokens), full(krs.shape),
         full(r2b.shape), full(krb.shape), of_layer(l, q["gate_gain"].shape, True)], 9,
        name="bwd_gate",
        grid=(inner // LANE,),
        out_specs=[cols(tokens), cols(tokens), cols(tokens), rowsb(states), cols(1), cols(1)],
        out_shape=[S((tokens, inner), F32), S((tokens, inner), BF16), S((tokens, inner), BF16), S((inner, states), F32),
                   S((1, inner), F32), S((1, inner), F32)],
    )


def bwd_local(heads, size, gy, mixed, krs, cum, steps, cT, gram, entry, enter, aux, segrow, qloc, dec, cid, after):
    tokens, inner = gy.shape
    two = krs.shape[1]
    rows, states = qloc.shape
    bits = bits_of("seq")
    return kcall(
        partial(bwd_local_body, partial(carry_stages, bits, True, heads, size), size),
        [gy, mixed, krs, cum, steps, cT, gram, entry, enter, aux, segrow, qloc, dec],
        [cols(tokens), cols(tokens), full(krs.shape), full(cum.shape), full(steps.shape), full(cT.shape), full(gram.shape),
         cols(tokens), rowsb(two // 2), pl.BlockSpec((None, tokens, LANE), lambda p: (5, 0, 0)), full(segrow.shape),
         full(qloc.shape), full(dec.shape)], 20, after, cid,
        name="bwd_local",
        grid=(inner // LANE,),
        out_specs=[cols(tokens), full((tokens, LANE)), full((LANE, tokens)), full((tokens, two)), full((rows, states))],
        out_shape=[S((tokens, inner), F32), S((tokens, LANE), F32), S((LANE, tokens), F32), S((tokens, two), F32), S((rows, states), F32)],
        scratch_shapes=[pltpu.VMEM((tokens, LANE), F32), pltpu.VMEM((tokens, LANE), F32), pltpu.VMEM((tokens, tokens), F32),
                        pltpu.VMEM((tokens, tokens), F32), pltpu.VMEM((tokens, LANE), BF16), pltpu.VMEM((tokens, LANE), BF16)]
        + carry_scratch(len(bits), rows, states, BF16),
    )


def bwd_carry(l, size, gy, dvd, mixed, carr, entry, krs, cum, steps, pdt, q, ux, aux, later, enter, dd, rowT, dkr, decl, after):
    tokens, inner = gy.shape
    ext = ux.shape[0]
    two = krs.shape[1]
    return kcall(
        partial(bwd_carry_body, size),
        [gy, dvd, mixed, carr, entry, krs, cum, steps, pdt, q["dt_bias"], q["a_log"], q["skip"], ux, q["conv_x"], aux, later, enter,
         dd, rowT, dkr, decl],
        [cols(tokens), cols(tokens), cols(tokens), cols(tokens), cols(tokens), full(krs.shape), full(cum.shape), full(steps.shape),
         full(pdt.shape), of_layer(l, q["dt_bias"].shape), of_layer(l, q["a_log"].shape), of_layer(l, q["skip"].shape, True), cols(ext),
         of_layer(l, q["conv_x"].shape, True), full(aux.shape), rowsb(two // 2), rowsb(two // 2), full(dd.shape), full(rowT.shape),
         full(dkr.shape), full(decl.shape)], 11, after,
        name="bwd_carry",
        grid=(inner // LANE,),
        out_specs=[cols(8), cols(tokens), cols(16), cols(8), full((tokens, LANE)), full((8, LANE)), full((tokens, two))],
        out_shape=[S((8, inner), F32), S((tokens, inner), BF16), S((16, inner), F32), S((8, inner), F32), S((tokens, LANE), BF16),
                   S((8, LANE), F32), S((tokens, two), F32)],
        scratch_shapes=[pltpu.VMEM((ext, LANE), F32), pltpu.VMEM((tokens + 8, LANE), F32), pltpu.VMEM((tokens, LANE), F32),
                        pltpu.VMEM((tokens, LANE), F32), pltpu.VMEM((1, LANE), F32)],
    )


def head_fwd(l, gated, sq, q, h_own, extra, last, width, cid):
    tokens, inner = gated.shape
    d = q["w_out"].shape[2]
    return kcall(
        partial(head_fwd_body, l, tokens, last, width), [gated, sq, q["gate_gain"], q["w_out"], h_own, extra],
        [VM, VM, VM, pl.BlockSpec(memory_space=pl.ANY), VM, VM], 30, (), cid,
        name="head_fwd_last" if last else "head_fwd",
        out_specs=[VM] * 5,
        out_shape=[S((tokens if last else tokens + HALO, d), BF16), S((tokens // 4, d), F32), S((tokens // 4, d), F32),
                   S((tokens, LANE), F32), S((32, LANE), F32)],
        scratch_shapes=[pltpu.VMEM((3, 8, tokens), F32)] + head_scratch(tokens, d, BF16 if last else F32)
        + [pltpu.SemaphoreType.DMA((3,)), pltpu.SemaphoreType.DMA((3,)), pltpu.SemaphoreType.DMA((1,)), pltpu.SemaphoreType.DMA((1,)), pltpu.VMEM((inner, d), BF16), pltpu.SemaphoreType.DMA((1,))],
    )


def head_bwd(l, gz, gu, small, q, h_own, g_own, branch, cid, after=()):
    tokens = gz.shape[0]
    d = h_own.shape[1]
    return kcall(
        partial(head_bwd_body, l, tokens), [gz, gu, small, q["w_zx"], q["w_small"], h_own, q["gain"], g_own, branch],
        [VM, VM, VM, pl.BlockSpec(memory_space=pl.ANY), VM, VM, VM, VM, VM], 29, after, cid,
        name="head_bwd",
        out_specs=[VM] * 4,
        out_shape=[S((tokens, d), BF16), S((tokens // 4, d), F32), S((1, d), F32), S((32, LANE), F32)],
        scratch_shapes=head_scratch(tokens, d) + [pltpu.VMEM(q["w_zx"].shape[1:], BF16), pltpu.SemaphoreType.DMA((1,))],
    )


def maps_bwd(l, dkr, ubc, q, aux, gdt, gtail, gm8, cid, after=()):
    tokens = dkr.shape[0]
    inner = gtail.shape[1]
    tile = pltpu.VMEM((tokens, LANE), F32)
    return kcall(
        partial(maps_bwd_body, l, tokens), [dkr, ubc, q["conv_bc"], aux, gdt, gtail, gm8, q["conv_x"]],
        [VM] * 8, 14, after, cid,
        name="maps_bwd",
        out_specs=[VM] * 3,
        out_shape=[S((tokens, LANE), BF16), S((8, LANE), F32), S((16, inner), BF16)],
        scratch_shapes=[tile, tile, tile, tile, tile, pltpu.VMEM((tokens + HALO, LANE), F32), pltpu.VMEM((tokens + 8, LANE), F32),
                        pltpu.VMEM((8, inner), F32), pltpu.VMEM((8, LANE), F32), pltpu.VMEM((8, LANE), F32),
                        pltpu.SemaphoreType.DMA((4,)), pltpu.SemaphoreType.DMA((4,))],
    )


def tail(sums, smalls, inner, d, cid):
    parts = len(smalls)
    plan = [(left, steps) for _, _, left, steps in sums]
    heads, n = len(bits_of("head")), len(bits_of("seq"))
    arrays, scratch, outs = [], [], []
    for got, keep, left, steps in sums:
        arrays += [got, keep]
        blocks, block, width = keep.shape
        outs.append(S((block, width), F32))
        for _ in steps:
            blocks //= 2
            buf = pltpu.VMEM((blocks, block, width), BF16)
            scratch += [buf, pltpu.VMEM((blocks, block, width), F32), buf]
        scratch += [pltpu.SemaphoreType.DMA((max(len(steps), 1),))] * 2
    return kcall(
        partial(tail_body, parts, plan), arrays + [x for part in smalls for x in part], [VM] * (2 * len(sums) + 6 * parts), 45, (), cid,
        name="tail",
        out_specs=[VM] * (len(sums) + 6),
        out_shape=outs + [S((parts, CONV + 1, inner), F32), S((parts, CONV + 1, 2 * LANE), F32), S((parts, inner), F32), S((parts, inner), F32),
                          S((parts, 2 * LANE), F32), S((parts, d), F32)],
        scratch_shapes=[pltpu.VMEM((parts, 16, inner), F32), pltpu.VMEM((n, parts, 16, inner), F32), pltpu.VMEM((heads, parts, 8, inner), F32),
                        pltpu.SemaphoreType.DMA((heads + n,)), pltpu.SemaphoreType.DMA((heads + n,))] + scratch,
    )


def wgrad_body(blocks, bit, off, n_rhs, lhs, *refs):
    rhs, (away, keep, lt) = refs[:n_rhs], refs[n_rhs:]
    tokens = rhs[0].shape[0]
    lt[...] = jnp.transpose(lhs[pl.ds(off, tokens), :])
    mine = (lax.axis_index("seq") // bit) % 2
    block = lt.shape[0] // blocks

    def one(k, carry):
        for dst, want in ((away, 1 - mine), (keep, mine)):
            at = (k // bit) * (2 * bit) + want * bit + lax.rem(k, bit)
            rows = lt[pl.ds(pl.multiple_of(at * block, 16), block), :]
            c = 0
            for r in rhs:
                w = r.shape[1]
                dst[k, :, c : c + w] = bdot(rows, r[...], NN).astype(BF16)
                c += w
        return carry

    lax.fori_loop(0, blocks // 2, one, 0)


def wgrad(lhs, rhs, bit, after=()):
    blocks = lax.axis_size("seq")
    tokens = rhs[0].shape[0]
    d = lhs.shape[1]
    width = sum(r.shape[1] for r in rhs)
    shape = (blocks // 2, d // blocks, width)
    return kcall(
        partial(wgrad_body, blocks, bit, lhs.shape[0] - tokens, len(rhs)), [lhs] + list(rhs), [VM] * (1 + len(rhs)), 3, after,
        name="wgrad",
        out_specs=[VM] * 2,
        out_shape=[S(shape, BF16)] * 2,
        scratch_shapes=[pltpu.VMEM((d, tokens), BF16)],
    )


class Halving:
    def __init__(self, lhs, rhs, order, after=()):
        bits = bits_of("seq")
        self.order = [bits[i % len(bits)] for i in order] + [b for i, b in enumerate(bits) if i not in order]
        self.left = [b for b in reversed(bits)]
        self.away, self.keep = wgrad(lhs, rhs, self.order[0], after)
        self.left.remove(self.order[0])
        self.step = 0
        self.got = None

    def go(self):
        self.got = swap(self.away, "seq", self.order[self.step])
        self.step += 1
        return self.got

    def rest(self):
        shape = (-1,) + self.keep.shape[-2:]
        return self.got.reshape(shape), self.keep.reshape(shape), tuple(self.left), tuple(self.order[self.step :])

    def fold(self):
        total = self.keep.astype(F32) + self.got.astype(F32)
        if self.step == len(self.order):
            self.total = total[0] if total.ndim == 3 else total
            return self.total
        bit = self.order[self.step]
        axis = self.left.index(bit)
        view = total.reshape((2,) * len(self.left) + total.shape[-2:])
        me = my_bit("seq", bit)
        pick = lambda i: take(view, axis, i).astype(BF16).reshape((-1,) + total.shape[-2:])
        self.away, self.keep = pick(1 - me), pick(me)
        self.left.remove(bit)

    def finish(self):
        while self.step < len(self.order):
            self.go()
            self.fold()
        return self.total


def pad_lanes(x, to=LANE):
    return jnp.pad(x, [(0, 0)] * (x.ndim - 1) + [(0, to - x.shape[-1])])


def forward_layer(nx, h_own, extra, q, aux, segrow, layer):
    heads, size, inner = q["heads"], q["size"], q["inner"]
    (gate, ux, ubc, krs, pdt, steps, cum, cT, gram, mixed, entry, state, dec, decl) = fwd_mix(layer, size, nx, q, aux, segrow)
    ypart, enter = fwd_inside(layer, heads, size, mixed, steps, cum, cT, gram, q, state, dec, layer)
    y, carr, gated, sq = fwd_gate(ypart, entry, gate, krs, enter)
    width = inner * lax.axis_size("head")
    nx_next, h_new, branch, r2b, side = head_fwd(layer, gated, sq, q, h_own, extra, layer == LAYERS - 1, width, LAYERS + layer)
    stored = dict(nx=nx, gate=gate, ux=ux, ubc=ubc, krs=krs, pdt=pdt, steps=steps, cum=cum, cT=cT, gram=gram, mixed=mixed,
                  entry=entry, dec=dec, decl=decl, enter=enter, y=y, carr=carr, r2b=r2b, branch=branch, h_own=h_own)
    return nx_next, h_new, side, stored


def backward_gate(gb, side, s, q, layer):
    tokens = gb.shape[0]
    width = q["inner"] * lax.axis_size("head")
    kr = side.reshape(4, 8, LANE)[:, 0, :].reshape(tokens)
    r2b = s["r2b"]
    krb = r2b * r2b * (kr[:, None] / width)
    return bwd_gate(layer, gb, q, s["gate"], s["y"], s["mixed"], s["entry"], s["krs"], r2b, krb)


def local(hidden_in, seg, cot, norm_gain, w_zx, w_bc, w_dt, conv_x, conv_bc, dt_bias, a_log, skip_d, gate_gain, w_out):
    tokens = hidden_in.shape[0]
    inner = w_zx.shape[3]
    heads = w_dt.shape[2]
    size = inner // heads
    rank = lax.axis_index("head")
    segf = seg.astype(F32)
    ext = jnp.concatenate([jnp.full((HALO,), segf[0], F32), segf], 0)
    vecs = [(ext[HALO - j : HALO - j + tokens] == segf).astype(F32) for j in range(1, CONV)]
    vecs += [(segf == segf[0]).astype(F32), (segf == segf[-1]).astype(F32), segf]
    aux = jnp.broadcast_to(jnp.stack(vecs, 0)[:, :, None], (len(vecs), tokens, LANE))
    segrow = segf[None]
    lanes = jnp.arange(LANE)
    even = rank % 2 == 0
    own = jnp.where(even, lanes, LANE - 1 - lanes) < LANE // 2
    dt_pad = pad_lanes(w_dt)
    tile = lax.dynamic_slice_in_dim(w_bc, (rank // 2) * LANE, LANE, 2)
    w_small = jnp.where(own[None, None], tile, jnp.where(even, jnp.roll(dt_pad, LANE // 2, axis=2), dt_pad))
    q = dict(heads=heads, size=size, inner=inner, gain=norm_gain[:, None, :], w_zx=jnp.transpose(w_zx, (0, 2, 1, 3)), w_bc=w_bc, w_dt=dt_pad,
             w_small=w_small, conv_x=conv_x, conv_bc=conv_bc, dt_bias=pad_lanes(dt_bias[:, None, :]), a_log=pad_lanes(a_log[:, None, :]),
             skip=jnp.repeat(skip_d, size, axis=1)[:, None, :], gate_gain=gate_gain[:, None, :], w_out=w_out)
    h = hidden_in.astype(F32)
    h_own = own_rows(h)
    cot_own = own_rows(cot)
    normed = (h * lax.rsqrt(jnp.mean(h * h, axis=1, keepdims=True) + EPS) * norm_gain[0][None]).astype(BF16)
    nx = jnp.concatenate([shift(normed[tokens - HALO :], "seq", 1), normed], 0)
    stored = []
    for l in range(LAYERS):
        extra = cot_own if l == LAYERS - 1 else q["gain"]
        nx, h_own, side, s = forward_layer(nx, h_own, extra, q, aux, segrow, l)
        stored.append(s)
    hidden_out = nx
    gb = cot
    g_own = cot_own.astype(F32)
    smalls = [None] * LAYERS
    sums = [None] * LAYERS
    pending = []
    for l in reversed(range(LAYERS)):
        s = stored[l]
        gy, gz, scaled, qloc, ggate, gskip = backward_gate(gb, side, s, q, l)
        dvd, dd, rowT, dkr, later = bwd_local(heads, size, gy, s["mixed"], s["krs"], s["cum"], s["steps"], s["cT"], s["gram"], s["entry"], s["enter"],
                                              aux, segrow, qloc, s["dec"], 2 * LAYERS + l, [p.got for p in pending])
        for p in pending:
            p.fold()
            p.go()
        out = Halving(gb, [scaled], (0, 1, 2), after=[later])
        z = Halving(s["nx"], [gz], Z_ORDER, after=[later])
        out.go()
        z.go()
        gm8, gu, gtail, gtaps_x, gdt, gvec, dkr = bwd_carry(
            l, size, gy, dvd, s["mixed"], s["carr"], s["entry"], s["krs"], s["cum"], s["steps"], s["pdt"], q, s["ux"], aux, later, s["enter"],
            dd, rowT, dkr, s["decl"], [out.away, z.away])
        small, gtaps_bc, gtail = maps_bwd(l, dkr, s["ubc"], q, aux, gdt, gtail, gm8, 3 * LAYERS + l)
        gu = lax.dynamic_update_slice(gu, gtail, (tokens - 16, 0))
        x = Halving(s["nx"], [gu, small], (0, 1, 2))
        x.go()
        out.fold()
        z.fold()
        z.go()
        out.go()
        before = stored[max(l - 1, 0)]["branch"]
        gb, g_own, g_gain, side = head_bwd(l, gz, gu, small, q, s["h_own"], g_own, before, 4 * LAYERS + l, after=[x.away, out.away, z.away])
        smalls[l] = (gtaps_x, ggate, gskip, gvec, gtaps_bc, g_gain)
        pending = [out, z, x]
        sums[l] = pending
    grad_in = gb.astype(F32)
    under_way = [p for l in range(LAYERS) for p in reversed(sums[l])]
    done = tail([p.rest() for p in under_way], smalls, inner, norm_gain.shape[1], 5 * LAYERS)
    for p, total in zip(under_way, done):
        p.total = total
    g_conv_x, g_conv_bc, g_gate, g_skip, g_vec, g_gain = done[len(under_way) :]
    g_w_zx = jnp.stack([jnp.stack([z.total, x.total[:, :inner]], 1) for _, z, x in sums], 0)
    g_small = jnp.stack([x.total[:, inner:] for _, _, x in sums], 0)
    g_w_bc = jnp.where(even, g_small[:, :, : LANE // 2], g_small[:, :, LANE // 2 :])
    g_w_dt = jnp.where(even, g_small[:, :, LANE // 2 : LANE // 2 + heads], g_small[:, :, :heads])
    g_w_out = jnp.stack([jnp.transpose(out.total) for out, _, _ in sums], 0)
    g_skip = jnp.sum(g_skip.reshape(LAYERS, heads, size), axis=2)
    part = g_gain.shape[1] // lax.axis_size("seq")
    g_gain = lax.dynamic_slice_in_dim(g_gain, lax.axis_index("seq") * part, part, 1)
    return (hidden_out, grad_in, g_gain, g_w_zx, g_w_bc, g_w_dt, g_conv_x, g_conv_bc,
            g_vec[:, :heads], g_vec[:, LANE : LANE + heads], g_skip, g_gate, g_w_out)


def solution(mesh):
    placed = (
        P("seq", None), P("seq"), P("seq", None), P(), P(None, None, None, "head"), P(), P(None, None, "head"),
        P(None, None, "head"), P(), P(None, "head"), P(None, "head"), P(None, "head"), P(None, "head"), P(None, "head", None),
    )
    return jax.shard_map(
        local,
        mesh=mesh,
        in_specs=placed,
        out_specs=(
            P("seq", None), P("seq", None), P(None, "seq"), P(None, "seq", None, "head"), P(None, "seq", "head"),
            P(None, "seq", "head"), P(None, None, "head"), P(), P(None, "head"), P(None, "head"), P(None, "head"),
            P(None, "head"), P(None, "head", "seq"),
        ),
        check_vma=False,
    )
```

```python
from functools import partial

import jax
import jax.numpy as jnp
from jax import lax
from jax.experimental import pallas as pl
from jax.experimental.pallas import tpu as pltpu
from jax.sharding import PartitionSpec as P

CONV = 4
LAYERS = 2
OUT_ORDER = (0, 1, 2)
Z_ORDER = (1, 2, 0)
EPS = 1e-05
F32 = jnp.float32
BF16 = jnp.bfloat16


def dot(a, b, dims):
    return lax.dot_general(a.astype(BF16), b.astype(BF16), (dims, ((), ())), preferred_element_type=F32)


def mm(a, b):
    return dot(a, b, ((1,), (0,)))


def mm_nt(a, b):
    return dot(a, b, ((1,), (1,)))


def mm_tn(a, b):
    return dot(a, b, ((0,), (0,)))


def swap(x, axis, bit):
    n = lax.axis_size(axis)
    return lax.ppermute(x, axis, [(i, i ^ bit) for i in range(n)])


def shift(x, axis, by):
    n = lax.axis_size(axis)
    return lax.ppermute(x, axis, [(i, i + by) for i in range(n) if 0 <= i + by < n])


def bits_of(axis):
    n = lax.axis_size(axis)
    bits = []
    b = 1
    while b < n:
        bits.append(b)
        b *= 2
    return bits


def my_bit(axis, bit):
    return (lax.axis_index(axis) // bit) % 2


def take(x, dim, index):
    return lax.dynamic_index_in_dim(x, index, dim, keepdims=False)


def head_scatter(x):
    for bit in bits_of("head"):
        me = my_bit("head", bit)
        halves = x.reshape((2, x.shape[0] // 2) + x.shape[1:])
        got = swap(take(halves, 0, 1 - me).astype(BF16), "head", bit)
        x = take(halves, 0, me).astype(F32) + got.astype(F32)
    return x


def head_scatter_exact(x):
    for bit in bits_of("head"):
        me = my_bit("head", bit)
        halves = x.reshape((2, x.shape[0] // 2) + x.shape[1:])
        x = take(halves, 0, me) + swap(take(halves, 0, 1 - me), "head", bit)
    return x


def head_gather(x):
    for bit in reversed(bits_of("head")):
        me = my_bit("head", bit)
        got = swap(x, "head", bit)
        x = jnp.where(me == 0, jnp.concatenate([x, got], 0), jnp.concatenate([got, x], 0))
    return x


def own_rows(x):
    rank = lax.axis_index("head")
    quarter = x.shape[0] // 4
    return lax.dynamic_slice_in_dim(x, ((rank % 2) * 2 + rank // 2) * quarter, quarter, 0)


def carry_scan(state, decay, reverse):
    total, total_d = state, decay
    entering = jnp.zeros_like(state)
    enter_d = jnp.ones_like(decay)
    for bit in bits_of("seq"):
        me = my_bit("seq", bit)
        other = swap(total.astype(BF16), "seq", bit).astype(F32)
        other_d = swap(total_d, "seq", bit)
        second = (me == 0) if reverse else (me == 1)
        entering = jnp.where(second, entering + enter_d[:, None, None] * other, entering)
        enter_d = jnp.where(second, enter_d * other_d, enter_d)
        total = jnp.where(
            second, total_d[:, None, None] * other + total, other_d[:, None, None] * total + other
        )
        total_d = total_d * other_d
    return entering


def silu_slope(v):
    s = jax.nn.sigmoid(v)
    return s * (1.0 + v * (1.0 - s))


def scatter_rows(x):
    bits = bits_of("seq")
    k = len(bits)
    n = lax.axis_size("seq")
    x = x.reshape((2,) * k + (x.shape[0] // n, x.shape[1]))
    for b in range(k):
        axis = k - 1 - b
        me = my_bit("seq", bits[b])
        got = swap(take(x, axis, 1 - me).astype(BF16), "seq", bits[b])
        x = take(x, axis, me).astype(F32) + got.astype(F32)
    return x


HALO = 16
LANE = 128
NT = ((1,), (1,))
NN = ((1,), (0,))
TN = ((0,), (0,))


def bdot(a, b, dims):
    return lax.dot_general(a.astype(BF16), b.astype(BF16), (dims, ((), ())), preferred_element_type=F32)


def halves(x):
    high = x.astype(BF16)
    return high, (x - high.astype(F32)).astype(BF16)


def dot3(a, b, dims):
    ah, al = halves(a)
    bh, bl = halves(b)
    return bdot(ah, bh, dims) + (bdot(ah, bl, dims) + bdot(al, bh, dims))


def hdot(a, b, dims):
    return lax.dot_general(a, b, (dims, ((), ())), precision=lax.Precision.HIGHEST, preferred_element_type=F32)


def sig(v):
    return 0.5 * jnp.tanh(0.5 * v) + 0.5


def softplus(v):
    e = jnp.exp(-jnp.abs(v))
    s = e / (2.0 + e)
    q = s * s
    series = 1.0 / 13.0
    for k in (11, 9, 7, 5, 3, 1):
        series = series * q + 1.0 / k
    return jnp.maximum(v, 0.0) + 2.0 * s * series


def mix_taps(us, taps, aux, width):
    tokens = aux.shape[1]
    wide = lambda m: m if width == LANE else jnp.concatenate([m] * (width // LANE), axis=1)
    acc = us[pl.ds(HALO, tokens), :] * taps[0:1, :] + taps[CONV : CONV + 1, :]
    for j in range(1, CONV):
        acc = acc + us[pl.ds(HALO - j, tokens), :] * wide(aux[j - 1]) * taps[j : j + 1, :]
    return acc


def pick_lane(values, h, lanes):
    return jnp.sum(jnp.where(lanes == h, values, 0.0), axis=1, keepdims=True)


def fwd_mix_body(size, nx, wx, wbc, wdt, tapx, tapbc, dtb, lograte, aux, segrow,
                 ux, ubc, krs, pdt, steps_o, cum_o, cT, gram, mixed_o, entry_o, state, dec, decl,
                 us, usbc):
    p = pl.program_id(0)
    tokens = aux.shape[1]
    states = wbc.shape[1] // 2
    lanes = lax.broadcasted_iota(jnp.int32, (tokens, LANE), 1)
    half = lanes < size

    @pl.when(p == 0)
    def _():
        bc = bdot(nx[...], wbc[...], NN).astype(BF16)
        ubc[...] = bc
        usbc[...] = bc.astype(F32)
        m = mix_taps(usbc, tapbc, aux, 2 * states)
        act = m * sig(m)
        krs[...] = act
        g = dot3(act[:, states:], act[:, :states], NT)
        ii = lax.broadcasted_iota(jnp.int32, (tokens, tokens), 0)
        jj = lax.broadcasted_iota(jnp.int32, (tokens, tokens), 1)
        segc = jnp.concatenate([aux[5]] * (tokens // LANE), axis=1)
        keep = (ii >= jj) & (segc == segrow[...])
        gram[...] = jnp.where(keep, g, 0.0)
        pd = bdot(nx[pl.ds(HALO, tokens), :], wdt[...], NN).astype(BF16)
        pdt[...] = pd
        st = softplus(pd.astype(F32) + dtb[...])
        steps_o[...] = st
        log = st * -jnp.exp(lograte[...])
        cum = hdot(jnp.where(ii >= jj, 1.0, 0.0), log, NN)
        cum_o[...] = cum
        cT[...] = cum.T
        keeps = aux[3, tokens - 1 : tokens, :]
        decl[...] = jnp.broadcast_to(jnp.exp(cum[tokens - 1 : tokens, :]) * keeps, (8, LANE))
        dec[...] = jnp.exp(jnp.broadcast_to(cT[0:16, tokens - 1 : tokens], (16, LANE))) * keeps

    u = bdot(nx[...], wx[...], NN).astype(BF16)
    ux[...] = u
    us[...] = u.astype(F32)
    m = mix_taps(us, tapx, aux, LANE)
    mixed_o[...] = m
    v = m * sig(m)
    cum = cum_o[...]
    st = steps_o[...]
    h0 = p * (LANE // size)
    dd = jnp.where(half, pick_lane(st, h0, lanes), pick_lane(st, h0 + 1, lanes))
    vd = v * dd
    ct = jnp.where(half, pick_lane(cum, h0, lanes), pick_lane(cum, h0 + 1, lanes))
    entry_o[...] = jnp.exp(ct) * aux[3]
    tail = jnp.exp(ct[tokens - 1 : tokens, :] - ct) * aux[4]
    state[...] = dot3(vd * tail, krs[:, :states], TN)


def fwd_inside_body(stages_of, size, nx, wz, mixed, steps, cum, cT, gram, skip, state, dec, ypart, enter, gate, cb, *rest):
    p = pl.program_id(0)
    tokens = mixed.shape[0]
    stages = stages_of(state, dec, enter, *rest)
    for k, stage in enumerate(stages[:-1]):
        pl.when(p == k)(stage)
    gate[...] = bdot(nx[pl.ds(HALO, tokens), :], wz[...], NN).astype(BF16)
    lanes = lax.broadcasted_iota(jnp.int32, (tokens, LANE), 1)
    half = lanes < size
    h0 = p * (LANE // size)
    m = mixed[...]
    v = m * sig(m)
    st = steps[...]
    vh, vl = halves(v * jnp.where(half, pick_lane(st, h0, lanes), pick_lane(st, h0 + 1, lanes)))
    vhl = jnp.concatenate([vh, vl], axis=1)
    ys = []
    for k in range(LANE // size):
        h = h0 + k
        cb[k] = jnp.broadcast_to(pick_lane(cum[...], h, lanes), (tokens, LANE))
        row = cT[pl.ds(h, 1), :]
        parts = []
        for ib in range(tokens // LANE):
            tiles, lows = [], []
            ci = cb[k, pl.ds(ib * LANE, LANE), :]
            for jb in range(ib + 1):
                spread = ci - row[:, jb * LANE : (jb + 1) * LANE]
                if jb == ib:
                    spread = jnp.minimum(spread, 0.0)
                wh, wl = halves(jnp.exp(spread) * gram[pl.ds(ib * LANE, LANE), pl.ds(jb * LANE, LANE)])
                tiles.append(wh)
                lows.append(wl)
            joined = lambda t: t[0] if ib == 0 else jnp.concatenate(t, axis=1)
            both = bdot(joined(tiles), vhl[: (ib + 1) * LANE], NN)
            parts.append(both[:, :LANE] + (both[:, LANE:] + bdot(joined(lows), vh[: (ib + 1) * LANE], NN)))
        ys.append(jnp.concatenate(parts, axis=0))
    ypart[...] = jnp.where(half, ys[0], ys[1]) + skip[...] * v
    pl.when(p == pl.num_programs(0) - 1)(stages[-1])


def full(shape):
    n = len(shape)
    return pl.BlockSpec(shape, lambda p: (0,) * n)


WIDE = 2 * LANE


def cols(rows, width=LANE):
    return pl.BlockSpec((rows, width), lambda p: (0, p))


def rowsb(width, rows=LANE):
    return pl.BlockSpec((rows, width), lambda p: (p, 0))


def fwd_gate_body(ypart, entry, gate, krs, enter, y, carr, gated, sq, sqacc):
    p = pl.program_id(0)
    states = krs.shape[1] // 2
    c = dot3(krs[:, states:], enter[...], NT) * entry[...]
    carr[...] = c
    yy = ypart[...] + c
    y[...] = yy
    z = gate[...].astype(F32)
    g = yy * (z * sig(z))
    gated[...] = g
    gg = g[:, :LANE] * g[:, :LANE] + g[:, LANE:] * g[:, LANE:]

    @pl.when(p == 0)
    def _():
        sqacc[...] = gg

    @pl.when(p > 0)
    def _():
        sqacc[...] += gg

    @pl.when(p == pl.num_programs(0) - 1)
    def _():
        sq[...] = jnp.broadcast_to(jnp.sum(jnp.transpose(sqacc[...]), axis=0, keepdims=True), sq.shape)


def bwd_gate_body(gb, wout, gate, y, mixed, entry, krs, r2b, krb, gain, gy_o, gz_o, scaled_o, qloc, ggate, gskip):
    states = krs.shape[1] // 2
    gs = bdot(gb[...], wout[...], NT)
    z = gate[...].astype(F32)
    s = sig(z)
    sil = z * s
    yy = y[...]
    gated = yy * sil
    twice = lambda v: jnp.concatenate([v, v], axis=1)
    r2 = twice(r2b[...])
    gr = gated * r2
    ggate[...] = jnp.sum(gs * gr, axis=0, keepdims=True)
    scaled_o[...] = (gr * gain[...]).astype(BF16)
    gg = r2 * gain[...] * gs - gated * twice(krb[...])
    gy = gg * sil
    gy_o[...] = gy
    gz_o[...] = (gg * yy * (s * (1.0 + z * (1.0 - s)))).astype(BF16)
    m = mixed[...]
    gskip[...] = jnp.sum(gy * (m * sig(m)), axis=0, keepdims=True)
    qloc[...] = bdot(gy * entry[...], krs[:, states:], TN)


def wgrad_into(blocks, bit, off, lhs, rhs, away, keep, lt):
    tokens = rhs[0].shape[0]
    mine = (lax.axis_index("seq") // bit) % 2
    block = lt.shape[0] // blocks
    half = blocks // 2
    turned = jnp.transpose(lhs[pl.ds(off, tokens), :])
    for at in range(blocks):
        first = (at // bit) % 2 != mine
        k = at // (2 * bit) * bit + at % bit
        place = jnp.where(first, k, half + k) * block
        lt[pl.ds(pl.multiple_of(place, 16), block), :] = turned[at * block : (at + 1) * block]
    for dst, base in ((away, 0), (keep, half * block)):
        c = 0
        for r in rhs:
            w = r.shape[1]
            out = bdot(lt[pl.ds(base, half * block), :], r[...], NN).astype(BF16)
            dst[:, :, c : c + w] = out.reshape(half, block, w)
            c += w


def wgrad_body(blocks, bit, off, n_rhs, lhs, *refs):
    wgrad_into(blocks, bit, off, lhs, refs[:n_rhs], *refs[n_rhs:])


def halve(dst, got, keep, stride, want):
    for k in range(dst.shape[0]):
        at = (k // stride) * 2 * stride + want * stride + k % stride
        dst[k] = (keep[at].astype(F32) + got[at].astype(F32)).astype(dst.dtype)


def fold_body(bit, stride, got, keep, away, kept):
    me = (lax.axis_index("seq") // bit) % 2
    halve(away, got, keep, stride, 1 - me)
    halve(kept, got, keep, stride, me)


def bwd_local_body(stages_of, size, blocks, bits, folds, gy_r, mixed, krs, cum, steps, cT, gram, entry, enter, segc, segrow, qloc, dec, *refs):
    p = pl.program_id(0)
    n = len(folds)
    gb, scaled, nx, gz = refs[:4]
    pairs, refs = refs[4 : 4 + 2 * n], refs[4 + 2 * n :]
    dvd, dd_o, rowT, dkr, later, out_away, out_keep, z_away, z_keep = refs[:9]
    halved, refs = refs[9 : 9 + 2 * n], refs[9 + 2 * n :]
    cb, db, gramT, dgT, vb, gk, lt = refs[:7]
    stages = stages_of(qloc, dec, later, *refs[7:])
    for k, stage in enumerate(stages[:-1]):
        pl.when(p == k)(stage)
    tokens = gy_r.shape[0]

    def beside(k, fn):
        pl.when(p == k)(fn)

    beside(1, lambda: wgrad_into(blocks, bits[0], gb.shape[0] - tokens, gb, [scaled], out_away, out_keep, lt))
    beside(2, lambda: wgrad_into(blocks, bits[1], nx.shape[0] - tokens, nx, [gz], z_away, z_keep, lt))
    for i, (bit, stride) in enumerate(folds):
        beside((0, 3, 4)[i], partial(fold_body, bit, stride, *pairs[2 * i : 2 * i + 2], *halved[2 * i : 2 * i + 2]))
    states = krs.shape[1] // 2
    lanes = lax.broadcasted_iota(jnp.int32, (tokens, LANE), 1)
    half = lanes < size

    @pl.when(p == 0)
    def _():
        gramT[...] = gram[...].T
        dgT[...] = jnp.zeros_like(dgT)
        dd_o[...] = jnp.zeros_like(dd_o)
        rowT[...] = jnp.zeros_like(rowT)
        dkr[...] = jnp.zeros_like(dkr)

    m = mixed[...]
    vb[...] = (m * sig(m)).astype(BF16)
    gy = gy_r[...]
    gyb = gy.astype(BF16)
    h0 = p * (LANE // size)
    outs = []
    for k in range(LANE // size):
        h = h0 + k
        gk[...] = jnp.where(half if k == 0 else jnp.logical_not(half), gy, 0.0).astype(BF16)
        cb[...] = jnp.broadcast_to(pick_lane(cum[...], h, lanes), (tokens, LANE))
        db[...] = jnp.broadcast_to(pick_lane(steps[...], h, lanes), (tokens, LANE))
        row = cT[pl.ds(h, 1), :]
        parts = []
        dds = []
        rows_acc = [jnp.zeros((8, LANE), F32) for _ in range(tokens // LANE)]
        for jb in range(tokens // LANE):
            js = pl.ds(jb * LANE, LANE)
            cj = cb[js, :]
            dj = db[js, :]
            pt = bdot(vb[js, :], gk[pl.ds(jb * LANE, tokens - jb * LANE), :], NT)
            ws = []
            dsum = None
            for ib in range(jb, tokens // LANE):
                sl = pl.ds(ib * LANE, LANE)
                spread = row[:, ib * LANE : (ib + 1) * LANE] - cj
                if jb == ib:
                    spread = jnp.minimum(spread, 0.0)
                e = jnp.exp(spread)
                w = e * gramT[js, sl]
                ws.append(w.astype(BF16))
                pp = pt[:, (ib - jb) * LANE : (ib - jb + 1) * LANE]
                wp = w * pp
                dgT[js, sl] += e * (pp * dj)
                x = wp * dj
                rows_acc[ib] = rows_acc[ib] + jnp.sum(x.reshape(LANE // 8, 8, LANE), axis=0)
                dsum = wp if dsum is None else dsum + wp
            dds.append(jnp.sum(dsum, axis=1, keepdims=True))
            w = ws[0] if len(ws) == 1 else jnp.concatenate(ws, axis=1)
            parts.append(bdot(w, gyb[jb * LANE :], NN))
        outs.append(jnp.concatenate(parts, axis=0))
        dd_o[...] += jnp.where(lanes == h, jnp.concatenate(dds, axis=0), 0.0)
        rowT[pl.ds(h, 1), :] = jnp.concatenate([jnp.sum(r, axis=0, keepdims=True) for r in rows_acc], axis=1)
    dvd[...] = jnp.where(half, outs[0], outs[1])
    dkr[:, states:] += bdot(gy * entry[...], enter[...], NN)

    @pl.when(p == pl.num_programs(0) - 1)
    def _():
        jj = lax.broadcasted_iota(jnp.int32, (tokens, tokens), 0)
        ii = lax.broadcasted_iota(jnp.int32, (tokens, tokens), 1)
        segs = jnp.concatenate([segc[...]] * (tokens // LANE), axis=1)
        g = jnp.where((ii >= jj) & (segs == segrow[...]), dgT[...], 0.0)
        dkr[:, :states] += bdot(g, krs[:, states:], NN)
        dkr[:, states:] += bdot(g, krs[:, :states], TN)
        stages[-1]()


def bwd_carry_body(size, gy_r, dvd_r, mixed, carr, entry, krs, cum, steps, pdt, dtb, lograte, skip, ux, tapx, aux, later, enter,
                   dd_r, rowT, dkr_r, decay,
                   gm_o, gu_o, gtail_o, gtaps, gdt_o, gvec, dkr, us, ms, ddacc, dcum, last):
    p = pl.program_id(0)
    tokens = gy_r.shape[0]
    states = krs.shape[1] // 2
    lanes = lax.broadcasted_iota(jnp.int32, (tokens, LANE), 1)
    lane1 = lax.broadcasted_iota(jnp.int32, (1, LANE), 1)
    half = lanes < size

    @pl.when(p == 0)
    def _():
        ddacc[...] = dd_r[...]
        dcum[...] = jnp.transpose(rowT[...]) - dd_r[...] * steps[...]
        last[...] = jnp.zeros_like(last)
        dkr[...] = dkr_r[...]

    h0 = p * (LANE // size)
    st = steps[...]
    cu = cum[...]
    cc = [pick_lane(cu, h0 + k, lanes) for k in range(2)]
    dcol = [pick_lane(st, h0 + k, lanes) for k in range(2)]
    ct = jnp.where(half, cc[0], cc[1])
    dpair = jnp.where(half, dcol[0], dcol[1])
    tail = jnp.exp(ct[tokens - 1 : tokens, :] - ct) * aux[4]
    m = mixed[...]
    s = sig(m)
    v = m * s
    gy = gy_r[...]
    qk = bdot(krs[:, :states], later[...], NT) * tail
    dvd = dvd_r[...] + qk
    dkr[:, :states] += bdot(v * dpair * tail, later[...], NN)
    tq = v * qk
    eq = gy * carr[...]
    qs = later[...] * enter[...]
    for k in range(2):
        h = h0 + k
        mine = half if k == 0 else jnp.logical_not(half)
        td = jnp.sum(jnp.where(mine, tq, 0.0), axis=1, keepdims=True)
        ec = jnp.sum(jnp.where(mine, eq, 0.0), axis=1, keepdims=True)
        tdd = td * dcol[k]
        ddacc[...] += jnp.where(lanes == h, td, 0.0)
        dcum[...] += jnp.where(lanes == h, ec - tdd, 0.0)
        dot_qs = jnp.sum(jnp.sum(qs[k * size : (k + 1) * size, :], axis=0, keepdims=True), axis=1, keepdims=True)
        last[...] += jnp.where(lane1 == h, jnp.sum(tdd, axis=0, keepdims=True) + dot_qs * decay[0:1, :], 0.0)
    dv = dvd * dpair + skip[...] * gy
    gm = dv * (s * (1.0 + m * (1.0 - s)))
    gm_o[...] = gm[:8]
    us[...] = ux[...].astype(F32)
    acc = gm * tapx[0:1, :]
    gtaps[0:1, :] = jnp.sum(gm * us[pl.ds(HALO, tokens), :], axis=0, keepdims=True)
    gtaps[CONV : CONV + 1, :] = jnp.sum(gm, axis=0, keepdims=True)
    ms[pl.ds(tokens, 8), :] = jnp.zeros((8, LANE), F32)
    for j in range(1, CONV):
        gmj = gm * aux[j - 1]
        gtaps[j : j + 1, :] = jnp.sum(gmj * us[pl.ds(HALO - j, tokens), :], axis=0, keepdims=True)
        ms[pl.ds(0, tokens), :] = gmj
        acc = acc + ms[pl.ds(j, tokens), :] * tapx[j : j + 1, :]
    gu_o[...] = acc.astype(BF16)
    gtail_o[...] = acc[tokens - 16 :]

    @pl.when(p == pl.num_programs(0) - 1)
    def _():
        ii = lax.broadcasted_iota(jnp.int32, (tokens, tokens), 0)
        jj = lax.broadcasted_iota(jnp.int32, (tokens, tokens), 1)
        dlog = hdot(jnp.where(jj >= ii, 1.0, 0.0), dcum[...], NN) + last[...]
        rates = -jnp.exp(lograte[...])
        dsteps = ddacc[...] + rates * dlog
        gdt = dsteps * sig(pdt[...].astype(F32) + dtb[...])
        gdt_o[...] = gdt.astype(BF16)
        gvec[0:1, :] = jnp.sum(gdt, axis=0, keepdims=True)
        gvec[1:2, :] = jnp.sum(st * dlog, axis=0, keepdims=True) * rates


MESH = pl.DeviceIdType.MESH
VMEM_LIMIT = 56 * 1024 * 1024
SUBS = 2


def greet(partners):
    barrier = pltpu.get_barrier_semaphore()
    for where in partners:
        pl.semaphore_signal(barrier, inc=1, device_id=where, device_id_type=MESH)
    pl.semaphore_wait(barrier, len(partners))


def send(src, dst, sems, where):
    copy = pltpu.make_async_remote_copy(
        src_ref=src, dst_ref=dst, send_sem=sems[0], recv_sem=sems[1], device_id=where, device_id_type=MESH)
    copy.start()
    return copy


def flip(me, bit):
    return me + bit * (1 - 2 * ((me // bit) % 2))


def carry_stages(bits, reverse, heads, size, st, dec, out, tx, rx, rxd, tot, zp, btx, brx, bdtx, bdrx, pd, ed, ptx, prx, ssem, rsem):
    me = lax.axis_index("seq")
    n = len(bits)
    hh = heads // 2
    rows = hh * size
    x = me % 2
    r = (1 - x) if reverse else x
    pair_at = {"seq": flip(me, bits[0])}
    wheres = [{"seq": flip(me, b)} for b in bits[1:]]
    kind = tx.dtype
    mine = pl.ds(pl.multiple_of(r * rows, rows), rows)
    theirs = pl.ds(pl.multiple_of((1 - r) * rows, rows), rows)

    def copy(k, src, dst, where):
        return pltpu.make_async_remote_copy(src_ref=src, dst_ref=dst, send_sem=ssem.at[k], recv_sem=rsem.at[k],
                                            device_id=where, device_id_type=MESH)

    one = [copy(0, tx, rx, pair_at), copy(1, dec, rxd, pair_at)]
    steps = [[copy(2 + 2 * i, btx, brx.at[i], w), copy(3 + 2 * i, bdtx, bdrx.at[i], w)] for i, w in enumerate(wheres)]
    last = [copy(2 * n, ptx, prx, pair_at)]

    def begin(copies):
        for c in copies:
            c.start()

    def end(copies):
        for c in copies:
            c.wait()

    def per_head(fn):
        for k in range(hh):
            fn(pl.ds(k * size, size), r * hh + k, pl.ds(pl.multiple_of(r * rows + k * size, size), size))

    def open_():
        greet([pair_at] + wheres)
        tx[...] = st[theirs, :].astype(kind)
        begin(one)

    def pair():
        end(one)
        pd[...] = dec[...] * rxd[...]
        ed[...] = jnp.ones_like(ed)
        zp[...] = jnp.zeros_like(zp)

        def add(rk, h, own):
            a, b = st[own, :], rx[rk, :].astype(F32)
            row = pl.ds(h, 1)
            tot[rk, :] = jnp.where(r == 0, rxd[row, :] * a + b, dec[row, :] * b + a)

        per_head(add)
        go(0)

    def go(i):
        btx[...] = tot[...].astype(kind)
        bdtx[...] = pd[...]
        begin(steps[i])

    def butterfly(i):
        end(steps[i])
        bit = (me // bits[1 + i]) % 2
        second = (1 - bit) if reverse else bit
        keep = second.astype(F32)

        def add(rk, h, own):
            other = brx[i, rk, :].astype(F32)
            row = pl.ds(h, 1)
            zp[rk, :] += other * (ed[row, :] * keep)
            if i + 1 < len(steps):
                a = jnp.where(second == 1, pd[row, :], 1.0)
                c = jnp.where(second == 1, 1.0, bdrx[i, row, :])
                tot[rk, :] = a * other + c * tot[rk, :]

        per_head(add)
        ed[...] = jnp.where(second == 1, ed[...] * bdrx[i], ed[...])
        pd[...] = pd[...] * bdrx[i]
        if i + 1 < len(steps):
            go(i + 1)
        else:
            hand()

    def hand():
        def add(rk, h, own):
            row = pl.ds(h, 1)
            z = zp[rk, :]
            after = jnp.where(r == 0, dec[row, :], rxd[row, :]) * z + jnp.where(r == 0, st[own, :], rx[rk, :].astype(F32))
            out[own, :] = jnp.where(r == 0, z, after)
            ptx[rk, :] = jnp.where(r == 0, after, z).astype(kind)

        per_head(add)
        begin(last)

    def close():
        end(last)
        out[theirs, :] = prx[...].astype(F32)

    return [open_, pair] + [partial(butterfly, i) for i in range(len(steps))] + [close]


def carry_scratch(n, rows, states, kind):
    part = pltpu.VMEM((rows // 2, states), kind)
    wide = pltpu.VMEM((rows // 2, states), F32)
    dec = pltpu.VMEM((16, states), F32)
    return [part, part, dec, wide, wide, part, pltpu.VMEM((n - 1, rows // 2, states), kind), dec, pltpu.VMEM((n - 1, 16, states), F32),
            dec, dec, part, part, pltpu.SemaphoreType.DMA((2 * n + 1,)), pltpu.SemaphoreType.DMA((2 * n + 1,))]


def head_core(tokens, part, middle, nx, off, side, tx0, rx0, tx1, rx1, acc, ssem, rsem, me, core_at, y_at, gather=True):
    quarter = tokens // 4
    sub = quarter // SUBS
    c = me % 2
    y = me // 2
    half = 2 * quarter
    other_y = pl.multiple_of((1 - y) * quarter, quarter)
    own_y = pl.multiple_of(y * quarter, quarter)
    n = 0
    sends = []

    def go(src, dst, where):
        nonlocal n
        copy = send(src, dst, (ssem.at[n], rsem.at[n]), where)
        sends.append(copy)
        n += 1
        return copy

    acc[...] = part(pl.multiple_of((1 - c) * half, half), half)
    first = []
    for i, base in enumerate((other_y, own_y)):
        for s in range(SUBS):
            tx0[i, s] = acc[pl.ds(pl.multiple_of(base + s * sub, sub), sub), :].astype(tx0.dtype)
            first.append(go(tx0.at[i, s], rx0.at[i, s], core_at))
    acc[...] = part(pl.multiple_of(c * half, half), half)
    second = []
    for s in range(SUBS):
        first[s].wait_recv()
        tx1[s] = (acc[pl.ds(pl.multiple_of(other_y + s * sub, sub), sub), :] + rx0[0, s].astype(F32)).astype(tx1.dtype)
        second.append(go(tx1.at[s], rx1.at[s], y_at))
    own = (c * 2 + y) * quarter
    theirs = (c * 2 + 1 - y) * quarter
    to_y, to_core, onward = [], [], []
    for s in range(SUBS):
        first[SUBS + s].wait_recv()
        second[s].wait_recv()
        total = acc[pl.ds(pl.multiple_of(own_y + s * sub, sub), sub), :] + rx0[1, s].astype(F32) + rx1[s].astype(F32)
        if not gather:
            nx[pl.ds(s * sub, sub), :] = middle(s, sub, total)
            continue
        rows = pl.ds(pl.multiple_of(off + own + s * sub, 16), sub)
        nx[rows, :] = middle(s, sub, total)
        to_y.append(go(nx.at[rows, :], nx.at[rows, :], y_at))
        to_core.append(go(nx.at[rows, :], nx.at[rows, :], core_at))
    if not gather:
        for copy in sends:
            copy.wait_send()
        return
    if side is not None:
        srows = pl.ds(pl.multiple_of((c * 2 + y) * 8, 8), 8)
        to_y.append(go(side.at[srows, :], side.at[srows, :], y_at))
        to_core.append(go(side.at[srows, :], side.at[srows, :], core_at))
    for s in range(SUBS):
        to_y[s].wait_recv()
        rows = pl.ds(pl.multiple_of(off + theirs + s * sub, 16), sub)
        onward.append(go(nx.at[rows, :], nx.at[rows, :], core_at))
    if side is not None:
        to_y[SUBS].wait_recv()
        srows = pl.ds(pl.multiple_of((c * 2 + 1 - y) * 8, 8), 8)
        onward.append(go(side.at[srows, :], side.at[srows, :], core_at))
    for copy in to_core + onward:
        copy.wait_recv()
    for copy in sends:
        copy.wait_send()


HEAD_COPIES = 3 * SUBS + 3 * SUBS + 3


def head_fwd_body(l, tokens, last, width, gated, sq, ggain_all, wout_all, h_own, extra,
                  nx, h_new, branch, r2b, side, sqrx, tx0, rx0, tx1, rx1, acc, krc, ssem, rsem, qs, qr, hs, hr, wout, wsem):
    load = pltpu.make_async_copy(wout_all.at[l], wout, wsem.at[0])
    load.start()
    ggain = ggain_all.at[l]
    extra = extra if last else extra.at[l + 1]
    me = lax.axis_index("head")
    at = lax.axis_index("seq")
    count = lax.axis_size("seq")
    peers = [lax.rem(me + k, 4) for k in (1, 2, 3)]
    barrier = pltpu.get_barrier_semaphore()
    for pr in peers:
        pl.semaphore_signal(barrier, inc=1, device_id={"head": pr}, device_id_type=MESH)
    if not last:
        @pl.when(at > 0)
        def _():
            pl.semaphore_signal(barrier, inc=1, device_id={"seq": at - 1}, device_id_type=MESH)
    if last:
        pl.semaphore_wait(barrier, 3)
    else:
        pl.semaphore_wait(barrier, 3 + (at < count - 1).astype(jnp.int32))
    copies = [send(sq, sqrx.at[2 - k], (qs.at[k], qr.at[2 - k]), {"head": pr}) for k, pr in enumerate(peers)]
    for copy in copies:
        copy.wait_send()
    for k in range(3):
        pltpu.make_async_remote_copy(src_ref=sq, dst_ref=sqrx.at[k], send_sem=qs.at[k], recv_sem=qr.at[k],
                                     device_id={"head": peers[2 - k]}, device_id_type=MESH).wait_recv()
    total_sq = ((sq[...] + sqrx[0]) + (sqrx[1] + sqrx[2]))[0:1, :]
    r2row = lax.rsqrt(total_sq / width + EPS)
    r2b[...] = jnp.transpose(jnp.broadcast_to(r2row, (LANE, tokens)))
    inner = gated.shape[1]

    def part(start, rows):
        where = pl.ds(start, rows)
        r2 = jnp.concatenate([r2b[where, :]] * (inner // LANE), axis=1)
        return bdot(gated[where, :] * r2 * ggain[...], wout[...], NN)

    d = wout.shape[1]

    def middle(s, sub, total):
        rows = pl.ds(s * sub, sub)
        branch[rows, :] = total
        h = h_own[rows, :] + total
        h_new[rows, :] = h
        if last:
            krc[rows, :] = jnp.broadcast_to(jnp.sum(extra[rows, :].astype(F32) * total, axis=1, keepdims=True), (sub, LANE))
            if s == SUBS - 1:
                mine = pl.ds(pl.multiple_of(((me % 2) * 2 + me // 2) * 8, 8), 8)
                side[mine, :] = jnp.transpose(krc[...])[0:8, :]
            return h.astype(BF16)
        r1 = lax.rsqrt(jnp.sum(h * h, axis=1, keepdims=True) / d + EPS)
        return (h * r1 * extra[...]).astype(BF16)

    off = 0 if last else HALO
    load.wait()
    if not last:
        side[...] = jnp.zeros_like(side)
    head_core(tokens, part, middle, nx, off, side if last else None, tx0, rx0, tx1, rx1, acc, ssem, rsem, me,
              {"head": flip(me, 1)}, {"head": flip(me, 2)})
    if not last:
        src = nx.at[pl.ds(tokens, HALO), :]
        dst = nx.at[pl.ds(0, HALO), :]
        copy = pltpu.make_async_remote_copy(src_ref=src, dst_ref=dst, send_sem=hs.at[0], recv_sem=hr.at[0],
                                            device_id={"seq": lax.rem(at + 1, count)}, device_id_type=MESH)

        @pl.when(at < count - 1)
        def _():
            copy.start()
            copy.wait_send()

        @pl.when(at > 0)
        def _():
            copy.wait_recv()

        @pl.when(at == 0)
        def _():
            nx[pl.ds(0, HALO), :] = jnp.zeros((HALO, d), BF16)


def head_scratch(tokens, d, kind=BF16):
    sub = tokens // 4 // SUBS
    return [pltpu.VMEM((2, SUBS, sub, d), kind), pltpu.VMEM((2, SUBS, sub, d), kind), pltpu.VMEM((SUBS, sub, d), kind),
            pltpu.VMEM((SUBS, sub, d), kind), pltpu.VMEM((tokens // 2, d), F32), pltpu.VMEM((tokens // 4, LANE), F32),
            pltpu.SemaphoreType.DMA((HEAD_COPIES,)), pltpu.SemaphoreType.DMA((HEAD_COPIES,))]


def head_bwd_body(l, gather, tokens, gz, gu, small, wzx_all, wsmall_all, h_own, gain_all, g_own, branch,
                  gb, g_new, ggain, side, tx0, rx0, tx1, rx1, acc, krc, ssem, rsem, wzx, wsem):
    load = pltpu.make_async_copy(wzx_all.at[l], wzx, wsem.at[0])
    load.start()
    wsmall = wsmall_all.at[l]
    gain = gain_all.at[l]
    me = lax.axis_index("head")
    core_at, y_at = {"head": flip(me, 1)}, {"head": flip(me, 2)}
    greet([core_at, y_at])
    d = gain.shape[1]

    def part(start, rows):
        where = pl.ds(start, rows)
        return bdot(gz[where, :], wzx[0], NT) + bdot(gu[where, :], wzx[1], NT) + bdot(small[where, :], wsmall[...], NT)

    def middle(s, sub, total):
        rows = pl.ds(s * sub, sub)
        h = h_own[rows, :]
        r1 = lax.rsqrt(jnp.sum(h * h, axis=1, keepdims=True) / d + EPS)
        th = total * h
        gg = jnp.sum(th * r1, axis=0, keepdims=True)
        if s == 0:
            ggain[...] = gg
        else:
            ggain[...] += gg
        k1 = jnp.sum(th * gain[...], axis=1, keepdims=True)
        g = g_own[rows, :] + r1 * (gain[...] * total) - h * (r1 * r1 * r1 * (k1 / d))
        g_new[rows, :] = g
        low = g.astype(BF16)
        krc[rows, :] = jnp.broadcast_to(jnp.sum(low.astype(F32) * branch[rows, :], axis=1, keepdims=True), (sub, LANE))
        if s == SUBS - 1:
            mine = pl.ds(pl.multiple_of(((me % 2) * 2 + me // 2) * 8, 8), 8)
            if not gather:
                side[...] = jnp.zeros_like(side)
            side[mine, :] = jnp.transpose(krc[...])[0:8, :]
        return low

    load.wait()
    head_core(tokens, part, middle, gb, 0, side, tx0, rx0, tx1, rx1, acc, ssem, rsem, me, core_at, y_at, gather)


def maps_bwd_body(l, tokens, dkr, ubc, taps_all, aux, gdt, gtail, gm8, tapx_all,
                  small, gtaps, gtail_o, ytx, yrx, yacc, ctx, crx, us, ms, nextx, nextb, gmb, sems, semr):
    taps, tapx = taps_all.at[l], tapx_all.at[l]
    me = lax.axis_index("head")
    at = lax.axis_index("seq")
    count = lax.axis_size("seq")
    c = me % 2
    y = me // 2
    core_at, y_at = {"head": flip(me, 1)}, {"head": flip(me, 2)}
    barrier = pltpu.get_barrier_semaphore()
    for where in (core_at, y_at):
        pl.semaphore_signal(barrier, inc=1, device_id=where, device_id_type=MESH)

    @pl.when(at < count - 1)
    def _():
        pl.semaphore_signal(barrier, inc=1, device_id={"seq": at + 1}, device_id_type=MESH)
    pl.semaphore_wait(barrier, 2 + (at > 0).astype(jnp.int32))
    lanes = lax.broadcasted_iota(jnp.int32, (tokens, LANE), 1)
    before = {"seq": lax.rem(at + count - 1, count)}
    ahead_x = pltpu.make_async_remote_copy(src_ref=gm8, dst_ref=nextx, send_sem=sems.at[2], recv_sem=semr.at[2],
                                           device_id=before, device_id_type=MESH)

    @pl.when(at > 0)
    def _():
        ahead_x.start()
    low, high = dkr[:, :LANE], dkr[:, LANE:]
    ytx[...] = jnp.where(y == 0, high, low).astype(BF16)
    one = send(ytx, yrx, (sems.at[0], semr.at[0]), y_at)
    tile = pl.ds(pl.multiple_of(y * LANE, LANE), LANE)
    us[...] = ubc[:, tile].astype(F32)
    tp = taps[:, tile]
    m = mix_taps(us, tp, aux, LANE)
    s = sig(m)
    slope = s * (1.0 + m * (1.0 - s))
    one.wait()
    ctx[...] = jnp.where(y == 0, low, high) + yrx[...].astype(F32)
    two = send(ctx, crx, (sems.at[1], semr.at[1]), core_at)
    two.wait()
    gm = (ctx[...] + crx[...]) * slope
    gmb[...] = gm[0:8]
    ahead_b = pltpu.make_async_remote_copy(src_ref=gmb, dst_ref=nextb, send_sem=sems.at[3], recv_sem=semr.at[3],
                                           device_id=before, device_id_type=MESH)

    @pl.when(at > 0)
    def _():
        ahead_b.start()

    @pl.when(at == count - 1)
    def _():
        nextx[...] = jnp.zeros_like(nextx)
        nextb[...] = jnp.zeros_like(nextb)
    gtaps[...] = jnp.zeros_like(gtaps)
    gtaps[0:1, :] = jnp.sum(gm * us[pl.ds(HALO, tokens), :], axis=0, keepdims=True)
    gtaps[CONV : CONV + 1, :] = jnp.sum(gm, axis=0, keepdims=True)
    for j in range(1, CONV):
        gtaps[j : j + 1, :] = jnp.sum(gm * aux[j - 1] * us[pl.ds(HALO - j, tokens), :], axis=0, keepdims=True)

    @pl.when(at < count - 1)
    def _():
        ahead_x.wait_recv()
        ahead_b.wait_recv()
    acc = gm * tp[0:1, :]
    for j in range(1, CONV):
        ms[pl.ds(0, tokens), :] = gm * aux[j - 1]
        ms[pl.ds(tokens, 8), :] = nextb[...]
        acc = acc + ms[pl.ds(j, tokens), :] * tp[j : j + 1, :]
    own = jnp.where(c == 0, lanes, LANE - 1 - lanes) < 64
    g = gdt[...].astype(F32)
    moved = jnp.concatenate([g[:, 64:], g[:, :64]], axis=1)
    small[...] = jnp.where(own, acc, jnp.where(c == 0, moved, g)).astype(BF16)
    gtail_o[...] = gtail[...].astype(BF16)
    nx = nextx[...]
    tail = gtail[...]
    rows = lax.broadcasted_iota(jnp.int32, tail.shape, 0)
    for j in range(1, CONV):
        for k in range(j):
            tail = tail + jnp.where(rows == 16 - j + k, nx[k : k + 1, :] * tapx[j : j + 1, :], 0.0)
    gtail_o[...] = tail.astype(BF16)

    @pl.when(at > 0)
    def _():
        ahead_x.wait_send()
        ahead_b.wait_send()


class Job:
    def __init__(self, got, keep, left, steps, out, bufs, sems):
        self.got, self.keep, self.left, self.steps, self.out = got, keep, list(left), list(steps), out
        self.bufs, (self.ssem, self.rsem) = bufs, sems
        self.copy = None

    def advance(self):
        got, keep = self.got, self.keep
        if self.copy is not None:
            self.copy.wait()
        if not self.steps:
            if self.out is not None:
                self.out[...] = keep[0].astype(F32) + got[0].astype(F32)
            return
        bit = self.steps.pop(0)
        away, kept, came = self.bufs.pop(0)
        stride = 1 << (len(self.left) - 1 - self.left.index(bit))
        self.left.remove(bit)
        me = (lax.axis_index("seq") // bit) % 2
        halve(away, got, keep, stride, 1 - me)
        halve(kept, got, keep, stride, me)
        where = {"seq": flip(lax.axis_index("seq"), bit)}
        k = len(self.steps)
        self.copy = send(away, came, (self.ssem.at[k], self.rsem.at[k]), where)
        self.got, self.keep = came, kept


def tail_body(parts, plan, *refs):
    jobs_n = len(plan)
    pairs = refs[: 2 * jobs_n]
    ins = refs[2 * jobs_n : 2 * jobs_n + 6 * parts]
    rest = refs[2 * jobs_n + 6 * parts :]
    low, rest = rest[0], rest[1:]
    outs, rest = rest[:jobs_n], rest[jobs_n:]
    grad, rest = rest[0], rest[1:]
    gsend, grecv, rest = rest[-2], rest[-1], rest[:-2]
    conv_x, conv_bc, ggate, gskip, gvec, ggain = rest[:6]
    stage, rx, hx, ssem, rsem = rest[6:11]
    rest = list(rest[11:])
    jobs = []
    for i, (left, steps) in enumerate(plan):
        bufs = []
        for _ in steps:
            bufs.append((rest.pop(0), rest.pop(0), rest.pop(0)))
        jobs.append(Job(pairs[2 * i], pairs[2 * i + 1], left, steps, outs[i], bufs, (rest.pop(0), rest.pop(0))))
    inner = stage.shape[2]
    me = lax.axis_index("head")
    steps = [("head", b) for b in bits_of("head")] + [("seq", b) for b in bits_of("seq")]
    wheres = [{axis: flip(lax.axis_index(axis), b)} for axis, b in steps]
    greet(wheres)
    jobs[0].advance()
    quarter = low.shape[0]
    spot = lambda c, y: pl.ds(pl.multiple_of((c * 2 + y) * quarter, quarter), quarter)
    c, y = me % 2, me // 2
    grad[spot(c, y), :] = low[...]
    core_at, y_at = wheres[0], wheres[1]
    here = grad.at[spot(c, y), :]
    there = grad.at[spot(c, 1 - y), :]
    over_y = send(here, here, (gsend.at[0], grecv.at[0]), y_at)
    over_core = send(here, here, (gsend.at[1], grecv.at[1]), core_at)
    for job in jobs[1:]:
        job.advance()
    stage[...] = jnp.zeros_like(stage)
    for l in range(parts):
        taps, gate, skip, vec, maps, gain = ins[6 * l : 6 * l + 6]
        stage[l, 0 : CONV + 1, :] = taps[0 : CONV + 1, :]
        stage[l, 5:6, :] = gate[...]
        stage[l, 6:7, :] = skip[...]
        stage[l, 7:8, 0:LANE] = vec[0:1, :]
        stage[l, 7:8, LANE : 2 * LANE] = vec[1:2, :]
        stage[l, 8:9, :] = gain[:, :inner]
        stage[l, 9:10, :] = gain[:, inner:]
        for r in range(CONV + 1):
            row = maps[r : r + 1, :] * 0.5
            here = [jnp.where(me // 2 == k, row, 0.0) for k in range(2)]
            stage[l, 10 + r // 3 : 11 + r // 3, (r % 3) * 2 * LANE : ((r % 3) * 2 + 2) * LANE] = jnp.concatenate(here, axis=1)
    where = pl.ds(8, 8)
    heads = len(bits_of("head"))
    longest = max(len(job.steps) for job in jobs)
    for i, (axis, b) in enumerate(steps):
        if axis == "head":
            copy = send(stage.at[:, where, :], hx.at[i], (ssem.at[i], rsem.at[i]), wheres[i])
            copy.wait()
            stage[:, 8:16, :] += hx[i]
        else:
            copy = send(stage, rx.at[i - heads], (ssem.at[i], rsem.at[i]), wheres[i])
            if i == heads:
                for job in jobs:
                    if len(job.steps) == longest:
                        job.advance()
            copy.wait()
            stage[...] += rx[i - heads]
    over_y.wait_recv()
    onward = send(there, there, (gsend.at[2], grecv.at[2]), core_at)
    for _ in range(longest + 1):
        for job in jobs:
            if job.copy is not None and (job.steps or job.out is not None):
                done = not job.steps
                job.advance()
                if done:
                    job.out = None
    over_core.wait_recv()
    onward.wait_recv()
    for copy in (over_y, over_core, onward):
        copy.wait_send()
    for l in range(parts):
        conv_x[l] = stage[l, 0 : CONV + 1, :]
        ggate[l : l + 1, :] = stage[l, 5:6, :]
        gskip[l : l + 1, :] = stage[l, 6:7, :]
        gvec[l : l + 1, :] = stage[l, 7:8, 0 : 2 * LANE]
        ggain[l : l + 1, :inner] = stage[l, 8:9, :]
        ggain[l : l + 1, inner:] = stage[l, 9:10, :]
        for r in range(CONV + 1):
            conv_bc[l, r : r + 1, :] = stage[l, 10 + r // 3 : 11 + r // 3, (r % 3) * 2 * LANE : ((r % 3) * 2 + 2) * LANE]


VM = pl.BlockSpec(memory_space=pltpu.VMEM)
S = jax.ShapeDtypeStruct


def of_layer(l, shape, steps=False):
    n = len(shape) - 1
    if steps:
        return pl.BlockSpec((None,) + shape[1:-1] + (LANE if steps is True else steps,), lambda p: (l,) + (0,) * (n - 1) + (p,))
    return pl.BlockSpec((None,) + shape[1:], lambda *p: (l,) + (0,) * n)


def projection(l, which, d):
    return pl.BlockSpec((None, None, d, LANE), lambda p: (l, which, 0, p))


def rows_of_layer(l, shape):
    return pl.BlockSpec((None, WIDE, shape[2]), lambda p: (l, p, 0))


def kcall(body, args, specs, us, after=(), cid=None, **kw):
    n, k = len(args), len(after)

    def wrapped(*refs):
        body(*refs[:n], *refs[n + k :])

    extra = {} if cid is None else dict(collective_id=cid, has_side_effects=True)
    return pl.pallas_call(
        wrapped,
        in_specs=list(specs) + [pl.BlockSpec(memory_space=pl.ANY)] * k,
        compiler_params=pltpu.CompilerParams(vmem_limit_bytes=VMEM_LIMIT, **extra),
        cost_estimate=pl.CostEstimate(flops=int(us * 1e9), bytes_accessed=int(us * 3e6), transcendentals=0),
        **kw,
    )(*args, *after)


def fwd_mix(l, size, nx, q, aux, segrow):
    tokens = aux.shape[1]
    ext, d = nx.shape
    inner = q["conv_x"].shape[2]
    two = q["w_bc"].shape[2]
    args = [nx, q["w_zx"], q["w_bc"], q["w_dt"], q["conv_x"], q["conv_bc"], q["dt_bias"], q["a_log"], aux, segrow]
    specs = [full(nx.shape), projection(l, 1, d), of_layer(l, q["w_bc"].shape), of_layer(l, q["w_dt"].shape),
             of_layer(l, q["conv_x"].shape, True), of_layer(l, q["conv_bc"].shape), of_layer(l, q["dt_bias"].shape),
             of_layer(l, q["a_log"].shape), full(aux.shape), full(segrow.shape)]
    return kcall(
        partial(fwd_mix_body, size), args, specs, 12,
        name="fwd_mix",
        grid=(inner // LANE,),
        out_specs=[cols(ext), full((ext, two)), full((tokens, two)), full((tokens, LANE)), full((tokens, LANE)),
                   full((tokens, LANE)), full((LANE, tokens)), full((tokens, tokens)), cols(tokens),
                   cols(tokens), rowsb(two // 2), full((16, LANE)), full((8, LANE))],
        out_shape=[S((ext, inner), BF16), S((ext, two), BF16), S((tokens, two), F32),
                   S((tokens, LANE), BF16), S((tokens, LANE), F32), S((tokens, LANE), F32), S((LANE, tokens), F32),
                   S((tokens, tokens), F32), S((tokens, inner), F32), S((tokens, inner), F32),
                   S((inner, two // 2), F32), S((16, LANE), F32), S((8, LANE), F32)],
        scratch_shapes=[pltpu.VMEM((ext, LANE), F32), pltpu.VMEM((ext, two), F32)],
    )


def fwd_inside(l, heads, size, nx, mixed, steps, cum, cT, gram, q, state, dec, cid):
    tokens, inner = mixed.shape
    rows, states = state.shape
    bits = bits_of("seq")
    return kcall(
        partial(fwd_inside_body, partial(carry_stages, bits, False, heads, size), size),
        [nx, q["w_zx"], mixed, steps, cum, cT, gram, q["skip"], state, dec],
        [full(nx.shape), projection(l, 0, nx.shape[1]), cols(tokens), full(steps.shape), full(cum.shape), full(cT.shape), full(gram.shape), of_layer(l, q["skip"].shape, True),
         full(state.shape), full(dec.shape)], 28, (), cid,
        name="fwd_inside",
        grid=(inner // LANE,),
        out_specs=[cols(tokens), full((rows, states)), cols(tokens)],
        out_shape=[S((tokens, inner), F32), S((rows, states), F32), S((tokens, inner), BF16)],
        scratch_shapes=[pltpu.VMEM((2, tokens, LANE), F32)] + carry_scratch(len(bits), rows, states, F32),
    )


def fwd_gate(ypart, entry, gate, krs, enter):
    tokens, inner = ypart.shape
    return kcall(
        fwd_gate_body, [ypart, entry, gate, krs, enter],
        [cols(tokens, WIDE), cols(tokens, WIDE), cols(tokens, WIDE), full(krs.shape), rowsb(enter.shape[1], WIDE)], 7,
        name="fwd_gate",
        grid=(inner // WIDE,),
        out_specs=[cols(tokens, WIDE), cols(tokens, WIDE), cols(tokens, WIDE), full((8, tokens))],
        out_shape=[S((tokens, inner), F32)] * 3 + [S((8, tokens), F32)],
        scratch_shapes=[pltpu.VMEM((tokens, LANE), F32)],
    )


def bwd_gate(l, gb, q, gate, y, mixed, entry, krs, r2b, krb):
    tokens, inner = y.shape
    states = krs.shape[1] // 2
    return kcall(
        bwd_gate_body, [gb, q["w_out"], gate, y, mixed, entry, krs, r2b, krb, q["gate_gain"]],
        [full(gb.shape), rows_of_layer(l, q["w_out"].shape), cols(tokens, WIDE), cols(tokens, WIDE), cols(tokens, WIDE), cols(tokens, WIDE), full(krs.shape),
         full(r2b.shape), full(krb.shape), of_layer(l, q["gate_gain"].shape, WIDE)], 9,
        name="bwd_gate",
        grid=(inner // WIDE,),
        out_specs=[cols(tokens, WIDE), cols(tokens, WIDE), cols(tokens, WIDE), rowsb(states, WIDE), cols(1, WIDE), cols(1, WIDE)],
        out_shape=[S((tokens, inner), F32), S((tokens, inner), BF16), S((tokens, inner), BF16), S((inner, states), F32),
                   S((1, inner), F32), S((1, inner), F32)],
    )


def bwd_local(heads, size, gy, mixed, krs, cum, steps, cT, gram, entry, enter, aux, segrow, qloc, dec, cid, gb, scaled, nx, gz, under_way, also):
    tokens, inner = gy.shape
    d = gb.shape[1]
    two = krs.shape[1]
    rows, states = qloc.shape
    bits = bits_of("seq")
    blocks = lax.axis_size("seq")
    part = (blocks // 2, d // blocks, inner)
    out, z = Halving(OUT_ORDER), Halving(Z_ORDER)
    folds = [p.plan() for p in under_way]
    pairs = [x for p in under_way for x in (p.got, p.keep)]
    shapes = [(p.keep.shape[0] // 2,) + p.keep.shape[1:] for p in under_way for _ in range(2)]
    got = kcall(
        partial(bwd_local_body, partial(carry_stages, bits, True, heads, size), size, blocks, (out.order[0], z.order[0]), folds),
        [gy, mixed, krs, cum, steps, cT, gram, entry, enter, aux, segrow, qloc, dec, gb, scaled, nx, gz] + pairs,
        [cols(tokens), cols(tokens), full(krs.shape), full(cum.shape), full(steps.shape), full(cT.shape), full(gram.shape),
         cols(tokens), rowsb(two // 2), pl.BlockSpec((None, tokens, LANE), lambda p: (5, 0, 0)), full(segrow.shape),
         full(qloc.shape), full(dec.shape), full(gb.shape), full(scaled.shape), full(nx.shape), full(gz.shape)]
        + [full(x.shape) for x in pairs], 24, [p.got for p in also], cid,
        name="bwd_local",
        grid=(inner // LANE,),
        out_specs=[cols(tokens), full((tokens, LANE)), full((LANE, tokens)), full((tokens, two)), full((rows, states))]
        + [full(part)] * 4 + [full(x) for x in shapes],
        out_shape=[S((tokens, inner), F32), S((tokens, LANE), F32), S((LANE, tokens), F32), S((tokens, two), F32), S((rows, states), F32)]
        + [S(part, BF16)] * 4 + [S(x, BF16) for x in shapes],
        scratch_shapes=[pltpu.VMEM((tokens, LANE), F32), pltpu.VMEM((tokens, LANE), F32), pltpu.VMEM((tokens, tokens), F32),
                        pltpu.VMEM((tokens, tokens), F32), pltpu.VMEM((tokens, LANE), BF16), pltpu.VMEM((tokens, LANE), BF16),
                        pltpu.VMEM((d, tokens), BF16)]
        + carry_scratch(len(bits), rows, states, BF16),
    )
    out.away, out.keep, z.away, z.keep = got[5:9]
    for i, p in enumerate(under_way):
        p.away, p.keep = got[9 + 2 * i : 11 + 2 * i]
    return got[:5], out, z


def bwd_carry(l, size, gy, dvd, mixed, carr, entry, krs, cum, steps, pdt, q, ux, aux, later, enter, dd, rowT, dkr, decl, after):
    tokens, inner = gy.shape
    ext = ux.shape[0]
    two = krs.shape[1]
    return kcall(
        partial(bwd_carry_body, size),
        [gy, dvd, mixed, carr, entry, krs, cum, steps, pdt, q["dt_bias"], q["a_log"], q["skip"], ux, q["conv_x"], aux, later, enter,
         dd, rowT, dkr, decl],
        [cols(tokens), cols(tokens), cols(tokens), cols(tokens), cols(tokens), full(krs.shape), full(cum.shape), full(steps.shape),
         full(pdt.shape), of_layer(l, q["dt_bias"].shape), of_layer(l, q["a_log"].shape), of_layer(l, q["skip"].shape, True), cols(ext),
         of_layer(l, q["conv_x"].shape, True), full(aux.shape), rowsb(two // 2), rowsb(two // 2), full(dd.shape), full(rowT.shape),
         full(dkr.shape), full(decl.shape)], 11, after,
        name="bwd_carry",
        grid=(inner // LANE,),
        out_specs=[cols(8), cols(tokens), cols(16), cols(8), full((tokens, LANE)), full((8, LANE)), full((tokens, two))],
        out_shape=[S((8, inner), F32), S((tokens, inner), BF16), S((16, inner), F32), S((8, inner), F32), S((tokens, LANE), BF16),
                   S((8, LANE), F32), S((tokens, two), F32)],
        scratch_shapes=[pltpu.VMEM((ext, LANE), F32), pltpu.VMEM((tokens + 8, LANE), F32), pltpu.VMEM((tokens, LANE), F32),
                        pltpu.VMEM((tokens, LANE), F32), pltpu.VMEM((1, LANE), F32)],
    )


def head_fwd(l, gated, sq, q, h_own, extra, last, width, cid):
    tokens, inner = gated.shape
    d = q["w_out"].shape[2]
    return kcall(
        partial(head_fwd_body, l, tokens, last, width), [gated, sq, q["gate_gain"], q["w_out"], h_own, extra],
        [VM, VM, VM, pl.BlockSpec(memory_space=pl.ANY), VM, VM], 30, (), cid,
        name="head_fwd_last" if last else "head_fwd",
        out_specs=[VM] * 5,
        out_shape=[S((tokens if last else tokens + HALO, d), BF16), S((tokens // 4, d), F32), S((tokens // 4, d), F32),
                   S((tokens, LANE), F32), S((32, LANE), F32)],
        scratch_shapes=[pltpu.VMEM((3, 8, tokens), F32)] + head_scratch(tokens, d, BF16 if last else F32)
        + [pltpu.SemaphoreType.DMA((3,)), pltpu.SemaphoreType.DMA((3,)), pltpu.SemaphoreType.DMA((1,)), pltpu.SemaphoreType.DMA((1,)), pltpu.VMEM((inner, d), BF16), pltpu.SemaphoreType.DMA((1,))],
    )


def head_bwd(l, gz, gu, small, q, h_own, g_own, branch, cid, after=()):
    tokens = gz.shape[0]
    d = h_own.shape[1]
    return kcall(
        partial(head_bwd_body, l, l > 0, tokens), [gz, gu, small, q["w_zx"], q["w_small"], h_own, q["gain"], g_own, branch],
        [VM, VM, VM, pl.BlockSpec(memory_space=pl.ANY), VM, VM, VM, VM, VM], 29, after, cid,
        name="head_bwd",
        out_specs=[VM] * 4,
        out_shape=[S((tokens if l > 0 else tokens // 4, d), BF16), S((tokens // 4, d), F32), S((1, d), F32), S((32, LANE), F32)],
        scratch_shapes=head_scratch(tokens, d) + [pltpu.VMEM(q["w_zx"].shape[1:], BF16), pltpu.SemaphoreType.DMA((1,))],
    )


def maps_bwd(l, dkr, ubc, q, aux, gdt, gtail, gm8, cid, after=()):
    tokens = dkr.shape[0]
    inner = gtail.shape[1]
    tile = pltpu.VMEM((tokens, LANE), F32)
    return kcall(
        partial(maps_bwd_body, l, tokens), [dkr, ubc, q["conv_bc"], aux, gdt, gtail, gm8, q["conv_x"]],
        [VM] * 8, 14, after, cid,
        name="maps_bwd",
        out_specs=[VM] * 3,
        out_shape=[S((tokens, LANE), BF16), S((8, LANE), F32), S((16, inner), BF16)],
        scratch_shapes=[pltpu.VMEM((tokens, LANE), BF16)] * 2 + [tile, tile, tile, pltpu.VMEM((tokens + HALO, LANE), F32), pltpu.VMEM((tokens + 8, LANE), F32),
                        pltpu.VMEM((8, inner), F32), pltpu.VMEM((8, LANE), F32), pltpu.VMEM((8, LANE), F32),
                        pltpu.SemaphoreType.DMA((4,)), pltpu.SemaphoreType.DMA((4,))],
    )


def tail(sums, smalls, low, inner, cid):
    parts = len(smalls)
    quarter, d = low.shape
    plan = [(left, steps) for _, _, left, steps in sums]
    heads, n = len(bits_of("head")), len(bits_of("seq"))
    arrays, scratch, outs = [], [], []
    for got, keep, left, steps in sums:
        arrays += [got, keep]
        blocks, block, width = keep.shape
        outs.append(S((block, width), F32))
        for _ in steps:
            blocks //= 2
            buf = pltpu.VMEM((blocks, block, width), BF16)
            scratch += [buf, pltpu.VMEM((blocks, block, width), F32), buf]
        scratch += [pltpu.SemaphoreType.DMA((max(len(steps), 1),))] * 2
    return kcall(
        partial(tail_body, parts, plan), arrays + [x for part in smalls for x in part] + [low], [VM] * (2 * len(sums) + 6 * parts + 1), 45, (), cid,
        name="tail",
        out_specs=[VM] * (len(sums) + 7),
        out_shape=outs + [S((4 * quarter, d), BF16), S((parts, CONV + 1, inner), F32), S((parts, CONV + 1, 2 * LANE), F32), S((parts, inner), F32), S((parts, inner), F32),
                          S((parts, 2 * LANE), F32), S((parts, d), F32)],
        scratch_shapes=[pltpu.VMEM((parts, 16, inner), F32), pltpu.VMEM((n, parts, 16, inner), F32), pltpu.VMEM((heads, parts, 8, inner), F32),
                        pltpu.SemaphoreType.DMA((heads + n,)), pltpu.SemaphoreType.DMA((heads + n,))] + scratch
        + [pltpu.SemaphoreType.DMA((3,)), pltpu.SemaphoreType.DMA((3,))],
    )


def wgrad(lhs, rhs, bit, after=()):
    blocks = lax.axis_size("seq")
    tokens = rhs[0].shape[0]
    d = lhs.shape[1]
    width = sum(r.shape[1] for r in rhs)
    shape = (blocks // 2, d // blocks, width)
    return kcall(
        partial(wgrad_body, blocks, bit, lhs.shape[0] - tokens, len(rhs)), [lhs] + list(rhs), [VM] * (1 + len(rhs)), 3, after,
        name="wgrad",
        out_specs=[VM] * 2,
        out_shape=[S(shape, BF16)] * 2,
        scratch_shapes=[pltpu.VMEM((d, tokens), BF16)],
    )


class Halving:
    def __init__(self, order):
        bits = bits_of("seq")
        self.order = [bits[i % len(bits)] for i in order] + [b for i, b in enumerate(bits) if i not in order]
        self.left = [b for b in reversed(bits) if b != self.order[0]]
        self.step = 0
        self.got = self.away = self.keep = None

    def plan(self):
        bit = self.order[self.step]
        stride = 1 << (len(self.left) - 1 - self.left.index(bit))
        self.left.remove(bit)
        return bit, stride

    def go(self):
        self.got = swap(self.away, "seq", self.order[self.step])
        self.step += 1

    def rest(self):
        return self.got, self.keep, tuple(self.left), tuple(self.order[self.step :])

    def fold(self, after=()):
        bit, stride = self.plan()
        blocks, block, width = self.keep.shape
        self.away, self.keep = kcall(
            partial(fold_body, bit, stride), [self.got, self.keep], [VM] * 2, 2, after,
            name="fold",
            out_specs=[VM] * 2,
            out_shape=[S((blocks // 2, block, width), BF16)] * 2,
        )


def pad_lanes(x, to=LANE):
    return jnp.pad(x, [(0, 0)] * (x.ndim - 1) + [(0, to - x.shape[-1])])


def forward_layer(nx, h_own, extra, q, aux, segrow, layer):
    heads, size, inner = q["heads"], q["size"], q["inner"]
    (ux, ubc, krs, pdt, steps, cum, cT, gram, mixed, entry, state, dec, decl) = fwd_mix(layer, size, nx, q, aux, segrow)
    ypart, enter, gate = fwd_inside(layer, heads, size, nx, mixed, steps, cum, cT, gram, q, state, dec, layer)
    y, carr, gated, sq = fwd_gate(ypart, entry, gate, krs, enter)
    width = inner * lax.axis_size("head")
    nx_next, h_new, branch, r2b, side = head_fwd(layer, gated, sq, q, h_own, extra, layer == LAYERS - 1, width, LAYERS + layer)
    stored = dict(nx=nx, gate=gate, ux=ux, ubc=ubc, krs=krs, pdt=pdt, steps=steps, cum=cum, cT=cT, gram=gram, mixed=mixed,
                  entry=entry, dec=dec, decl=decl, enter=enter, y=y, carr=carr, r2b=r2b, branch=branch, h_own=h_own)
    return nx_next, h_new, side, stored


def backward_gate(gb, side, s, q, layer):
    tokens = gb.shape[0]
    width = q["inner"] * lax.axis_size("head")
    kr = side.reshape(4, 8, LANE)[:, 0, :].reshape(tokens)
    r2b = s["r2b"]
    krb = r2b * r2b * (kr[:, None] / width)
    return bwd_gate(layer, gb, q, s["gate"], s["y"], s["mixed"], s["entry"], s["krs"], r2b, krb)


def local(hidden_in, seg, cot, norm_gain, w_zx, w_bc, w_dt, conv_x, conv_bc, dt_bias, a_log, skip_d, gate_gain, w_out):
    tokens = hidden_in.shape[0]
    inner = w_zx.shape[3]
    heads = w_dt.shape[2]
    size = inner // heads
    rank = lax.axis_index("head")
    segf = seg.astype(F32)
    ext = jnp.concatenate([jnp.full((HALO,), segf[0], F32), segf], 0)
    vecs = [(ext[HALO - j : HALO - j + tokens] == segf).astype(F32) for j in range(1, CONV)]
    vecs += [(segf == segf[0]).astype(F32), (segf == segf[-1]).astype(F32), segf]
    aux = jnp.broadcast_to(jnp.stack(vecs, 0)[:, :, None], (len(vecs), tokens, LANE))
    segrow = segf[None]
    lanes = jnp.arange(LANE)
    even = rank % 2 == 0
    own = jnp.where(even, lanes, LANE - 1 - lanes) < LANE // 2
    dt_pad = pad_lanes(w_dt)
    tile = lax.dynamic_slice_in_dim(w_bc, (rank // 2) * LANE, LANE, 2)
    w_small = jnp.where(own[None, None], tile, jnp.where(even, jnp.roll(dt_pad, LANE // 2, axis=2), dt_pad))
    q = dict(heads=heads, size=size, inner=inner, gain=norm_gain[:, None, :], w_zx=jnp.transpose(w_zx, (0, 2, 1, 3)), w_bc=w_bc, w_dt=dt_pad,
             w_small=w_small, conv_x=conv_x, conv_bc=conv_bc, dt_bias=pad_lanes(dt_bias[:, None, :]), a_log=pad_lanes(a_log[:, None, :]),
             skip=jnp.repeat(skip_d, size, axis=1)[:, None, :], gate_gain=gate_gain[:, None, :], w_out=w_out)
    h = hidden_in.astype(F32)
    h_own = own_rows(hidden_in).astype(F32)
    cot_own = own_rows(cot)
    normed = (h * lax.rsqrt(jnp.mean(h * h, axis=1, keepdims=True) + EPS) * norm_gain[0][None]).astype(BF16)
    nx = jnp.concatenate([shift(normed[tokens - HALO :], "seq", 1), normed], 0)
    stored = []
    for l in range(LAYERS):
        extra = cot_own if l == LAYERS - 1 else q["gain"]
        nx, h_own, side, s = forward_layer(nx, h_own, extra, q, aux, segrow, l)
        stored.append(s)
    hidden_out = nx
    gb = cot
    g_own = cot_own.astype(F32)
    smalls = [None] * LAYERS
    sums = [None] * LAYERS
    pending = []
    for l in reversed(range(LAYERS)):
        s = stored[l]
        gy, gz, scaled, qloc, ggate, gskip = backward_gate(gb, side, s, q, l)
        (dvd, dd, rowT, dkr, later), out, z = bwd_local(
            heads, size, gy, s["mixed"], s["krs"], s["cum"], s["steps"], s["cT"], s["gram"], s["entry"], s["enter"], aux, segrow, qloc,
            s["dec"], 2 * LAYERS + l, gb, scaled, s["nx"], gz, pending[:2], pending[2:])
        for p in pending[:2]:
            p.go()
        out.go()
        z.go()
        gm8, gu, gtail, gtaps_x, gdt, gvec, dkr = bwd_carry(
            l, size, gy, dvd, s["mixed"], s["carr"], s["entry"], s["krs"], s["cum"], s["steps"], s["pdt"], q, s["ux"], aux, later, s["enter"],
            dd, rowT, dkr, s["decl"], ())
        small, gtaps_bc, gtail = maps_bwd(l, dkr, s["ubc"], q, aux, gdt, gtail, gm8, 3 * LAYERS + l)
        gu = lax.dynamic_update_slice(gu, gtail, (tokens - 16, 0))
        x = Halving((0, 1, 2))
        x.away, x.keep = wgrad(s["nx"], [gu, small], x.order[0])
        x.go()
        out.fold()
        z.fold()
        z.go()
        out.go()
        if pending:
            pending[2].fold()
            pending[2].go()
        before = stored[max(l - 1, 0)]["branch"]
        gb, g_own, g_gain, side = head_bwd(l, gz, gu, small, q, s["h_own"], g_own, before, 4 * LAYERS + l, after=[p.away for p in [x, out, z] + pending[2:]])
        smalls[l] = (gtaps_x, ggate, gskip, gvec, gtaps_bc, g_gain)
        pending = [out, z, x]
        sums[l] = pending
    under_way = [p for l in range(LAYERS) for p in reversed(sums[l])]
    done = tail([p.rest() for p in under_way], smalls, gb, inner, 5 * LAYERS)
    for p, total in zip(under_way, done):
        p.total = total
    grad_in, g_conv_x, g_conv_bc, g_gate, g_skip, g_vec, g_gain = done[len(under_way) :]
    grad_in = grad_in.astype(F32)
    g_w_zx = jnp.stack([jnp.stack([z.total, x.total[:, :inner]], 1) for _, z, x in sums], 0)
    g_small = jnp.stack([x.total[:, inner:] for _, _, x in sums], 0)
    g_w_bc = jnp.where(even, g_small[:, :, : LANE // 2], g_small[:, :, LANE // 2 :])
    g_w_dt = jnp.where(even, g_small[:, :, LANE // 2 : LANE // 2 + heads], g_small[:, :, :heads])
    g_w_out = jnp.stack([jnp.transpose(out.total) for out, _, _ in sums], 0)
    g_skip = jnp.sum(g_skip.reshape(LAYERS, heads, size), axis=2)
    part = g_gain.shape[1] // lax.axis_size("seq")
    g_gain = lax.dynamic_slice_in_dim(g_gain, lax.axis_index("seq") * part, part, 1)
    return (hidden_out, grad_in, g_gain, g_w_zx, g_w_bc, g_w_dt, g_conv_x, g_conv_bc,
            g_vec[:, :heads], g_vec[:, LANE : LANE + heads], g_skip, g_gate, g_w_out)


def solution(mesh):
    placed = (
        P("seq", None), P("seq"), P("seq", None), P(), P(None, None, None, "head"), P(), P(None, None, "head"),
        P(None, None, "head"), P(), P(None, "head"), P(None, "head"), P(None, "head"), P(None, "head"), P(None, "head", None),
    )
    return jax.shard_map(
        local,
        mesh=mesh,
        in_specs=placed,
        out_specs=(
            P("seq", None), P("seq", None), P(None, "seq"), P(None, "seq", None, "head"), P(None, "seq", "head"),
            P(None, "seq", "head"), P(None, None, "head"), P(), P(None, "head"), P(None, "head"), P(None, "head"),
            P(None, "head"), P(None, "head", "seq"),
        ),
        check_vma=False,
    )
```

```python
from functools import partial

import jax
import jax.numpy as jnp
from jax import lax
from jax.experimental import pallas as pl
from jax.experimental.pallas import tpu as pltpu
from jax.sharding import PartitionSpec as P

CONV = 4
LAYERS = 2
OUT_ORDER = (0, 1, 2)
Z_ORDER = (1, 2, 0)
EPS = 1e-05
F32 = jnp.float32
BF16 = jnp.bfloat16


def dot(a, b, dims):
    return lax.dot_general(a.astype(BF16), b.astype(BF16), (dims, ((), ())), preferred_element_type=F32)


def mm(a, b):
    return dot(a, b, ((1,), (0,)))


def mm_nt(a, b):
    return dot(a, b, ((1,), (1,)))


def mm_tn(a, b):
    return dot(a, b, ((0,), (0,)))


def swap(x, axis, bit):
    n = lax.axis_size(axis)
    return lax.ppermute(x, axis, [(i, i ^ bit) for i in range(n)])


def shift(x, axis, by):
    n = lax.axis_size(axis)
    return lax.ppermute(x, axis, [(i, i + by) for i in range(n) if 0 <= i + by < n])


def bits_of(axis):
    n = lax.axis_size(axis)
    bits = []
    b = 1
    while b < n:
        bits.append(b)
        b *= 2
    return bits


def my_bit(axis, bit):
    return (lax.axis_index(axis) // bit) % 2


def take(x, dim, index):
    return lax.dynamic_index_in_dim(x, index, dim, keepdims=False)


def head_scatter(x):
    for bit in bits_of("head"):
        me = my_bit("head", bit)
        halves = x.reshape((2, x.shape[0] // 2) + x.shape[1:])
        got = swap(take(halves, 0, 1 - me).astype(BF16), "head", bit)
        x = take(halves, 0, me).astype(F32) + got.astype(F32)
    return x


def head_scatter_exact(x):
    for bit in bits_of("head"):
        me = my_bit("head", bit)
        halves = x.reshape((2, x.shape[0] // 2) + x.shape[1:])
        x = take(halves, 0, me) + swap(take(halves, 0, 1 - me), "head", bit)
    return x


def head_gather(x):
    for bit in reversed(bits_of("head")):
        me = my_bit("head", bit)
        got = swap(x, "head", bit)
        x = jnp.where(me == 0, jnp.concatenate([x, got], 0), jnp.concatenate([got, x], 0))
    return x


def own_rows(x):
    rank = lax.axis_index("head")
    quarter = x.shape[0] // 4
    return lax.dynamic_slice_in_dim(x, ((rank % 2) * 2 + rank // 2) * quarter, quarter, 0)


def carry_scan(state, decay, reverse):
    total, total_d = state, decay
    entering = jnp.zeros_like(state)
    enter_d = jnp.ones_like(decay)
    for bit in bits_of("seq"):
        me = my_bit("seq", bit)
        other = swap(total.astype(BF16), "seq", bit).astype(F32)
        other_d = swap(total_d, "seq", bit)
        second = (me == 0) if reverse else (me == 1)
        entering = jnp.where(second, entering + enter_d[:, None, None] * other, entering)
        enter_d = jnp.where(second, enter_d * other_d, enter_d)
        total = jnp.where(
            second, total_d[:, None, None] * other + total, other_d[:, None, None] * total + other
        )
        total_d = total_d * other_d
    return entering


def silu_slope(v):
    s = jax.nn.sigmoid(v)
    return s * (1.0 + v * (1.0 - s))


def scatter_rows(x):
    bits = bits_of("seq")
    k = len(bits)
    n = lax.axis_size("seq")
    x = x.reshape((2,) * k + (x.shape[0] // n, x.shape[1]))
    for b in range(k):
        axis = k - 1 - b
        me = my_bit("seq", bits[b])
        got = swap(take(x, axis, 1 - me).astype(BF16), "seq", bits[b])
        x = take(x, axis, me).astype(F32) + got.astype(F32)
    return x


HALO = 16
LANE = 128
NT = ((1,), (1,))
NN = ((1,), (0,))
TN = ((0,), (0,))


def bdot(a, b, dims):
    return lax.dot_general(a.astype(BF16), b.astype(BF16), (dims, ((), ())), preferred_element_type=F32)


def halves(x):
    high = x.astype(BF16)
    return high, (x - high.astype(F32)).astype(BF16)


def dot3(a, b, dims):
    ah, al = halves(a)
    bh, bl = halves(b)
    return bdot(ah, bh, dims) + (bdot(ah, bl, dims) + bdot(al, bh, dims))


def hdot(a, b, dims):
    return lax.dot_general(a, b, (dims, ((), ())), precision=lax.Precision.HIGHEST, preferred_element_type=F32)


def sig(v):
    return 0.5 * jnp.tanh(0.5 * v) + 0.5


def softplus(v):
    e = jnp.exp(-jnp.abs(v))
    s = e / (2.0 + e)
    q = s * s
    series = 1.0 / 13.0
    for k in (11, 9, 7, 5, 3, 1):
        series = series * q + 1.0 / k
    return jnp.maximum(v, 0.0) + 2.0 * s * series


def mix_taps(us, taps, aux, width):
    tokens = aux.shape[1]
    wide = lambda m: m if width == LANE else jnp.concatenate([m] * (width // LANE), axis=1)
    acc = us[pl.ds(HALO, tokens), :] * taps[0:1, :] + taps[CONV : CONV + 1, :]
    for j in range(1, CONV):
        acc = acc + us[pl.ds(HALO - j, tokens), :] * wide(aux[j - 1]) * taps[j : j + 1, :]
    return acc


def pick_lane(values, h, lanes):
    return jnp.sum(jnp.where(lanes == h, values, 0.0), axis=1, keepdims=True)


def fwd_mix_body(size, nx, wx, wbc, wdt, tapx, tapbc, dtb, lograte, aux,
                 ux, ubc, krs, pdt, steps_o, cum_o, cT, mixed_o, entry_o, state, dec, decl,
                 us, usbc):
    p = pl.program_id(0)
    tokens = aux.shape[1]
    states = wbc.shape[1] // 2
    lanes = lax.broadcasted_iota(jnp.int32, (tokens, LANE), 1)
    half = lanes < size

    @pl.when(p == 0)
    def _():
        bc = bdot(nx[...], wbc[...], NN).astype(BF16)
        ubc[...] = bc
        usbc[...] = bc.astype(F32)
        m = mix_taps(usbc, tapbc, aux, 2 * states)
        act = m * sig(m)
        krs[...] = act
        ii = lax.broadcasted_iota(jnp.int32, (tokens, tokens), 0)
        jj = lax.broadcasted_iota(jnp.int32, (tokens, tokens), 1)
        pd = bdot(nx[pl.ds(HALO, tokens), :], wdt[...], NN).astype(BF16)
        pdt[...] = pd
        st = softplus(pd.astype(F32) + dtb[...])
        steps_o[...] = st
        log = st * -jnp.exp(lograte[...])
        cum = hdot(jnp.where(ii >= jj, 1.0, 0.0), log, NN)
        cum_o[...] = cum
        cT[...] = cum.T
        keeps = aux[3, tokens - 1 : tokens, :]
        decl[...] = jnp.broadcast_to(jnp.exp(cum[tokens - 1 : tokens, :]) * keeps, (8, LANE))
        dec[...] = jnp.exp(jnp.broadcast_to(cT[0:16, tokens - 1 : tokens], (16, LANE))) * keeps

    u = bdot(nx[...], wx[...], NN).astype(BF16)
    ux[...] = u
    us[...] = u.astype(F32)
    m = mix_taps(us, tapx, aux, LANE)
    mixed_o[...] = m
    v = m * sig(m)
    cum = cum_o[...]
    st = steps_o[...]
    h0 = p * (LANE // size)
    dd = jnp.where(half, pick_lane(st, h0, lanes), pick_lane(st, h0 + 1, lanes))
    vd = v * dd
    ct = jnp.where(half, pick_lane(cum, h0, lanes), pick_lane(cum, h0 + 1, lanes))
    entry_o[...] = jnp.exp(ct) * aux[3]
    tail = jnp.exp(ct[tokens - 1 : tokens, :] - ct) * aux[4]
    state[...] = dot3(vd * tail, krs[:, :states], TN)


def fwd_inside_body(stages_of, size, nx, wz, mixed, steps, cum, cT, krs, segc, segrow, skip, state, dec, ypart, enter, gate, gram, cb, *rest):
    p = pl.program_id(0)
    tokens = mixed.shape[0]
    stages = stages_of(state, dec, enter, *rest)
    for k, stage in enumerate(stages[:-1]):
        pl.when(p == k)(stage)
    gate[...] = bdot(nx[pl.ds(HALO, tokens), :], wz[...], NN).astype(BF16)
    states = krs.shape[1] // 2

    @pl.when(p == 0)
    def _():
        ii = lax.broadcasted_iota(jnp.int32, (tokens, tokens), 0)
        jj = lax.broadcasted_iota(jnp.int32, (tokens, tokens), 1)
        segs = jnp.concatenate([segc[...]] * (tokens // LANE), axis=1)
        gram[...] = jnp.where((ii >= jj) & (segs == segrow[...]), dot3(krs[:, states:], krs[:, :states], NT), 0.0)

    lanes = lax.broadcasted_iota(jnp.int32, (tokens, LANE), 1)
    half = lanes < size
    h0 = p * (LANE // size)
    m = mixed[...]
    v = m * sig(m)
    st = steps[...]
    vh, vl = halves(v * jnp.where(half, pick_lane(st, h0, lanes), pick_lane(st, h0 + 1, lanes)))
    vhl = jnp.concatenate([vh, vl], axis=1)
    ys = []
    for k in range(LANE // size):
        h = h0 + k
        cb[k] = jnp.broadcast_to(pick_lane(cum[...], h, lanes), (tokens, LANE))
        row = cT[pl.ds(h, 1), :]
        parts = []
        for ib in range(tokens // LANE):
            tiles, lows = [], []
            ci = cb[k, pl.ds(ib * LANE, LANE), :]
            for jb in range(ib + 1):
                spread = ci - row[:, jb * LANE : (jb + 1) * LANE]
                if jb == ib:
                    spread = jnp.minimum(spread, 0.0)
                wh, wl = halves(jnp.exp(spread) * gram[pl.ds(ib * LANE, LANE), pl.ds(jb * LANE, LANE)])
                tiles.append(wh)
                lows.append(wl)
            joined = lambda t: t[0] if ib == 0 else jnp.concatenate(t, axis=1)
            both = bdot(joined(tiles), vhl[: (ib + 1) * LANE], NN)
            parts.append(both[:, :LANE] + (both[:, LANE:] + bdot(joined(lows), vh[: (ib + 1) * LANE], NN)))
        ys.append(jnp.concatenate(parts, axis=0))
    ypart[...] = jnp.where(half, ys[0], ys[1]) + skip[...] * v
    pl.when(p == pl.num_programs(0) - 1)(stages[-1])


def full(shape):
    n = len(shape)
    return pl.BlockSpec(shape, lambda p: (0,) * n)


WIDE = 2 * LANE


def cols(rows, width=LANE):
    return pl.BlockSpec((rows, width), lambda p: (0, p))


def rowsb(width, rows=LANE):
    return pl.BlockSpec((rows, width), lambda p: (p, 0))


def fwd_gate_body(ypart, entry, gate, krs, enter, y, carr, gated, sq, sqacc):
    p = pl.program_id(0)
    states = krs.shape[1] // 2
    c = dot3(krs[:, states:], enter[...], NT) * entry[...]
    carr[...] = c
    yy = ypart[...] + c
    y[...] = yy
    z = gate[...].astype(F32)
    g = yy * (z * sig(z))
    gated[...] = g
    gg = g[:, :LANE] * g[:, :LANE] + g[:, LANE:] * g[:, LANE:]

    @pl.when(p == 0)
    def _():
        sqacc[...] = gg

    @pl.when(p > 0)
    def _():
        sqacc[...] += gg

    @pl.when(p == pl.num_programs(0) - 1)
    def _():
        sq[...] = jnp.broadcast_to(jnp.sum(jnp.transpose(sqacc[...]), axis=0, keepdims=True), sq.shape)


def bwd_gate_body(width, gb, wout, gate, y, mixed, entry, krs, r2b, side, gain, gy_o, gz_o, scaled_o, qloc, ggate, gskip, krb):
    @pl.when(pl.program_id(0) == 0)
    def _():
        quarter = r2b.shape[0] // 4
        for k in range(4):
            here = pl.ds(k * quarter, quarter)
            r = r2b[here, :]
            krb[here, :] = jnp.transpose(jnp.broadcast_to(side[8 * k : 8 * k + 1, :], (quarter, LANE))) * (r * r * (1.0 / width))

    states = krs.shape[1] // 2
    gs = bdot(gb[...], wout[...], NT)
    z = gate[...].astype(F32)
    s = sig(z)
    sil = z * s
    yy = y[...]
    gated = yy * sil
    twice = lambda v: jnp.concatenate([v, v], axis=1)
    r2 = twice(r2b[...])
    gr = gated * r2
    ggate[...] = jnp.sum(gs * gr, axis=0, keepdims=True)
    scaled_o[...] = (gr * gain[...]).astype(BF16)
    gg = r2 * gain[...] * gs - gated * twice(krb[...])
    gy = gg * sil
    gy_o[...] = gy
    gz_o[...] = (gg * yy * (s * (1.0 + z * (1.0 - s)))).astype(BF16)
    m = mixed[...]
    gskip[...] = jnp.sum(gy * (m * sig(m)), axis=0, keepdims=True)
    qloc[...] = bdot(gy * entry[...], krs[:, states:], TN)


def wgrad_into(blocks, bit, off, lhs, rhs, away, keep, lt):
    tokens = rhs[0].shape[0]
    mine = (lax.axis_index("seq") // bit) % 2
    block = lt.shape[0] // blocks
    half = blocks // 2
    turned = jnp.transpose(lhs[pl.ds(off, tokens), :])
    for at in range(blocks):
        first = (at // bit) % 2 != mine
        k = at // (2 * bit) * bit + at % bit
        place = jnp.where(first, k, half + k) * block
        lt[pl.ds(pl.multiple_of(place, 16), block), :] = turned[at * block : (at + 1) * block]
    for dst, base in ((away, 0), (keep, half * block)):
        c = 0
        for r in rhs:
            w = r.shape[1]
            out = bdot(lt[pl.ds(base, half * block), :], r[...], NN).astype(BF16)
            dst[:, :, c : c + w] = out.reshape(half, block, w)
            c += w


def wgrad_body(blocks, bit, off, n_rhs, lhs, *refs):
    wgrad_into(blocks, bit, off, lhs, refs[:n_rhs], *refs[n_rhs:])


def halve(dst, got, keep, stride, want):
    for k in range(dst.shape[0]):
        at = (k // stride) * 2 * stride + want * stride + k % stride
        dst[k] = (keep[at].astype(F32) + got[at].astype(F32)).astype(dst.dtype)


def fold_body(bit, stride, got, keep, away, kept):
    me = (lax.axis_index("seq") // bit) % 2
    halve(away, got, keep, stride, 1 - me)
    halve(kept, got, keep, stride, me)


def bwd_local_body(stages_of, size, blocks, bits, folds, gy_r, mixed, krs, cum, steps, cT, gram, entry, enter, segc, segrow, qloc, dec, *refs):
    p = pl.program_id(0)
    n = len(folds)
    gb, scaled, nx, gz = refs[:4]
    pairs, refs = refs[4 : 4 + 2 * n], refs[4 + 2 * n :]
    dvd, dd_o, rowT, dkr, later, out_away, out_keep, z_away, z_keep = refs[:9]
    halved, refs = refs[9 : 9 + 2 * n], refs[9 + 2 * n :]
    cb, db, gramT, dgT, vb, gk, lt = refs[:7]
    stages = stages_of(qloc, dec, later, *refs[7:])
    for k, stage in enumerate(stages[:-1]):
        pl.when(p == k)(stage)
    tokens = gy_r.shape[0]

    def beside(k, fn):
        pl.when(p == k)(fn)

    beside(1, lambda: wgrad_into(blocks, bits[0], gb.shape[0] - tokens, gb, [scaled], out_away, out_keep, lt))
    beside(2, lambda: wgrad_into(blocks, bits[1], nx.shape[0] - tokens, nx, [gz], z_away, z_keep, lt))
    for i, (bit, stride) in enumerate(folds):
        beside((0, 3, 4)[i], partial(fold_body, bit, stride, *pairs[2 * i : 2 * i + 2], *halved[2 * i : 2 * i + 2]))
    states = krs.shape[1] // 2
    lanes = lax.broadcasted_iota(jnp.int32, (tokens, LANE), 1)
    half = lanes < size

    @pl.when(p == 0)
    def _():
        gramT[...] = gram[...].T
        dgT[...] = jnp.zeros_like(dgT)
        dd_o[...] = jnp.zeros_like(dd_o)
        rowT[...] = jnp.zeros_like(rowT)
        dkr[...] = jnp.zeros_like(dkr)

    m = mixed[...]
    vb[...] = (m * sig(m)).astype(BF16)
    gy = gy_r[...]
    gyb = gy.astype(BF16)
    h0 = p * (LANE // size)
    outs = []
    for k in range(LANE // size):
        h = h0 + k
        gk[...] = jnp.where(half if k == 0 else jnp.logical_not(half), gy, 0.0).astype(BF16)
        cb[...] = jnp.broadcast_to(pick_lane(cum[...], h, lanes), (tokens, LANE))
        db[...] = jnp.broadcast_to(pick_lane(steps[...], h, lanes), (tokens, LANE))
        row = cT[pl.ds(h, 1), :]
        parts = []
        dds = []
        rows_acc = [jnp.zeros((8, LANE), F32) for _ in range(tokens // LANE)]
        for jb in range(tokens // LANE):
            js = pl.ds(jb * LANE, LANE)
            cj = cb[js, :]
            dj = db[js, :]
            pt = bdot(vb[js, :], gk[pl.ds(jb * LANE, tokens - jb * LANE), :], NT)
            ws = []
            dsum = None
            for ib in range(jb, tokens // LANE):
                sl = pl.ds(ib * LANE, LANE)
                spread = row[:, ib * LANE : (ib + 1) * LANE] - cj
                if jb == ib:
                    spread = jnp.minimum(spread, 0.0)
                e = jnp.exp(spread)
                w = e * gramT[js, sl]
                ws.append(w.astype(BF16))
                pp = pt[:, (ib - jb) * LANE : (ib - jb + 1) * LANE]
                wp = w * pp
                dgT[js, sl] += e * (pp * dj)
                x = wp * dj
                rows_acc[ib] = rows_acc[ib] + jnp.sum(x.reshape(LANE // 8, 8, LANE), axis=0)
                dsum = wp if dsum is None else dsum + wp
            dds.append(jnp.sum(dsum, axis=1, keepdims=True))
            w = ws[0] if len(ws) == 1 else jnp.concatenate(ws, axis=1)
            parts.append(bdot(w, gyb[jb * LANE :], NN))
        outs.append(jnp.concatenate(parts, axis=0))
        dd_o[...] += jnp.where(lanes == h, jnp.concatenate(dds, axis=0), 0.0)
        rowT[pl.ds(h, 1), :] = jnp.concatenate([jnp.sum(r, axis=0, keepdims=True) for r in rows_acc], axis=1)
    dvd[...] = jnp.where(half, outs[0], outs[1])
    dkr[:, states:] += bdot(gy * entry[...], enter[...], NN)

    @pl.when(p == pl.num_programs(0) - 1)
    def _():
        jj = lax.broadcasted_iota(jnp.int32, (tokens, tokens), 0)
        ii = lax.broadcasted_iota(jnp.int32, (tokens, tokens), 1)
        segs = jnp.concatenate([segc[...]] * (tokens // LANE), axis=1)
        g = jnp.where((ii >= jj) & (segs == segrow[...]), dgT[...], 0.0)
        dkr[:, :states] += bdot(g, krs[:, states:], NN)
        dkr[:, states:] += bdot(g, krs[:, :states], TN)
        stages[-1]()


def bwd_carry_body(size, gy_r, dvd_r, mixed, carr, entry, krs, cum, steps, pdt, dtb, lograte, skip, ux, tapx, aux, later, enter,
                   dd_r, rowT, dkr_r, decay,
                   gm_o, gu_o, gtail_o, gtaps, gdt_o, gvec, dkr, us, ms, ddacc, dcum, last):
    p = pl.program_id(0)
    tokens = gy_r.shape[0]
    states = krs.shape[1] // 2
    lanes = lax.broadcasted_iota(jnp.int32, (tokens, LANE), 1)
    lane1 = lax.broadcasted_iota(jnp.int32, (1, LANE), 1)
    half = lanes < size

    @pl.when(p == 0)
    def _():
        ddacc[...] = dd_r[...]
        dcum[...] = jnp.transpose(rowT[...]) - dd_r[...] * steps[...]
        last[...] = jnp.zeros_like(last)
        dkr[...] = dkr_r[...]

    h0 = p * (LANE // size)
    st = steps[...]
    cu = cum[...]
    cc = [pick_lane(cu, h0 + k, lanes) for k in range(2)]
    dcol = [pick_lane(st, h0 + k, lanes) for k in range(2)]
    ct = jnp.where(half, cc[0], cc[1])
    dpair = jnp.where(half, dcol[0], dcol[1])
    tail = jnp.exp(ct[tokens - 1 : tokens, :] - ct) * aux[4]
    m = mixed[...]
    s = sig(m)
    v = m * s
    gy = gy_r[...]
    qk = bdot(krs[:, :states], later[...], NT) * tail
    dvd = dvd_r[...] + qk
    dkr[:, :states] += bdot(v * dpair * tail, later[...], NN)
    tq = v * qk
    eq = gy * carr[...]
    qs = later[...] * enter[...]
    for k in range(2):
        h = h0 + k
        mine = half if k == 0 else jnp.logical_not(half)
        td = jnp.sum(jnp.where(mine, tq, 0.0), axis=1, keepdims=True)
        ec = jnp.sum(jnp.where(mine, eq, 0.0), axis=1, keepdims=True)
        tdd = td * dcol[k]
        ddacc[...] += jnp.where(lanes == h, td, 0.0)
        dcum[...] += jnp.where(lanes == h, ec - tdd, 0.0)
        dot_qs = jnp.sum(jnp.sum(qs[k * size : (k + 1) * size, :], axis=0, keepdims=True), axis=1, keepdims=True)
        last[...] += jnp.where(lane1 == h, jnp.sum(tdd, axis=0, keepdims=True) + dot_qs * decay[0:1, :], 0.0)
    dv = dvd * dpair + skip[...] * gy
    gm = dv * (s * (1.0 + m * (1.0 - s)))
    gm_o[...] = gm[:8]
    us[...] = ux[...].astype(F32)
    acc = gm * tapx[0:1, :]
    gtaps[0:1, :] = jnp.sum(gm * us[pl.ds(HALO, tokens), :], axis=0, keepdims=True)
    gtaps[CONV : CONV + 1, :] = jnp.sum(gm, axis=0, keepdims=True)
    ms[pl.ds(tokens, 8), :] = jnp.zeros((8, LANE), F32)
    for j in range(1, CONV):
        gmj = gm * aux[j - 1]
        gtaps[j : j + 1, :] = jnp.sum(gmj * us[pl.ds(HALO - j, tokens), :], axis=0, keepdims=True)
        ms[pl.ds(0, tokens), :] = gmj
        acc = acc + ms[pl.ds(j, tokens), :] * tapx[j : j + 1, :]
    gu_o[...] = acc.astype(BF16)
    gtail_o[...] = acc[tokens - 16 :]

    @pl.when(p == pl.num_programs(0) - 1)
    def _():
        ii = lax.broadcasted_iota(jnp.int32, (tokens, tokens), 0)
        jj = lax.broadcasted_iota(jnp.int32, (tokens, tokens), 1)
        dlog = hdot(jnp.where(jj >= ii, 1.0, 0.0), dcum[...], NN) + last[...]
        rates = -jnp.exp(lograte[...])
        dsteps = ddacc[...] + rates * dlog
        gdt = dsteps * sig(pdt[...].astype(F32) + dtb[...])
        gdt_o[...] = gdt.astype(BF16)
        gvec[0:1, :] = jnp.sum(gdt, axis=0, keepdims=True)
        gvec[1:2, :] = jnp.sum(st * dlog, axis=0, keepdims=True) * rates


MESH = pl.DeviceIdType.MESH
VMEM_LIMIT = 56 * 1024 * 1024
SUBS = 2


def greet(partners):
    barrier = pltpu.get_barrier_semaphore()
    for where in partners:
        pl.semaphore_signal(barrier, inc=1, device_id=where, device_id_type=MESH)
    pl.semaphore_wait(barrier, len(partners))


def send(src, dst, sems, where):
    copy = pltpu.make_async_remote_copy(
        src_ref=src, dst_ref=dst, send_sem=sems[0], recv_sem=sems[1], device_id=where, device_id_type=MESH)
    copy.start()
    return copy


def flip(me, bit):
    return me + bit * (1 - 2 * ((me // bit) % 2))


def carry_stages(bits, reverse, heads, size, st, dec, out, tx, rx, rxd, tot, zp, btx, brx, bdtx, bdrx, pd, ed, ptx, prx, ssem, rsem):
    me = lax.axis_index("seq")
    n = len(bits)
    hh = heads // 2
    rows = hh * size
    x = me % 2
    r = (1 - x) if reverse else x
    pair_at = {"seq": flip(me, bits[0])}
    wheres = [{"seq": flip(me, b)} for b in bits[1:]]
    kind = tx.dtype
    mine = pl.ds(pl.multiple_of(r * rows, rows), rows)
    theirs = pl.ds(pl.multiple_of((1 - r) * rows, rows), rows)

    def copy(k, src, dst, where):
        return pltpu.make_async_remote_copy(src_ref=src, dst_ref=dst, send_sem=ssem.at[k], recv_sem=rsem.at[k],
                                            device_id=where, device_id_type=MESH)

    one = [copy(0, tx, rx, pair_at), copy(1, dec, rxd, pair_at)]
    steps = [[copy(2 + 2 * i, btx, brx.at[i], w), copy(3 + 2 * i, bdtx, bdrx.at[i], w)] for i, w in enumerate(wheres)]
    last = [copy(2 * n, ptx, prx, pair_at)]

    def begin(copies):
        for c in copies:
            c.start()

    def end(copies):
        for c in copies:
            c.wait()

    def per_head(fn):
        for k in range(hh):
            fn(pl.ds(k * size, size), r * hh + k, pl.ds(pl.multiple_of(r * rows + k * size, size), size))

    def open_():
        greet([pair_at] + wheres)
        tx[...] = st[theirs, :].astype(kind)
        begin(one)

    def pair():
        end(one)
        pd[...] = dec[...] * rxd[...]
        ed[...] = jnp.ones_like(ed)
        zp[...] = jnp.zeros_like(zp)

        def add(rk, h, own):
            a, b = st[own, :], rx[rk, :].astype(F32)
            row = pl.ds(h, 1)
            tot[rk, :] = jnp.where(r == 0, rxd[row, :] * a + b, dec[row, :] * b + a)

        per_head(add)
        go(0)

    def go(i):
        btx[...] = tot[...].astype(kind)
        bdtx[...] = pd[...]
        begin(steps[i])

    def butterfly(i):
        end(steps[i])
        bit = (me // bits[1 + i]) % 2
        second = (1 - bit) if reverse else bit
        keep = second.astype(F32)

        def add(rk, h, own):
            other = brx[i, rk, :].astype(F32)
            row = pl.ds(h, 1)
            zp[rk, :] += other * (ed[row, :] * keep)
            if i + 1 < len(steps):
                a = jnp.where(second == 1, pd[row, :], 1.0)
                c = jnp.where(second == 1, 1.0, bdrx[i, row, :])
                tot[rk, :] = a * other + c * tot[rk, :]

        per_head(add)
        ed[...] = jnp.where(second == 1, ed[...] * bdrx[i], ed[...])
        pd[...] = pd[...] * bdrx[i]
        if i + 1 < len(steps):
            go(i + 1)
        else:
            hand()

    def hand():
        def add(rk, h, own):
            row = pl.ds(h, 1)
            z = zp[rk, :]
            after = jnp.where(r == 0, dec[row, :], rxd[row, :]) * z + jnp.where(r == 0, st[own, :], rx[rk, :].astype(F32))
            out[own, :] = jnp.where(r == 0, z, after)
            ptx[rk, :] = jnp.where(r == 0, after, z).astype(kind)

        per_head(add)
        begin(last)

    def close():
        end(last)
        out[theirs, :] = prx[...].astype(F32)

    return [open_, pair] + [partial(butterfly, i) for i in range(len(steps))] + [close]


def carry_scratch(n, rows, states, kind):
    part = pltpu.VMEM((rows // 2, states), kind)
    wide = pltpu.VMEM((rows // 2, states), F32)
    dec = pltpu.VMEM((16, states), F32)
    return [part, part, dec, wide, wide, part, pltpu.VMEM((n - 1, rows // 2, states), kind), dec, pltpu.VMEM((n - 1, 16, states), F32),
            dec, dec, part, part, pltpu.SemaphoreType.DMA((2 * n + 1,)), pltpu.SemaphoreType.DMA((2 * n + 1,))]


def head_core(tokens, part, middle, nx, off, side, tx0, rx0, tx1, rx1, acc, ssem, rsem, me, core_at, y_at, gather=True):
    quarter = tokens // 4
    sub = quarter // SUBS
    c = me % 2
    y = me // 2
    half = 2 * quarter
    other_y = pl.multiple_of((1 - y) * quarter, quarter)
    own_y = pl.multiple_of(y * quarter, quarter)
    n = 0
    sends = []

    def go(src, dst, where):
        nonlocal n
        copy = send(src, dst, (ssem.at[n], rsem.at[n]), where)
        sends.append(copy)
        n += 1
        return copy

    acc[...] = part(pl.multiple_of((1 - c) * half, half), half)
    first = []
    for i, base in enumerate((other_y, own_y)):
        for s in range(SUBS):
            tx0[i, s] = acc[pl.ds(pl.multiple_of(base + s * sub, sub), sub), :].astype(tx0.dtype)
            first.append(go(tx0.at[i, s], rx0.at[i, s], core_at))
    acc[...] = part(pl.multiple_of(c * half, half), half)
    second = []
    for s in range(SUBS):
        first[s].wait_recv()
        tx1[s] = (acc[pl.ds(pl.multiple_of(other_y + s * sub, sub), sub), :] + rx0[0, s].astype(F32)).astype(tx1.dtype)
        second.append(go(tx1.at[s], rx1.at[s], y_at))
    own = (c * 2 + y) * quarter
    theirs = (c * 2 + 1 - y) * quarter
    to_y, to_core, onward = [], [], []
    for s in range(SUBS):
        first[SUBS + s].wait_recv()
        second[s].wait_recv()
        total = acc[pl.ds(pl.multiple_of(own_y + s * sub, sub), sub), :] + rx0[1, s].astype(F32) + rx1[s].astype(F32)
        if not gather:
            nx[pl.ds(s * sub, sub), :] = middle(s, sub, total)
            continue
        rows = pl.ds(pl.multiple_of(off + own + s * sub, 16), sub)
        nx[rows, :] = middle(s, sub, total)
        to_y.append(go(nx.at[rows, :], nx.at[rows, :], y_at))
        to_core.append(go(nx.at[rows, :], nx.at[rows, :], core_at))
    if not gather:
        for copy in sends:
            copy.wait_send()
        return
    if side is not None:
        srows = pl.ds(pl.multiple_of((c * 2 + y) * 8, 8), 8)
        to_y.append(go(side.at[srows, :], side.at[srows, :], y_at))
        to_core.append(go(side.at[srows, :], side.at[srows, :], core_at))
    for s in range(SUBS):
        to_y[s].wait_recv()
        rows = pl.ds(pl.multiple_of(off + theirs + s * sub, 16), sub)
        onward.append(go(nx.at[rows, :], nx.at[rows, :], core_at))
    if side is not None:
        to_y[SUBS].wait_recv()
        srows = pl.ds(pl.multiple_of((c * 2 + 1 - y) * 8, 8), 8)
        onward.append(go(side.at[srows, :], side.at[srows, :], core_at))
    for copy in to_core + onward:
        copy.wait_recv()
    for copy in sends:
        copy.wait_send()


HEAD_COPIES = 3 * SUBS + 3 * SUBS + 3


def head_fwd_body(l, tokens, last, width, gated, sq, ggain_all, wout_all, h_own, extra,
                  nx, h_new, branch, r2b, side, sqrx, tx0, rx0, tx1, rx1, acc, krc, ssem, rsem, qs, qr, hs, hr, wout, wsem):
    load = pltpu.make_async_copy(wout_all.at[l], wout, wsem.at[0])
    load.start()
    ggain = ggain_all.at[l]
    extra = extra if last else extra.at[l + 1]
    me = lax.axis_index("head")
    at = lax.axis_index("seq")
    count = lax.axis_size("seq")
    peers = [lax.rem(me + k, 4) for k in (1, 2, 3)]
    barrier = pltpu.get_barrier_semaphore()
    for pr in peers:
        pl.semaphore_signal(barrier, inc=1, device_id={"head": pr}, device_id_type=MESH)
    if not last:
        @pl.when(at > 0)
        def _():
            pl.semaphore_signal(barrier, inc=1, device_id={"seq": at - 1}, device_id_type=MESH)
    if last:
        pl.semaphore_wait(barrier, 3)
    else:
        pl.semaphore_wait(barrier, 3 + (at < count - 1).astype(jnp.int32))
    copies = [send(sq, sqrx.at[2 - k], (qs.at[k], qr.at[2 - k]), {"head": pr}) for k, pr in enumerate(peers)]
    for copy in copies:
        copy.wait_send()
    for k in range(3):
        pltpu.make_async_remote_copy(src_ref=sq, dst_ref=sqrx.at[k], send_sem=qs.at[k], recv_sem=qr.at[k],
                                     device_id={"head": peers[2 - k]}, device_id_type=MESH).wait_recv()
    total_sq = ((sq[...] + sqrx[0]) + (sqrx[1] + sqrx[2]))[0:1, :]
    r2row = lax.rsqrt(total_sq / width + EPS)
    r2b[...] = jnp.transpose(jnp.broadcast_to(r2row, (LANE, tokens)))
    inner = gated.shape[1]

    def part(start, rows):
        where = pl.ds(start, rows)
        r2 = jnp.concatenate([r2b[where, :]] * (inner // LANE), axis=1)
        return bdot(gated[where, :] * r2 * ggain[...], wout[...], NN)

    d = wout.shape[1]

    def middle(s, sub, total):
        rows = pl.ds(s * sub, sub)
        branch[rows, :] = total
        h = h_own[rows, :] + total
        h_new[rows, :] = h
        if last:
            krc[rows, :] = jnp.broadcast_to(jnp.sum(extra[rows, :].astype(F32) * total, axis=1, keepdims=True), (sub, LANE))
            if s == SUBS - 1:
                mine = pl.ds(pl.multiple_of(((me % 2) * 2 + me // 2) * 8, 8), 8)
                side[mine, :] = jnp.transpose(krc[...])[0:8, :]
            return h.astype(BF16)
        r1 = lax.rsqrt(jnp.sum(h * h, axis=1, keepdims=True) / d + EPS)
        return (h * r1 * extra[...]).astype(BF16)

    off = 0 if last else HALO
    load.wait()
    if not last:
        side[...] = jnp.zeros_like(side)
    head_core(tokens, part, middle, nx, off, side if last else None, tx0, rx0, tx1, rx1, acc, ssem, rsem, me,
              {"head": flip(me, 1)}, {"head": flip(me, 2)})
    if not last:
        src = nx.at[pl.ds(tokens, HALO), :]
        dst = nx.at[pl.ds(0, HALO), :]
        copy = pltpu.make_async_remote_copy(src_ref=src, dst_ref=dst, send_sem=hs.at[0], recv_sem=hr.at[0],
                                            device_id={"seq": lax.rem(at + 1, count)}, device_id_type=MESH)

        @pl.when(at < count - 1)
        def _():
            copy.start()
            copy.wait_send()

        @pl.when(at > 0)
        def _():
            copy.wait_recv()

        @pl.when(at == 0)
        def _():
            nx[pl.ds(0, HALO), :] = jnp.zeros((HALO, d), BF16)


def head_scratch(tokens, d, kind=BF16):
    sub = tokens // 4 // SUBS
    return [pltpu.VMEM((2, SUBS, sub, d), kind), pltpu.VMEM((2, SUBS, sub, d), kind), pltpu.VMEM((SUBS, sub, d), kind),
            pltpu.VMEM((SUBS, sub, d), kind), pltpu.VMEM((tokens // 2, d), F32), pltpu.VMEM((tokens // 4, LANE), F32),
            pltpu.SemaphoreType.DMA((HEAD_COPIES,)), pltpu.SemaphoreType.DMA((HEAD_COPIES,))]


def head_bwd_body(l, gather, tokens, gz, gu, small, wzx_all, wsmall_all, h_own, gain_all, g_own, branch,
                  gb, g_new, ggain, side, tx0, rx0, tx1, rx1, acc, krc, ssem, rsem, wzx, wsem):
    load = pltpu.make_async_copy(wzx_all.at[l], wzx, wsem.at[0])
    load.start()
    wsmall = wsmall_all.at[l]
    gain = gain_all.at[l]
    me = lax.axis_index("head")
    core_at, y_at = {"head": flip(me, 1)}, {"head": flip(me, 2)}
    greet([core_at, y_at])
    d = gain.shape[1]

    def part(start, rows):
        where = pl.ds(start, rows)
        return bdot(gz[where, :], wzx[0], NT) + bdot(gu[where, :], wzx[1], NT) + bdot(small[where, :], wsmall[...], NT)

    def middle(s, sub, total):
        rows = pl.ds(s * sub, sub)
        h = h_own[rows, :]
        r1 = lax.rsqrt(jnp.sum(h * h, axis=1, keepdims=True) / d + EPS)
        th = total * h
        gg = jnp.sum(th * r1, axis=0, keepdims=True)
        if s == 0:
            ggain[...] = gg
        else:
            ggain[...] += gg
        k1 = jnp.sum(th * gain[...], axis=1, keepdims=True)
        g = g_own[rows, :] + r1 * (gain[...] * total) - h * (r1 * r1 * r1 * (k1 / d))
        g_new[rows, :] = g
        low = g.astype(BF16)
        krc[rows, :] = jnp.broadcast_to(jnp.sum(low.astype(F32) * branch[rows, :], axis=1, keepdims=True), (sub, LANE))
        if s == SUBS - 1:
            mine = pl.ds(pl.multiple_of(((me % 2) * 2 + me // 2) * 8, 8), 8)
            if not gather:
                side[...] = jnp.zeros_like(side)
            side[mine, :] = jnp.transpose(krc[...])[0:8, :]
        return low

    load.wait()
    head_core(tokens, part, middle, gb, 0, side, tx0, rx0, tx1, rx1, acc, ssem, rsem, me, core_at, y_at, gather)


def maps_bwd_body(l, tokens, dkr, ubc, taps_all, aux, gdt, gtail, gm8, tapx_all,
                  small, gtaps, gtail_o, ytx, yrx, yacc, ctx, crx, us, ms, nextx, nextb, gmb, sems, semr):
    taps, tapx = taps_all.at[l], tapx_all.at[l]
    me = lax.axis_index("head")
    at = lax.axis_index("seq")
    count = lax.axis_size("seq")
    c = me % 2
    y = me // 2
    core_at, y_at = {"head": flip(me, 1)}, {"head": flip(me, 2)}
    barrier = pltpu.get_barrier_semaphore()
    for where in (core_at, y_at):
        pl.semaphore_signal(barrier, inc=1, device_id=where, device_id_type=MESH)

    @pl.when(at < count - 1)
    def _():
        pl.semaphore_signal(barrier, inc=1, device_id={"seq": at + 1}, device_id_type=MESH)
    pl.semaphore_wait(barrier, 2 + (at > 0).astype(jnp.int32))
    lanes = lax.broadcasted_iota(jnp.int32, (tokens, LANE), 1)
    before = {"seq": lax.rem(at + count - 1, count)}
    ahead_x = pltpu.make_async_remote_copy(src_ref=gm8, dst_ref=nextx, send_sem=sems.at[2], recv_sem=semr.at[2],
                                           device_id=before, device_id_type=MESH)

    @pl.when(at > 0)
    def _():
        ahead_x.start()
    low, high = dkr[:, :LANE], dkr[:, LANE:]
    ytx[...] = jnp.where(y == 0, high, low).astype(BF16)
    one = send(ytx, yrx, (sems.at[0], semr.at[0]), y_at)
    tile = pl.ds(pl.multiple_of(y * LANE, LANE), LANE)
    us[...] = ubc[:, tile].astype(F32)
    tp = taps[:, tile]
    m = mix_taps(us, tp, aux, LANE)
    s = sig(m)
    slope = s * (1.0 + m * (1.0 - s))
    one.wait()
    ctx[...] = jnp.where(y == 0, low, high) + yrx[...].astype(F32)
    two = send(ctx, crx, (sems.at[1], semr.at[1]), core_at)
    two.wait()
    gm = (ctx[...] + crx[...]) * slope
    gmb[...] = gm[0:8]
    ahead_b = pltpu.make_async_remote_copy(src_ref=gmb, dst_ref=nextb, send_sem=sems.at[3], recv_sem=semr.at[3],
                                           device_id=before, device_id_type=MESH)

    @pl.when(at > 0)
    def _():
        ahead_b.start()

    @pl.when(at == count - 1)
    def _():
        nextx[...] = jnp.zeros_like(nextx)
        nextb[...] = jnp.zeros_like(nextb)
    gtaps[...] = jnp.zeros_like(gtaps)
    gtaps[0:1, :] = jnp.sum(gm * us[pl.ds(HALO, tokens), :], axis=0, keepdims=True)
    gtaps[CONV : CONV + 1, :] = jnp.sum(gm, axis=0, keepdims=True)
    for j in range(1, CONV):
        gtaps[j : j + 1, :] = jnp.sum(gm * aux[j - 1] * us[pl.ds(HALO - j, tokens), :], axis=0, keepdims=True)

    @pl.when(at < count - 1)
    def _():
        ahead_x.wait_recv()
        ahead_b.wait_recv()
    acc = gm * tp[0:1, :]
    for j in range(1, CONV):
        ms[pl.ds(0, tokens), :] = gm * aux[j - 1]
        ms[pl.ds(tokens, 8), :] = nextb[...]
        acc = acc + ms[pl.ds(j, tokens), :] * tp[j : j + 1, :]
    own = jnp.where(c == 0, lanes, LANE - 1 - lanes) < 64
    g = gdt[...].astype(F32)
    moved = jnp.concatenate([g[:, 64:], g[:, :64]], axis=1)
    small[...] = jnp.where(own, acc, jnp.where(c == 0, moved, g)).astype(BF16)
    gtail_o[...] = gtail[...].astype(BF16)
    nx = nextx[...]
    tail = gtail[...]
    rows = lax.broadcasted_iota(jnp.int32, tail.shape, 0)
    for j in range(1, CONV):
        for k in range(j):
            tail = tail + jnp.where(rows == 16 - j + k, nx[k : k + 1, :] * tapx[j : j + 1, :], 0.0)
    gtail_o[...] = tail.astype(BF16)

    @pl.when(at > 0)
    def _():
        ahead_x.wait_send()
        ahead_b.wait_send()


class Job:
    def __init__(self, got, keep, left, steps, out, bufs, sems):
        self.got, self.keep, self.left, self.steps, self.out = got, keep, list(left), list(steps), out
        self.bufs, (self.ssem, self.rsem) = bufs, sems
        self.copy = None

    def advance(self):
        got, keep = self.got, self.keep
        if self.copy is not None:
            self.copy.wait()
        if not self.steps:
            if self.out is not None:
                self.out[...] = keep[0].astype(F32) + got[0].astype(F32)
            return
        bit = self.steps.pop(0)
        away, kept, came = self.bufs.pop(0)
        stride = 1 << (len(self.left) - 1 - self.left.index(bit))
        self.left.remove(bit)
        me = (lax.axis_index("seq") // bit) % 2
        halve(away, got, keep, stride, 1 - me)
        halve(kept, got, keep, stride, me)
        where = {"seq": flip(lax.axis_index("seq"), bit)}
        k = len(self.steps)
        self.copy = send(away, came, (self.ssem.at[k], self.rsem.at[k]), where)
        self.got, self.keep = came, kept


def tail_body(parts, plan, *refs):
    jobs_n = len(plan)
    pairs = refs[: 2 * jobs_n]
    ins = refs[2 * jobs_n : 2 * jobs_n + 6 * parts]
    rest = refs[2 * jobs_n + 6 * parts :]
    low, rest = rest[0], rest[1:]
    outs, rest = rest[:jobs_n], rest[jobs_n:]
    grad, rest = rest[0], rest[1:]
    gsend, grecv, rest = rest[-2], rest[-1], rest[:-2]
    conv_x, conv_bc, ggate, gskip, gvec, ggain = rest[:6]
    stage, rx, hx, ssem, rsem = rest[6:11]
    rest = list(rest[11:])
    jobs = []
    for i, (left, steps) in enumerate(plan):
        bufs = []
        for _ in steps:
            bufs.append((rest.pop(0), rest.pop(0), rest.pop(0)))
        jobs.append(Job(pairs[2 * i], pairs[2 * i + 1], left, steps, outs[i], bufs, (rest.pop(0), rest.pop(0))))
    inner = stage.shape[2]
    me = lax.axis_index("head")
    steps = [("head", b) for b in bits_of("head")] + [("seq", b) for b in bits_of("seq")]
    wheres = [{axis: flip(lax.axis_index(axis), b)} for axis, b in steps]
    greet(wheres)
    jobs[0].advance()
    quarter = low.shape[0]
    spot = lambda c, y: pl.ds(pl.multiple_of((c * 2 + y) * quarter, quarter), quarter)
    c, y = me % 2, me // 2
    grad[spot(c, y), :] = low[...]
    core_at, y_at = wheres[0], wheres[1]
    here = grad.at[spot(c, y), :]
    there = grad.at[spot(c, 1 - y), :]
    over_y = send(here, here, (gsend.at[0], grecv.at[0]), y_at)
    over_core = send(here, here, (gsend.at[1], grecv.at[1]), core_at)
    for job in jobs[1:]:
        job.advance()
    stage[...] = jnp.zeros_like(stage)
    for l in range(parts):
        taps, gate, skip, vec, maps, gain = ins[6 * l : 6 * l + 6]
        stage[l, 0 : CONV + 1, :] = taps[0 : CONV + 1, :]
        stage[l, 5:6, :] = gate[...]
        stage[l, 6:7, :] = skip[...]
        stage[l, 7:8, 0:LANE] = vec[0:1, :]
        stage[l, 7:8, LANE : 2 * LANE] = vec[1:2, :]
        stage[l, 8:9, :] = gain[:, :inner]
        stage[l, 9:10, :] = gain[:, inner:]
        for r in range(CONV + 1):
            row = maps[r : r + 1, :] * 0.5
            here = [jnp.where(me // 2 == k, row, 0.0) for k in range(2)]
            stage[l, 10 + r // 3 : 11 + r // 3, (r % 3) * 2 * LANE : ((r % 3) * 2 + 2) * LANE] = jnp.concatenate(here, axis=1)
    where = pl.ds(8, 8)
    heads = len(bits_of("head"))
    longest = max(len(job.steps) for job in jobs)
    for i, (axis, b) in enumerate(steps):
        if axis == "head":
            copy = send(stage.at[:, where, :], hx.at[i], (ssem.at[i], rsem.at[i]), wheres[i])
            copy.wait()
            stage[:, 8:16, :] += hx[i]
        else:
            copy = send(stage, rx.at[i - heads], (ssem.at[i], rsem.at[i]), wheres[i])
            if i == heads:
                for job in jobs:
                    if len(job.steps) == longest:
                        job.advance()
            copy.wait()
            stage[...] += rx[i - heads]
    over_y.wait_recv()
    onward = send(there, there, (gsend.at[2], grecv.at[2]), core_at)
    for _ in range(longest + 1):
        for job in jobs:
            if job.copy is not None and (job.steps or job.out is not None):
                done = not job.steps
                job.advance()
                if done:
                    job.out = None
    over_core.wait_recv()
    onward.wait_recv()
    for copy in (over_y, over_core, onward):
        copy.wait_send()
    for l in range(parts):
        conv_x[l] = stage[l, 0 : CONV + 1, :]
        ggate[l : l + 1, :] = stage[l, 5:6, :]
        gskip[l : l + 1, :] = stage[l, 6:7, :]
        gvec[l : l + 1, :] = stage[l, 7:8, 0 : 2 * LANE]
        ggain[l : l + 1, :inner] = stage[l, 8:9, :]
        ggain[l : l + 1, inner:] = stage[l, 9:10, :]
        for r in range(CONV + 1):
            conv_bc[l, r : r + 1, :] = stage[l, 10 + r // 3 : 11 + r // 3, (r % 3) * 2 * LANE : ((r % 3) * 2 + 2) * LANE]


VM = pl.BlockSpec(memory_space=pltpu.VMEM)
S = jax.ShapeDtypeStruct


def of_layer(l, shape, steps=False):
    n = len(shape) - 1
    if steps:
        return pl.BlockSpec((None,) + shape[1:-1] + (LANE if steps is True else steps,), lambda p: (l,) + (0,) * (n - 1) + (p,))
    return pl.BlockSpec((None,) + shape[1:], lambda *p: (l,) + (0,) * n)


def projection(l, which, d):
    return pl.BlockSpec((None, None, d, LANE), lambda p: (l, which, 0, p))


def rows_of_layer(l, shape):
    return pl.BlockSpec((None, WIDE, shape[2]), lambda p: (l, p, 0))


def kcall(body, args, specs, us, after=(), cid=None, **kw):
    n, k = len(args), len(after)

    def wrapped(*refs):
        body(*refs[:n], *refs[n + k :])

    extra = {} if cid is None else dict(collective_id=cid, has_side_effects=True)
    return pl.pallas_call(
        wrapped,
        in_specs=list(specs) + [pl.BlockSpec(memory_space=pl.ANY)] * k,
        compiler_params=pltpu.CompilerParams(vmem_limit_bytes=VMEM_LIMIT, **extra),
        cost_estimate=pl.CostEstimate(flops=int(us * 1e9), bytes_accessed=int(us * 3e6), transcendentals=0),
        **kw,
    )(*args, *after)


def fwd_mix(l, size, nx, q, aux):
    tokens = aux.shape[1]
    ext, d = nx.shape
    inner = q["conv_x"].shape[2]
    two = q["w_bc"].shape[2]
    args = [nx, q["w_zx"], q["w_bc"], q["w_dt"], q["conv_x"], q["conv_bc"], q["dt_bias"], q["a_log"], aux]
    specs = [full(nx.shape), projection(l, 1, d), of_layer(l, q["w_bc"].shape), of_layer(l, q["w_dt"].shape),
             of_layer(l, q["conv_x"].shape, True), of_layer(l, q["conv_bc"].shape), of_layer(l, q["dt_bias"].shape),
             of_layer(l, q["a_log"].shape), full(aux.shape)]
    return kcall(
        partial(fwd_mix_body, size), args, specs, 12,
        name="fwd_mix",
        grid=(inner // LANE,),
        out_specs=[cols(ext), full((ext, two)), full((tokens, two)), full((tokens, LANE)), full((tokens, LANE)),
                   full((tokens, LANE)), full((LANE, tokens)), cols(tokens),
                   cols(tokens), rowsb(two // 2), full((16, LANE)), full((8, LANE))],
        out_shape=[S((ext, inner), BF16), S((ext, two), BF16), S((tokens, two), F32),
                   S((tokens, LANE), BF16), S((tokens, LANE), F32), S((tokens, LANE), F32), S((LANE, tokens), F32),
                   S((tokens, inner), F32), S((tokens, inner), F32),
                   S((inner, two // 2), F32), S((16, LANE), F32), S((8, LANE), F32)],
        scratch_shapes=[pltpu.VMEM((ext, LANE), F32), pltpu.VMEM((ext, two), F32)],
    )


def fwd_inside(l, heads, size, nx, mixed, steps, cum, cT, krs, aux, segrow, q, state, dec, cid):
    tokens, inner = mixed.shape
    rows, states = state.shape
    bits = bits_of("seq")
    return kcall(
        partial(fwd_inside_body, partial(carry_stages, bits, False, heads, size), size),
        [nx, q["w_zx"], mixed, steps, cum, cT, krs, aux, segrow, q["skip"], state, dec],
        [full(nx.shape), projection(l, 0, nx.shape[1]), cols(tokens), full(steps.shape), full(cum.shape), full(cT.shape), full(krs.shape),
         pl.BlockSpec((None, tokens, LANE), lambda p: (5, 0, 0)), full(segrow.shape), of_layer(l, q["skip"].shape, True),
         full(state.shape), full(dec.shape)], 28, (), cid,
        name="fwd_inside",
        grid=(inner // LANE,),
        out_specs=[cols(tokens), full((rows, states)), cols(tokens), full((tokens, tokens))],
        out_shape=[S((tokens, inner), F32), S((rows, states), F32), S((tokens, inner), BF16), S((tokens, tokens), F32)],
        scratch_shapes=[pltpu.VMEM((2, tokens, LANE), F32)] + carry_scratch(len(bits), rows, states, F32),
    )


def fwd_gate(ypart, entry, gate, krs, enter):
    tokens, inner = ypart.shape
    return kcall(
        fwd_gate_body, [ypart, entry, gate, krs, enter],
        [cols(tokens, WIDE), cols(tokens, WIDE), cols(tokens, WIDE), full(krs.shape), rowsb(enter.shape[1], WIDE)], 7,
        name="fwd_gate",
        grid=(inner // WIDE,),
        out_specs=[cols(tokens, WIDE), cols(tokens, WIDE), cols(tokens, WIDE), full((8, tokens))],
        out_shape=[S((tokens, inner), F32)] * 3 + [S((8, tokens), F32)],
        scratch_shapes=[pltpu.VMEM((tokens, LANE), F32)],
    )


def bwd_gate(l, gb, q, gate, y, mixed, entry, krs, r2b, side, width):
    tokens, inner = y.shape
    states = krs.shape[1] // 2
    return kcall(
        partial(bwd_gate_body, width), [gb, q["w_out"], gate, y, mixed, entry, krs, r2b, side, q["gate_gain"]],
        [full(gb.shape), rows_of_layer(l, q["w_out"].shape), cols(tokens, WIDE), cols(tokens, WIDE), cols(tokens, WIDE), cols(tokens, WIDE), full(krs.shape),
         full(r2b.shape), full(side.shape), of_layer(l, q["gate_gain"].shape, WIDE)], 9,
        name="bwd_gate",
        grid=(inner // WIDE,),
        out_specs=[cols(tokens, WIDE), cols(tokens, WIDE), cols(tokens, WIDE), rowsb(states, WIDE), cols(1, WIDE), cols(1, WIDE)],
        out_shape=[S((tokens, inner), F32), S((tokens, inner), BF16), S((tokens, inner), BF16), S((inner, states), F32),
                   S((1, inner), F32), S((1, inner), F32)],
        scratch_shapes=[pltpu.VMEM((tokens, LANE), F32)],
    )


def bwd_local(heads, size, gy, mixed, krs, cum, steps, cT, gram, entry, enter, aux, segrow, qloc, dec, cid, gb, scaled, nx, gz, under_way, also):
    tokens, inner = gy.shape
    d = gb.shape[1]
    two = krs.shape[1]
    rows, states = qloc.shape
    bits = bits_of("seq")
    blocks = lax.axis_size("seq")
    part = (blocks // 2, d // blocks, inner)
    out, z = Halving(OUT_ORDER), Halving(Z_ORDER)
    folds = [p.plan() for p in under_way]
    pairs = [x for p in under_way for x in (p.got, p.keep)]
    shapes = [(p.keep.shape[0] // 2,) + p.keep.shape[1:] for p in under_way for _ in range(2)]
    got = kcall(
        partial(bwd_local_body, partial(carry_stages, bits, True, heads, size), size, blocks, (out.order[0], z.order[0]), folds),
        [gy, mixed, krs, cum, steps, cT, gram, entry, enter, aux, segrow, qloc, dec, gb, scaled, nx, gz] + pairs,
        [cols(tokens), cols(tokens), full(krs.shape), full(cum.shape), full(steps.shape), full(cT.shape), full(gram.shape),
         cols(tokens), rowsb(two // 2), pl.BlockSpec((None, tokens, LANE), lambda p: (5, 0, 0)), full(segrow.shape),
         full(qloc.shape), full(dec.shape), full(gb.shape), full(scaled.shape), full(nx.shape), full(gz.shape)]
        + [full(x.shape) for x in pairs], 24, [p.got for p in also], cid,
        name="bwd_local",
        grid=(inner // LANE,),
        out_specs=[cols(tokens), full((tokens, LANE)), full((LANE, tokens)), full((tokens, two)), full((rows, states))]
        + [full(part)] * 4 + [full(x) for x in shapes],
        out_shape=[S((tokens, inner), F32), S((tokens, LANE), F32), S((LANE, tokens), F32), S((tokens, two), F32), S((rows, states), F32)]
        + [S(part, BF16)] * 4 + [S(x, BF16) for x in shapes],
        scratch_shapes=[pltpu.VMEM((tokens, LANE), F32), pltpu.VMEM((tokens, LANE), F32), pltpu.VMEM((tokens, tokens), F32),
                        pltpu.VMEM((tokens, tokens), F32), pltpu.VMEM((tokens, LANE), BF16), pltpu.VMEM((tokens, LANE), BF16),
                        pltpu.VMEM((d, tokens), BF16)]
        + carry_scratch(len(bits), rows, states, BF16),
    )
    out.away, out.keep, z.away, z.keep = got[5:9]
    for i, p in enumerate(under_way):
        p.away, p.keep = got[9 + 2 * i : 11 + 2 * i]
    return got[:5], out, z


def bwd_carry(l, size, gy, dvd, mixed, carr, entry, krs, cum, steps, pdt, q, ux, aux, later, enter, dd, rowT, dkr, decl, after):
    tokens, inner = gy.shape
    ext = ux.shape[0]
    two = krs.shape[1]
    return kcall(
        partial(bwd_carry_body, size),
        [gy, dvd, mixed, carr, entry, krs, cum, steps, pdt, q["dt_bias"], q["a_log"], q["skip"], ux, q["conv_x"], aux, later, enter,
         dd, rowT, dkr, decl],
        [cols(tokens), cols(tokens), cols(tokens), cols(tokens), cols(tokens), full(krs.shape), full(cum.shape), full(steps.shape),
         full(pdt.shape), of_layer(l, q["dt_bias"].shape), of_layer(l, q["a_log"].shape), of_layer(l, q["skip"].shape, True), cols(ext),
         of_layer(l, q["conv_x"].shape, True), full(aux.shape), rowsb(two // 2), rowsb(two // 2), full(dd.shape), full(rowT.shape),
         full(dkr.shape), full(decl.shape)], 11, after,
        name="bwd_carry",
        grid=(inner // LANE,),
        out_specs=[cols(8), cols(tokens), cols(16), cols(8), full((tokens, LANE)), full((8, LANE)), full((tokens, two))],
        out_shape=[S((8, inner), F32), S((tokens, inner), BF16), S((16, inner), F32), S((8, inner), F32), S((tokens, LANE), BF16),
                   S((8, LANE), F32), S((tokens, two), F32)],
        scratch_shapes=[pltpu.VMEM((ext, LANE), F32), pltpu.VMEM((tokens + 8, LANE), F32), pltpu.VMEM((tokens, LANE), F32),
                        pltpu.VMEM((tokens, LANE), F32), pltpu.VMEM((1, LANE), F32)],
    )


def head_fwd(l, gated, sq, q, h_own, extra, last, width, cid):
    tokens, inner = gated.shape
    d = q["w_out"].shape[2]
    return kcall(
        partial(head_fwd_body, l, tokens, last, width), [gated, sq, q["gate_gain"], q["w_out"], h_own, extra],
        [VM, VM, VM, pl.BlockSpec(memory_space=pl.ANY), VM, VM], 30, (), cid,
        name="head_fwd_last" if last else "head_fwd",
        out_specs=[VM] * 5,
        out_shape=[S((tokens if last else tokens + HALO, d), BF16), S((tokens // 4, d), F32), S((tokens // 4, d), F32),
                   S((tokens, LANE), F32), S((32, LANE), F32)],
        scratch_shapes=[pltpu.VMEM((3, 8, tokens), F32)] + head_scratch(tokens, d, BF16 if last else F32)
        + [pltpu.SemaphoreType.DMA((3,)), pltpu.SemaphoreType.DMA((3,)), pltpu.SemaphoreType.DMA((1,)), pltpu.SemaphoreType.DMA((1,)), pltpu.VMEM((inner, d), BF16), pltpu.SemaphoreType.DMA((1,))],
    )


def head_bwd(l, gz, gu, small, q, h_own, g_own, branch, cid, after=()):
    tokens = gz.shape[0]
    d = h_own.shape[1]
    return kcall(
        partial(head_bwd_body, l, l > 0, tokens), [gz, gu, small, q["w_zx"], q["w_small"], h_own, q["gain"], g_own, branch],
        [VM, VM, VM, pl.BlockSpec(memory_space=pl.ANY), VM, VM, VM, VM, VM], 29, after, cid,
        name="head_bwd",
        out_specs=[VM] * 4,
        out_shape=[S((tokens if l > 0 else tokens // 4, d), BF16), S((tokens // 4, d), F32), S((1, d), F32), S((32, LANE), F32)],
        scratch_shapes=head_scratch(tokens, d) + [pltpu.VMEM(q["w_zx"].shape[1:], BF16), pltpu.SemaphoreType.DMA((1,))],
    )


def maps_bwd(l, dkr, ubc, q, aux, gdt, gtail, gm8, cid, after=()):
    tokens = dkr.shape[0]
    inner = gtail.shape[1]
    tile = pltpu.VMEM((tokens, LANE), F32)
    return kcall(
        partial(maps_bwd_body, l, tokens), [dkr, ubc, q["conv_bc"], aux, gdt, gtail, gm8, q["conv_x"]],
        [VM] * 8, 14, after, cid,
        name="maps_bwd",
        out_specs=[VM] * 3,
        out_shape=[S((tokens, LANE), BF16), S((8, LANE), F32), S((16, inner), BF16)],
        scratch_shapes=[pltpu.VMEM((tokens, LANE), BF16)] * 2 + [tile, tile, tile, pltpu.VMEM((tokens + HALO, LANE), F32), pltpu.VMEM((tokens + 8, LANE), F32),
                        pltpu.VMEM((8, inner), F32), pltpu.VMEM((8, LANE), F32), pltpu.VMEM((8, LANE), F32),
                        pltpu.SemaphoreType.DMA((4,)), pltpu.SemaphoreType.DMA((4,))],
    )


def tail(sums, smalls, low, inner, cid):
    parts = len(smalls)
    quarter, d = low.shape
    plan = [(left, steps) for _, _, left, steps in sums]
    heads, n = len(bits_of("head")), len(bits_of("seq"))
    arrays, scratch, outs = [], [], []
    for got, keep, left, steps in sums:
        arrays += [got, keep]
        blocks, block, width = keep.shape
        outs.append(S((block, width), F32))
        for _ in steps:
            blocks //= 2
            buf = pltpu.VMEM((blocks, block, width), BF16)
            scratch += [buf, pltpu.VMEM((blocks, block, width), F32), buf]
        scratch += [pltpu.SemaphoreType.DMA((max(len(steps), 1),))] * 2
    return kcall(
        partial(tail_body, parts, plan), arrays + [x for part in smalls for x in part] + [low], [VM] * (2 * len(sums) + 6 * parts + 1), 45, (), cid,
        name="tail",
        out_specs=[VM] * (len(sums) + 7),
        out_shape=outs + [S((4 * quarter, d), BF16), S((parts, CONV + 1, inner), F32), S((parts, CONV + 1, 2 * LANE), F32), S((parts, inner), F32), S((parts, inner), F32),
                          S((parts, 2 * LANE), F32), S((parts, d), F32)],
        scratch_shapes=[pltpu.VMEM((parts, 16, inner), F32), pltpu.VMEM((n, parts, 16, inner), F32), pltpu.VMEM((heads, parts, 8, inner), F32),
                        pltpu.SemaphoreType.DMA((heads + n,)), pltpu.SemaphoreType.DMA((heads + n,))] + scratch
        + [pltpu.SemaphoreType.DMA((3,)), pltpu.SemaphoreType.DMA((3,))],
    )


def wgrad(lhs, rhs, bit, after=()):
    blocks = lax.axis_size("seq")
    tokens = rhs[0].shape[0]
    d = lhs.shape[1]
    width = sum(r.shape[1] for r in rhs)
    shape = (blocks // 2, d // blocks, width)
    return kcall(
        partial(wgrad_body, blocks, bit, lhs.shape[0] - tokens, len(rhs)), [lhs] + list(rhs), [VM] * (1 + len(rhs)), 3, after,
        name="wgrad",
        out_specs=[VM] * 2,
        out_shape=[S(shape, BF16)] * 2,
        scratch_shapes=[pltpu.VMEM((d, tokens), BF16)],
    )


class Halving:
    def __init__(self, order):
        bits = bits_of("seq")
        self.order = [bits[i % len(bits)] for i in order] + [b for i, b in enumerate(bits) if i not in order]
        self.left = [b for b in reversed(bits) if b != self.order[0]]
        self.step = 0
        self.got = self.away = self.keep = None

    def plan(self):
        bit = self.order[self.step]
        stride = 1 << (len(self.left) - 1 - self.left.index(bit))
        self.left.remove(bit)
        return bit, stride

    def go(self):
        self.got = swap(self.away, "seq", self.order[self.step])
        self.step += 1

    def rest(self):
        return self.got, self.keep, tuple(self.left), tuple(self.order[self.step :])

    def fold(self):
        bit, stride = self.plan()
        me = my_bit("seq", bit)
        blocks, block, width = self.keep.shape
        view = lambda v: v.reshape(blocks // (2 * stride), 2, stride, block, width)
        keep, got = view(self.keep), view(self.got)
        pick = lambda v, i: take(v, 1, i).astype(F32)
        both = [(pick(keep, i) + pick(got, i)).astype(BF16).reshape(blocks // 2, block, width) for i in (1 - me, me)]
        self.away, self.keep = both


def pad_lanes(x, to=LANE):
    return jnp.pad(x, [(0, 0)] * (x.ndim - 1) + [(0, to - x.shape[-1])])


def forward_layer(nx, h_own, extra, q, aux, segrow, layer):
    heads, size, inner = q["heads"], q["size"], q["inner"]
    (ux, ubc, krs, pdt, steps, cum, cT, mixed, entry, state, dec, decl) = fwd_mix(layer, size, nx, q, aux)
    ypart, enter, gate, gram = fwd_inside(layer, heads, size, nx, mixed, steps, cum, cT, krs, aux, segrow, q, state, dec, layer)
    y, carr, gated, sq = fwd_gate(ypart, entry, gate, krs, enter)
    width = inner * lax.axis_size("head")
    nx_next, h_new, branch, r2b, side = head_fwd(layer, gated, sq, q, h_own, extra, layer == LAYERS - 1, width, LAYERS + layer)
    stored = dict(nx=nx, gate=gate, ux=ux, ubc=ubc, krs=krs, pdt=pdt, steps=steps, cum=cum, cT=cT, gram=gram, mixed=mixed,
                  entry=entry, dec=dec, decl=decl, enter=enter, y=y, carr=carr, r2b=r2b, branch=branch, h_own=h_own)
    return nx_next, h_new, side, stored


def backward_gate(gb, side, s, q, layer):
    width = q["inner"] * lax.axis_size("head")
    return bwd_gate(layer, gb, q, s["gate"], s["y"], s["mixed"], s["entry"], s["krs"], s["r2b"], side, width)


def local(hidden_in, seg, cot, norm_gain, w_zx, w_bc, w_dt, conv_x, conv_bc, dt_bias, a_log, skip_d, gate_gain, w_out):
    tokens = hidden_in.shape[0]
    inner = w_zx.shape[3]
    heads = w_dt.shape[2]
    size = inner // heads
    rank = lax.axis_index("head")
    segf = seg.astype(F32)
    ext = jnp.concatenate([jnp.full((HALO,), segf[0], F32), segf], 0)
    vecs = [(ext[HALO - j : HALO - j + tokens] == segf).astype(F32) for j in range(1, CONV)]
    vecs += [(segf == segf[0]).astype(F32), (segf == segf[-1]).astype(F32), segf]
    aux = jnp.broadcast_to(jnp.stack(vecs, 0)[:, :, None], (len(vecs), tokens, LANE))
    segrow = segf[None]
    lanes = jnp.arange(LANE)
    even = rank % 2 == 0
    own = jnp.where(even, lanes, LANE - 1 - lanes) < LANE // 2
    dt_pad = pad_lanes(w_dt)
    tile = lax.dynamic_slice_in_dim(w_bc, (rank // 2) * LANE, LANE, 2)
    w_small = jnp.where(own[None, None], tile, jnp.where(even, jnp.roll(dt_pad, LANE // 2, axis=2), dt_pad))
    q = dict(heads=heads, size=size, inner=inner, gain=norm_gain[:, None, :], w_zx=jnp.transpose(w_zx, (0, 2, 1, 3)), w_bc=w_bc, w_dt=dt_pad,
             w_small=w_small, conv_x=conv_x, conv_bc=conv_bc, dt_bias=pad_lanes(dt_bias[:, None, :]), a_log=pad_lanes(a_log[:, None, :]),
             skip=jnp.repeat(skip_d, size, axis=1)[:, None, :], gate_gain=gate_gain[:, None, :], w_out=w_out)
    h = hidden_in.astype(F32)
    h_own = own_rows(hidden_in).astype(F32)
    cot_own = own_rows(cot)
    normed = (h * lax.rsqrt(jnp.mean(h * h, axis=1, keepdims=True) + EPS) * norm_gain[0][None]).astype(BF16)
    nx = jnp.concatenate([shift(normed[tokens - HALO :], "seq", 1), normed], 0)
    stored = []
    for l in range(LAYERS):
        extra = cot_own if l == LAYERS - 1 else q["gain"]
        nx, h_own, side, s = forward_layer(nx, h_own, extra, q, aux, segrow, l)
        stored.append(s)
    hidden_out = nx
    gb = cot
    g_own = cot_own.astype(F32)
    smalls = [None] * LAYERS
    sums = [None] * LAYERS
    pending = []
    for l in reversed(range(LAYERS)):
        s = stored[l]
        gy, gz, scaled, qloc, ggate, gskip = backward_gate(gb, side, s, q, l)
        if pending:
            pending[2].fold()
            pending[2].go()
        (dvd, dd, rowT, dkr, later), out, z = bwd_local(
            heads, size, gy, s["mixed"], s["krs"], s["cum"], s["steps"], s["cT"], s["gram"], s["entry"], s["enter"], aux, segrow, qloc,
            s["dec"], 2 * LAYERS + l, gb, scaled, s["nx"], gz, pending[:2], ())
        if pending:
            pending[2].keep, _ = lax.optimization_barrier((pending[2].keep, later))
            pending[2].fold()
            pending[2].go()
        for p in pending[:2]:
            p.go()
        out.go()
        z.go()
        gm8, gu, gtail, gtaps_x, gdt, gvec, dkr = bwd_carry(
            l, size, gy, dvd, s["mixed"], s["carr"], s["entry"], s["krs"], s["cum"], s["steps"], s["pdt"], q, s["ux"], aux, later, s["enter"],
            dd, rowT, dkr, s["decl"], [p.away for p in pending[2:]])
        small, gtaps_bc, gtail = maps_bwd(l, dkr, s["ubc"], q, aux, gdt, gtail, gm8, 3 * LAYERS + l)
        gu = lax.dynamic_update_slice(gu, gtail, (tokens - 16, 0))
        x = Halving((0, 1, 2))
        x.away, x.keep = wgrad(s["nx"], [gu, small], x.order[0])
        x.go()
        out.fold()
        z.fold()
        z.go()
        out.go()
        before = stored[max(l - 1, 0)]["branch"]
        gb, g_own, g_gain, side = head_bwd(l, gz, gu, small, q, s["h_own"], g_own, before, 4 * LAYERS + l, after=[p.away for p in [x, out, z]])
        smalls[l] = (gtaps_x, ggate, gskip, gvec, gtaps_bc, g_gain)
        pending = [out, z, x]
        sums[l] = pending
    under_way = [p for l in range(LAYERS) for p in reversed(sums[l])]
    done = tail([p.rest() for p in under_way], smalls, gb, inner, 5 * LAYERS)
    for p, total in zip(under_way, done):
        p.total = total
    grad_in, g_conv_x, g_conv_bc, g_gate, g_skip, g_vec, g_gain = done[len(under_way) :]
    grad_in = grad_in.astype(F32)
    g_w_zx = jnp.stack([jnp.stack([z.total, x.total[:, :inner]], 1) for _, z, x in sums], 0)
    g_small = jnp.stack([x.total[:, inner:] for _, _, x in sums], 0)
    g_w_bc = jnp.where(even, g_small[:, :, : LANE // 2], g_small[:, :, LANE // 2 :])
    g_w_dt = jnp.where(even, g_small[:, :, LANE // 2 : LANE // 2 + heads], g_small[:, :, :heads])
    g_w_out = jnp.stack([jnp.transpose(out.total) for out, _, _ in sums], 0)
    g_skip = jnp.sum(g_skip.reshape(LAYERS, heads, size), axis=2)
    part = g_gain.shape[1] // lax.axis_size("seq")
    g_gain = lax.dynamic_slice_in_dim(g_gain, lax.axis_index("seq") * part, part, 1)
    return (hidden_out, grad_in, g_gain, g_w_zx, g_w_bc, g_w_dt, g_conv_x, g_conv_bc,
            g_vec[:, :heads], g_vec[:, LANE : LANE + heads], g_skip, g_gate, g_w_out)


def solution(mesh):
    placed = (
        P("seq", None), P("seq"), P("seq", None), P(), P(None, None, None, "head"), P(), P(None, None, "head"),
        P(None, None, "head"), P(), P(None, "head"), P(None, "head"), P(None, "head"), P(None, "head"), P(None, "head", None),
    )
    return jax.shard_map(
        local,
        mesh=mesh,
        in_specs=placed,
        out_specs=(
            P("seq", None), P("seq", None), P(None, "seq"), P(None, "seq", None, "head"), P(None, "seq", "head"),
            P(None, "seq", "head"), P(None, None, "head"), P(), P(None, "head"), P(None, "head"), P(None, "head"),
            P(None, "head"), P(None, "head", "seq"),
        ),
        check_vma=False,
    )
```

```python
from functools import partial

import jax
import jax.numpy as jnp
from jax import lax
from jax.experimental import pallas as pl
from jax.experimental.pallas import tpu as pltpu
from jax.sharding import PartitionSpec as P

CONV = 4
LAYERS = 2
OUT_ORDER = (0, 1, 2)
Z_ORDER = (1, 2, 0)
EPS = 1e-05
F32 = jnp.float32
BF16 = jnp.bfloat16


def dot(a, b, dims):
    return lax.dot_general(a.astype(BF16), b.astype(BF16), (dims, ((), ())), preferred_element_type=F32)


def mm(a, b):
    return dot(a, b, ((1,), (0,)))


def mm_nt(a, b):
    return dot(a, b, ((1,), (1,)))


def mm_tn(a, b):
    return dot(a, b, ((0,), (0,)))


def swap(x, axis, bit):
    n = lax.axis_size(axis)
    return lax.ppermute(x, axis, [(i, i ^ bit) for i in range(n)])


def shift(x, axis, by):
    n = lax.axis_size(axis)
    return lax.ppermute(x, axis, [(i, i + by) for i in range(n) if 0 <= i + by < n])


def bits_of(axis):
    n = lax.axis_size(axis)
    bits = []
    b = 1
    while b < n:
        bits.append(b)
        b *= 2
    return bits


def my_bit(axis, bit):
    return (lax.axis_index(axis) // bit) % 2


def take(x, dim, index):
    return lax.dynamic_index_in_dim(x, index, dim, keepdims=False)


def head_scatter(x):
    for bit in bits_of("head"):
        me = my_bit("head", bit)
        halves = x.reshape((2, x.shape[0] // 2) + x.shape[1:])
        got = swap(take(halves, 0, 1 - me).astype(BF16), "head", bit)
        x = take(halves, 0, me).astype(F32) + got.astype(F32)
    return x


def head_scatter_exact(x):
    for bit in bits_of("head"):
        me = my_bit("head", bit)
        halves = x.reshape((2, x.shape[0] // 2) + x.shape[1:])
        x = take(halves, 0, me) + swap(take(halves, 0, 1 - me), "head", bit)
    return x


def head_gather(x):
    for bit in reversed(bits_of("head")):
        me = my_bit("head", bit)
        got = swap(x, "head", bit)
        x = jnp.where(me == 0, jnp.concatenate([x, got], 0), jnp.concatenate([got, x], 0))
    return x


def own_rows(x):
    rank = lax.axis_index("head")
    quarter = x.shape[0] // 4
    return lax.dynamic_slice_in_dim(x, ((rank % 2) * 2 + rank // 2) * quarter, quarter, 0)


def carry_scan(state, decay, reverse):
    total, total_d = state, decay
    entering = jnp.zeros_like(state)
    enter_d = jnp.ones_like(decay)
    for bit in bits_of("seq"):
        me = my_bit("seq", bit)
        other = swap(total.astype(BF16), "seq", bit).astype(F32)
        other_d = swap(total_d, "seq", bit)
        second = (me == 0) if reverse else (me == 1)
        entering = jnp.where(second, entering + enter_d[:, None, None] * other, entering)
        enter_d = jnp.where(second, enter_d * other_d, enter_d)
        total = jnp.where(
            second, total_d[:, None, None] * other + total, other_d[:, None, None] * total + other
        )
        total_d = total_d * other_d
    return entering


def silu_slope(v):
    s = jax.nn.sigmoid(v)
    return s * (1.0 + v * (1.0 - s))


def scatter_rows(x):
    bits = bits_of("seq")
    k = len(bits)
    n = lax.axis_size("seq")
    x = x.reshape((2,) * k + (x.shape[0] // n, x.shape[1]))
    for b in range(k):
        axis = k - 1 - b
        me = my_bit("seq", bits[b])
        got = swap(take(x, axis, 1 - me).astype(BF16), "seq", bits[b])
        x = take(x, axis, me).astype(F32) + got.astype(F32)
    return x


HALO = 16
LANE = 128
NT = ((1,), (1,))
NN = ((1,), (0,))
TN = ((0,), (0,))


def bdot(a, b, dims):
    return lax.dot_general(a.astype(BF16), b.astype(BF16), (dims, ((), ())), preferred_element_type=F32)


def halves(x):
    high = x.astype(BF16)
    return high, (x - high.astype(F32)).astype(BF16)


def dot3(a, b, dims):
    ah, al = halves(a)
    bh, bl = halves(b)
    return bdot(ah, bh, dims) + (bdot(ah, bl, dims) + bdot(al, bh, dims))


def hdot(a, b, dims):
    return lax.dot_general(a, b, (dims, ((), ())), precision=lax.Precision.HIGHEST, preferred_element_type=F32)


def sig(v):
    return 0.5 * jnp.tanh(0.5 * v) + 0.5


def softplus(v):
    e = jnp.exp(-jnp.abs(v))
    s = e / (2.0 + e)
    q = s * s
    series = 1.0 / 13.0
    for k in (11, 9, 7, 5, 3, 1):
        series = series * q + 1.0 / k
    return jnp.maximum(v, 0.0) + 2.0 * s * series


def mix_taps(us, taps, aux, width):
    tokens = aux.shape[1]
    wide = lambda m: m if width == LANE else jnp.concatenate([m] * (width // LANE), axis=1)
    acc = us[pl.ds(HALO, tokens), :] * taps[0:1, :] + taps[CONV : CONV + 1, :]
    for j in range(1, CONV):
        acc = acc + us[pl.ds(HALO - j, tokens), :] * wide(aux[j - 1]) * taps[j : j + 1, :]
    return acc


def pick_lane(values, h, lanes):
    return jnp.sum(jnp.where(lanes == h, values, 0.0), axis=1, keepdims=True)


def fwd_mix_body(size, nx, wx, wbc, wdt, tapx, tapbc, dtb, lograte, aux,
                 ux, ubc, krs, pdt, steps_o, cum_o, cT, mixed_o, entry_o, state, dec, decl,
                 us, usbc):
    p = pl.program_id(0)
    tokens = aux.shape[1]
    states = wbc.shape[1] // 2
    lanes = lax.broadcasted_iota(jnp.int32, (tokens, LANE), 1)
    half = lanes < size

    @pl.when(p == 0)
    def _():
        bc = bdot(nx[...], wbc[...], NN).astype(BF16)
        ubc[...] = bc
        usbc[...] = bc.astype(F32)
        m = mix_taps(usbc, tapbc, aux, 2 * states)
        act = m * sig(m)
        krs[...] = act
        ii = lax.broadcasted_iota(jnp.int32, (tokens, tokens), 0)
        jj = lax.broadcasted_iota(jnp.int32, (tokens, tokens), 1)
        pd = bdot(nx[pl.ds(HALO, tokens), :], wdt[...], NN).astype(BF16)
        pdt[...] = pd
        st = softplus(pd.astype(F32) + dtb[...])
        steps_o[...] = st
        log = st * -jnp.exp(lograte[...])
        cum = hdot(jnp.where(ii >= jj, 1.0, 0.0), log, NN)
        cum_o[...] = cum
        cT[...] = cum.T
        keeps = aux[3, tokens - 1 : tokens, :]
        decl[...] = jnp.broadcast_to(jnp.exp(cum[tokens - 1 : tokens, :]) * keeps, (8, LANE))
        dec[...] = jnp.exp(jnp.broadcast_to(cT[0:16, tokens - 1 : tokens], (16, LANE))) * keeps

    u = bdot(nx[...], wx[...], NN).astype(BF16)
    ux[...] = u
    us[...] = u.astype(F32)
    m = mix_taps(us, tapx, aux, LANE)
    mixed_o[...] = m
    v = m * sig(m)
    cum = cum_o[...]
    st = steps_o[...]
    h0 = p * (LANE // size)
    dd = jnp.where(half, pick_lane(st, h0, lanes), pick_lane(st, h0 + 1, lanes))
    vd = v * dd
    ct = jnp.where(half, pick_lane(cum, h0, lanes), pick_lane(cum, h0 + 1, lanes))
    entry_o[...] = jnp.exp(ct) * aux[3]
    tail = jnp.exp(ct[tokens - 1 : tokens, :] - ct) * aux[4]
    state[...] = dot3(vd * tail, krs[:, :states], TN)


def fwd_inside_body(stages_of, size, nx, wz, mixed, steps, cum, cT, krs, segc, segrow, skip, state, dec, ypart, enter, gate, gram, cb, *rest):
    p = pl.program_id(0)
    tokens = mixed.shape[0]
    stages = stages_of(state, dec, enter, *rest)
    for k, stage in enumerate(stages[:-1]):
        pl.when(p == k)(stage)
    gate[...] = bdot(nx[pl.ds(HALO, tokens), :], wz[...], NN).astype(BF16)
    states = krs.shape[1] // 2

    @pl.when(p == 0)
    def _():
        ii = lax.broadcasted_iota(jnp.int32, (tokens, tokens), 0)
        jj = lax.broadcasted_iota(jnp.int32, (tokens, tokens), 1)
        segs = jnp.concatenate([segc[...]] * (tokens // LANE), axis=1)
        gram[...] = jnp.where((ii >= jj) & (segs == segrow[...]), dot3(krs[:, states:], krs[:, :states], NT), 0.0)

    lanes = lax.broadcasted_iota(jnp.int32, (tokens, LANE), 1)
    half = lanes < size
    h0 = p * (LANE // size)
    m = mixed[...]
    v = m * sig(m)
    st = steps[...]
    vh, vl = halves(v * jnp.where(half, pick_lane(st, h0, lanes), pick_lane(st, h0 + 1, lanes)))
    vhl = jnp.concatenate([vh, vl], axis=1)
    ys = []
    for k in range(LANE // size):
        h = h0 + k
        cb[k] = jnp.broadcast_to(pick_lane(cum[...], h, lanes), (tokens, LANE))
        row = cT[pl.ds(h, 1), :]
        parts = []
        for ib in range(tokens // LANE):
            tiles, lows = [], []
            ci = cb[k, pl.ds(ib * LANE, LANE), :]
            for jb in range(ib + 1):
                spread = ci - row[:, jb * LANE : (jb + 1) * LANE]
                if jb == ib:
                    spread = jnp.minimum(spread, 0.0)
                wh, wl = halves(jnp.exp(spread) * gram[pl.ds(ib * LANE, LANE), pl.ds(jb * LANE, LANE)])
                tiles.append(wh)
                lows.append(wl)
            joined = lambda t: t[0] if ib == 0 else jnp.concatenate(t, axis=1)
            both = bdot(joined(tiles), vhl[: (ib + 1) * LANE], NN)
            parts.append(both[:, :LANE] + (both[:, LANE:] + bdot(joined(lows), vh[: (ib + 1) * LANE], NN)))
        ys.append(jnp.concatenate(parts, axis=0))
    ypart[...] = jnp.where(half, ys[0], ys[1]) + skip[...] * v
    pl.when(p == pl.num_programs(0) - 1)(stages[-1])


def full(shape):
    n = len(shape)
    return pl.BlockSpec(shape, lambda p: (0,) * n)


WIDE = 2 * LANE


def cols(rows, width=LANE):
    return pl.BlockSpec((rows, width), lambda p: (0, p))


def rowsb(width, rows=LANE):
    return pl.BlockSpec((rows, width), lambda p: (p, 0))


def fwd_gate_body(ypart, entry, gate, krs, enter, y, carr, gated, sq, sqacc):
    p = pl.program_id(0)
    states = krs.shape[1] // 2
    c = dot3(krs[:, states:], enter[...], NT) * entry[...]
    carr[...] = c
    yy = ypart[...] + c
    y[...] = yy
    z = gate[...].astype(F32)
    g = yy * (z * sig(z))
    gated[...] = g
    gg = g[:, :LANE] * g[:, :LANE] + g[:, LANE:] * g[:, LANE:]

    @pl.when(p == 0)
    def _():
        sqacc[...] = gg

    @pl.when(p > 0)
    def _():
        sqacc[...] += gg

    @pl.when(p == pl.num_programs(0) - 1)
    def _():
        sq[...] = jnp.broadcast_to(jnp.sum(jnp.transpose(sqacc[...]), axis=0, keepdims=True), sq.shape)


def bwd_gate_body(width, gb, wout, gate, y, mixed, entry, krs, r2b, side, gain, gy_o, gz_o, scaled_o, qloc, ggate, gskip, krb):
    @pl.when(pl.program_id(0) == 0)
    def _():
        quarter = r2b.shape[0] // 4
        for k in range(4):
            here = pl.ds(k * quarter, quarter)
            r = r2b[here, :]
            krb[here, :] = jnp.transpose(jnp.broadcast_to(side[8 * k : 8 * k + 1, :], (quarter, LANE))) * (r * r * (1.0 / width))

    states = krs.shape[1] // 2
    gs = bdot(gb[...], wout[...], NT)
    z = gate[...].astype(F32)
    s = sig(z)
    sil = z * s
    yy = y[...]
    gated = yy * sil
    twice = lambda v: jnp.concatenate([v, v], axis=1)
    r2 = twice(r2b[...])
    gr = gated * r2
    ggate[...] = jnp.sum(gs * gr, axis=0, keepdims=True)
    scaled_o[...] = (gr * gain[...]).astype(BF16)
    gg = r2 * gain[...] * gs - gated * twice(krb[...])
    gy = gg * sil
    gy_o[...] = gy
    gz_o[...] = (gg * yy * (s * (1.0 + z * (1.0 - s)))).astype(BF16)
    m = mixed[...]
    gskip[...] = jnp.sum(gy * (m * sig(m)), axis=0, keepdims=True)
    qloc[...] = bdot(gy * entry[...], krs[:, states:], TN)


def wgrad_into(blocks, bit, off, lhs, rhs, away, keep, lt):
    tokens = rhs[0].shape[0]
    mine = (lax.axis_index("seq") // bit) % 2
    block = lt.shape[0] // blocks
    half = blocks // 2
    turned = jnp.transpose(lhs[pl.ds(off, tokens), :])
    for at in range(blocks):
        first = (at // bit) % 2 != mine
        k = at // (2 * bit) * bit + at % bit
        place = jnp.where(first, k, half + k) * block
        lt[pl.ds(pl.multiple_of(place, 16), block), :] = turned[at * block : (at + 1) * block]
    for dst, base in ((away, 0), (keep, half * block)):
        c = 0
        for r in rhs:
            w = r.shape[1]
            out = bdot(lt[pl.ds(base, half * block), :], r[...], NN).astype(BF16)
            dst[:, :, c : c + w] = out.reshape(half, block, w)
            c += w


def wgrad_body(blocks, bit, off, n_rhs, lhs, *refs):
    wgrad_into(blocks, bit, off, lhs, refs[:n_rhs], *refs[n_rhs:])


def halve(dst, got, keep, stride, want):
    for k in range(dst.shape[0]):
        at = (k // stride) * 2 * stride + want * stride + k % stride
        dst[k] = (keep[at].astype(F32) + got[at].astype(F32)).astype(dst.dtype)


def fold_body(bit, stride, got, keep, away, kept):
    me = (lax.axis_index("seq") // bit) % 2
    halve(away, got, keep, stride, 1 - me)
    halve(kept, got, keep, stride, me)


def bwd_local_body(stages_of, size, blocks, bits, folds, gy_r, mixed, krs, cum, steps, cT, gram, entry, enter, segc, segrow, qloc, dec, *refs):
    p = pl.program_id(0)
    n = len(folds)
    gb, scaled, nx, gz = refs[:4]
    pairs, refs = refs[4 : 4 + 2 * n], refs[4 + 2 * n :]
    dvd, dd_o, rowT, dkr, later, out_away, out_keep, z_away, z_keep = refs[:9]
    halved, refs = refs[9 : 9 + 2 * n], refs[9 + 2 * n :]
    cb, db, gramT, dgT, vb, gk, lt = refs[:7]
    stages = stages_of(qloc, dec, later, *refs[7:])
    for k, stage in enumerate(stages[:-1]):
        pl.when(p == k)(stage)
    tokens = gy_r.shape[0]

    def beside(k, fn):
        pl.when(p == k)(fn)

    beside(1, lambda: wgrad_into(blocks, bits[0], gb.shape[0] - tokens, gb, [scaled], out_away, out_keep, lt))
    beside(2, lambda: wgrad_into(blocks, bits[1], nx.shape[0] - tokens, nx, [gz], z_away, z_keep, lt))
    for i, (bit, stride) in enumerate(folds):
        beside((0, 3, 4)[i], partial(fold_body, bit, stride, *pairs[2 * i : 2 * i + 2], *halved[2 * i : 2 * i + 2]))
    states = krs.shape[1] // 2
    lanes = lax.broadcasted_iota(jnp.int32, (tokens, LANE), 1)
    half = lanes < size

    @pl.when(p == 0)
    def _():
        gramT[...] = gram[...].T
        dgT[...] = jnp.zeros_like(dgT)
        dd_o[...] = jnp.zeros_like(dd_o)
        rowT[...] = jnp.zeros_like(rowT)
        dkr[...] = jnp.zeros_like(dkr)

    m = mixed[...]
    vb[...] = (m * sig(m)).astype(BF16)
    gy = gy_r[...]
    gyb = gy.astype(BF16)
    h0 = p * (LANE // size)
    outs = []
    for k in range(LANE // size):
        h = h0 + k
        gk[...] = jnp.where(half if k == 0 else jnp.logical_not(half), gy, 0.0).astype(BF16)
        cb[...] = jnp.broadcast_to(pick_lane(cum[...], h, lanes), (tokens, LANE))
        db[...] = jnp.broadcast_to(pick_lane(steps[...], h, lanes), (tokens, LANE))
        row = cT[pl.ds(h, 1), :]
        parts = []
        dds = []
        rows_acc = [jnp.zeros((8, LANE), F32) for _ in range(tokens // LANE)]
        for jb in range(tokens // LANE):
            js = pl.ds(jb * LANE, LANE)
            cj = cb[js, :]
            dj = db[js, :]
            pt = bdot(vb[js, :], gk[pl.ds(jb * LANE, tokens - jb * LANE), :], NT)
            ws = []
            dsum = None
            for ib in range(jb, tokens // LANE):
                sl = pl.ds(ib * LANE, LANE)
                spread = row[:, ib * LANE : (ib + 1) * LANE] - cj
                if jb == ib:
                    spread = jnp.minimum(spread, 0.0)
                e = jnp.exp(spread)
                w = e * gramT[js, sl]
                ws.append(w.astype(BF16))
                pp = pt[:, (ib - jb) * LANE : (ib - jb + 1) * LANE]
                wp = w * pp
                dgT[js, sl] += e * (pp * dj)
                x = wp * dj
                rows_acc[ib] = rows_acc[ib] + jnp.sum(x.reshape(LANE // 8, 8, LANE), axis=0)
                dsum = wp if dsum is None else dsum + wp
            dds.append(jnp.sum(dsum, axis=1, keepdims=True))
            w = ws[0] if len(ws) == 1 else jnp.concatenate(ws, axis=1)
            parts.append(bdot(w, gyb[jb * LANE :], NN))
        outs.append(jnp.concatenate(parts, axis=0))
        dd_o[...] += jnp.where(lanes == h, jnp.concatenate(dds, axis=0), 0.0)
        rowT[pl.ds(h, 1), :] = jnp.concatenate([jnp.sum(r, axis=0, keepdims=True) for r in rows_acc], axis=1)
    dvd[...] = jnp.where(half, outs[0], outs[1])
    dkr[:, states:] += bdot(gy * entry[...], enter[...], NN)

    @pl.when(p == pl.num_programs(0) - 1)
    def _():
        jj = lax.broadcasted_iota(jnp.int32, (tokens, tokens), 0)
        ii = lax.broadcasted_iota(jnp.int32, (tokens, tokens), 1)
        segs = jnp.concatenate([segc[...]] * (tokens // LANE), axis=1)
        g = jnp.where((ii >= jj) & (segs == segrow[...]), dgT[...], 0.0)
        dkr[:, :states] += bdot(g, krs[:, states:], NN)
        dkr[:, states:] += bdot(g, krs[:, :states], TN)
        stages[-1]()


def bwd_carry_body(size, gy_r, dvd_r, mixed, carr, entry, krs, cum, steps, pdt, dtb, lograte, skip, ux, tapx, aux, later, enter,
                   dd_r, rowT, dkr_r, decay,
                   gm_o, gu_o, gtail_o, gtaps, gdt_o, gvec, dkr, us, ms, ddacc, dcum, last):
    p = pl.program_id(0)
    tokens = gy_r.shape[0]
    states = krs.shape[1] // 2
    lanes = lax.broadcasted_iota(jnp.int32, (tokens, LANE), 1)
    lane1 = lax.broadcasted_iota(jnp.int32, (1, LANE), 1)
    half = lanes < size

    @pl.when(p == 0)
    def _():
        ddacc[...] = dd_r[...]
        dcum[...] = jnp.transpose(rowT[...]) - dd_r[...] * steps[...]
        last[...] = jnp.zeros_like(last)
        dkr[...] = dkr_r[...]

    h0 = p * (LANE // size)
    st = steps[...]
    cu = cum[...]
    cc = [pick_lane(cu, h0 + k, lanes) for k in range(2)]
    dcol = [pick_lane(st, h0 + k, lanes) for k in range(2)]
    ct = jnp.where(half, cc[0], cc[1])
    dpair = jnp.where(half, dcol[0], dcol[1])
    tail = jnp.exp(ct[tokens - 1 : tokens, :] - ct) * aux[4]
    m = mixed[...]
    s = sig(m)
    v = m * s
    gy = gy_r[...]
    qk = bdot(krs[:, :states], later[...], NT) * tail
    dvd = dvd_r[...] + qk
    dkr[:, :states] += bdot(v * dpair * tail, later[...], NN)
    tq = v * qk
    eq = gy * carr[...]
    qs = later[...] * enter[...]
    for k in range(2):
        h = h0 + k
        mine = half if k == 0 else jnp.logical_not(half)
        td = jnp.sum(jnp.where(mine, tq, 0.0), axis=1, keepdims=True)
        ec = jnp.sum(jnp.where(mine, eq, 0.0), axis=1, keepdims=True)
        tdd = td * dcol[k]
        ddacc[...] += jnp.where(lanes == h, td, 0.0)
        dcum[...] += jnp.where(lanes == h, ec - tdd, 0.0)
        dot_qs = jnp.sum(jnp.sum(qs[k * size : (k + 1) * size, :], axis=0, keepdims=True), axis=1, keepdims=True)
        last[...] += jnp.where(lane1 == h, jnp.sum(tdd, axis=0, keepdims=True) + dot_qs * decay[0:1, :], 0.0)
    dv = dvd * dpair + skip[...] * gy
    gm = dv * (s * (1.0 + m * (1.0 - s)))
    gm_o[...] = gm[:8]
    us[...] = ux[...].astype(F32)
    acc = gm * tapx[0:1, :]
    gtaps[0:1, :] = jnp.sum(gm * us[pl.ds(HALO, tokens), :], axis=0, keepdims=True)
    gtaps[CONV : CONV + 1, :] = jnp.sum(gm, axis=0, keepdims=True)
    ms[pl.ds(tokens, 8), :] = jnp.zeros((8, LANE), F32)
    for j in range(1, CONV):
        gmj = gm * aux[j - 1]
        gtaps[j : j + 1, :] = jnp.sum(gmj * us[pl.ds(HALO - j, tokens), :], axis=0, keepdims=True)
        ms[pl.ds(0, tokens), :] = gmj
        acc = acc + ms[pl.ds(j, tokens), :] * tapx[j : j + 1, :]
    gu_o[...] = acc.astype(BF16)
    gtail_o[...] = acc[tokens - 16 :]

    @pl.when(p == pl.num_programs(0) - 1)
    def _():
        ii = lax.broadcasted_iota(jnp.int32, (tokens, tokens), 0)
        jj = lax.broadcasted_iota(jnp.int32, (tokens, tokens), 1)
        dlog = hdot(jnp.where(jj >= ii, 1.0, 0.0), dcum[...], NN) + last[...]
        rates = -jnp.exp(lograte[...])
        dsteps = ddacc[...] + rates * dlog
        gdt = dsteps * sig(pdt[...].astype(F32) + dtb[...])
        gdt_o[...] = gdt.astype(BF16)
        gvec[0:1, :] = jnp.sum(gdt, axis=0, keepdims=True)
        gvec[1:2, :] = jnp.sum(st * dlog, axis=0, keepdims=True) * rates


MESH = pl.DeviceIdType.MESH
VMEM_LIMIT = 56 * 1024 * 1024
SUBS = 2


def greet(partners):
    barrier = pltpu.get_barrier_semaphore()
    for where in partners:
        pl.semaphore_signal(barrier, inc=1, device_id=where, device_id_type=MESH)
    pl.semaphore_wait(barrier, len(partners))


def send(src, dst, sems, where):
    copy = pltpu.make_async_remote_copy(
        src_ref=src, dst_ref=dst, send_sem=sems[0], recv_sem=sems[1], device_id=where, device_id_type=MESH)
    copy.start()
    return copy


def flip(me, bit):
    return me + bit * (1 - 2 * ((me // bit) % 2))


def carry_stages(bits, reverse, heads, size, st, dec, out, tx, rx, rxd, tot, zp, btx, brx, bdtx, bdrx, pd, ed, ptx, prx, ssem, rsem):
    me = lax.axis_index("seq")
    n = len(bits)
    hh = heads // 2
    rows = hh * size
    x = me % 2
    r = (1 - x) if reverse else x
    pair_at = {"seq": flip(me, bits[0])}
    wheres = [{"seq": flip(me, b)} for b in bits[1:]]
    kind = tx.dtype
    mine = pl.ds(pl.multiple_of(r * rows, rows), rows)
    theirs = pl.ds(pl.multiple_of((1 - r) * rows, rows), rows)

    def copy(k, src, dst, where):
        return pltpu.make_async_remote_copy(src_ref=src, dst_ref=dst, send_sem=ssem.at[k], recv_sem=rsem.at[k],
                                            device_id=where, device_id_type=MESH)

    one = [copy(0, tx, rx, pair_at), copy(1, dec, rxd, pair_at)]
    steps = [[copy(2 + 2 * i, btx, brx.at[i], w), copy(3 + 2 * i, bdtx, bdrx.at[i], w)] for i, w in enumerate(wheres)]
    last = [copy(2 * n, ptx, prx, pair_at)]

    def begin(copies):
        for c in copies:
            c.start()

    def end(copies):
        for c in copies:
            c.wait()

    def per_head(fn):
        for k in range(hh):
            fn(pl.ds(k * size, size), r * hh + k, pl.ds(pl.multiple_of(r * rows + k * size, size), size))

    def open_():
        greet([pair_at] + wheres)
        tx[...] = st[theirs, :].astype(kind)
        begin(one)

    def pair():
        end(one)
        pd[...] = dec[...] * rxd[...]
        ed[...] = jnp.ones_like(ed)
        zp[...] = jnp.zeros_like(zp)

        def add(rk, h, own):
            a, b = st[own, :], rx[rk, :].astype(F32)
            row = pl.ds(h, 1)
            tot[rk, :] = jnp.where(r == 0, rxd[row, :] * a + b, dec[row, :] * b + a)

        per_head(add)
        go(0)

    def go(i):
        btx[...] = tot[...].astype(kind)
        bdtx[...] = pd[...]
        begin(steps[i])

    def butterfly(i):
        end(steps[i])
        bit = (me // bits[1 + i]) % 2
        second = (1 - bit) if reverse else bit
        keep = second.astype(F32)

        def add(rk, h, own):
            other = brx[i, rk, :].astype(F32)
            row = pl.ds(h, 1)
            zp[rk, :] += other * (ed[row, :] * keep)
            if i + 1 < len(steps):
                a = jnp.where(second == 1, pd[row, :], 1.0)
                c = jnp.where(second == 1, 1.0, bdrx[i, row, :])
                tot[rk, :] = a * other + c * tot[rk, :]

        per_head(add)
        ed[...] = jnp.where(second == 1, ed[...] * bdrx[i], ed[...])
        pd[...] = pd[...] * bdrx[i]
        if i + 1 < len(steps):
            go(i + 1)
        else:
            hand()

    def hand():
        def add(rk, h, own):
            row = pl.ds(h, 1)
            z = zp[rk, :]
            after = jnp.where(r == 0, dec[row, :], rxd[row, :]) * z + jnp.where(r == 0, st[own, :], rx[rk, :].astype(F32))
            out[own, :] = jnp.where(r == 0, z, after)
            ptx[rk, :] = jnp.where(r == 0, after, z).astype(kind)

        per_head(add)
        begin(last)

    def close():
        end(last)
        out[theirs, :] = prx[...].astype(F32)

    return [open_, pair] + [partial(butterfly, i) for i in range(len(steps))] + [close]


def carry_scratch(n, rows, states, kind):
    part = pltpu.VMEM((rows // 2, states), kind)
    wide = pltpu.VMEM((rows // 2, states), F32)
    dec = pltpu.VMEM((16, states), F32)
    return [part, part, dec, wide, wide, part, pltpu.VMEM((n - 1, rows // 2, states), kind), dec, pltpu.VMEM((n - 1, 16, states), F32),
            dec, dec, part, part, pltpu.SemaphoreType.DMA((2 * n + 1,)), pltpu.SemaphoreType.DMA((2 * n + 1,))]


def head_core(tokens, part, middle, nx, off, side, tx0, rx0, tx1, rx1, acc, ssem, rsem, me, core_at, y_at, gather=True):
    quarter = tokens // 4
    sub = quarter // SUBS
    c = me % 2
    y = me // 2
    half = 2 * quarter
    other_y = pl.multiple_of((1 - y) * quarter, quarter)
    own_y = pl.multiple_of(y * quarter, quarter)
    n = 0
    sends = []

    def go(src, dst, where):
        nonlocal n
        copy = send(src, dst, (ssem.at[n], rsem.at[n]), where)
        sends.append(copy)
        n += 1
        return copy

    acc[...] = part(pl.multiple_of((1 - c) * half, half), half)
    first = []
    for i, base in enumerate((other_y, own_y)):
        for s in range(SUBS):
            tx0[i, s] = acc[pl.ds(pl.multiple_of(base + s * sub, sub), sub), :].astype(tx0.dtype)
            first.append(go(tx0.at[i, s], rx0.at[i, s], core_at))
    acc[...] = part(pl.multiple_of(c * half, half), half)
    second = []
    for s in range(SUBS):
        first[s].wait_recv()
        tx1[s] = (acc[pl.ds(pl.multiple_of(other_y + s * sub, sub), sub), :] + rx0[0, s].astype(F32)).astype(tx1.dtype)
        second.append(go(tx1.at[s], rx1.at[s], y_at))
    own = (c * 2 + y) * quarter
    theirs = (c * 2 + 1 - y) * quarter
    to_y, to_core, onward = [], [], []
    for s in range(SUBS):
        first[SUBS + s].wait_recv()
        second[s].wait_recv()
        total = acc[pl.ds(pl.multiple_of(own_y + s * sub, sub), sub), :] + rx0[1, s].astype(F32) + rx1[s].astype(F32)
        if not gather:
            nx[pl.ds(s * sub, sub), :] = middle(s, sub, total)
            continue
        rows = pl.ds(pl.multiple_of(off + own + s * sub, 16), sub)
        nx[rows, :] = middle(s, sub, total)
        to_y.append(go(nx.at[rows, :], nx.at[rows, :], y_at))
        to_core.append(go(nx.at[rows, :], nx.at[rows, :], core_at))
    if not gather:
        for copy in sends:
            copy.wait_send()
        return
    if side is not None:
        srows = pl.ds(pl.multiple_of((c * 2 + y) * 8, 8), 8)
        to_y.append(go(side.at[srows, :], side.at[srows, :], y_at))
        to_core.append(go(side.at[srows, :], side.at[srows, :], core_at))
    for s in range(SUBS):
        to_y[s].wait_recv()
        rows = pl.ds(pl.multiple_of(off + theirs + s * sub, 16), sub)
        onward.append(go(nx.at[rows, :], nx.at[rows, :], core_at))
    if side is not None:
        to_y[SUBS].wait_recv()
        srows = pl.ds(pl.multiple_of((c * 2 + 1 - y) * 8, 8), 8)
        onward.append(go(side.at[srows, :], side.at[srows, :], core_at))
    for copy in to_core + onward:
        copy.wait_recv()
    for copy in sends:
        copy.wait_send()


HEAD_COPIES = 3 * SUBS + 3 * SUBS + 3


def head_fwd_body(l, tokens, last, width, gated, sq, ggain_all, wout_all, h_own, extra,
                  nx, h_new, branch, r2b, side, sqrx, tx0, rx0, tx1, rx1, acc, krc, ssem, rsem, qs, qr, hs, hr, wout, wsem):
    load = pltpu.make_async_copy(wout_all.at[l], wout, wsem.at[0])
    load.start()
    ggain = ggain_all.at[l]
    extra = extra if last else extra.at[l + 1]
    me = lax.axis_index("head")
    at = lax.axis_index("seq")
    count = lax.axis_size("seq")
    peers = [lax.rem(me + k, 4) for k in (1, 2, 3)]
    barrier = pltpu.get_barrier_semaphore()
    for pr in peers:
        pl.semaphore_signal(barrier, inc=1, device_id={"head": pr}, device_id_type=MESH)
    if not last:
        @pl.when(at > 0)
        def _():
            pl.semaphore_signal(barrier, inc=1, device_id={"seq": at - 1}, device_id_type=MESH)
    if last:
        pl.semaphore_wait(barrier, 3)
    else:
        pl.semaphore_wait(barrier, 3 + (at < count - 1).astype(jnp.int32))
    copies = [send(sq, sqrx.at[2 - k], (qs.at[k], qr.at[2 - k]), {"head": pr}) for k, pr in enumerate(peers)]
    for copy in copies:
        copy.wait_send()
    for k in range(3):
        pltpu.make_async_remote_copy(src_ref=sq, dst_ref=sqrx.at[k], send_sem=qs.at[k], recv_sem=qr.at[k],
                                     device_id={"head": peers[2 - k]}, device_id_type=MESH).wait_recv()
    total_sq = ((sq[...] + sqrx[0]) + (sqrx[1] + sqrx[2]))[0:1, :]
    r2row = lax.rsqrt(total_sq / width + EPS)
    r2b[...] = jnp.transpose(jnp.broadcast_to(r2row, (LANE, tokens)))
    inner = gated.shape[1]

    def part(start, rows):
        where = pl.ds(start, rows)
        r2 = jnp.concatenate([r2b[where, :]] * (inner // LANE), axis=1)
        return bdot(gated[where, :] * r2 * ggain[...], wout[...], NN)

    d = wout.shape[1]

    def middle(s, sub, total):
        rows = pl.ds(s * sub, sub)
        branch[rows, :] = total
        h = h_own[rows, :] + total
        h_new[rows, :] = h
        if last:
            krc[rows, :] = jnp.broadcast_to(jnp.sum(extra[rows, :].astype(F32) * total, axis=1, keepdims=True), (sub, LANE))
            if s == SUBS - 1:
                mine = pl.ds(pl.multiple_of(((me % 2) * 2 + me // 2) * 8, 8), 8)
                side[mine, :] = jnp.transpose(krc[...])[0:8, :]
            return h.astype(BF16)
        r1 = lax.rsqrt(jnp.sum(h * h, axis=1, keepdims=True) / d + EPS)
        return (h * r1 * extra[...]).astype(BF16)

    off = 0 if last else HALO
    load.wait()
    if not last:
        side[...] = jnp.zeros_like(side)
    head_core(tokens, part, middle, nx, off, side if last else None, tx0, rx0, tx1, rx1, acc, ssem, rsem, me,
              {"head": flip(me, 1)}, {"head": flip(me, 2)})
    if not last:
        src = nx.at[pl.ds(tokens, HALO), :]
        dst = nx.at[pl.ds(0, HALO), :]
        copy = pltpu.make_async_remote_copy(src_ref=src, dst_ref=dst, send_sem=hs.at[0], recv_sem=hr.at[0],
                                            device_id={"seq": lax.rem(at + 1, count)}, device_id_type=MESH)

        @pl.when(at < count - 1)
        def _():
            copy.start()
            copy.wait_send()

        @pl.when(at > 0)
        def _():
            copy.wait_recv()

        @pl.when(at == 0)
        def _():
            nx[pl.ds(0, HALO), :] = jnp.zeros((HALO, d), BF16)


def head_scratch(tokens, d, kind=BF16):
    sub = tokens // 4 // SUBS
    return [pltpu.VMEM((2, SUBS, sub, d), kind), pltpu.VMEM((2, SUBS, sub, d), kind), pltpu.VMEM((SUBS, sub, d), kind),
            pltpu.VMEM((SUBS, sub, d), kind), pltpu.VMEM((tokens // 2, d), F32), pltpu.VMEM((tokens // 4, LANE), F32),
            pltpu.SemaphoreType.DMA((HEAD_COPIES,)), pltpu.SemaphoreType.DMA((HEAD_COPIES,))]


def head_bwd_body(l, gather, tokens, gz, gu, small, wzx_all, wsmall_all, h_own, gain_all, g_own, branch,
                  gb, g_new, ggain, side, tx0, rx0, tx1, rx1, acc, krc, ssem, rsem, wzx, wsem):
    load = pltpu.make_async_copy(wzx_all.at[l], wzx, wsem.at[0])
    load.start()
    wsmall = wsmall_all.at[l]
    gain = gain_all.at[l]
    me = lax.axis_index("head")
    core_at, y_at = {"head": flip(me, 1)}, {"head": flip(me, 2)}
    greet([core_at, y_at])
    d = gain.shape[1]

    def part(start, rows):
        where = pl.ds(start, rows)
        return bdot(gz[where, :], wzx[0], NT) + bdot(gu[where, :], wzx[1], NT) + bdot(small[where, :], wsmall[...], NT)

    def middle(s, sub, total):
        rows = pl.ds(s * sub, sub)
        h = h_own[rows, :]
        r1 = lax.rsqrt(jnp.sum(h * h, axis=1, keepdims=True) / d + EPS)
        th = total * h
        gg = jnp.sum(th * r1, axis=0, keepdims=True)
        if s == 0:
            ggain[...] = gg
        else:
            ggain[...] += gg
        k1 = jnp.sum(th * gain[...], axis=1, keepdims=True)
        g = g_own[rows, :] + r1 * (gain[...] * total) - h * (r1 * r1 * r1 * (k1 / d))
        g_new[rows, :] = g
        low = g.astype(BF16)
        krc[rows, :] = jnp.broadcast_to(jnp.sum(low.astype(F32) * branch[rows, :], axis=1, keepdims=True), (sub, LANE))
        if s == SUBS - 1:
            mine = pl.ds(pl.multiple_of(((me % 2) * 2 + me // 2) * 8, 8), 8)
            if not gather:
                side[...] = jnp.zeros_like(side)
            side[mine, :] = jnp.transpose(krc[...])[0:8, :]
        return low

    load.wait()
    head_core(tokens, part, middle, gb, 0, side, tx0, rx0, tx1, rx1, acc, ssem, rsem, me, core_at, y_at, gather)


def maps_bwd_body(l, tokens, dkr, ubc, taps_all, aux, gdt, gtail, gm8, tapx_all,
                  small, gtaps, gtail_o, ytx, yrx, yacc, ctx, crx, us, ms, nextx, nextb, gmb, sems, semr):
    taps, tapx = taps_all.at[l], tapx_all.at[l]
    me = lax.axis_index("head")
    at = lax.axis_index("seq")
    count = lax.axis_size("seq")
    c = me % 2
    y = me // 2
    core_at, y_at = {"head": flip(me, 1)}, {"head": flip(me, 2)}
    barrier = pltpu.get_barrier_semaphore()
    for where in (core_at, y_at):
        pl.semaphore_signal(barrier, inc=1, device_id=where, device_id_type=MESH)

    @pl.when(at < count - 1)
    def _():
        pl.semaphore_signal(barrier, inc=1, device_id={"seq": at + 1}, device_id_type=MESH)
    pl.semaphore_wait(barrier, 2 + (at > 0).astype(jnp.int32))
    lanes = lax.broadcasted_iota(jnp.int32, (tokens, LANE), 1)
    before = {"seq": lax.rem(at + count - 1, count)}
    ahead_x = pltpu.make_async_remote_copy(src_ref=gm8, dst_ref=nextx, send_sem=sems.at[2], recv_sem=semr.at[2],
                                           device_id=before, device_id_type=MESH)

    @pl.when(at > 0)
    def _():
        ahead_x.start()
    low, high = dkr[:, :LANE], dkr[:, LANE:]
    ytx[...] = jnp.where(y == 0, high, low).astype(BF16)
    one = send(ytx, yrx, (sems.at[0], semr.at[0]), y_at)
    tile = pl.ds(pl.multiple_of(y * LANE, LANE), LANE)
    us[...] = ubc[:, tile].astype(F32)
    tp = taps[:, tile]
    m = mix_taps(us, tp, aux, LANE)
    s = sig(m)
    slope = s * (1.0 + m * (1.0 - s))
    one.wait()
    ctx[...] = jnp.where(y == 0, low, high) + yrx[...].astype(F32)
    two = send(ctx, crx, (sems.at[1], semr.at[1]), core_at)
    two.wait()
    gm = (ctx[...] + crx[...]) * slope
    gmb[...] = gm[0:8]
    ahead_b = pltpu.make_async_remote_copy(src_ref=gmb, dst_ref=nextb, send_sem=sems.at[3], recv_sem=semr.at[3],
                                           device_id=before, device_id_type=MESH)

    @pl.when(at > 0)
    def _():
        ahead_b.start()

    @pl.when(at == count - 1)
    def _():
        nextx[...] = jnp.zeros_like(nextx)
        nextb[...] = jnp.zeros_like(nextb)
    gtaps[...] = jnp.zeros_like(gtaps)
    gtaps[0:1, :] = jnp.sum(gm * us[pl.ds(HALO, tokens), :], axis=0, keepdims=True)
    gtaps[CONV : CONV + 1, :] = jnp.sum(gm, axis=0, keepdims=True)
    for j in range(1, CONV):
        gtaps[j : j + 1, :] = jnp.sum(gm * aux[j - 1] * us[pl.ds(HALO - j, tokens), :], axis=0, keepdims=True)

    @pl.when(at < count - 1)
    def _():
        ahead_x.wait_recv()
        ahead_b.wait_recv()
    acc = gm * tp[0:1, :]
    for j in range(1, CONV):
        ms[pl.ds(0, tokens), :] = gm * aux[j - 1]
        ms[pl.ds(tokens, 8), :] = nextb[...]
        acc = acc + ms[pl.ds(j, tokens), :] * tp[j : j + 1, :]
    own = jnp.where(c == 0, lanes, LANE - 1 - lanes) < 64
    g = gdt[...].astype(F32)
    moved = jnp.concatenate([g[:, 64:], g[:, :64]], axis=1)
    small[...] = jnp.where(own, acc, jnp.where(c == 0, moved, g)).astype(BF16)
    gtail_o[...] = gtail[...].astype(BF16)
    nx = nextx[...]
    tail = gtail[...]
    rows = lax.broadcasted_iota(jnp.int32, tail.shape, 0)
    for j in range(1, CONV):
        for k in range(j):
            tail = tail + jnp.where(rows == 16 - j + k, nx[k : k + 1, :] * tapx[j : j + 1, :], 0.0)
    gtail_o[...] = tail.astype(BF16)

    @pl.when(at > 0)
    def _():
        ahead_x.wait_send()
        ahead_b.wait_send()


class Job:
    def __init__(self, got, keep, left, steps, out, bufs, sems):
        self.got, self.keep, self.left, self.steps, self.out = got, keep, list(left), list(steps), out
        self.bufs, (self.ssem, self.rsem) = bufs, sems
        self.copy = None

    def advance(self):
        got, keep = self.got, self.keep
        if self.copy is not None:
            self.copy.wait()
        if not self.steps:
            if self.out is not None:
                self.out[...] = keep[0].astype(F32) + got[0].astype(F32)
            return
        bit = self.steps.pop(0)
        away, kept, came = self.bufs.pop(0)
        stride = 1 << (len(self.left) - 1 - self.left.index(bit))
        self.left.remove(bit)
        me = (lax.axis_index("seq") // bit) % 2
        halve(away, got, keep, stride, 1 - me)
        halve(kept, got, keep, stride, me)
        where = {"seq": flip(lax.axis_index("seq"), bit)}
        k = len(self.steps)
        self.copy = send(away, came, (self.ssem.at[k], self.rsem.at[k]), where)
        self.got, self.keep = came, kept


def tail_body(parts, plan, *refs):
    jobs_n = len(plan)
    pairs = refs[: 2 * jobs_n]
    ins = refs[2 * jobs_n : 2 * jobs_n + 6 * parts]
    rest = refs[2 * jobs_n + 6 * parts :]
    low, rest = rest[0], rest[1:]
    outs, rest = rest[:jobs_n], rest[jobs_n:]
    grad, rest = rest[0], rest[1:]
    gsend, grecv, rest = rest[-2], rest[-1], rest[:-2]
    conv_x, conv_bc, ggate, gskip, gvec, ggain = rest[:6]
    stage, rx, hx, ssem, rsem = rest[6:11]
    rest = list(rest[11:])
    jobs = []
    for i, (left, steps) in enumerate(plan):
        bufs = []
        for _ in steps:
            bufs.append((rest.pop(0), rest.pop(0), rest.pop(0)))
        jobs.append(Job(pairs[2 * i], pairs[2 * i + 1], left, steps, outs[i], bufs, (rest.pop(0), rest.pop(0))))
    inner = stage.shape[2]
    me = lax.axis_index("head")
    steps = [("head", b) for b in bits_of("head")] + [("seq", b) for b in bits_of("seq")]
    wheres = [{axis: flip(lax.axis_index(axis), b)} for axis, b in steps]
    greet(wheres)
    jobs[0].advance()
    quarter = low.shape[0]
    spot = lambda c, y: pl.ds(pl.multiple_of((c * 2 + y) * quarter, quarter), quarter)
    c, y = me % 2, me // 2
    grad[spot(c, y), :] = low[...]
    core_at, y_at = wheres[0], wheres[1]
    here = grad.at[spot(c, y), :]
    there = grad.at[spot(c, 1 - y), :]
    over_y = send(here, here, (gsend.at[0], grecv.at[0]), y_at)
    over_core = send(here, here, (gsend.at[1], grecv.at[1]), core_at)
    for job in jobs[1:]:
        job.advance()
    stage[...] = jnp.zeros_like(stage)
    for l in range(parts):
        taps, gate, skip, vec, maps, gain = ins[6 * l : 6 * l + 6]
        stage[l, 0 : CONV + 1, :] = taps[0 : CONV + 1, :]
        stage[l, 5:6, :] = gate[...]
        stage[l, 6:7, :] = skip[...]
        stage[l, 7:8, 0:LANE] = vec[0:1, :]
        stage[l, 7:8, LANE : 2 * LANE] = vec[1:2, :]
        stage[l, 8:9, :] = gain[:, :inner]
        stage[l, 9:10, :] = gain[:, inner:]
        for r in range(CONV + 1):
            row = maps[r : r + 1, :] * 0.5
            here = [jnp.where(me // 2 == k, row, 0.0) for k in range(2)]
            stage[l, 10 + r // 3 : 11 + r // 3, (r % 3) * 2 * LANE : ((r % 3) * 2 + 2) * LANE] = jnp.concatenate(here, axis=1)
    where = pl.ds(8, 8)
    heads = len(bits_of("head"))
    longest = max(len(job.steps) for job in jobs)
    for i, (axis, b) in enumerate(steps):
        if axis == "head":
            copy = send(stage.at[:, where, :], hx.at[i], (ssem.at[i], rsem.at[i]), wheres[i])
            copy.wait()
            stage[:, 8:16, :] += hx[i]
        else:
            copy = send(stage, rx.at[i - heads], (ssem.at[i], rsem.at[i]), wheres[i])
            if i == heads:
                for job in jobs:
                    if len(job.steps) == longest:
                        job.advance()
            copy.wait()
            stage[...] += rx[i - heads]
    over_y.wait_recv()
    onward = send(there, there, (gsend.at[2], grecv.at[2]), core_at)
    for _ in range(longest + 1):
        for job in jobs:
            if job.copy is not None and (job.steps or job.out is not None):
                done = not job.steps
                job.advance()
                if done:
                    job.out = None
    over_core.wait_recv()
    onward.wait_recv()
    for copy in (over_y, over_core, onward):
        copy.wait_send()
    for l in range(parts):
        conv_x[l] = stage[l, 0 : CONV + 1, :]
        ggate[l : l + 1, :] = stage[l, 5:6, :]
        gskip[l : l + 1, :] = stage[l, 6:7, :]
        gvec[l : l + 1, :] = stage[l, 7:8, 0 : 2 * LANE]
        ggain[l : l + 1, :inner] = stage[l, 8:9, :]
        ggain[l : l + 1, inner:] = stage[l, 9:10, :]
        for r in range(CONV + 1):
            conv_bc[l, r : r + 1, :] = stage[l, 10 + r // 3 : 11 + r // 3, (r % 3) * 2 * LANE : ((r % 3) * 2 + 2) * LANE]


VM = pl.BlockSpec(memory_space=pltpu.VMEM)
S = jax.ShapeDtypeStruct


def of_layer(l, shape, steps=False):
    n = len(shape) - 1
    if steps:
        return pl.BlockSpec((None,) + shape[1:-1] + (LANE if steps is True else steps,), lambda p: (l,) + (0,) * (n - 1) + (p,))
    return pl.BlockSpec((None,) + shape[1:], lambda *p: (l,) + (0,) * n)


def projection(l, which, d):
    return pl.BlockSpec((None, None, d, LANE), lambda p: (l, which, 0, p))


def rows_of_layer(l, shape):
    return pl.BlockSpec((None, WIDE, shape[2]), lambda p: (l, p, 0))


def kcall(body, args, specs, us, after=(), cid=None, **kw):
    n, k = len(args), len(after)

    def wrapped(*refs):
        body(*refs[:n], *refs[n + k :])

    extra = {} if cid is None else dict(collective_id=cid, has_side_effects=True)
    return pl.pallas_call(
        wrapped,
        in_specs=list(specs) + [pl.BlockSpec(memory_space=pl.ANY)] * k,
        compiler_params=pltpu.CompilerParams(vmem_limit_bytes=VMEM_LIMIT, **extra),
        cost_estimate=pl.CostEstimate(flops=int(us * 1e9), bytes_accessed=int(us * 3e6), transcendentals=0),
        **kw,
    )(*args, *after)


def fwd_mix(l, size, nx, q, aux):
    tokens = aux.shape[1]
    ext, d = nx.shape
    inner = q["conv_x"].shape[2]
    two = q["w_bc"].shape[2]
    args = [nx, q["w_zx"], q["w_bc"], q["w_dt"], q["conv_x"], q["conv_bc"], q["dt_bias"], q["a_log"], aux]
    specs = [full(nx.shape), projection(l, 1, d), of_layer(l, q["w_bc"].shape), of_layer(l, q["w_dt"].shape),
             of_layer(l, q["conv_x"].shape, True), of_layer(l, q["conv_bc"].shape), of_layer(l, q["dt_bias"].shape),
             of_layer(l, q["a_log"].shape), full(aux.shape)]
    return kcall(
        partial(fwd_mix_body, size), args, specs, 12,
        name="fwd_mix",
        grid=(inner // LANE,),
        out_specs=[cols(ext), full((ext, two)), full((tokens, two)), full((tokens, LANE)), full((tokens, LANE)),
                   full((tokens, LANE)), full((LANE, tokens)), cols(tokens),
                   cols(tokens), rowsb(two // 2), full((16, LANE)), full((8, LANE))],
        out_shape=[S((ext, inner), BF16), S((ext, two), BF16), S((tokens, two), F32),
                   S((tokens, LANE), BF16), S((tokens, LANE), F32), S((tokens, LANE), F32), S((LANE, tokens), F32),
                   S((tokens, inner), F32), S((tokens, inner), F32),
                   S((inner, two // 2), F32), S((16, LANE), F32), S((8, LANE), F32)],
        scratch_shapes=[pltpu.VMEM((ext, LANE), F32), pltpu.VMEM((ext, two), F32)],
    )


def fwd_inside(l, heads, size, nx, mixed, steps, cum, cT, krs, aux, segrow, q, state, dec, cid):
    tokens, inner = mixed.shape
    rows, states = state.shape
    bits = bits_of("seq")
    return kcall(
        partial(fwd_inside_body, partial(carry_stages, bits, False, heads, size), size),
        [nx, q["w_zx"], mixed, steps, cum, cT, krs, aux, segrow, q["skip"], state, dec],
        [full(nx.shape), projection(l, 0, nx.shape[1]), cols(tokens), full(steps.shape), full(cum.shape), full(cT.shape), full(krs.shape),
         pl.BlockSpec((None, tokens, LANE), lambda p: (5, 0, 0)), full(segrow.shape), of_layer(l, q["skip"].shape, True),
         full(state.shape), full(dec.shape)], 28, (), cid,
        name="fwd_inside",
        grid=(inner // LANE,),
        out_specs=[cols(tokens), full((rows, states)), cols(tokens), full((tokens, tokens))],
        out_shape=[S((tokens, inner), F32), S((rows, states), F32), S((tokens, inner), BF16), S((tokens, tokens), F32)],
        scratch_shapes=[pltpu.VMEM((2, tokens, LANE), F32)] + carry_scratch(len(bits), rows, states, F32),
    )


def fwd_gate(ypart, entry, gate, krs, enter):
    tokens, inner = ypart.shape
    return kcall(
        fwd_gate_body, [ypart, entry, gate, krs, enter],
        [cols(tokens, WIDE), cols(tokens, WIDE), cols(tokens, WIDE), full(krs.shape), rowsb(enter.shape[1], WIDE)], 7,
        name="fwd_gate",
        grid=(inner // WIDE,),
        out_specs=[cols(tokens, WIDE), cols(tokens, WIDE), cols(tokens, WIDE), full((8, tokens))],
        out_shape=[S((tokens, inner), F32)] * 3 + [S((8, tokens), F32)],
        scratch_shapes=[pltpu.VMEM((tokens, LANE), F32)],
    )


def bwd_gate(l, gb, q, gate, y, mixed, entry, krs, r2b, side, width, after):
    tokens, inner = y.shape
    states = krs.shape[1] // 2
    return kcall(
        partial(bwd_gate_body, width), [gb, q["w_out"], gate, y, mixed, entry, krs, r2b, side, q["gate_gain"]],
        [full(gb.shape), rows_of_layer(l, q["w_out"].shape), cols(tokens, WIDE), cols(tokens, WIDE), cols(tokens, WIDE), cols(tokens, WIDE), full(krs.shape),
         full(r2b.shape), full(side.shape), of_layer(l, q["gate_gain"].shape, WIDE)], 9, after,
        name="bwd_gate",
        grid=(inner // WIDE,),
        out_specs=[cols(tokens, WIDE), cols(tokens, WIDE), cols(tokens, WIDE), rowsb(states, WIDE), cols(1, WIDE), cols(1, WIDE)],
        out_shape=[S((tokens, inner), F32), S((tokens, inner), BF16), S((tokens, inner), BF16), S((inner, states), F32),
                   S((1, inner), F32), S((1, inner), F32)],
        scratch_shapes=[pltpu.VMEM((tokens, LANE), F32)],
    )


def bwd_local(heads, size, gy, mixed, krs, cum, steps, cT, gram, entry, enter, aux, segrow, qloc, dec, cid, gb, scaled, nx, gz, under_way, also):
    tokens, inner = gy.shape
    d = gb.shape[1]
    two = krs.shape[1]
    rows, states = qloc.shape
    bits = bits_of("seq")
    blocks = lax.axis_size("seq")
    part = (blocks // 2, d // blocks, inner)
    out, z = Halving(OUT_ORDER), Halving(Z_ORDER)
    folds = [p.plan() for p in under_way]
    pairs = [x for p in under_way for x in (p.got, p.keep)]
    shapes = [(p.keep.shape[0] // 2,) + p.keep.shape[1:] for p in under_way for _ in range(2)]
    got = kcall(
        partial(bwd_local_body, partial(carry_stages, bits, True, heads, size), size, blocks, (out.order[0], z.order[0]), folds),
        [gy, mixed, krs, cum, steps, cT, gram, entry, enter, aux, segrow, qloc, dec, gb, scaled, nx, gz] + pairs,
        [cols(tokens), cols(tokens), full(krs.shape), full(cum.shape), full(steps.shape), full(cT.shape), full(gram.shape),
         cols(tokens), rowsb(two // 2), pl.BlockSpec((None, tokens, LANE), lambda p: (5, 0, 0)), full(segrow.shape),
         full(qloc.shape), full(dec.shape), full(gb.shape), full(scaled.shape), full(nx.shape), full(gz.shape)]
        + [full(x.shape) for x in pairs], 24, [p.got for p in also], cid,
        name="bwd_local",
        grid=(inner // LANE,),
        out_specs=[cols(tokens), full((tokens, LANE)), full((LANE, tokens)), full((tokens, two)), full((rows, states))]
        + [full(part)] * 4 + [full(x) for x in shapes],
        out_shape=[S((tokens, inner), F32), S((tokens, LANE), F32), S((LANE, tokens), F32), S((tokens, two), F32), S((rows, states), F32)]
        + [S(part, BF16)] * 4 + [S(x, BF16) for x in shapes],
        scratch_shapes=[pltpu.VMEM((tokens, LANE), F32), pltpu.VMEM((tokens, LANE), F32), pltpu.VMEM((tokens, tokens), F32),
                        pltpu.VMEM((tokens, tokens), F32), pltpu.VMEM((tokens, LANE), BF16), pltpu.VMEM((tokens, LANE), BF16),
                        pltpu.VMEM((d, tokens), BF16)]
        + carry_scratch(len(bits), rows, states, BF16),
    )
    out.away, out.keep, z.away, z.keep = got[5:9]
    for i, p in enumerate(under_way):
        p.away, p.keep = got[9 + 2 * i : 11 + 2 * i]
    return got[:5], out, z


def bwd_carry(l, size, gy, dvd, mixed, carr, entry, krs, cum, steps, pdt, q, ux, aux, later, enter, dd, rowT, dkr, decl, after):
    tokens, inner = gy.shape
    ext = ux.shape[0]
    two = krs.shape[1]
    return kcall(
        partial(bwd_carry_body, size),
        [gy, dvd, mixed, carr, entry, krs, cum, steps, pdt, q["dt_bias"], q["a_log"], q["skip"], ux, q["conv_x"], aux, later, enter,
         dd, rowT, dkr, decl],
        [cols(tokens), cols(tokens), cols(tokens), cols(tokens), cols(tokens), full(krs.shape), full(cum.shape), full(steps.shape),
         full(pdt.shape), of_layer(l, q["dt_bias"].shape), of_layer(l, q["a_log"].shape), of_layer(l, q["skip"].shape, True), cols(ext),
         of_layer(l, q["conv_x"].shape, True), full(aux.shape), rowsb(two // 2), rowsb(two // 2), full(dd.shape), full(rowT.shape),
         full(dkr.shape), full(decl.shape)], 11, after,
        name="bwd_carry",
        grid=(inner // LANE,),
        out_specs=[cols(8), cols(tokens), cols(16), cols(8), full((tokens, LANE)), full((8, LANE)), full((tokens, two))],
        out_shape=[S((8, inner), F32), S((tokens, inner), BF16), S((16, inner), F32), S((8, inner), F32), S((tokens, LANE), BF16),
                   S((8, LANE), F32), S((tokens, two), F32)],
        scratch_shapes=[pltpu.VMEM((ext, LANE), F32), pltpu.VMEM((tokens + 8, LANE), F32), pltpu.VMEM((tokens, LANE), F32),
                        pltpu.VMEM((tokens, LANE), F32), pltpu.VMEM((1, LANE), F32)],
    )


def head_fwd(l, gated, sq, q, h_own, extra, last, width, cid):
    tokens, inner = gated.shape
    d = q["w_out"].shape[2]
    return kcall(
        partial(head_fwd_body, l, tokens, last, width), [gated, sq, q["gate_gain"], q["w_out"], h_own, extra],
        [VM, VM, VM, pl.BlockSpec(memory_space=pl.ANY), VM, VM], 30, (), cid,
        name="head_fwd_last" if last else "head_fwd",
        out_specs=[VM] * 5,
        out_shape=[S((tokens if last else tokens + HALO, d), BF16), S((tokens // 4, d), F32), S((tokens // 4, d), F32),
                   S((tokens, LANE), F32), S((32, LANE), F32)],
        scratch_shapes=[pltpu.VMEM((3, 8, tokens), F32)] + head_scratch(tokens, d, BF16 if last else F32)
        + [pltpu.SemaphoreType.DMA((3,)), pltpu.SemaphoreType.DMA((3,)), pltpu.SemaphoreType.DMA((1,)), pltpu.SemaphoreType.DMA((1,)), pltpu.VMEM((inner, d), BF16), pltpu.SemaphoreType.DMA((1,))],
    )


def head_bwd(l, gz, gu, small, q, h_own, g_own, branch, cid, after=()):
    tokens = gz.shape[0]
    d = h_own.shape[1]
    return kcall(
        partial(head_bwd_body, l, l > 0, tokens), [gz, gu, small, q["w_zx"], q["w_small"], h_own, q["gain"], g_own, branch],
        [VM, VM, VM, pl.BlockSpec(memory_space=pl.ANY), VM, VM, VM, VM, VM], 29, after, cid,
        name="head_bwd",
        out_specs=[VM] * 4,
        out_shape=[S((tokens if l > 0 else tokens // 4, d), BF16), S((tokens // 4, d), F32), S((1, d), F32), S((32, LANE), F32)],
        scratch_shapes=head_scratch(tokens, d) + [pltpu.VMEM(q["w_zx"].shape[1:], BF16), pltpu.SemaphoreType.DMA((1,))],
    )


def maps_bwd(l, dkr, ubc, q, aux, gdt, gtail, gm8, cid, after=()):
    tokens = dkr.shape[0]
    inner = gtail.shape[1]
    tile = pltpu.VMEM((tokens, LANE), F32)
    return kcall(
        partial(maps_bwd_body, l, tokens), [dkr, ubc, q["conv_bc"], aux, gdt, gtail, gm8, q["conv_x"]],
        [VM] * 8, 14, after, cid,
        name="maps_bwd",
        out_specs=[VM] * 3,
        out_shape=[S((tokens, LANE), BF16), S((8, LANE), F32), S((16, inner), BF16)],
        scratch_shapes=[pltpu.VMEM((tokens, LANE), BF16)] * 2 + [tile, tile, tile, pltpu.VMEM((tokens + HALO, LANE), F32), pltpu.VMEM((tokens + 8, LANE), F32),
                        pltpu.VMEM((8, inner), F32), pltpu.VMEM((8, LANE), F32), pltpu.VMEM((8, LANE), F32),
                        pltpu.SemaphoreType.DMA((4,)), pltpu.SemaphoreType.DMA((4,))],
    )


def tail(sums, smalls, low, inner, cid):
    parts = len(smalls)
    quarter, d = low.shape
    plan = [(left, steps) for _, _, left, steps in sums]
    heads, n = len(bits_of("head")), len(bits_of("seq"))
    arrays, scratch, outs = [], [], []
    for got, keep, left, steps in sums:
        arrays += [got, keep]
        blocks, block, width = keep.shape
        outs.append(S((block, width), F32))
        for _ in steps:
            blocks //= 2
            buf = pltpu.VMEM((blocks, block, width), BF16)
            scratch += [buf, pltpu.VMEM((blocks, block, width), F32), buf]
        scratch += [pltpu.SemaphoreType.DMA((max(len(steps), 1),))] * 2
    return kcall(
        partial(tail_body, parts, plan), arrays + [x for part in smalls for x in part] + [low], [VM] * (2 * len(sums) + 6 * parts + 1), 45, (), cid,
        name="tail",
        out_specs=[VM] * (len(sums) + 7),
        out_shape=outs + [S((4 * quarter, d), BF16), S((parts, CONV + 1, inner), F32), S((parts, CONV + 1, 2 * LANE), F32), S((parts, inner), F32), S((parts, inner), F32),
                          S((parts, 2 * LANE), F32), S((parts, d), F32)],
        scratch_shapes=[pltpu.VMEM((parts, 16, inner), F32), pltpu.VMEM((n, parts, 16, inner), F32), pltpu.VMEM((heads, parts, 8, inner), F32),
                        pltpu.SemaphoreType.DMA((heads + n,)), pltpu.SemaphoreType.DMA((heads + n,))] + scratch
        + [pltpu.SemaphoreType.DMA((3,)), pltpu.SemaphoreType.DMA((3,))],
    )


def wgrad(lhs, rhs, bit, after=()):
    blocks = lax.axis_size("seq")
    tokens = rhs[0].shape[0]
    d = lhs.shape[1]
    width = sum(r.shape[1] for r in rhs)
    shape = (blocks // 2, d // blocks, width)
    return kcall(
        partial(wgrad_body, blocks, bit, lhs.shape[0] - tokens, len(rhs)), [lhs] + list(rhs), [VM] * (1 + len(rhs)), 3, after,
        name="wgrad",
        out_specs=[VM] * 2,
        out_shape=[S(shape, BF16)] * 2,
        scratch_shapes=[pltpu.VMEM((d, tokens), BF16)],
    )


class Halving:
    def __init__(self, order):
        bits = bits_of("seq")
        self.order = [bits[i % len(bits)] for i in order] + [b for i, b in enumerate(bits) if i not in order]
        self.left = [b for b in reversed(bits) if b != self.order[0]]
        self.step = 0
        self.got = self.away = self.keep = None

    def plan(self):
        bit = self.order[self.step]
        stride = 1 << (len(self.left) - 1 - self.left.index(bit))
        self.left.remove(bit)
        return bit, stride

    def go(self):
        self.got = swap(self.away, "seq", self.order[self.step])
        self.step += 1

    def rest(self):
        return self.got, self.keep, tuple(self.left), tuple(self.order[self.step :])

    def fold(self):
        bit, stride = self.plan()
        me = my_bit("seq", bit)
        blocks, block, width = self.keep.shape
        view = lambda v: v.reshape(blocks // (2 * stride), 2, stride, block, width)
        keep, got = view(self.keep), view(self.got)
        pick = lambda v, i: take(v, 1, i).astype(F32)
        both = [(pick(keep, i) + pick(got, i)).astype(BF16).reshape(blocks // 2, block, width) for i in (1 - me, me)]
        self.away, self.keep = both


def pad_lanes(x, to=LANE):
    return jnp.pad(x, [(0, 0)] * (x.ndim - 1) + [(0, to - x.shape[-1])])


def forward_layer(nx, h_own, extra, q, aux, segrow, layer):
    heads, size, inner = q["heads"], q["size"], q["inner"]
    (ux, ubc, krs, pdt, steps, cum, cT, mixed, entry, state, dec, decl) = fwd_mix(layer, size, nx, q, aux)
    ypart, enter, gate, gram = fwd_inside(layer, heads, size, nx, mixed, steps, cum, cT, krs, aux, segrow, q, state, dec, layer)
    y, carr, gated, sq = fwd_gate(ypart, entry, gate, krs, enter)
    width = inner * lax.axis_size("head")
    nx_next, h_new, branch, r2b, side = head_fwd(layer, gated, sq, q, h_own, extra, layer == LAYERS - 1, width, LAYERS + layer)
    stored = dict(nx=nx, gate=gate, ux=ux, ubc=ubc, krs=krs, pdt=pdt, steps=steps, cum=cum, cT=cT, gram=gram, mixed=mixed,
                  entry=entry, dec=dec, decl=decl, enter=enter, y=y, carr=carr, r2b=r2b, branch=branch, h_own=h_own)
    return nx_next, h_new, side, stored


def backward_gate(gb, side, s, q, layer, after):
    width = q["inner"] * lax.axis_size("head")
    return bwd_gate(layer, gb, q, s["gate"], s["y"], s["mixed"], s["entry"], s["krs"], s["r2b"], side, width, after)


def local(hidden_in, seg, cot, norm_gain, w_zx, w_bc, w_dt, conv_x, conv_bc, dt_bias, a_log, skip_d, gate_gain, w_out):
    tokens = hidden_in.shape[0]
    inner = w_zx.shape[3]
    heads = w_dt.shape[2]
    size = inner // heads
    rank = lax.axis_index("head")
    segf = seg.astype(F32)
    ext = jnp.concatenate([jnp.full((HALO,), segf[0], F32), segf], 0)
    vecs = [(ext[HALO - j : HALO - j + tokens] == segf).astype(F32) for j in range(1, CONV)]
    vecs += [(segf == segf[0]).astype(F32), (segf == segf[-1]).astype(F32), segf]
    aux = jnp.broadcast_to(jnp.stack(vecs, 0)[:, :, None], (len(vecs), tokens, LANE))
    segrow = segf[None]
    lanes = jnp.arange(LANE)
    even = rank % 2 == 0
    own = jnp.where(even, lanes, LANE - 1 - lanes) < LANE // 2
    dt_pad = pad_lanes(w_dt)
    tile = lax.dynamic_slice_in_dim(w_bc, (rank // 2) * LANE, LANE, 2)
    w_small = jnp.where(own[None, None], tile, jnp.where(even, jnp.roll(dt_pad, LANE // 2, axis=2), dt_pad))
    q = dict(heads=heads, size=size, inner=inner, gain=norm_gain[:, None, :], w_zx=jnp.transpose(w_zx, (0, 2, 1, 3)), w_bc=w_bc, w_dt=dt_pad,
             w_small=w_small, conv_x=conv_x, conv_bc=conv_bc, dt_bias=pad_lanes(dt_bias[:, None, :]), a_log=pad_lanes(a_log[:, None, :]),
             skip=jnp.repeat(skip_d, size, axis=1)[:, None, :], gate_gain=gate_gain[:, None, :], w_out=w_out)
    h = hidden_in.astype(F32)
    h_own = own_rows(hidden_in).astype(F32)
    cot_own = own_rows(cot)
    normed = (h * lax.rsqrt(jnp.mean(h * h, axis=1, keepdims=True) + EPS) * norm_gain[0][None]).astype(BF16)
    nx = jnp.concatenate([shift(normed[tokens - HALO :], "seq", 1), normed], 0)
    stored = []
    for l in range(LAYERS):
        extra = cot_own if l == LAYERS - 1 else q["gain"]
        nx, h_own, side, s = forward_layer(nx, h_own, extra, q, aux, segrow, l)
        stored.append(s)
    hidden_out = nx
    gb = cot
    g_own = cot_own.astype(F32)
    smalls = [None] * LAYERS
    sums = [None] * LAYERS
    pending = []
    for l in reversed(range(LAYERS)):
        s = stored[l]
        if pending:
            pending[2].fold()
            pending[2].go()
        gy, gz, scaled, qloc, ggate, gskip = backward_gate(gb, side, s, q, l, [p.away for p in pending[2:]])
        (dvd, dd, rowT, dkr, later), out, z = bwd_local(
            heads, size, gy, s["mixed"], s["krs"], s["cum"], s["steps"], s["cT"], s["gram"], s["entry"], s["enter"], aux, segrow, qloc,
            s["dec"], 2 * LAYERS + l, gb, scaled, s["nx"], gz, pending[:2], ())
        if pending:
            pending[2].keep, _ = lax.optimization_barrier((pending[2].keep, later))
            pending[2].fold()
            pending[2].go()
        for p in pending[:2]:
            p.go()
        out.go()
        z.go()
        gm8, gu, gtail, gtaps_x, gdt, gvec, dkr = bwd_carry(
            l, size, gy, dvd, s["mixed"], s["carr"], s["entry"], s["krs"], s["cum"], s["steps"], s["pdt"], q, s["ux"], aux, later, s["enter"],
            dd, rowT, dkr, s["decl"], [p.away for p in pending[2:]])
        small, gtaps_bc, gtail = maps_bwd(l, dkr, s["ubc"], q, aux, gdt, gtail, gm8, 3 * LAYERS + l)
        gu = lax.dynamic_update_slice(gu, gtail, (tokens - 16, 0))
        x = Halving((0, 1, 2))
        x.away, x.keep = wgrad(s["nx"], [gu, small], x.order[0])
        x.go()
        out.fold()
        z.fold()
        z.go()
        out.go()
        before = stored[max(l - 1, 0)]["branch"]
        gb, g_own, g_gain, side = head_bwd(l, gz, gu, small, q, s["h_own"], g_own, before, 4 * LAYERS + l, after=[p.away for p in [x, out, z]])
        smalls[l] = (gtaps_x, ggate, gskip, gvec, gtaps_bc, g_gain)
        pending = [out, z, x]
        sums[l] = pending
    under_way = [p for l in range(LAYERS) for p in reversed(sums[l])]
    done = tail([p.rest() for p in under_way], smalls, gb, inner, 5 * LAYERS)
    for p, total in zip(under_way, done):
        p.total = total
    grad_in, g_conv_x, g_conv_bc, g_gate, g_skip, g_vec, g_gain = done[len(under_way) :]
    grad_in = grad_in.astype(F32)
    g_w_zx = jnp.stack([jnp.stack([z.total, x.total[:, :inner]], 1) for _, z, x in sums], 0)
    g_small = jnp.stack([x.total[:, inner:] for _, _, x in sums], 0)
    g_w_bc = jnp.where(even, g_small[:, :, : LANE // 2], g_small[:, :, LANE // 2 :])
    g_w_dt = jnp.where(even, g_small[:, :, LANE // 2 : LANE // 2 + heads], g_small[:, :, :heads])
    g_w_out = jnp.stack([jnp.transpose(out.total) for out, _, _ in sums], 0)
    g_skip = jnp.sum(g_skip.reshape(LAYERS, heads, size), axis=2)
    part = g_gain.shape[1] // lax.axis_size("seq")
    g_gain = lax.dynamic_slice_in_dim(g_gain, lax.axis_index("seq") * part, part, 1)
    return (hidden_out, grad_in, g_gain, g_w_zx, g_w_bc, g_w_dt, g_conv_x, g_conv_bc,
            g_vec[:, :heads], g_vec[:, LANE : LANE + heads], g_skip, g_gate, g_w_out)


def solution(mesh):
    placed = (
        P("seq", None), P("seq"), P("seq", None), P(), P(None, None, None, "head"), P(), P(None, None, "head"),
        P(None, None, "head"), P(), P(None, "head"), P(None, "head"), P(None, "head"), P(None, "head"), P(None, "head", None),
    )
    return jax.shard_map(
        local,
        mesh=mesh,
        in_specs=placed,
        out_specs=(
            P("seq", None), P("seq", None), P(None, "seq"), P(None, "seq", None, "head"), P(None, "seq", "head"),
            P(None, "seq", "head"), P(None, None, "head"), P(), P(None, "head"), P(None, "head"), P(None, "head"),
            P(None, "head"), P(None, "head", "seq"),
        ),
        check_vma=False,
    )
```
